32 devices in a mesh: ty: 4 (over x, core), tx: 8 (over z, y).
Axes of the slice: x: 2, y: 2, z: 4, core: 2. Of those that a mesh axis runs over, the one named last changes fastest.
Arguments:
- gaussians: float32 [3072, 59, 128], P(('ty', 'tx')), may hold values from -14 to 18, as said below
- tile_lists: int32 [4, 8, 24], P('ty', 'tx'), may hold values from 0 to 3071, as said below
- tile_counts: int32 [4, 8], P('ty', 'tx'), may hold values from 3 to 24, as said below
- depth_order: int32 [3072], replicated, may hold values from 0 to 3071, as said below
- target: float32 [3, 128, 256], P(None, 'ty', 'tx'), may hold values from 0 to 1
Outputs:
- gaussian_grads: float32 [3072, 59, 128], P(('ty', 'tx'))
- loss: float32 [], replicated
The draws below stay inside these ranges and needn't reach their ends.
Inputs may be any that keep to these rules, and one draw needn't show every extreme that they name: `tile_lists`: entries beyond a tile's count are arbitrary ranks. The live entries of a tile are rising depth ranks of blocks owned by devices in the tile's own row of ty (block b belongs to device b // 96 of ty+tx, ty slowest). At most 3 live entries of one tile name blocks of one owner; in every row some owner is named 3 times by every tile of the row. No block is live in two entries. `tile_counts`: some tile has 24 in every draw. A permutation: depth_order[r] is the block at depth rank r. `gaussians`: row 2 (Z) lies between 1.5 and 12, row 6 (the quaternion's w) between 0.5 and 1.5.
All inputs are finite; a program needn't handle non-finite values.
Results may differ from the reference program's by a relative error of at most 0.0003.
Values sent between devices are 32-bit elements; how exact they have to be, the bound alone decides.
No kernel may reach another device: no remote copies, remote signals or barrier semaphores. Data moves between devices by JAX's collectives and lax.ppermute only.
A program may use at most 64 MiB of HBM per device.

```python
import math
import jax
import jax.numpy as jnp
from jax import lax

TILE = 32
BLOCK = 128
FIELDS = 59
GROUP = 4
LMAX = 24
CAP = 3
BPD = 96
NB = 3072
HEIGHT = 128
WIDTH = 256
N_TY = 4
N_TX = 8


FOCAL = 1000.0


def owner_order(key):
    return jax.random.permutation(key, N_TX - 1)


def layout(key):
    keys = jax.random.split(jax.random.fold_in(key, 31), 8)
    devices = N_TY * N_TX
    depth_order = jax.random.permutation(keys[0], NB).astype(jnp.int32)
    rank_of = jnp.zeros((NB,), jnp.int32).at[depth_order].set(jnp.arange(NB, dtype=jnp.int32))
    special = jax.random.randint(keys[1], (N_TY,), 0, N_TX)
    tails = jax.vmap(owner_order)(jax.random.split(keys[2], devices)).astype(jnp.int32) + 1
    order = jnp.concatenate([jnp.zeros((devices, 1), jnp.int32), tails], axis=1)
    triples = LMAX // CAP
    row_of = jnp.arange(devices, dtype=jnp.int32) // N_TX
    col_of = jnp.arange(devices, dtype=jnp.int32) % N_TX
    owner_col = (special[row_of][:, None] + order[:, :triples]) % N_TX
    owner = row_of[:, None] * N_TX + owner_col
    shift = jax.random.randint(keys[3], (devices,), 0, N_TX)
    base = CAP * ((col_of[:, None] + shift[owner]) % N_TX)
    local = base[:, :, None] + jnp.arange(CAP, dtype=jnp.int32)[None, None, :]
    blocks = (owner[:, :, None] * BPD + local).reshape(devices, LMAX)
    short = jax.random.randint(keys[5], (devices,), 0, LMAX // 3 + 1)
    counts = jnp.maximum(CAP, LMAX - short)
    busy = jax.random.randint(keys[6], (), 0, devices)
    counts = jnp.where(jnp.arange(devices) == busy, LMAX, counts).astype(jnp.int32)
    slot = jnp.arange(LMAX, dtype=jnp.int32)
    live = slot[None, :] < counts[:, None]
    keyed = jnp.where(live, rank_of[blocks], NB + slot[None, :])
    ordered = jnp.sort(keyed, axis=1)
    filler = jax.random.randint(keys[7], (devices, LMAX), 0, NB)
    lists = jnp.where(live, ordered, filler).astype(jnp.int32)
    live_blocks = jnp.where(live, blocks, NB).reshape(-1)
    home = jnp.full((NB,), -1, jnp.int32).at[live_blocks].set(jnp.repeat(jnp.arange(devices, dtype=jnp.int32), LMAX), mode='drop')
    return (lists.reshape(N_TY, N_TX, LMAX), counts.reshape(N_TY, N_TX), depth_order, home)


def draw_tile_lists(key, part):
    return layout(key)[0]


def draw_tile_counts(key, part):
    return layout(key)[1]


def draw_depth_order(key, part):
    return layout(key)[2]


def draw_gaussians(key, part):
    home = layout(key)[3]
    keys = jax.random.split(jax.random.fold_in(key, 57), 12)
    shape = (NB, BLOCK)
    reach, small, large, dimmest, brightest, tint = (0.6, 1.0, 6.0, -4.0, -1.0, 1.0)
    width = float(TILE * N_TX)
    height = float(TILE * N_TY)
    placed = (home >= 0)[:, None]
    tile_col = (jnp.maximum(home, 0) % N_TX).astype(jnp.float32)[:, None]
    tile_row = (jnp.maximum(home, 0) // N_TX).astype(jnp.float32)[:, None]
    near_u = (tile_col + 0.5) * TILE + jax.random.uniform(keys[0], shape, minval=-reach, maxval=reach) * TILE
    near_v = (tile_row + 0.5) * TILE + jax.random.uniform(keys[1], shape, minval=-reach, maxval=reach) * TILE
    pos_u = jnp.where(placed, near_u, jax.random.uniform(keys[2], shape, minval=0.0, maxval=width))
    pos_v = jnp.where(placed, near_v, jax.random.uniform(keys[3], shape, minval=0.0, maxval=height))
    depth = jnp.exp(jax.random.uniform(keys[4], shape, minval=math.log(1.5), maxval=math.log(12.0)))
    mean_x = (pos_u - 0.5 * width) * depth / FOCAL
    mean_y = (pos_v - 0.5 * height) * depth / FOCAL
    pixel_sigma = jnp.exp(jax.random.uniform(keys[5], (3,) + shape, minval=math.log(small), maxval=math.log(large)))
    log_scale = jnp.log(pixel_sigma * depth[None] / FOCAL)
    quat_real = jax.random.uniform(keys[6], shape, minval=0.5, maxval=1.5)
    quat_imag = jax.random.uniform(keys[7], (3,) + shape, minval=-0.7, maxval=0.7)
    logit = jax.random.uniform(keys[8], shape, minval=dimmest, maxval=brightest)
    base_color = jax.random.uniform(keys[9], (3,) + shape, minval=-tint, maxval=tint)
    detail = jax.random.uniform(keys[10], (45,) + shape, minval=-0.3, maxval=0.3)
    rows = jnp.concatenate([jnp.stack([mean_x, mean_y, depth]), log_scale, quat_real[None], quat_imag, logit[None], base_color, detail], axis=0)
    return jnp.transpose(rows, (1, 0, 2)).astype(jnp.float32)


def block_scale(stream_key, extent, pieces, least, largest):
    level, own = 1.0, jax.random.fold_in(stream_key, 6)
    for dim, blocks in pieces:
        draws = jnp.exp(jax.random.uniform(jax.random.fold_in(own, dim), (blocks,), jnp.float32, least / len(pieces), largest / len(pieces)))
        level = level * jnp.repeat(draws, extent[dim] // blocks).reshape([-1 if axis == dim else 1 for axis in range(len(extent))])
    return level


def setup_inputs(seed: int = 0) -> dict:
    streams_of = jax.random.split(jax.random.key(seed), 6)
    gaussians = draw_gaussians(jax.random.fold_in(streams_of[5], 71), 0)
    tile_lists = draw_tile_lists(jax.random.fold_in(streams_of[5], 71), 0)
    tile_counts = draw_tile_counts(jax.random.fold_in(streams_of[5], 71), 0)
    depth_order = draw_depth_order(jax.random.fold_in(streams_of[5], 71), 0)
    target = jnp.clip(1.0 * jax.random.uniform(streams_of[4], (3, HEIGHT, WIDTH), jnp.float32) ** block_scale(streams_of[4], (3, HEIGHT, WIDTH), ((1, 4), (2, 8)), -0.2, 0.2), 0.0, 1.0)
    return {"gaussians": gaussians, "tile_lists": tile_lists, "tile_counts": tile_counts, "depth_order": depth_order, "target": target}


FOCAL = 1000.0
LOW_PASS = 0.3
STRUCT_WEIGHT = 0.2
LUMA_TERM = 0.0001
CONTRAST_TERM = 0.0009
ROBUST_TERM = 1e-06
HARMONIC_ZERO = 0.28209479177387814
HARMONIC_ONE = 0.4886025119029199
HARMONIC_TWO = (1.0925484305920792, -1.0925484305920792, 0.31539156525252005, -1.0925484305920792, 0.5462742152960396)
HARMONIC_THREE = (-0.5900435899266435, 2.890611442640554, -0.4570457994644658, 0.3731763325901154, -0.4570457994644658, 1.445305721320277, -0.5900435899266435)

def harmonics(dir_x, dir_y, dir_z):
    square_x = dir_x * dir_x
    square_y = dir_y * dir_y
    square_z = dir_z * dir_z
    pair_xy = dir_x * dir_y
    pair_yz = dir_y * dir_z
    pair_xz = dir_x * dir_z
    return jnp.stack([HARMONIC_ZERO * jnp.ones_like(dir_x), -HARMONIC_ONE * dir_y, HARMONIC_ONE * dir_z, -HARMONIC_ONE * dir_x, HARMONIC_TWO[0] * pair_xy, HARMONIC_TWO[1] * pair_yz, HARMONIC_TWO[2] * (2.0 * square_z - square_x - square_y), HARMONIC_TWO[3] * pair_xz, HARMONIC_TWO[4] * (square_x - square_y), HARMONIC_THREE[0] * dir_y * (3.0 * square_x - square_y), HARMONIC_THREE[1] * pair_xy * dir_z, HARMONIC_THREE[2] * dir_y * (4.0 * square_z - square_x - square_y), HARMONIC_THREE[3] * dir_z * (2.0 * square_z - 3.0 * square_x - 3.0 * square_y), HARMONIC_THREE[4] * dir_x * (4.0 * square_z - square_x - square_y), HARMONIC_THREE[5] * dir_z * (square_x - square_y), HARMONIC_THREE[6] * dir_x * (square_x - 3.0 * square_y)], axis=1)

def project(raw, center_x, center_y):
    count_rows = raw.shape[0]
    block = raw.shape[2]
    mean_x, mean_y, mean_z = (raw[:, 0], raw[:, 1], raw[:, 2])
    scale = jnp.exp(raw[:, 3:6])
    quat = raw[:, 6:10] / jnp.sqrt(lax.optimization_barrier(jnp.sum(raw[:, 6:10] * raw[:, 6:10], axis=1, keepdims=True)))
    real, imag_i, imag_j, imag_k = (quat[:, 0], quat[:, 1], quat[:, 2], quat[:, 3])
    rotation = [[1.0 - 2.0 * (imag_j * imag_j + imag_k * imag_k), 2.0 * (imag_i * imag_j - real * imag_k), 2.0 * (imag_i * imag_k + real * imag_j)], [2.0 * (imag_i * imag_j + real * imag_k), 1.0 - 2.0 * (imag_i * imag_i + imag_k * imag_k), 2.0 * (imag_j * imag_k - real * imag_i)], [2.0 * (imag_i * imag_k - real * imag_j), 2.0 * (imag_j * imag_k + real * imag_i), 1.0 - 2.0 * (imag_i * imag_i + imag_j * imag_j)]]
    scaled = [[rotation[row][col] * scale[:, col] for col in range(3)] for row in range(3)]
    sigma = [[sum((scaled[row][col] * scaled[other][col] for col in range(3))) for other in range(3)] for row in range(3)]
    inverse_z = 1.0 / mean_z
    jac_diag = FOCAL * inverse_z
    jac_xz = -FOCAL * mean_x * inverse_z * inverse_z
    jac_yz = -FOCAL * mean_y * inverse_z * inverse_z
    row_u = [jac_diag * sigma[0][col] + jac_xz * sigma[2][col] for col in range(3)]
    row_v = [jac_diag * sigma[1][col] + jac_yz * sigma[2][col] for col in range(3)]
    cov_uu = row_u[0] * jac_diag + row_u[2] * jac_xz + LOW_PASS
    cov_uv = row_u[1] * jac_diag + row_u[2] * jac_yz
    cov_vv = row_v[1] * jac_diag + row_v[2] * jac_yz + LOW_PASS
    determinant = cov_uu * cov_vv - cov_uv * cov_uv
    pos_u = FOCAL * mean_x * inverse_z + center_x
    pos_v = FOCAL * mean_y * inverse_z + center_y
    opacity = 0.99 * jax.nn.sigmoid(raw[:, 10])
    length = jnp.sqrt(mean_x * mean_x + mean_y * mean_y + mean_z * mean_z)
    basis = harmonics(mean_x / length, mean_y / length, mean_z / length)
    coeffs = raw[:, 11:59].reshape(count_rows, 16, 3, block)
    color = 0.5 + lax.optimization_barrier(jnp.sum(coeffs * basis[:, :, None, :], axis=1))
    shape_rows = jnp.stack([pos_u, pos_v, cov_vv / determinant, -cov_uv / determinant, cov_uu / determinant, opacity], axis=1)
    return jnp.concatenate([shape_rows, color], axis=1)

def composite(flat, live, pixel_x, pixel_y):
    delta_x = pixel_x[None, :] - flat[0][:, None]
    delta_y = pixel_y[None, :] - flat[1][:, None]
    power = flat[2][:, None] * delta_x * delta_x + 2.0 * flat[3][:, None] * delta_x * delta_y + flat[4][:, None] * delta_y * delta_y
    alpha = (live * flat[5])[:, None] * jnp.exp(-0.5 * power)
    keep = jnp.log1p(-alpha)
    before = jnp.cumsum(keep, axis=0) - keep
    weight = alpha * jnp.exp(before)
    color = jnp.dot(flat[6:9], weight, precision=lax.Precision.HIGHEST, preferred_element_type=jnp.float32)
    return (color, lax.optimization_barrier(jnp.sum(keep, axis=0)))

def to_groups(slot_flat, live):
    lmax, fields, block = slot_flat.shape
    steps_total = lmax // GROUP
    groups = slot_flat.reshape(steps_total, GROUP, fields, block).transpose(0, 2, 1, 3).reshape(steps_total, fields, GROUP * block)
    live_groups = jnp.repeat(live.astype(slot_flat.dtype), block).reshape(steps_total, GROUP * block)
    return (groups, live_groups)

def from_groups(grads, block):
    steps_total, fields, spread = grads.shape
    return grads.reshape(steps_total, fields, GROUP, block).transpose(0, 2, 1, 3).reshape(steps_total * GROUP, fields, block)

def render_forward(groups, live_groups, used, pixel_x, pixel_y):
    pixels = pixel_x.shape[0]

    def advance(index, carry):
        color, log_light, store = carry
        group_color, log_keep = composite(groups[index], live_groups[index], pixel_x, pixel_y)
        store = store.at[index].set(log_light)
        return (color + jnp.exp(log_light)[None, :] * group_color, log_light + log_keep, store)
    start = (jnp.zeros((3, pixels), jnp.float32), jnp.zeros((pixels,), jnp.float32), jnp.zeros((groups.shape[0], pixels), jnp.float32))
    color, final_light, store = lax.fori_loop(0, used, advance, start)
    return (color, store)

def render_backward(groups, live_groups, used, store, pixel_x, pixel_y, color_grad):

    def retreat(step, carry):
        behind, grads = carry
        index = used - 1 - step
        live_now = live_groups[index]

        def shade(flat):
            return composite(flat, live_now, pixel_x, pixel_y)
        (group_color, log_keep), pull = jax.vjp(shade, groups[index])
        light = jnp.exp(store[index])
        passed = light * jnp.exp(log_keep)
        flat_grad = pull((light[None, :] * color_grad, passed * lax.optimization_barrier(jnp.sum(color_grad * behind, axis=0))))[0]
        behind = group_color + jnp.exp(log_keep)[None, :] * behind
        return (behind, grads.at[index].set(flat_grad))
    start = (jnp.zeros_like(color_grad), jnp.zeros_like(groups))
    return lax.fori_loop(0, used, retreat, start)[1]

def window_taps():
    offsets = jnp.arange(11, dtype=jnp.float32) - 5.0
    taps = jnp.exp(-offsets * offsets / 4.5)
    return taps / jnp.sum(taps)

def filtered(field, taps):
    rows = field.shape[-2] - 10
    cols = field.shape[-1] - 10
    sideways = sum((taps[shift] * field[..., :, shift:shift + cols] for shift in range(11)))
    return sum((taps[shift] * sideways[..., shift:shift + rows, :] for shift in range(11)))

def similarity(mean_a, mean_b, square_a, square_b, cross):
    var_a = square_a - mean_a * mean_a
    var_b = square_b - mean_b * mean_b
    covar = cross - mean_a * mean_b
    top = (2.0 * mean_a * mean_b + LUMA_TERM) * (2.0 * covar + CONTRAST_TERM)
    bottom = (mean_a * mean_a + mean_b * mean_b + LUMA_TERM) * (var_a + var_b + CONTRAST_TERM)
    return top / bottom

def objective(image, target):
    taps = window_taps()

    def padded(field):
        return jnp.pad(field, ((0, 0), (5, 5), (5, 5)))
    score = similarity(filtered(padded(image), taps), filtered(padded(target), taps), filtered(padded(image * image), taps), filtered(padded(target * target), taps), filtered(padded(image * target), taps))
    gap = image - target
    robust = jnp.sqrt(gap * gap + ROBUST_TERM)
    return jnp.sum((1.0 - STRUCT_WEIGHT) * robust + STRUCT_WEIGHT * (1.0 - score))

def reference(gaussians, tile_lists, tile_counts, depth_order, target):
    height = TILE * N_TY
    width = TILE * N_TX
    center_x = 0.5 * width
    center_y = 0.5 * height

    def projector(raw):
        return project(raw, center_x, center_y)

    def tile_inputs(index):
        tile_row = index // N_TX
        tile_col = index % N_TX
        ranks = tile_lists[tile_row, tile_col]
        count = tile_counts[tile_row, tile_col]
        blocks = depth_order[ranks]
        raw = gaussians[blocks]
        live = jnp.arange(LMAX, dtype=jnp.int32) < count
        offsets = jnp.arange(TILE * TILE, dtype=jnp.int32)
        pixel_x = (tile_col * TILE + offsets % TILE).astype(jnp.float32) + 0.5
        pixel_y = (tile_row * TILE + offsets // TILE).astype(jnp.float32) + 0.5
        used = (count + GROUP - 1) // GROUP
        return (blocks, raw, live, pixel_x, pixel_y, used)

    def forward_tile(index):
        blocks, raw, live, pixel_x, pixel_y, used = tile_inputs(index)
        groups, live_groups = to_groups(projector(raw), live)
        return render_forward(groups, live_groups, used, pixel_x, pixel_y)
    tiles = jnp.arange(N_TY * N_TX, dtype=jnp.int32)
    colors, stores = lax.map(forward_tile, tiles)
    image = colors.reshape(N_TY, N_TX, 3, TILE, TILE).transpose(2, 0, 3, 1, 4).reshape(3, height, width)

    def scored(picture):
        return objective(picture, target)
    total, pull_total = jax.vjp(scored, image)
    image_grad = pull_total(jnp.ones_like(total))[0]
    tile_grads = image_grad.reshape(3, N_TY, TILE, N_TX, TILE).transpose(1, 3, 0, 2, 4).reshape(N_TY * N_TX, 3, TILE * TILE)

    def backward_tile(inputs):
        index, store, color_grad = inputs
        blocks, raw, live, pixel_x, pixel_y, used = tile_inputs(index)
        slot_flat, pull_raw = jax.vjp(projector, raw)
        groups, live_groups = to_groups(slot_flat, live)
        flat_grads = render_backward(groups, live_groups, used, store, pixel_x, pixel_y, color_grad)
        raw_grads = pull_raw(from_groups(flat_grads, BLOCK))[0]
        return (raw_grads * live.astype(raw_grads.dtype)[:, None, None], blocks)
    raw_grads, blocks = lax.map(backward_tile, (tiles, stores, tile_grads))
    gaussian_grads = jnp.zeros_like(gaussians).at[blocks.reshape(-1)].add(raw_grads.reshape(-1, FIELDS, BLOCK))
    return (gaussian_grads, total / (3.0 * height * width))
```

```python
import functools

import jax
import jax.numpy as jnp
import ml_dtypes
import numpy as np
from jax import lax
from jax.experimental import pallas as pl
from jax.experimental.pallas import tpu as pltpu
from jax.sharding import PartitionSpec as P

CAP = 3
SEGS = 8
LANES = 128
CHUNK = 128
STEPS = CHUNK // SEGS
RIM = 5
TAPS = 2 * RIM + 1
LOG2E = 1.4426950408889634
LN2 = 0.6931471805599453
DARK = -1e30

FOCAL = 1000.0
LOW_PASS = 0.3
STRUCT_WEIGHT = 0.2
LUMA_TERM = 0.0001
CONTRAST_TERM = 0.0009
ROBUST_TERM = 1e-06
HARMONIC_ZERO = 0.28209479177387814
HARMONIC_ONE = 0.4886025119029199
HARMONIC_TWO = (
    1.0925484305920792,
    -1.0925484305920792,
    0.31539156525252005,
    -1.0925484305920792,
    0.5462742152960396,
)
HARMONIC_THREE = (
    -0.5900435899266435,
    2.890611442640554,
    -0.4570457994644658,
    0.3731763325901154,
    -0.4570457994644658,
    1.445305721320277,
    -0.5900435899266435,
)

HIGH = lax.Precision.HIGHEST
F32 = jnp.float32
BF16 = jnp.bfloat16
ANY = pl.BlockSpec(memory_space=pl.ANY)
SMEM = pl.BlockSpec(memory_space=pltpu.SMEM)
VMEM = pl.BlockSpec(memory_space=pltpu.VMEM)
PARAMS = pltpu.CompilerParams(vmem_limit_bytes=56 * 1024 * 1024)


def harmonics(x, y, z):
    xx, yy, zz = x * x, y * y, z * z
    xy, yz, xz = x * y, y * z, x * z
    return [
        HARMONIC_ZERO * jnp.ones_like(x),
        -HARMONIC_ONE * y,
        HARMONIC_ONE * z,
        -HARMONIC_ONE * x,
        HARMONIC_TWO[0] * xy,
        HARMONIC_TWO[1] * yz,
        HARMONIC_TWO[2] * (2.0 * zz - xx - yy),
        HARMONIC_TWO[3] * xz,
        HARMONIC_TWO[4] * (xx - yy),
        HARMONIC_THREE[0] * y * (3.0 * xx - yy),
        HARMONIC_THREE[1] * xy * z,
        HARMONIC_THREE[2] * y * (4.0 * zz - xx - yy),
        HARMONIC_THREE[3] * z * (2.0 * zz - 3.0 * xx - 3.0 * yy),
        HARMONIC_THREE[4] * x * (4.0 * zz - xx - yy),
        HARMONIC_THREE[5] * z * (xx - yy),
        HARMONIC_THREE[6] * x * (xx - 3.0 * yy),
    ]


def directions(x, y, z):
    length = jnp.sqrt(x * x + y * y + z * z)
    return harmonics(x / length, y / length, z / length)


def exponent(mean_x, mean_y, mean_z, log_scale, quat, log_opacity, shift_x, shift_y):
    scale = [jnp.exp(s) for s in log_scale]
    norm = jnp.sqrt(quat[0] * quat[0] + quat[1] * quat[1] + quat[2] * quat[2] + quat[3] * quat[3])
    w, i, j, k = (q / norm for q in quat)
    rotation = [
        [1.0 - 2.0 * (j * j + k * k), 2.0 * (i * j - w * k), 2.0 * (i * k + w * j)],
        [2.0 * (i * j + w * k), 1.0 - 2.0 * (i * i + k * k), 2.0 * (j * k - w * i)],
        [2.0 * (i * k - w * j), 2.0 * (j * k + w * i), 1.0 - 2.0 * (i * i + j * j)],
    ]
    scaled = [[rotation[r][c] * scale[c] for c in range(3)] for r in range(3)]

    def sigma(r, c):
        return scaled[r][0] * scaled[c][0] + scaled[r][1] * scaled[c][1] + scaled[r][2] * scaled[c][2]

    s00, s01, s02, s11, s12, s22 = (
        sigma(0, 0), sigma(0, 1), sigma(0, 2), sigma(1, 1), sigma(1, 2), sigma(2, 2),
    )
    inverse_z = 1.0 / mean_z
    diag = FOCAL * inverse_z
    jac_xz = -FOCAL * mean_x * inverse_z * inverse_z
    jac_yz = -FOCAL * mean_y * inverse_z * inverse_z
    u0, u1, u2 = diag * s00 + jac_xz * s02, diag * s01 + jac_xz * s12, diag * s02 + jac_xz * s22
    v1, v2 = diag * s11 + jac_yz * s12, diag * s12 + jac_yz * s22
    cov_uu = u0 * diag + u2 * jac_xz + LOW_PASS
    cov_uv = u1 * diag + u2 * jac_yz
    cov_vv = v1 * diag + v2 * jac_yz + LOW_PASS
    determinant = cov_uu * cov_vv - cov_uv * cov_uv
    pos_u = FOCAL * mean_x * inverse_z + shift_x
    pos_v = FOCAL * mean_y * inverse_z + shift_y
    half = -0.5 * LOG2E
    xx = half * (cov_vv / determinant)
    xy = (-2.0 * half) * (cov_uv / determinant)
    yy = half * (cov_uu / determinant)
    x1 = -2.0 * xx * pos_u - xy * pos_v
    y1 = -2.0 * yy * pos_v - xy * pos_u
    one = xx * pos_u * pos_u + xy * pos_u * pos_v + yy * pos_v * pos_v + log_opacity
    return xx, xy, yy, x1, y1, one


def tile_shifts(across, side, height, width):
    column = lax.broadcasted_iota(jnp.int32, (across, LANES), 0).astype(F32)
    column = jnp.concatenate([column] * CAP, axis=0)
    row = lax.axis_index("ty").astype(F32)
    shift_x = (0.5 * width - 0.5 * side - 0.5) - side * column
    shift_y = jnp.full(column.shape, (0.5 * height - 0.5 * side - 0.5) - side * row, F32)
    return shift_x, shift_y


def request_kernel(owned, across, lists, count, order, request, slot, seen):
    base = lax.axis_index("ty") * across
    for o in range(across):
        seen[o] = 0
        for c in range(CAP):
            request[o * CAP + c] = -1
    used = count[0, 0]

    def entry(k, _):
        @pl.when(k < used)
        def _():
            block = order[lists[0, 0, k]]
            home = block // owned
            local = block - home * owned
            home = home - base
            at = seen[home]
            seen[home] = at + 1
            request[home * CAP + at] = local
            slot[k] = home * CAP + at

        @pl.when(k >= used)
        def _():
            slot[k] = -1

        return 0

    lax.fori_loop(0, slot.shape[0], entry, 0)


def serve_kernel(across, side, height, width, asked, gaussians, send, raw, empty, zeros, in_sem, zero_sem):
    slots = across * CAP
    for s in range(slots):
        c, t = divmod(s, across)
        index = jnp.maximum(asked[t * CAP + c], 0)
        pltpu.make_async_copy(gaussians.at[index], raw.at[s], in_sem.at[s]).start()
    zeros[...] = jnp.zeros_like(zeros)
    span = zeros.shape[0]
    fills = empty.shape[0] // span
    for n in range(fills):
        pltpu.make_async_copy(zeros, empty.at[pl.ds(n * span, span)], zero_sem.at[n]).start()
    for s in range(slots):
        pltpu.make_async_copy(gaussians.at[0], raw.at[s], in_sem.at[s]).wait()
    field = [raw[:, f, :] for f in range(11)]
    shift_x, shift_y = tile_shifts(across, side, height, width)
    light = -LOG2E * jnp.log(1.0 + jnp.exp(-field[10])) + float(np.log2(0.99))
    light = jnp.maximum(light, DARK)
    rows = list(
        exponent(field[0], field[1], field[2], field[3:6], field[6:10], light, shift_x, shift_y)
    )
    basis = directions(field[0], field[1], field[2])
    for ch in range(3):
        color = 0.5 + basis[0] * raw[:, 11 + ch, :]
        for m in range(1, 16):
            color = color + basis[m] * raw[:, 11 + 3 * m + ch, :]
        rows.append(color)
    for c in range(CAP):
        for f in range(9):
            at = c * 8 + f if f < 8 else CAP * 8 + c
            send[:, at, :] = rows[f][c * across : (c + 1) * across]
    for n in range(fills):
        pltpu.make_async_copy(zeros, empty.at[pl.ds(n * span, span)], zero_sem.at[n]).wait()


def repeated(x, times):
    return jnp.concatenate([x] * times, axis=1)


def forward_kernel(
    slot, recv, planes, target, table, checks, prefix, behind, dense, spread, buf_a, buf_b, ends
):
    lmax = slot.shape[0]
    per = lmax // SEGS
    pixels = prefix.shape[1]
    groups = pixels // LANES
    zero_rows = jnp.zeros((7, LANES), F32)
    dead = jnp.where(lax.broadcasted_iota(jnp.int32, (16, LANES), 0) == 5, DARK, 0.0)
    is_color = lax.broadcasted_iota(jnp.int32, (16, LANES), 0) >= 6
    filler = jnp.zeros((LANES - 48, LANES), F32)

    def place(k, _):
        s = slot[k]
        live = s >= 0
        s = jnp.maximum(s, 0)
        o = s // CAP
        c = s - o * CAP
        head = recv[o, pl.ds(pl.multiple_of(c * 8, 8), 8), :]
        tail = recv[o, pl.ds(CAP * 8 + c, 1), :]
        rows = jnp.concatenate([head, tail, zero_rows], axis=0)
        rows = jnp.where(live, rows, dead)
        hi = rows.astype(BF16).astype(F32)
        rest = rows - hi
        mid = rest.astype(BF16).astype(F32)
        low = (rest - mid).astype(BF16).astype(F32)
        third = jnp.where(is_color, hi, low)
        stacked = jnp.concatenate([hi, mid, third, filler], axis=0)
        seg = k // per
        m = k - seg * per
        spread[pl.ds(m * (SEGS * LANES) + seg, LANES, stride=SEGS), :] = stacked.T
        return 0

    lax.fori_loop(0, lmax, place, 0)

    def products(n, buf):
        part = spread[pl.ds(pl.multiple_of(n * CHUNK, CHUNK), CHUNK), :].astype(BF16)
        table[pl.ds(pl.multiple_of(n * CHUNK, CHUNK), CHUNK), :] = part
        buf[...] = jnp.dot(part, planes[...], preferred_element_type=F32)

    def blend(n, buf, carry):
        light, red, green, blue = carry
        checks[n] = light
        for i in range(STEPS):
            rows = pl.ds(i * SEGS, SEGS)
            weight = light * jnp.exp2(buf[rows, :pixels])
            light = light - weight
            red = red + weight * repeated(buf[rows, pixels : pixels + LANES], groups)
            green = green + weight * repeated(buf[rows, pixels + LANES : pixels + 2 * LANES], groups)
            blue = blue + weight * repeated(
                buf[rows, pixels + 2 * LANES : pixels + 3 * LANES], groups
            )
        return light, red, green, blue

    products(0, buf_a)
    chunks = lmax * LANES // CHUNK

    def pair(h, carry):
        n = 2 * h
        products(n + 1, buf_b)
        carry = blend(n, buf_a, carry)
        products(jnp.minimum(n + 2, chunks - 1), buf_a)
        return blend(n + 1, buf_b, carry)

    start = (jnp.ones((SEGS, pixels), F32),) + (jnp.zeros((SEGS, pixels), F32),) * 3
    carry = lax.fori_loop(0, chunks // 2, pair, start)
    for f in range(4):
        ends[f] = carry[f]
    ahead = jnp.ones((1, pixels), F32)
    for seg in range(SEGS):
        prefix[pl.ds(seg, 1), :] = ahead
        ahead = ahead * ends[0, pl.ds(seg, 1), :]
    for ch in range(3):
        seen = jnp.zeros((1, pixels), F32)
        for seg in reversed(range(SEGS)):
            behind[ch, pl.ds(seg, 1), :] = seen
            seen = ends[1 + ch, pl.ds(seg, 1), :] + ends[0, pl.ds(seg, 1), :] * seen
        for j in range(groups):
            dense[pl.ds(ch * groups + j, 1), :] = seen[:, j * LANES : (j + 1) * LANES]
    dense[3 * groups :, :] = target[...]


def similarity(mean_a, mean_b, square_a, square_b, cross):
    var_a = square_a - mean_a * mean_a
    var_b = square_b - mean_b * mean_b
    covar = cross - mean_a * mean_b
    top = (2.0 * mean_a * mean_b + LUMA_TERM) * (2.0 * covar + CONTRAST_TERM)
    bottom = (mean_a * mean_a + mean_b * mean_b + LUMA_TERM) * (var_a + var_b + CONTRAST_TERM)
    return top / bottom


def score_kernel(side, height, width, near, fa, fb, fc, fd, slope, loss):
    rows3 = near[0].shape[0] // 2
    groups = rows3 // 3
    fold = LANES // side
    fields = [[], [], [], [], []]
    for v in range(3):
        strip = jnp.concatenate([near[3 * v + h][...] for h in range(3)], axis=1)
        image, target = strip[:rows3], strip[rows3:]
        for f, plane in enumerate([image, target, image * image, target * target, image * target]):
            fields[f].append(plane)
    stack = jnp.concatenate([fields[f][v] for f in range(5) for v in range(3)], axis=0)
    wide = jnp.dot(stack, fa[...], precision=HIGH, preferred_element_type=F32)
    columns = []
    for f in range(5):
        for ch in range(3):
            parts = []
            for t in range(fold):
                for v in range(3):
                    at = (f * 3 + v) * rows3 + ch * groups
                    parts.append(wide[at : at + groups, t * LANES : (t + 1) * LANES])
            columns.append(jnp.concatenate(parts, axis=0))
    tall = jnp.concatenate(columns, axis=1)
    maps = jnp.dot(fb[...], tall, precision=HIGH, preferred_element_type=F32)
    span = 3 * LANES
    score, pull = jax.vjp(similarity, *[maps[:, f * span : (f + 1) * span] for f in range(5)])
    parts = pull(jnp.full(score.shape, -STRUCT_WEIGHT, F32))
    row = lax.broadcasted_iota(jnp.int32, score.shape, 0)
    col = lax.broadcasted_iota(jnp.int32, (score.shape[0], LANES), 1)
    col = jnp.concatenate([col] * 3, axis=1)
    row_at = row - RIM + lax.axis_index("ty") * side
    col_at = col - RIM + lax.axis_index("tx") * side
    reach = side + 2 * RIM
    inside = (
        (row_at >= 0) & (row_at < height) & (col_at >= 0) & (col_at < width)
        & (row < reach) & (col < reach)
    )
    own = (row >= RIM) & (row < RIM + side) & (col >= RIM) & (col < RIM + side)
    coeffs = jnp.concatenate(
        [jnp.where(inside, parts[f], 0.0) for f in (0, 2, 4)], axis=1
    )
    low = jnp.dot(fc[...], coeffs, precision=HIGH, preferred_element_type=F32)
    rows = []
    for n in range(9):
        rows.append(
            jnp.concatenate(
                [
                    low[t * groups : (t + 1) * groups, n * LANES : (n + 1) * LANES]
                    for t in range(fold)
                ],
                axis=1,
            )
        )
    smooth = jnp.dot(
        jnp.concatenate(rows, axis=0), fd[...], precision=HIGH, preferred_element_type=F32
    )
    image, target = near[4][:rows3, :], near[4][rows3:, :]
    gap = image - target
    robust = jnp.sqrt(gap * gap + ROBUST_TERM)
    slope[...] = (
        smooth[:rows3]
        + 2.0 * image * smooth[rows3 : 2 * rows3]
        + target * smooth[2 * rows3 :]
        + (1.0 - STRUCT_WEIGHT) * gap / robust
    )
    total = (1.0 - STRUCT_WEIGHT) * jnp.sum(robust) + STRUCT_WEIGHT * jnp.sum(
        jnp.where(own, 1.0 - score, 0.0)
    )
    loss[0] = total


def score_entry(side, height, width, *refs):
    score_kernel(side, height, width, refs[:9], *refs[9:])


def backward_kernel(
    slot, table, checks, prefix, behind, slope, planes, reduce, reply,
    rhs, wide, grows, buf_a, buf_b, weights, alphas, sums, moments,
):
    lmax = slot.shape[0]
    per = lmax // SEGS
    pixels = prefix.shape[1]
    groups = pixels // LANES
    chunks = lmax * LANES // CHUNK
    wide[...] = jnp.zeros_like(wide)
    for ch in range(3):
        for j in range(groups):
            lanes = pl.ds(j * LANES, LANES)
            wide[pl.ds(6 + ch, 1), lanes] = slope[pl.ds(ch * groups + j, 1), :]
    for ch in range(3):
        row = wide[pl.ds(6 + ch, 1), :]
        hi = row.astype(BF16).astype(F32)
        grows[ch] = jnp.broadcast_to(row, (SEGS, pixels))
        wide[pl.ds(6 + ch, 1), :] = hi
        wide[pl.ds(22 + ch, 1), :] = hi
        wide[pl.ds(38 + ch, 1), :] = row - hi
    rhs[:, :pixels] = planes[:, :pixels]
    rhs[:, pixels:] = wide[...].astype(BF16)

    def products(n, buf):
        part = table[pl.ds(pl.multiple_of(n * CHUNK, CHUNK), CHUNK), :]
        buf[...] = jnp.dot(part, rhs[...], preferred_element_type=F32)

    def sweep(n, buf, back):
        light = checks[n] * prefix[...]
        for i in range(STEPS):
            rows = pl.ds(i * SEGS, SEGS)
            alpha = jnp.exp2(buf[rows, :pixels])
            weight = light * alpha
            light = light - weight
            weights[rows, :] = weight
            alphas[rows, :] = alpha
        for i in reversed(range(STEPS)):
            rows = pl.ds(i * SEGS, SEGS)
            weight = weights[rows, :]
            gap = buf[rows, pixels:] - back
            back = back + alphas[rows, :] * gap
            pull = weight * gap
            zero = one = two = None
            for j in reversed(range(groups)):
                piece = pull[:, j * LANES : (j + 1) * LANES]
                zero = piece if zero is None else zero + piece
                if j > 0:
                    one = zero if one is None else one + zero
                    two = one if two is None else two + one
            sums[rows, 0:LANES] = zero
            sums[rows, LANES : 2 * LANES] = one
            sums[rows, 2 * LANES : 3 * LANES] = two
            for ch in range(3):
                tint = weight * grows[ch]
                total = tint[:, :LANES]
                for j in range(1, groups):
                    total = total + tint[:, j * LANES : (j + 1) * LANES]
                sums[rows, (3 + ch) * LANES : (4 + ch) * LANES] = total
        whole = sums[...]
        hi = whole.astype(BF16)
        low = (whole - hi.astype(F32)).astype(BF16)
        moments[pl.ds(pl.multiple_of(n * CHUNK, CHUNK), CHUNK), :] = jnp.dot(
            hi, reduce[...], preferred_element_type=F32
        ) + jnp.dot(low, reduce[...], preferred_element_type=F32)
        return back

    back = behind[0] * grows[0] + behind[1] * grows[1] + behind[2] * grows[2]
    products(chunks - 1, buf_a)

    def pair(h, back):
        n = chunks - 1 - 2 * h
        products(n - 1, buf_b)
        back = sweep(n, buf_a, back)
        products(jnp.maximum(n - 2, 0), buf_a)
        return sweep(n - 1, buf_b, back)

    lax.fori_loop(0, chunks // 2, pair, back)

    def collect(k, _):
        s = slot[k]

        @pl.when(s >= 0)
        def _():
            o = s // CAP
            c = s - o * CAP
            seg = k // per
            m = k - seg * per
            block = moments[pl.ds(m * (SEGS * LANES) + seg, LANES, stride=SEGS), :].T
            reply[o, pl.ds(pl.multiple_of(c * 8, 8), 8), :] = block[:8]
            reply[o, pl.ds(CAP * 8 + c, 1), :] = block[8:9]

        return 0

    lax.fori_loop(0, lmax, collect, 0)


def gather_kernel(across, side, height, width, asked, got, raw, empty, grads, pieces, sem):
    slots = across * CAP
    field = [raw[:, f, :] for f in range(11)]
    shift_x, shift_y = tile_shifts(across, side, height, width)

    def received(f):
        at = [c * 8 + f if f < 8 else CAP * 8 + c for c in range(CAP)]
        return jnp.concatenate([got[:, a, :] for a in at], axis=0)

    def shaped(x, y, z, log_scale, quat):
        light = jnp.zeros_like(x)
        return exponent(x, y, z, log_scale, quat, light, shift_x, shift_y)

    _, pull = jax.vjp(shaped, *field[:3], field[3:6], field[6:10])
    moments = [LN2 * received(f) for f in range(6)]
    gx, gy, gz, gscale, gquat = pull(tuple(moments))
    basis, pull_basis = jax.vjp(directions, *field[:3])
    tints = [received(6 + ch) for ch in range(3)]
    tilts = []
    for m in range(16):
        tilt = None
        for ch in range(3):
            term = tints[ch] * raw[:, 11 + 3 * m + ch, :]
            tilt = term if tilt is None else tilt + term
            pieces[:, 11 + 3 * m + ch, :] = tints[ch] * basis[m]
        tilts.append(tilt)
    dx, dy, dz = pull_basis(tilts)
    pieces[:, 0, :] = gx + dx
    pieces[:, 1, :] = gy + dy
    pieces[:, 2, :] = gz + dz
    for f in range(3):
        pieces[:, 3 + f, :] = gscale[f]
    for f in range(4):
        pieces[:, 6 + f, :] = gquat[f]
    pieces[:, 10, :] = moments[5] * (LOG2E / (1.0 + jnp.exp(field[10])))

    for s in range(slots):
        c, t = divmod(s, across)
        index = asked[t * CAP + c]

        @pl.when(index >= 0)
        def _():
            pltpu.make_async_copy(pieces.at[s], grads.at[index], sem.at[s]).start()

    for s in range(slots):
        c, t = divmod(s, across)
        index = asked[t * CAP + c]

        @pl.when(index >= 0)
        def _():
            pltpu.make_async_copy(pieces.at[s], grads.at[index], sem.at[s]).wait()


def tile_planes(side):
    pixel = np.arange(side * side)
    x = (pixel % side - side // 2).astype(np.float64)
    y = (pixel // side - side // 2).astype(np.float64)
    mono = np.stack([x * x, x * y, y * y, x, y, np.ones_like(x)])
    table = np.zeros((LANES, side * side + 3 * LANES))
    for g in range(3):
        table[16 * g : 16 * g + 6, : side * side] = mono
    for ch in range(3):
        at = side * side + ch * LANES
        table[6 + ch, at : at + LANES] = 1.0
        table[22 + ch, at : at + LANES] = 1.0
    return table.astype(ml_dtypes.bfloat16)


def moment_columns(side):
    lane = np.arange(LANES)
    x = lane % side - side // 2
    t = lane // side - side // 2
    step = LANES // side
    one = np.ones_like(x)
    out = np.zeros((6 * LANES, LANES))
    out[:LANES, :6] = np.stack([x * x, x * t, t * t, x, t, one], axis=1)
    out[LANES : 2 * LANES, 1] = step * x
    out[LANES : 2 * LANES, 2] = 2 * step * t - step * step
    out[LANES : 2 * LANES, 4] = step
    out[2 * LANES : 3 * LANES, 2] = 2 * step * step
    for ch in range(3):
        out[(3 + ch) * LANES : (4 + ch) * LANES, 6 + ch] = 1.0
    return out.astype(ml_dtypes.bfloat16)


def filters(side):
    offsets = np.arange(TAPS) - float(RIM)
    taps = np.exp(-offsets * offsets / 4.5)
    taps = taps / taps.sum()
    reach = side + 2 * RIM
    padded = -(-reach // 8) * 8
    fold = LANES // side
    groups = side // fold

    def tap(distance):
        at = distance + RIM
        return np.where((at >= 0) & (at < TAPS), taps[np.clip(at, 0, TAPS - 1)], 0.0)

    out = np.arange(reach) - RIM
    source = np.arange(-side, 2 * side)
    along = tap(source[:, None] - out[None, :])
    fa = np.zeros((3, fold, side, fold, LANES))
    for t in range(fold):
        fa[:, t, :, t, :reach] = along.reshape(3, side, reach)
    fa = fa.reshape(3 * LANES, fold * LANES)
    fb = np.zeros((padded, fold, 3, groups))
    fb[:reach] = along.reshape(3, groups, fold, reach).transpose(3, 2, 0, 1)
    fb = fb.reshape(padded, fold * 3 * groups)
    inner = np.arange(side)
    back = tap(out[:, None] - inner[None, :])
    fc = np.zeros((fold, groups, padded))
    fc[:, :, :reach] = back.reshape(reach, groups, fold).transpose(2, 1, 0)
    fc = fc.reshape(fold * groups, padded)
    fd = np.zeros((fold, LANES, fold, side))
    for t in range(fold):
        fd[t, :reach, t, :] = back
    fd = fd.reshape(fold * LANES, LANES)
    return [m.astype(np.float32) for m in (fa, fb, fc, fd)]


def neighbours(x):
    down, across = lax.axis_size("ty"), lax.axis_size("tx")
    out = []
    for dv in (-1, 0, 1):
        for dh in (-1, 0, 1):
            if dv == 0 and dh == 0:
                out.append(x)
                continue
            pairs = [
                ((r + dv) * across + c + dh, r * across + c)
                for r in range(down)
                for c in range(across)
                if 0 <= r + dv < down and 0 <= c + dh < across
            ]
            out.append(lax.ppermute(x, ("ty", "tx"), pairs))
    return out


def per_device(gaussians, tile_lists, tile_counts, depth_order, target):
    owned, fields, block = gaussians.shape
    lmax = tile_lists.shape[2]
    side = target.shape[1]
    pixels = side * side
    groups = pixels // LANES
    across = lax.axis_size("tx")
    height = side * lax.axis_size("ty")
    width = side * across
    slots = across * CAP
    depth = -(-CAP * 9 // 8) * 8
    f32 = functools.partial(jax.ShapeDtypeStruct, dtype=F32)
    i32 = functools.partial(jax.ShapeDtypeStruct, dtype=jnp.int32)
    planes = jnp.asarray(tile_planes(side))
    reduce = jnp.asarray(moment_columns(side))
    bands = [jnp.asarray(m) for m in filters(side)]

    request, slot = pl.pallas_call(
        functools.partial(request_kernel, owned, across),
        out_shape=(i32((slots,)), i32((lmax,))),
        in_specs=[SMEM] * 3,
        out_specs=(SMEM, SMEM),
        scratch_shapes=[pltpu.SMEM((across,), jnp.int32)],
        name="request",
    )(tile_lists, tile_counts, depth_order)
    asked = lax.all_to_all(
        request.reshape(across, CAP), "tx", split_axis=0, concat_axis=0, tiled=True
    ).reshape(slots)
    span = 8
    send, raw, empty = pl.pallas_call(
        functools.partial(serve_kernel, across, side, float(height), float(width)),
        out_shape=(f32((across, depth, block)), f32((slots, fields, block)), f32(gaussians.shape)),
        in_specs=[SMEM, ANY],
        out_specs=(VMEM, VMEM, ANY),
        scratch_shapes=[
            pltpu.VMEM((span, fields, block), F32),
            pltpu.SemaphoreType.DMA((slots,)),
            pltpu.SemaphoreType.DMA((owned // span,)),
        ],
        compiler_params=PARAMS,
        name="serve",
    )(asked, gaussians)
    recv = lax.all_to_all(send, "tx", split_axis=0, concat_axis=0, tiled=True)
    chunks = lmax * block // CHUNK
    wide = pixels + 3 * LANES
    table, checks, prefix, behind, dense = pl.pallas_call(
        forward_kernel,
        out_shape=(
            jax.ShapeDtypeStruct((lmax * block, LANES), BF16),
            f32((chunks, SEGS, pixels)),
            f32((SEGS, pixels)),
            f32((3, SEGS, pixels)),
            f32((6 * groups, LANES)),
        ),
        in_specs=[SMEM, VMEM, VMEM, VMEM],
        out_specs=(VMEM,) * 5,
        scratch_shapes=[
            pltpu.VMEM((lmax * block, LANES), F32),
            pltpu.VMEM((CHUNK, wide), F32),
            pltpu.VMEM((CHUNK, wide), F32),
            pltpu.VMEM((4, SEGS, pixels), F32),
        ],
        compiler_params=PARAMS,
        name="forward",
    )(slot, recv, planes, target.reshape(3 * groups, LANES))
    near = neighbours(dense)
    slope, part = pl.pallas_call(
        functools.partial(score_entry, side, height, width),
        out_shape=(f32((3 * groups, LANES)), f32((1,))),
        in_specs=[VMEM] * 13,
        out_specs=(VMEM, SMEM),
        compiler_params=PARAMS,
        name="score",
    )(*near, *bands)
    total = lax.psum(part[0], ("ty", "tx"))
    reply = pl.pallas_call(
        backward_kernel,
        out_shape=f32((across, depth, block)),
        in_specs=[SMEM] + [VMEM] * 7,
        out_specs=VMEM,
        scratch_shapes=[
            pltpu.VMEM((LANES, 2 * pixels), BF16),
            pltpu.VMEM((LANES, pixels), F32),
            pltpu.VMEM((3, SEGS, pixels), F32),
            pltpu.VMEM((CHUNK, 2 * pixels), F32),
            pltpu.VMEM((CHUNK, 2 * pixels), F32),
            pltpu.VMEM((CHUNK, pixels), F32),
            pltpu.VMEM((CHUNK, pixels), F32),
            pltpu.VMEM((CHUNK, 6 * LANES), F32),
            pltpu.VMEM((lmax * block, LANES), F32),
        ],
        compiler_params=PARAMS,
        name="backward",
    )(slot, table, checks, prefix, behind, slope, planes, reduce)
    got = lax.all_to_all(reply, "tx", split_axis=0, concat_axis=0, tiled=True)
    grads = pl.pallas_call(
        functools.partial(gather_kernel, across, side, float(height), float(width)),
        out_shape=f32(gaussians.shape),
        in_specs=[SMEM, VMEM, VMEM, ANY],
        out_specs=ANY,
        scratch_shapes=[
            pltpu.VMEM((slots, fields, block), F32),
            pltpu.SemaphoreType.DMA((slots,)),
        ],
        input_output_aliases={3: 0},
        compiler_params=PARAMS,
        name="gather",
    )(asked, got, raw, empty)
    return (grads, total / (3.0 * height * width))


def solution(mesh):
    return jax.shard_map(
        per_device,
        mesh=mesh,
        in_specs=(
            P(("ty", "tx"), None, None),
            P("ty", "tx", None),
            P("ty", "tx"),
            P(),
            P(None, "ty", "tx"),
        ),
        out_specs=(P(("ty", "tx"), None, None), P()),
        check_vma=False,
    )
```

```python
import functools

import jax
import jax.numpy as jnp
import ml_dtypes
import numpy as np
from jax import lax
from jax.experimental import pallas as pl
from jax.experimental.pallas import tpu as pltpu
from jax.sharding import PartitionSpec as P

CAP = 3
SEGS = 8
LANES = 128
CHUNK = 128
STEPS = CHUNK // SEGS
RIM = 5
TAPS = 2 * RIM + 1
LOG2E = 1.4426950408889634
LN2 = 0.6931471805599453
DARK = -1e30

FOCAL = 1000.0
LOW_PASS = 0.3
STRUCT_WEIGHT = 0.2
LUMA_TERM = 0.0001
CONTRAST_TERM = 0.0009
ROBUST_TERM = 1e-06
HARMONIC_ZERO = 0.28209479177387814
HARMONIC_ONE = 0.4886025119029199
HARMONIC_TWO = (
    1.0925484305920792,
    -1.0925484305920792,
    0.31539156525252005,
    -1.0925484305920792,
    0.5462742152960396,
)
HARMONIC_THREE = (
    -0.5900435899266435,
    2.890611442640554,
    -0.4570457994644658,
    0.3731763325901154,
    -0.4570457994644658,
    1.445305721320277,
    -0.5900435899266435,
)

HIGH = lax.Precision.HIGHEST
F32 = jnp.float32
BF16 = jnp.bfloat16
ANY = pl.BlockSpec(memory_space=pl.ANY)
SMEM = pl.BlockSpec(memory_space=pltpu.SMEM)
VMEM = pl.BlockSpec(memory_space=pltpu.VMEM)
PARAMS = pltpu.CompilerParams(vmem_limit_bytes=56 * 1024 * 1024)


def harmonics(x, y, z):
    xx, yy, zz = x * x, y * y, z * z
    xy, yz, xz = x * y, y * z, x * z
    return [
        HARMONIC_ZERO * jnp.ones_like(x),
        -HARMONIC_ONE * y,
        HARMONIC_ONE * z,
        -HARMONIC_ONE * x,
        HARMONIC_TWO[0] * xy,
        HARMONIC_TWO[1] * yz,
        HARMONIC_TWO[2] * (2.0 * zz - xx - yy),
        HARMONIC_TWO[3] * xz,
        HARMONIC_TWO[4] * (xx - yy),
        HARMONIC_THREE[0] * y * (3.0 * xx - yy),
        HARMONIC_THREE[1] * xy * z,
        HARMONIC_THREE[2] * y * (4.0 * zz - xx - yy),
        HARMONIC_THREE[3] * z * (2.0 * zz - 3.0 * xx - 3.0 * yy),
        HARMONIC_THREE[4] * x * (4.0 * zz - xx - yy),
        HARMONIC_THREE[5] * z * (xx - yy),
        HARMONIC_THREE[6] * x * (xx - 3.0 * yy),
    ]


def directions(x, y, z):
    length = jnp.sqrt(x * x + y * y + z * z)
    return harmonics(x / length, y / length, z / length)


def conic(mean_x, mean_y, mean_z, log_scale, quat):
    scale = [jnp.exp(s) for s in log_scale]
    norm = jnp.sqrt(quat[0] * quat[0] + quat[1] * quat[1] + quat[2] * quat[2] + quat[3] * quat[3])
    w, i, j, k = (q / norm for q in quat)
    rotation = [
        [1.0 - 2.0 * (j * j + k * k), 2.0 * (i * j - w * k), 2.0 * (i * k + w * j)],
        [2.0 * (i * j + w * k), 1.0 - 2.0 * (i * i + k * k), 2.0 * (j * k - w * i)],
        [2.0 * (i * k - w * j), 2.0 * (j * k + w * i), 1.0 - 2.0 * (i * i + j * j)],
    ]
    scaled = [[rotation[r][c] * scale[c] for c in range(3)] for r in range(3)]

    def sigma(r, c):
        return scaled[r][0] * scaled[c][0] + scaled[r][1] * scaled[c][1] + scaled[r][2] * scaled[c][2]

    s00, s01, s02, s11, s12, s22 = (
        sigma(0, 0), sigma(0, 1), sigma(0, 2), sigma(1, 1), sigma(1, 2), sigma(2, 2),
    )
    inverse_z = 1.0 / mean_z
    diag = FOCAL * inverse_z
    jac_xz = -FOCAL * mean_x * inverse_z * inverse_z
    jac_yz = -FOCAL * mean_y * inverse_z * inverse_z
    u0, u1, u2 = diag * s00 + jac_xz * s02, diag * s01 + jac_xz * s12, diag * s02 + jac_xz * s22
    v1, v2 = diag * s11 + jac_yz * s12, diag * s12 + jac_yz * s22
    cov_uu = u0 * diag + u2 * jac_xz + LOW_PASS
    cov_uv = u1 * diag + u2 * jac_yz
    cov_vv = v1 * diag + v2 * jac_yz + LOW_PASS
    determinant = cov_uu * cov_vv - cov_uv * cov_uv
    half = -0.5 * LOG2E
    xx = half * (cov_vv / determinant)
    xy = (-2.0 * half) * (cov_uv / determinant)
    yy = half * (cov_uu / determinant)
    return xx, xy, yy, FOCAL * mean_x * inverse_z, FOCAL * mean_y * inverse_z


def expanded(xx, xy, yy, pos_u, pos_v, log_opacity):
    x1 = -2.0 * xx * pos_u - xy * pos_v
    y1 = -2.0 * yy * pos_v - xy * pos_u
    one = xx * pos_u * pos_u + xy * pos_u * pos_v + yy * pos_v * pos_v + log_opacity
    return xx, xy, yy, x1, y1, one


def tile_shifts(across, side, height, width):
    column = lax.broadcasted_iota(jnp.int32, (across, LANES), 0).astype(F32)
    column = jnp.concatenate([column] * CAP, axis=0)
    row = lax.axis_index("ty").astype(F32)
    shift_x = (0.5 * width - 0.5 * side - 0.5) - side * column
    shift_y = jnp.full(column.shape, (0.5 * height - 0.5 * side - 0.5) - side * row, F32)
    return shift_x, shift_y


def request_kernel(owned, across, lists, count, order, request, slot, seen):
    base = lax.axis_index("ty") * across
    for o in range(across):
        seen[o] = 0
        for c in range(CAP):
            request[o, 0, c] = -1
    used = count[0, 0]

    def entry(k, _):
        @pl.when(k < used)
        def _():
            block = order[lists[0, 0, k]]
            home = block // owned
            local = block - home * owned
            home = home - base
            at = seen[home]
            seen[home] = at + 1
            request[home, 0, at] = local
            slot[k] = home * CAP + at

        @pl.when(k >= used)
        def _():
            slot[k] = -1

        return 0

    lax.fori_loop(0, slot.shape[0], entry, 0)


def project_kernel(span, gaussians, out):
    def part(n, _):
        rows = pl.ds(pl.multiple_of(n * span, span), span)
        field = [gaussians[f, rows, :] for f in range(11)]
        light = -LOG2E * jnp.log(1.0 + jnp.exp(-field[10])) + float(np.log2(0.99))
        values = list(conic(field[0], field[1], field[2], field[3:6], field[6:10]))
        values.append(jnp.maximum(light, DARK))
        basis = directions(field[0], field[1], field[2])
        for ch in range(3):
            color = 0.5 + basis[0] * gaussians[11 + ch, rows, :]
            for m in range(1, 16):
                color = color + basis[m] * gaussians[11 + 3 * m + ch, rows, :]
            values.append(color)
        for f in range(9):
            out[f, rows, :] = values[f]
        return 0

    lax.fori_loop(0, gaussians.shape[1] // span, part, 0)


def asked_index(asked, across, s):
    c = s // across
    return asked[s - c * across, 0, c]


def serve_kernel(across, side, height, width, asked, projected, send, chosen):
    def pick(s, _):
        index = jnp.maximum(asked_index(asked, across, s), 0)
        for f in range(9):
            chosen[f, pl.ds(s, 1), :] = projected[f, pl.ds(index, 1), :]
        return 0

    lax.fori_loop(0, across * CAP, pick, 0, unroll=True)
    shift_x, shift_y = tile_shifts(across, side, height, width)
    rows = list(
        expanded(
            chosen[0], chosen[1], chosen[2], chosen[3] + shift_x, chosen[4] + shift_y, chosen[5]
        )
    ) + [chosen[6], chosen[7], chosen[8]]
    for c in range(CAP):
        for f in range(9):
            at = c * 8 + f if f < 8 else CAP * 8 + c
            send[:, at, :] = rows[f][c * across : (c + 1) * across]


def pick_kernel(across, asked, gaussians, raw):
    def pick(s, _):
        index = jnp.maximum(asked_index(asked, across, s), 0)
        for f in range(gaussians.shape[0]):
            raw[f, pl.ds(s, 1), :] = gaussians[f, pl.ds(index, 1), :]
        return 0

    lax.fori_loop(0, across * CAP, pick, 0)


def repeated(x, times):
    return jnp.concatenate([x] * times, axis=1)


def forward_kernel(
    slot, recv, planes, target, table, checks, prefix, behind, dense, spread, buf_a, buf_b, ends
):
    lmax = slot.shape[0]
    per = lmax // SEGS
    pixels = prefix.shape[1]
    groups = pixels // LANES
    zero_rows = jnp.zeros((7, LANES), F32)
    dead = jnp.where(lax.broadcasted_iota(jnp.int32, (16, LANES), 0) == 5, DARK, 0.0)
    is_color = lax.broadcasted_iota(jnp.int32, (16, LANES), 0) >= 6
    filler = jnp.zeros((LANES - 48, LANES), F32)

    def place(m, seg):
        s = slot[seg * per + m]
        live = s >= 0
        s = jnp.maximum(s, 0)
        o = s // CAP
        c = s - o * CAP
        head = recv[o, pl.ds(pl.multiple_of(c * 8, 8), 8), :]
        tail = recv[o, pl.ds(CAP * 8 + c, 1), :]
        rows = jnp.concatenate([head, tail, zero_rows], axis=0)
        rows = jnp.where(live, rows, dead)
        hi = rows.astype(BF16).astype(F32)
        rest = rows - hi
        mid = rest.astype(BF16).astype(F32)
        low = (rest - mid).astype(BF16).astype(F32)
        third = jnp.where(is_color, hi, low)
        stacked = jnp.concatenate([hi, mid, third, filler], axis=0)
        spread[pl.ds(m * (SEGS * LANES) + seg, LANES, stride=SEGS), :] = stacked.T

    for seg in range(SEGS):
        place(0, seg)

    def products(n, buf):
        part = spread[pl.ds(pl.multiple_of(n * CHUNK, CHUNK), CHUNK), :].astype(BF16)
        table[pl.ds(pl.multiple_of(n * CHUNK, CHUNK), CHUNK), :] = part
        buf[...] = jnp.dot(part, planes[...], preferred_element_type=F32)

    def blend(n, buf, carry):
        light, red, green, blue = carry
        checks[n] = light
        for i in range(STEPS):
            rows = pl.ds(i * SEGS, SEGS)
            weight = light * jnp.exp2(buf[rows, :pixels])
            light = light - weight
            red = red + weight * repeated(buf[rows, pixels : pixels + LANES], groups)
            green = green + weight * repeated(buf[rows, pixels + LANES : pixels + 2 * LANES], groups)
            blue = blue + weight * repeated(
                buf[rows, pixels + 2 * LANES : pixels + 3 * LANES], groups
            )
        return light, red, green, blue

    products(0, buf_a)
    chunks = lmax * LANES // CHUNK

    turn = chunks // per

    def pair(h, carry):
        n = 2 * h
        m = (n // turn + 1) % per
        products(n + 1, buf_b)
        place(m, n % turn)
        carry = blend(n, buf_a, carry)
        place(m, n % turn + 1)
        products(jnp.minimum(n + 2, chunks - 1), buf_a)
        return blend(n + 1, buf_b, carry)

    start = (jnp.ones((SEGS, pixels), F32),) + (jnp.zeros((SEGS, pixels), F32),) * 3
    carry = lax.fori_loop(0, chunks // 2, pair, start)
    for f in range(4):
        ends[f] = carry[f]
    ahead = jnp.ones((1, pixels), F32)
    for seg in range(SEGS):
        prefix[pl.ds(seg, 1), :] = ahead
        ahead = ahead * ends[0, pl.ds(seg, 1), :]
    for ch in range(3):
        seen = jnp.zeros((1, pixels), F32)
        for seg in reversed(range(SEGS)):
            behind[ch, pl.ds(seg, 1), :] = seen
            seen = ends[1 + ch, pl.ds(seg, 1), :] + ends[0, pl.ds(seg, 1), :] * seen
        for j in range(groups):
            dense[pl.ds(ch * groups + j, 1), :] = seen[:, j * LANES : (j + 1) * LANES]
    dense[3 * groups :, :] = target[...]


def similarity(mean_a, mean_b, square_a, square_b, cross):
    var_a = square_a - mean_a * mean_a
    var_b = square_b - mean_b * mean_b
    covar = cross - mean_a * mean_b
    top = (2.0 * mean_a * mean_b + LUMA_TERM) * (2.0 * covar + CONTRAST_TERM)
    bottom = (mean_a * mean_a + mean_b * mean_b + LUMA_TERM) * (var_a + var_b + CONTRAST_TERM)
    return top / bottom


def score_kernel(side, height, width, near, fa, fb, fc, fd, slope, loss):
    rows3 = near[4].shape[0] // 2
    groups = rows3 // 3
    fold = LANES // side
    fields = [[], [], [], [], []]
    for v in range(3):
        strip = jnp.concatenate([near[3 * v + h] for h in range(3)], axis=1)
        image, target = strip[:rows3], strip[rows3:]
        for f, plane in enumerate([image, target, image * image, target * target, image * target]):
            fields[f].append(plane)
    stack = jnp.concatenate([fields[f][v] for f in range(5) for v in range(3)], axis=0)
    wide = jnp.dot(stack, fa[...], precision=HIGH, preferred_element_type=F32)
    columns = []
    for f in range(5):
        for ch in range(3):
            parts = []
            for t in range(fold):
                for v in range(3):
                    at = (f * 3 + v) * rows3 + ch * groups
                    parts.append(wide[at : at + groups, t * LANES : (t + 1) * LANES])
            columns.append(jnp.concatenate(parts, axis=0))
    tall = jnp.concatenate(columns, axis=1)
    maps = jnp.dot(fb[...], tall, precision=HIGH, preferred_element_type=F32)
    span = 3 * LANES
    score, pull = jax.vjp(similarity, *[maps[:, f * span : (f + 1) * span] for f in range(5)])
    parts = pull(jnp.full(score.shape, -STRUCT_WEIGHT, F32))
    row = lax.broadcasted_iota(jnp.int32, score.shape, 0)
    col = lax.broadcasted_iota(jnp.int32, (score.shape[0], LANES), 1)
    col = jnp.concatenate([col] * 3, axis=1)
    row_at = row - RIM + lax.axis_index("ty") * side
    col_at = col - RIM + lax.axis_index("tx") * side
    reach = side + 2 * RIM
    inside = (
        (row_at >= 0) & (row_at < height) & (col_at >= 0) & (col_at < width)
        & (row < reach) & (col < reach)
    )
    own = (row >= RIM) & (row < RIM + side) & (col >= RIM) & (col < RIM + side)
    coeffs = jnp.concatenate(
        [jnp.where(inside, parts[f], 0.0) for f in (0, 2, 4)], axis=1
    )
    low = jnp.dot(fc[...], coeffs, precision=HIGH, preferred_element_type=F32)
    rows = []
    for n in range(9):
        rows.append(
            jnp.concatenate(
                [
                    low[t * groups : (t + 1) * groups, n * LANES : (n + 1) * LANES]
                    for t in range(fold)
                ],
                axis=1,
            )
        )
    smooth = jnp.dot(
        jnp.concatenate(rows, axis=0), fd[...], precision=HIGH, preferred_element_type=F32
    )
    image, target = near[4][:rows3, :], near[4][rows3:, :]
    gap = image - target
    robust = jnp.sqrt(gap * gap + ROBUST_TERM)
    slope[...] = (
        smooth[:rows3]
        + 2.0 * image * smooth[rows3 : 2 * rows3]
        + target * smooth[2 * rows3 :]
        + (1.0 - STRUCT_WEIGHT) * gap / robust
    )
    total = (1.0 - STRUCT_WEIGHT) * jnp.sum(robust) + STRUCT_WEIGHT * jnp.sum(
        jnp.where(own, 1.0 - score, 0.0)
    )
    loss[...] = jnp.full(loss.shape, total, F32)


def score_entry(side, height, width, *refs):
    above, left, own, right, below = refs[:5]
    rows = own.shape[0]
    near = [above[h * rows : (h + 1) * rows, :] for h in range(3)]
    near += [left[...], own[...], right[...]]
    near += [below[h * rows : (h + 1) * rows, :] for h in range(3)]
    score_kernel(side, height, width, near, *refs[5:])


def backward_kernel(
    slot, table, checks, prefix, behind, slope, planes, reduce, reply,
    rhs, wide, grows, buf_a, buf_b, weights, sums, moments, stage,
):
    lmax = slot.shape[0]
    per = lmax // SEGS
    pixels = prefix.shape[1]
    groups = pixels // LANES
    chunks = lmax * LANES // CHUNK
    wide[...] = jnp.zeros_like(wide)
    for ch in range(3):
        for j in range(groups):
            lanes = pl.ds(j * LANES, LANES)
            wide[pl.ds(6 + ch, 1), lanes] = slope[pl.ds(ch * groups + j, 1), :]
    for ch in range(3):
        row = wide[pl.ds(6 + ch, 1), :]
        hi = row.astype(BF16).astype(F32)
        grows[ch] = jnp.broadcast_to(row, (SEGS, pixels))
        wide[pl.ds(6 + ch, 1), :] = hi
        wide[pl.ds(22 + ch, 1), :] = hi
        wide[pl.ds(38 + ch, 1), :] = row - hi
    rhs[:, :pixels] = planes[:, :pixels]
    rhs[:, pixels:] = wide[...].astype(BF16)

    def products(n, buf):
        part = table[pl.ds(pl.multiple_of(n * CHUNK, CHUNK), CHUNK), :]
        buf[...] = jnp.dot(part, rhs[...], preferred_element_type=F32)

    def sweep(n, buf, back):
        light = checks[n] * prefix[...]
        for i in range(STEPS):
            rows = pl.ds(i * SEGS, SEGS)
            weight = light * jnp.exp2(buf[rows, :pixels])
            light = light - weight
            weights[rows, :] = weight
        for i in reversed(range(STEPS)):
            rows = pl.ds(i * SEGS, SEGS)
            weight = weights[rows, :]
            gap = buf[rows, pixels:] - back
            back = back + jnp.exp2(buf[rows, :pixels]) * gap
            pull = weight * gap
            zero = one = two = None
            for j in reversed(range(groups)):
                piece = pull[:, j * LANES : (j + 1) * LANES]
                zero = piece if zero is None else zero + piece
                if j > 0:
                    one = zero if one is None else one + zero
                    two = one if two is None else two + one
            sums[rows, 0:LANES] = zero
            sums[rows, LANES : 2 * LANES] = one
            sums[rows, 2 * LANES : 3 * LANES] = two
            for ch in range(3):
                tint = weight * grows[ch]
                total = tint[:, :LANES]
                for j in range(1, groups):
                    total = total + tint[:, j * LANES : (j + 1) * LANES]
                sums[rows, (3 + ch) * LANES : (4 + ch) * LANES] = total
        whole = sums[...]
        hi = whole.astype(BF16)
        low = (whole - hi.astype(F32)).astype(BF16)
        moments[pl.ds(pl.multiple_of(n * CHUNK, CHUNK), CHUNK), :] = jnp.dot(
            hi, reduce[...], preferred_element_type=F32
        ) + jnp.dot(low, reduce[...], preferred_element_type=F32)
        return back

    back = behind[0] * grows[0] + behind[1] * grows[1] + behind[2] * grows[2]
    products(chunks - 1, buf_a)

    turn = chunks // per

    def collect(m, seg):
        block = moments[pl.ds(m * (SEGS * LANES) + seg, LANES, stride=SEGS), :].T
        stage[seg * per + m] = block[:16]

    def pair(h, back):
        n = chunks - 1 - 2 * h
        m = (n // turn + 1) % per
        products(n - 1, buf_b)
        collect(m, n % turn)
        back = sweep(n, buf_a, back)
        collect(m, n % turn - 1)
        products(jnp.maximum(n - 2, 0), buf_a)
        return sweep(n - 1, buf_b, back)

    lax.fori_loop(0, chunks // 2, pair, back)
    for seg in range(SEGS):
        collect(0, seg)

    def deliver(k, _):
        s = slot[k]

        @pl.when(s >= 0)
        def _():
            o = s // CAP
            c = s - o * CAP
            reply[o, pl.ds(pl.multiple_of(c * 8, 8), 8), :] = stage[k, :8, :]
            reply[o, pl.ds(CAP * 8 + c, 1), :] = stage[k, 8:9, :]

        return 0

    lax.fori_loop(0, lmax, deliver, 0)


def gather_kernel(across, side, height, width, asked, got, raw, grads, pieces):
    fields = grads.shape[0]
    field = [raw[f] for f in range(11)]
    shift_x, shift_y = tile_shifts(across, side, height, width)

    def clear(f, _):
        grads[f] = jnp.zeros(grads.shape[1:], F32)
        return 0

    lax.fori_loop(0, fields, clear, 0)

    def received(f):
        at = [c * 8 + f if f < 8 else CAP * 8 + c for c in range(CAP)]
        return jnp.concatenate([got[:, a, :] for a in at], axis=0)

    def shaped(x, y, z, log_scale, quat):
        xx, xy, yy, pos_u, pos_v = conic(x, y, z, log_scale, quat)
        return expanded(xx, xy, yy, pos_u + shift_x, pos_v + shift_y, jnp.zeros_like(x))

    _, pull = jax.vjp(shaped, *field[:3], field[3:6], field[6:10])
    moments = [LN2 * received(f) for f in range(6)]
    gx, gy, gz, gscale, gquat = pull(tuple(moments))
    basis, pull_basis = jax.vjp(directions, *field[:3])
    tints = [received(6 + ch) for ch in range(3)]
    tilts = []
    for m in range(16):
        tilt = None
        for ch in range(3):
            term = tints[ch] * raw[11 + 3 * m + ch]
            tilt = term if tilt is None else tilt + term
            pieces[11 + 3 * m + ch] = tints[ch] * basis[m]
        tilts.append(tilt)
    dx, dy, dz = pull_basis(tilts)
    pieces[0] = gx + dx
    pieces[1] = gy + dy
    pieces[2] = gz + dz
    for f in range(3):
        pieces[3 + f] = gscale[f]
    for f in range(4):
        pieces[6 + f] = gquat[f]
    pieces[10] = moments[5] * (LOG2E / (1.0 + jnp.exp(field[10])))

    def put(s, _):
        index = asked_index(asked, across, s)

        @pl.when(index >= 0)
        def _():
            for f in range(fields):
                grads[f, pl.ds(index, 1), :] = pieces[f, pl.ds(s, 1), :]

        return 0

    lax.fori_loop(0, across * CAP, put, 0)


def tile_planes(side):
    pixel = np.arange(side * side)
    x = (pixel % side - side // 2).astype(np.float64)
    y = (pixel // side - side // 2).astype(np.float64)
    mono = np.stack([x * x, x * y, y * y, x, y, np.ones_like(x)])
    table = np.zeros((LANES, side * side + 3 * LANES))
    for g in range(3):
        table[16 * g : 16 * g + 6, : side * side] = mono
    for ch in range(3):
        at = side * side + ch * LANES
        table[6 + ch, at : at + LANES] = 1.0
        table[22 + ch, at : at + LANES] = 1.0
    return table.astype(ml_dtypes.bfloat16)


def moment_columns(side):
    lane = np.arange(LANES)
    x = lane % side - side // 2
    t = lane // side - side // 2
    step = LANES // side
    one = np.ones_like(x)
    out = np.zeros((6 * LANES, LANES))
    out[:LANES, :6] = np.stack([x * x, x * t, t * t, x, t, one], axis=1)
    out[LANES : 2 * LANES, 1] = step * x
    out[LANES : 2 * LANES, 2] = 2 * step * t - step * step
    out[LANES : 2 * LANES, 4] = step
    out[2 * LANES : 3 * LANES, 2] = 2 * step * step
    for ch in range(3):
        out[(3 + ch) * LANES : (4 + ch) * LANES, 6 + ch] = 1.0
    return out.astype(ml_dtypes.bfloat16)


def filters(side):
    offsets = np.arange(TAPS) - float(RIM)
    taps = np.exp(-offsets * offsets / 4.5)
    taps = taps / taps.sum()
    reach = side + 2 * RIM
    padded = -(-reach // 8) * 8
    fold = LANES // side
    groups = side // fold

    def tap(distance):
        at = distance + RIM
        return np.where((at >= 0) & (at < TAPS), taps[np.clip(at, 0, TAPS - 1)], 0.0)

    out = np.arange(reach) - RIM
    source = np.arange(-side, 2 * side)
    along = tap(source[:, None] - out[None, :])
    fa = np.zeros((3, fold, side, fold, LANES))
    for t in range(fold):
        fa[:, t, :, t, :reach] = along.reshape(3, side, reach)
    fa = fa.reshape(3 * LANES, fold * LANES)
    fb = np.zeros((padded, fold, 3, groups))
    fb[:reach] = along.reshape(3, groups, fold, reach).transpose(3, 2, 0, 1)
    fb = fb.reshape(padded, fold * 3 * groups)
    inner = np.arange(side)
    back = tap(out[:, None] - inner[None, :])
    fc = np.zeros((fold, groups, padded))
    fc[:, :, :reach] = back.reshape(reach, groups, fold).transpose(2, 1, 0)
    fc = fc.reshape(fold * groups, padded)
    fd = np.zeros((fold, LANES, fold, side))
    for t in range(fold):
        fd[t, :reach, t, :] = back
    fd = fd.reshape(fold * LANES, LANES)
    return [m.astype(np.float32) for m in (fa, fb, fc, fd)]


def shifted(x, axis):
    size = lax.axis_size(axis)
    up = [(i, i + 1) for i in range(size - 1)]
    return lax.ppermute(x, axis, up), lax.ppermute(x, axis, [(j, i) for i, j in up])


def per_device(gaussians, tile_lists, tile_counts, depth_order, target):
    owned, fields, block = gaussians.shape
    lmax = tile_lists.shape[2]
    side = target.shape[1]
    pixels = side * side
    groups = pixels // LANES
    across = lax.axis_size("tx")
    height = side * lax.axis_size("ty")
    width = side * across
    slots = across * CAP
    depth = -(-CAP * 9 // 8) * 8
    f32 = functools.partial(jax.ShapeDtypeStruct, dtype=F32)
    i32 = functools.partial(jax.ShapeDtypeStruct, dtype=jnp.int32)
    planes = jnp.asarray(tile_planes(side))
    reduce = jnp.asarray(moment_columns(side))
    bands = [jnp.asarray(m) for m in filters(side)]

    fieldwise = jnp.transpose(gaussians, (1, 0, 2))
    request, slot = pl.pallas_call(
        functools.partial(request_kernel, owned, across),
        out_shape=(i32((across, 1, LANES)), i32((lmax,))),
        in_specs=[SMEM] * 3,
        out_specs=(SMEM, SMEM),
        scratch_shapes=[pltpu.SMEM((across,), jnp.int32)],
        name="request",
    )(tile_lists, tile_counts, depth_order)
    asked = lax.all_to_all(request, "tx", split_axis=0, concat_axis=0, tiled=True)
    projected = pl.pallas_call(
        functools.partial(project_kernel, 16),
        out_shape=f32((9, owned, block)),
        in_specs=[VMEM],
        out_specs=VMEM,
        compiler_params=PARAMS,
        name="project",
    )(fieldwise)
    send = pl.pallas_call(
        functools.partial(serve_kernel, across, side, float(height), float(width)),
        out_shape=f32((across, depth, block)),
        in_specs=[SMEM, VMEM],
        out_specs=VMEM,
        scratch_shapes=[pltpu.VMEM((9, slots, block), F32)],
        compiler_params=PARAMS,
        name="serve",
    )(asked, projected)
    recv = lax.all_to_all(send, "tx", split_axis=0, concat_axis=0, tiled=True)
    raw = pl.pallas_call(
        functools.partial(pick_kernel, across),
        out_shape=f32((fields, slots, block)),
        in_specs=[SMEM, VMEM],
        out_specs=VMEM,
        compiler_params=PARAMS,
        name="pick",
    )(asked, fieldwise)
    chunks = lmax * block // CHUNK
    wide = pixels + 3 * LANES
    table, checks, prefix, behind, dense = pl.pallas_call(
        forward_kernel,
        out_shape=(
            jax.ShapeDtypeStruct((lmax * block, LANES), BF16),
            f32((chunks, SEGS, pixels)),
            f32((SEGS, pixels)),
            f32((3, SEGS, pixels)),
            f32((6 * groups, LANES)),
        ),
        in_specs=[SMEM, VMEM, VMEM, VMEM],
        out_specs=(VMEM,) * 5,
        scratch_shapes=[
            pltpu.VMEM((lmax * block, LANES), F32),
            pltpu.VMEM((CHUNK, wide), F32),
            pltpu.VMEM((CHUNK, wide), F32),
            pltpu.VMEM((4, SEGS, pixels), F32),
        ],
        compiler_params=PARAMS,
        name="forward",
    )(slot, recv, planes, target.reshape(3 * groups, LANES))
    left, right = shifted(dense, "tx")
    above, below = shifted(jnp.concatenate([left, dense, right], axis=0), "ty")
    slope, part = pl.pallas_call(
        functools.partial(score_entry, side, height, width),
        out_shape=(f32((3 * groups, LANES)), f32((8, LANES))),
        in_specs=[VMEM] * 9,
        out_specs=(VMEM, VMEM),
        compiler_params=PARAMS,
        name="score",
    )(above, left, dense, right, below, *bands)
    shares = lax.all_gather(part, ("ty", "tx"))
    total = jnp.sum(shares[:, 0, 0])
    reply = pl.pallas_call(
        backward_kernel,
        out_shape=f32((across, depth, block)),
        in_specs=[SMEM] + [VMEM] * 7,
        out_specs=VMEM,
        scratch_shapes=[
            pltpu.VMEM((LANES, 2 * pixels), BF16),
            pltpu.VMEM((LANES, pixels), F32),
            pltpu.VMEM((3, SEGS, pixels), F32),
            pltpu.VMEM((CHUNK, 2 * pixels), F32),
            pltpu.VMEM((CHUNK, 2 * pixels), F32),
            pltpu.VMEM((CHUNK, pixels), F32),
            pltpu.VMEM((CHUNK, 6 * LANES), F32),
            pltpu.VMEM((lmax * block, LANES), F32),
            pltpu.VMEM((lmax, 16, LANES), F32),
        ],
        compiler_params=PARAMS,
        name="backward",
    )(slot, table, checks, prefix, behind, slope, planes, reduce)
    got = lax.all_to_all(reply, "tx", split_axis=0, concat_axis=0, tiled=True)
    grads = pl.pallas_call(
        functools.partial(gather_kernel, across, side, float(height), float(width)),
        out_shape=f32((fields, owned, block)),
        in_specs=[SMEM, VMEM, VMEM],
        out_specs=VMEM,
        scratch_shapes=[pltpu.VMEM((fields, slots, block), F32)],
        compiler_params=PARAMS,
        name="gather",
    )(asked, got, raw)
    return (jnp.transpose(grads, (1, 0, 2)), total / (3.0 * height * width))


def solution(mesh):
    return jax.shard_map(
        per_device,
        mesh=mesh,
        in_specs=(
            P(("ty", "tx"), None, None),
            P("ty", "tx", None),
            P("ty", "tx"),
            P(),
            P(None, "ty", "tx"),
        ),
        out_specs=(P(("ty", "tx"), None, None), P()),
        check_vma=False,
    )
```

```python
import functools

import jax
import jax.numpy as jnp
import ml_dtypes
import numpy as np
from jax import lax
from jax.experimental import pallas as pl
from jax.experimental.pallas import tpu as pltpu
from jax.sharding import PartitionSpec as P

CAP = 3
SEGS = 8
LANES = 128
CHUNK = 128
STEPS = CHUNK // SEGS
RIM = 5
TAPS = 2 * RIM + 1
LOG2E = 1.4426950408889634
LN2 = 0.6931471805599453
DARK = -1e30

FOCAL = 1000.0
LOW_PASS = 0.3
STRUCT_WEIGHT = 0.2
LUMA_TERM = 0.0001
CONTRAST_TERM = 0.0009
ROBUST_TERM = 1e-06
HARMONIC_ZERO = 0.28209479177387814
HARMONIC_ONE = 0.4886025119029199
HARMONIC_TWO = (
    1.0925484305920792,
    -1.0925484305920792,
    0.31539156525252005,
    -1.0925484305920792,
    0.5462742152960396,
)
HARMONIC_THREE = (
    -0.5900435899266435,
    2.890611442640554,
    -0.4570457994644658,
    0.3731763325901154,
    -0.4570457994644658,
    1.445305721320277,
    -0.5900435899266435,
)

HIGH = lax.Precision.HIGHEST
F32 = jnp.float32
BF16 = jnp.bfloat16
ANY = pl.BlockSpec(memory_space=pl.ANY)
SMEM = pl.BlockSpec(memory_space=pltpu.SMEM)
VMEM = pl.BlockSpec(memory_space=pltpu.VMEM)
PARAMS = pltpu.CompilerParams(vmem_limit_bytes=24 * 1024 * 1024)


def harmonics(x, y, z):
    xx, yy, zz = x * x, y * y, z * z
    xy, yz, xz = x * y, y * z, x * z
    return [
        HARMONIC_ZERO * jnp.ones_like(x),
        -HARMONIC_ONE * y,
        HARMONIC_ONE * z,
        -HARMONIC_ONE * x,
        HARMONIC_TWO[0] * xy,
        HARMONIC_TWO[1] * yz,
        HARMONIC_TWO[2] * (2.0 * zz - xx - yy),
        HARMONIC_TWO[3] * xz,
        HARMONIC_TWO[4] * (xx - yy),
        HARMONIC_THREE[0] * y * (3.0 * xx - yy),
        HARMONIC_THREE[1] * xy * z,
        HARMONIC_THREE[2] * y * (4.0 * zz - xx - yy),
        HARMONIC_THREE[3] * z * (2.0 * zz - 3.0 * xx - 3.0 * yy),
        HARMONIC_THREE[4] * x * (4.0 * zz - xx - yy),
        HARMONIC_THREE[5] * z * (xx - yy),
        HARMONIC_THREE[6] * x * (xx - 3.0 * yy),
    ]


def directions(x, y, z):
    length = jnp.sqrt(x * x + y * y + z * z)
    return harmonics(x / length, y / length, z / length)


def conic(mean_x, mean_y, mean_z, log_scale, quat):
    scale = [jnp.exp(s) for s in log_scale]
    norm = jnp.sqrt(quat[0] * quat[0] + quat[1] * quat[1] + quat[2] * quat[2] + quat[3] * quat[3])
    w, i, j, k = (q / norm for q in quat)
    rotation = [
        [1.0 - 2.0 * (j * j + k * k), 2.0 * (i * j - w * k), 2.0 * (i * k + w * j)],
        [2.0 * (i * j + w * k), 1.0 - 2.0 * (i * i + k * k), 2.0 * (j * k - w * i)],
        [2.0 * (i * k - w * j), 2.0 * (j * k + w * i), 1.0 - 2.0 * (i * i + j * j)],
    ]
    scaled = [[rotation[r][c] * scale[c] for c in range(3)] for r in range(3)]

    def sigma(r, c):
        return scaled[r][0] * scaled[c][0] + scaled[r][1] * scaled[c][1] + scaled[r][2] * scaled[c][2]

    s00, s01, s02, s11, s12, s22 = (
        sigma(0, 0), sigma(0, 1), sigma(0, 2), sigma(1, 1), sigma(1, 2), sigma(2, 2),
    )
    inverse_z = 1.0 / mean_z
    diag = FOCAL * inverse_z
    jac_xz = -FOCAL * mean_x * inverse_z * inverse_z
    jac_yz = -FOCAL * mean_y * inverse_z * inverse_z
    u0, u1, u2 = diag * s00 + jac_xz * s02, diag * s01 + jac_xz * s12, diag * s02 + jac_xz * s22
    v1, v2 = diag * s11 + jac_yz * s12, diag * s12 + jac_yz * s22
    cov_uu = u0 * diag + u2 * jac_xz + LOW_PASS
    cov_uv = u1 * diag + u2 * jac_yz
    cov_vv = v1 * diag + v2 * jac_yz + LOW_PASS
    determinant = cov_uu * cov_vv - cov_uv * cov_uv
    half = -0.5 * LOG2E
    xx = half * (cov_vv / determinant)
    xy = (-2.0 * half) * (cov_uv / determinant)
    yy = half * (cov_uu / determinant)
    return xx, xy, yy, FOCAL * mean_x * inverse_z, FOCAL * mean_y * inverse_z


def expanded(xx, xy, yy, pos_u, pos_v, log_opacity):
    x1 = -2.0 * xx * pos_u - xy * pos_v
    y1 = -2.0 * yy * pos_v - xy * pos_u
    one = xx * pos_u * pos_u + xy * pos_u * pos_v + yy * pos_v * pos_v + log_opacity
    return xx, xy, yy, x1, y1, one


def tile_shifts(across, side, height, width):
    column = lax.broadcasted_iota(jnp.int32, (across, LANES), 0).astype(F32)
    column = jnp.concatenate([column] * CAP, axis=0)
    row = lax.axis_index("ty").astype(F32)
    shift_x = (0.5 * width - 0.5 * side - 0.5) - side * column
    shift_y = jnp.full(column.shape, (0.5 * height - 0.5 * side - 0.5) - side * row, F32)
    return shift_x, shift_y


def request_kernel(owned, across, lists, count, order, request, slot, seen):
    base = lax.axis_index("ty") * across
    for o in range(across):
        seen[o] = 0
        for c in range(CAP):
            request[o, 0, c] = -1
    used = count[0, 0]

    def entry(k, _):
        @pl.when(k < used)
        def _():
            block = order[lists[0, 0, k]]
            home = block // owned
            local = block - home * owned
            home = home - base
            at = seen[home]
            seen[home] = at + 1
            request[home, 0, at] = local
            slot[k] = home * CAP + at

        @pl.when(k >= used)
        def _():
            slot[k] = -1

        return 0

    lax.fori_loop(0, slot.shape[0], entry, 0)


def project_kernel(span, gaussians, out):
    def part(n, _):
        rows = pl.ds(pl.multiple_of(n * span, span), span)
        field = [gaussians[f, rows, :] for f in range(11)]
        light = -LOG2E * jnp.log(1.0 + jnp.exp(-field[10])) + float(np.log2(0.99))
        values = list(conic(field[0], field[1], field[2], field[3:6], field[6:10]))
        values.append(jnp.maximum(light, DARK))
        basis = directions(field[0], field[1], field[2])
        for ch in range(3):
            color = 0.5 + basis[0] * gaussians[11 + ch, rows, :]
            for m in range(1, 16):
                color = color + basis[m] * gaussians[11 + 3 * m + ch, rows, :]
            values.append(color)
        for f in range(9):
            out[f, rows, :] = values[f]
        return 0

    lax.fori_loop(0, gaussians.shape[1] // span, part, 0)


def asked_index(asked, across, s):
    c = s // across
    return asked[s - c * across, 0, c]


def serve_kernel(across, side, height, width, asked, projected, send, chosen):
    def pick(s, _):
        index = jnp.maximum(asked_index(asked, across, s), 0)
        for f in range(9):
            chosen[f, pl.ds(s, 1), :] = projected[f, pl.ds(index, 1), :]
        return 0

    lax.fori_loop(0, across * CAP, pick, 0, unroll=True)
    shift_x, shift_y = tile_shifts(across, side, height, width)
    rows = list(
        expanded(
            chosen[0], chosen[1], chosen[2], chosen[3] + shift_x, chosen[4] + shift_y, chosen[5]
        )
    ) + [chosen[6], chosen[7], chosen[8]]
    for c in range(CAP):
        for f in range(9):
            at = c * 8 + f if f < 8 else CAP * 8 + c
            send[:, at, :] = rows[f][c * across : (c + 1) * across]


def pick_kernel(across, asked, gaussians, raw):
    def pick(s, _):
        index = jnp.maximum(asked_index(asked, across, s), 0)
        for f in range(gaussians.shape[0]):
            raw[f, pl.ds(s, 1), :] = gaussians[f, pl.ds(index, 1), :]
        return 0

    lax.fori_loop(0, across * CAP, pick, 0)


def repeated(x, times):
    return jnp.concatenate([x] * times, axis=1)


def forward_kernel(
    slot, recv, planes, target, table, checks, prefix, behind, dense, spread, buf_a, buf_b, ends
):
    lmax = slot.shape[0]
    per = lmax // SEGS
    pixels = prefix.shape[1]
    groups = pixels // LANES
    zero_rows = jnp.zeros((7, LANES), F32)
    dead = jnp.where(lax.broadcasted_iota(jnp.int32, (16, LANES), 0) == 5, DARK, 0.0)
    is_color = lax.broadcasted_iota(jnp.int32, (16, LANES), 0) >= 6
    filler = jnp.zeros((LANES - 48, LANES), F32)

    def place(m, seg):
        s = slot[seg * per + m]
        live = s >= 0
        s = jnp.maximum(s, 0)
        o = s // CAP
        c = s - o * CAP
        head = recv[o, pl.ds(pl.multiple_of(c * 8, 8), 8), :]
        tail = recv[o, pl.ds(CAP * 8 + c, 1), :]
        rows = jnp.concatenate([head, tail, zero_rows], axis=0)
        rows = jnp.where(live, rows, dead)
        hi = rows.astype(BF16).astype(F32)
        rest = rows - hi
        mid = rest.astype(BF16).astype(F32)
        low = (rest - mid).astype(BF16).astype(F32)
        third = jnp.where(is_color, hi, low)
        stacked = jnp.concatenate([hi, mid, third, filler], axis=0)
        spread[pl.ds(m * (SEGS * LANES) + seg, LANES, stride=SEGS), :] = stacked.T

    for seg in range(SEGS):
        place(0, seg)

    def products(n, buf):
        part = spread[pl.ds(pl.multiple_of(n * CHUNK, CHUNK), CHUNK), :].astype(BF16)
        table[pl.ds(pl.multiple_of(n * CHUNK, CHUNK), CHUNK), :] = part
        buf[...] = jnp.dot(part, planes[...], preferred_element_type=F32)

    def blend(n, buf, carry):
        light, red, green, blue = carry
        checks[n] = light
        for i in range(STEPS):
            rows = pl.ds(i * SEGS, SEGS)
            weight = light * jnp.exp2(buf[rows, :pixels])
            light = light - weight
            red = red + weight * repeated(buf[rows, pixels : pixels + LANES], groups)
            green = green + weight * repeated(buf[rows, pixels + LANES : pixels + 2 * LANES], groups)
            blue = blue + weight * repeated(
                buf[rows, pixels + 2 * LANES : pixels + 3 * LANES], groups
            )
        return light, red, green, blue

    products(0, buf_a)
    chunks = lmax * LANES // CHUNK

    turn = chunks // per

    def pair(h, carry):
        n = 2 * h
        m = (n // turn + 1) % per
        products(n + 1, buf_b)
        place(m, n % turn)
        carry = blend(n, buf_a, carry)
        place(m, n % turn + 1)
        products(jnp.minimum(n + 2, chunks - 1), buf_a)
        return blend(n + 1, buf_b, carry)

    start = (jnp.ones((SEGS, pixels), F32),) + (jnp.zeros((SEGS, pixels), F32),) * 3
    carry = lax.fori_loop(0, chunks // 2, pair, start)
    for f in range(4):
        ends[f] = carry[f]
    ahead = jnp.ones((1, pixels), F32)
    for seg in range(SEGS):
        prefix[pl.ds(seg, 1), :] = ahead
        ahead = ahead * ends[0, pl.ds(seg, 1), :]
    for ch in range(3):
        seen = jnp.zeros((1, pixels), F32)
        for seg in reversed(range(SEGS)):
            behind[ch, pl.ds(seg, 1), :] = seen
            seen = ends[1 + ch, pl.ds(seg, 1), :] + ends[0, pl.ds(seg, 1), :] * seen
        for j in range(groups):
            dense[pl.ds(ch * groups + j, 1), :] = seen[:, j * LANES : (j + 1) * LANES]
    dense[3 * groups :, :] = target[...]


def similarity(mean_a, mean_b, square_a, square_b, cross):
    var_a = square_a - mean_a * mean_a
    var_b = square_b - mean_b * mean_b
    covar = cross - mean_a * mean_b
    top = (2.0 * mean_a * mean_b + LUMA_TERM) * (2.0 * covar + CONTRAST_TERM)
    bottom = (mean_a * mean_a + mean_b * mean_b + LUMA_TERM) * (var_a + var_b + CONTRAST_TERM)
    return top / bottom


def score_kernel(side, height, width, near, fa, fb, fc, fd, slope, loss):
    rows3 = near[4].shape[0] // 2
    groups = rows3 // 3
    fold = LANES // side
    fields = [[], [], [], [], []]
    for v in range(3):
        strip = jnp.concatenate([near[3 * v + h] for h in range(3)], axis=1)
        image, target = strip[:rows3], strip[rows3:]
        for f, plane in enumerate([image, target, image * image, target * target, image * target]):
            fields[f].append(plane)
    stack = jnp.concatenate([fields[f][v] for f in range(5) for v in range(3)], axis=0)
    wide = jnp.dot(stack, fa[...], precision=HIGH, preferred_element_type=F32)
    columns = []
    for f in range(5):
        for ch in range(3):
            parts = []
            for t in range(fold):
                for v in range(3):
                    at = (f * 3 + v) * rows3 + ch * groups
                    parts.append(wide[at : at + groups, t * LANES : (t + 1) * LANES])
            columns.append(jnp.concatenate(parts, axis=0))
    tall = jnp.concatenate(columns, axis=1)
    maps = jnp.dot(fb[...], tall, precision=HIGH, preferred_element_type=F32)
    span = 3 * LANES
    score, pull = jax.vjp(similarity, *[maps[:, f * span : (f + 1) * span] for f in range(5)])
    parts = pull(jnp.full(score.shape, -STRUCT_WEIGHT, F32))
    row = lax.broadcasted_iota(jnp.int32, score.shape, 0)
    col = lax.broadcasted_iota(jnp.int32, (score.shape[0], LANES), 1)
    col = jnp.concatenate([col] * 3, axis=1)
    row_at = row - RIM + lax.axis_index("ty") * side
    col_at = col - RIM + lax.axis_index("tx") * side
    reach = side + 2 * RIM
    inside = (
        (row_at >= 0) & (row_at < height) & (col_at >= 0) & (col_at < width)
        & (row < reach) & (col < reach)
    )
    own = (row >= RIM) & (row < RIM + side) & (col >= RIM) & (col < RIM + side)
    coeffs = jnp.concatenate(
        [jnp.where(inside, parts[f], 0.0) for f in (0, 2, 4)], axis=1
    )
    low = jnp.dot(fc[...], coeffs, precision=HIGH, preferred_element_type=F32)
    rows = []
    for n in range(9):
        rows.append(
            jnp.concatenate(
                [
                    low[t * groups : (t + 1) * groups, n * LANES : (n + 1) * LANES]
                    for t in range(fold)
                ],
                axis=1,
            )
        )
    smooth = jnp.dot(
        jnp.concatenate(rows, axis=0), fd[...], precision=HIGH, preferred_element_type=F32
    )
    image, target = near[4][:rows3, :], near[4][rows3:, :]
    gap = image - target
    robust = jnp.sqrt(gap * gap + ROBUST_TERM)
    slope[...] = (
        smooth[:rows3]
        + 2.0 * image * smooth[rows3 : 2 * rows3]
        + target * smooth[2 * rows3 :]
        + (1.0 - STRUCT_WEIGHT) * gap / robust
    )
    total = (1.0 - STRUCT_WEIGHT) * jnp.sum(robust) + STRUCT_WEIGHT * jnp.sum(
        jnp.where(own, 1.0 - score, 0.0)
    )
    loss[...] = jnp.full(loss.shape, total, F32)


def score_entry(side, height, width, *refs):
    above, left, own, right, below = refs[:5]
    rows = own.shape[0]
    near = [above[h * rows : (h + 1) * rows, :] for h in range(3)]
    near += [left[...], own[...], right[...]]
    near += [below[h * rows : (h + 1) * rows, :] for h in range(3)]
    score_kernel(side, height, width, near, *refs[5:])


def backward_kernel(
    slot, table, checks, prefix, behind, slope, planes, reduce, reply,
    rhs, wide, grows, buf_a, buf_b, weights, sums, moments, stage,
):
    lmax = slot.shape[0]
    per = lmax // SEGS
    pixels = prefix.shape[1]
    groups = pixels // LANES
    chunks = lmax * LANES // CHUNK
    wide[...] = jnp.zeros_like(wide)
    for ch in range(3):
        for j in range(groups):
            lanes = pl.ds(j * LANES, LANES)
            wide[pl.ds(6 + ch, 1), lanes] = slope[pl.ds(ch * groups + j, 1), :]
    for ch in range(3):
        row = wide[pl.ds(6 + ch, 1), :]
        hi = row.astype(BF16).astype(F32)
        grows[ch] = jnp.broadcast_to(row, (SEGS, pixels))
        wide[pl.ds(6 + ch, 1), :] = hi
        wide[pl.ds(22 + ch, 1), :] = hi
        wide[pl.ds(38 + ch, 1), :] = row - hi
    rhs[:, :pixels] = planes[:, :pixels]
    rhs[:, pixels:] = wide[...].astype(BF16)

    def products(n, buf):
        part = table[pl.ds(pl.multiple_of(n * CHUNK, CHUNK), CHUNK), :]
        buf[...] = jnp.dot(part, rhs[...], preferred_element_type=F32)

    def sweep(n, buf, back):
        light = checks[n] * prefix[...]
        for i in range(STEPS):
            rows = pl.ds(i * SEGS, SEGS)
            weight = light * jnp.exp2(buf[rows, :pixels])
            light = light - weight
            weights[rows, :] = weight
        for i in reversed(range(STEPS)):
            rows = pl.ds(i * SEGS, SEGS)
            weight = weights[rows, :]
            gap = buf[rows, pixels:] - back
            back = back + jnp.exp2(buf[rows, :pixels]) * gap
            pull = weight * gap
            zero = one = two = None
            for j in reversed(range(groups)):
                piece = pull[:, j * LANES : (j + 1) * LANES]
                zero = piece if zero is None else zero + piece
                if j > 0:
                    one = zero if one is None else one + zero
                    two = one if two is None else two + one
            sums[rows, 0:LANES] = zero
            sums[rows, LANES : 2 * LANES] = one
            sums[rows, 2 * LANES : 3 * LANES] = two
            for ch in range(3):
                tint = weight * grows[ch]
                total = tint[:, :LANES]
                for j in range(1, groups):
                    total = total + tint[:, j * LANES : (j + 1) * LANES]
                sums[rows, (3 + ch) * LANES : (4 + ch) * LANES] = total
        whole = sums[...]
        hi = whole.astype(BF16)
        low = (whole - hi.astype(F32)).astype(BF16)
        moments[pl.ds(pl.multiple_of(n * CHUNK, CHUNK), CHUNK), :] = jnp.dot(
            hi, reduce[...], preferred_element_type=F32
        ) + jnp.dot(low, reduce[...], preferred_element_type=F32)
        return back

    back = behind[0] * grows[0] + behind[1] * grows[1] + behind[2] * grows[2]
    products(chunks - 1, buf_a)

    turn = chunks // per

    def collect(m, seg):
        block = moments[pl.ds(m * (SEGS * LANES) + seg, LANES, stride=SEGS), :].T
        stage[seg * per + m] = block[:16]

    def pair(h, back):
        n = chunks - 1 - 2 * h
        m = (n // turn + 1) % per
        products(n - 1, buf_b)
        collect(m, n % turn)
        back = sweep(n, buf_a, back)
        collect(m, n % turn - 1)
        products(jnp.maximum(n - 2, 0), buf_a)
        return sweep(n - 1, buf_b, back)

    lax.fori_loop(0, chunks // 2, pair, back)
    for seg in range(SEGS):
        collect(0, seg)

    def deliver(k, _):
        s = slot[k]

        @pl.when(s >= 0)
        def _():
            o = s // CAP
            c = s - o * CAP
            reply[o, pl.ds(pl.multiple_of(c * 8, 8), 8), :] = stage[k, :8, :]
            reply[o, pl.ds(CAP * 8 + c, 1), :] = stage[k, 8:9, :]

        return 0

    lax.fori_loop(0, lmax, deliver, 0)


def gather_kernel(across, side, height, width, asked, got, raw, grads, loss, pieces):
    fields = grads.shape[0]
    shares = got[:, got.shape[1] - 1, :]
    loss[0] = jnp.sum(shares[:, :1]) * (1.0 / (3.0 * height * width))
    field = [raw[f] for f in range(11)]
    shift_x, shift_y = tile_shifts(across, side, height, width)

    def clear(f, _):
        grads[f] = jnp.zeros(grads.shape[1:], F32)
        return 0

    lax.fori_loop(0, fields, clear, 0)

    def received(f):
        at = [c * 8 + f if f < 8 else CAP * 8 + c for c in range(CAP)]
        return jnp.concatenate([got[:, a, :] for a in at], axis=0)

    def shaped(x, y, z, log_scale, quat):
        xx, xy, yy, pos_u, pos_v = conic(x, y, z, log_scale, quat)
        return expanded(xx, xy, yy, pos_u + shift_x, pos_v + shift_y, jnp.zeros_like(x))

    _, pull = jax.vjp(shaped, *field[:3], field[3:6], field[6:10])
    moments = [LN2 * received(f) for f in range(6)]
    gx, gy, gz, gscale, gquat = pull(tuple(moments))
    basis, pull_basis = jax.vjp(directions, *field[:3])
    tints = [received(6 + ch) for ch in range(3)]
    tilts = []
    for m in range(16):
        tilt = None
        for ch in range(3):
            term = tints[ch] * raw[11 + 3 * m + ch]
            tilt = term if tilt is None else tilt + term
            pieces[11 + 3 * m + ch] = tints[ch] * basis[m]
        tilts.append(tilt)
    dx, dy, dz = pull_basis(tilts)
    pieces[0] = gx + dx
    pieces[1] = gy + dy
    pieces[2] = gz + dz
    for f in range(3):
        pieces[3 + f] = gscale[f]
    for f in range(4):
        pieces[6 + f] = gquat[f]
    pieces[10] = moments[5] * (LOG2E / (1.0 + jnp.exp(field[10])))

    def put(s, _):
        index = asked_index(asked, across, s)

        @pl.when(index >= 0)
        def _():
            for f in range(fields):
                grads[f, pl.ds(index, 1), :] = pieces[f, pl.ds(s, 1), :]

        return 0

    lax.fori_loop(0, across * CAP, put, 0)


def tile_planes(side):
    pixel = np.arange(side * side)
    x = (pixel % side - side // 2).astype(np.float64)
    y = (pixel // side - side // 2).astype(np.float64)
    mono = np.stack([x * x, x * y, y * y, x, y, np.ones_like(x)])
    table = np.zeros((LANES, side * side + 3 * LANES))
    for g in range(3):
        table[16 * g : 16 * g + 6, : side * side] = mono
    for ch in range(3):
        at = side * side + ch * LANES
        table[6 + ch, at : at + LANES] = 1.0
        table[22 + ch, at : at + LANES] = 1.0
    return table.astype(ml_dtypes.bfloat16)


def moment_columns(side):
    lane = np.arange(LANES)
    x = lane % side - side // 2
    t = lane // side - side // 2
    step = LANES // side
    one = np.ones_like(x)
    out = np.zeros((6 * LANES, LANES))
    out[:LANES, :6] = np.stack([x * x, x * t, t * t, x, t, one], axis=1)
    out[LANES : 2 * LANES, 1] = step * x
    out[LANES : 2 * LANES, 2] = 2 * step * t - step * step
    out[LANES : 2 * LANES, 4] = step
    out[2 * LANES : 3 * LANES, 2] = 2 * step * step
    for ch in range(3):
        out[(3 + ch) * LANES : (4 + ch) * LANES, 6 + ch] = 1.0
    return out.astype(ml_dtypes.bfloat16)


def filters(side):
    offsets = np.arange(TAPS) - float(RIM)
    taps = np.exp(-offsets * offsets / 4.5)
    taps = taps / taps.sum()
    reach = side + 2 * RIM
    padded = -(-reach // 8) * 8
    fold = LANES // side
    groups = side // fold

    def tap(distance):
        at = distance + RIM
        return np.where((at >= 0) & (at < TAPS), taps[np.clip(at, 0, TAPS - 1)], 0.0)

    out = np.arange(reach) - RIM
    source = np.arange(-side, 2 * side)
    along = tap(source[:, None] - out[None, :])
    fa = np.zeros((3, fold, side, fold, LANES))
    for t in range(fold):
        fa[:, t, :, t, :reach] = along.reshape(3, side, reach)
    fa = fa.reshape(3 * LANES, fold * LANES)
    fb = np.zeros((padded, fold, 3, groups))
    fb[:reach] = along.reshape(3, groups, fold, reach).transpose(3, 2, 0, 1)
    fb = fb.reshape(padded, fold * 3 * groups)
    inner = np.arange(side)
    back = tap(out[:, None] - inner[None, :])
    fc = np.zeros((fold, groups, padded))
    fc[:, :, :reach] = back.reshape(reach, groups, fold).transpose(2, 1, 0)
    fc = fc.reshape(fold * groups, padded)
    fd = np.zeros((fold, LANES, fold, side))
    for t in range(fold):
        fd[t, :reach, t, :] = back
    fd = fd.reshape(fold * LANES, LANES)
    return [m.astype(np.float32) for m in (fa, fb, fc, fd)]


def shifted(x, axis):
    size = lax.axis_size(axis)
    up = [(i, i + 1) for i in range(size - 1)]
    return lax.ppermute(x, axis, up), lax.ppermute(x, axis, [(j, i) for i, j in up])


def per_device(gaussians, tile_lists, tile_counts, depth_order, target):
    owned, fields, block = gaussians.shape
    lmax = tile_lists.shape[2]
    side = target.shape[1]
    pixels = side * side
    groups = pixels // LANES
    across = lax.axis_size("tx")
    height = side * lax.axis_size("ty")
    width = side * across
    slots = across * CAP
    depth = -(-(CAP * 9 + 1) // 8) * 8
    f32 = functools.partial(jax.ShapeDtypeStruct, dtype=F32)
    i32 = functools.partial(jax.ShapeDtypeStruct, dtype=jnp.int32)
    planes = jnp.asarray(tile_planes(side))
    reduce = jnp.asarray(moment_columns(side))
    bands = [jnp.asarray(m) for m in filters(side)]

    fieldwise = jnp.transpose(gaussians, (1, 0, 2))
    request, slot = pl.pallas_call(
        functools.partial(request_kernel, owned, across),
        out_shape=(i32((across, 1, LANES)), i32((lmax,))),
        in_specs=[SMEM] * 3,
        out_specs=(SMEM, SMEM),
        scratch_shapes=[pltpu.SMEM((across,), jnp.int32)],
        compiler_params=PARAMS,
        name="request",
    )(tile_lists, tile_counts, depth_order)
    asked = lax.all_to_all(request, "tx", split_axis=0, concat_axis=0, tiled=True)
    projected = pl.pallas_call(
        functools.partial(project_kernel, 16),
        out_shape=f32((9, owned, block)),
        in_specs=[VMEM],
        out_specs=VMEM,
        compiler_params=PARAMS,
        name="project",
    )(fieldwise)
    send = pl.pallas_call(
        functools.partial(serve_kernel, across, side, float(height), float(width)),
        out_shape=f32((across, depth, block)),
        in_specs=[SMEM, VMEM],
        out_specs=VMEM,
        scratch_shapes=[pltpu.VMEM((9, slots, block), F32)],
        compiler_params=PARAMS,
        name="serve",
    )(asked, projected)
    recv = lax.all_to_all(send, "tx", split_axis=0, concat_axis=0, tiled=True)
    raw = pl.pallas_call(
        functools.partial(pick_kernel, across),
        out_shape=f32((fields, slots, block)),
        in_specs=[SMEM, VMEM],
        out_specs=VMEM,
        compiler_params=PARAMS,
        name="pick",
    )(asked, fieldwise)
    chunks = lmax * block // CHUNK
    wide = pixels + 3 * LANES
    table, checks, prefix, behind, dense = pl.pallas_call(
        forward_kernel,
        out_shape=(
            jax.ShapeDtypeStruct((lmax * block, LANES), BF16),
            f32((chunks, SEGS, pixels)),
            f32((SEGS, pixels)),
            f32((3, SEGS, pixels)),
            f32((6 * groups, LANES)),
        ),
        in_specs=[SMEM, VMEM, VMEM, VMEM],
        out_specs=(VMEM,) * 5,
        scratch_shapes=[
            pltpu.VMEM((lmax * block, LANES), F32),
            pltpu.VMEM((CHUNK, wide), F32),
            pltpu.VMEM((CHUNK, wide), F32),
            pltpu.VMEM((4, SEGS, pixels), F32),
        ],
        compiler_params=PARAMS,
        name="forward",
    )(slot, recv, planes, target.reshape(3 * groups, LANES))
    left, right = shifted(dense, "tx")
    above, below = shifted(jnp.concatenate([left, dense, right], axis=0), "ty")
    slope, part = pl.pallas_call(
        functools.partial(score_entry, side, height, width),
        out_shape=(f32((3 * groups, LANES)), f32((8, LANES))),
        in_specs=[VMEM] * 9,
        out_specs=(VMEM, VMEM),
        compiler_params=PARAMS,
        name="score",
    )(above, left, dense, right, below, *bands)
    down = lax.axis_size("ty")
    shares = [
        lax.ppermute(part, "ty", [(i, (i + k) % down) for i in range(down)]) for k in range(1, down)
    ]
    reply = pl.pallas_call(
        backward_kernel,
        out_shape=f32((across, depth, block)),
        in_specs=[SMEM] + [VMEM] * 7,
        out_specs=VMEM,
        scratch_shapes=[
            pltpu.VMEM((LANES, 2 * pixels), BF16),
            pltpu.VMEM((LANES, pixels), F32),
            pltpu.VMEM((3, SEGS, pixels), F32),
            pltpu.VMEM((CHUNK, 2 * pixels), F32),
            pltpu.VMEM((CHUNK, 2 * pixels), F32),
            pltpu.VMEM((CHUNK, pixels), F32),
            pltpu.VMEM((CHUNK, 6 * LANES), F32),
            pltpu.VMEM((lmax * block, LANES), F32),
            pltpu.VMEM((lmax, 16, LANES), F32),
        ],
        compiler_params=PARAMS,
        name="backward",
    )(slot, table, checks, prefix, behind, slope, planes, reduce)
    column = sum(shares, part)[:1]
    reply = reply.at[:, depth - 1, :].set(jnp.broadcast_to(column, (across, LANES)))
    got = lax.all_to_all(reply, "tx", split_axis=0, concat_axis=0, tiled=True)
    grads, loss = pl.pallas_call(
        functools.partial(gather_kernel, across, side, float(height), float(width)),
        out_shape=(f32((fields, owned, block)), f32((1,))),
        in_specs=[SMEM, VMEM, VMEM],
        out_specs=(VMEM, SMEM),
        scratch_shapes=[pltpu.VMEM((fields, slots, block), F32)],
        compiler_params=PARAMS,
        name="gather",
    )(asked, got, raw)
    return (jnp.transpose(grads, (1, 0, 2)), loss[0])


def solution(mesh):
    return jax.shard_map(
        per_device,
        mesh=mesh,
        in_specs=(
            P(("ty", "tx"), None, None),
            P("ty", "tx", None),
            P("ty", "tx"),
            P(),
            P(None, "ty", "tx"),
        ),
        out_specs=(P(("ty", "tx"), None, None), P()),
        check_vma=False,
    )
```

```python
import functools

import jax
import jax.numpy as jnp
import ml_dtypes
import numpy as np
from jax import lax
from jax.experimental import pallas as pl
from jax.experimental.pallas import tpu as pltpu
from jax.sharding import PartitionSpec as P

CAP = 3
SEGS = 8
LANES = 128
CHUNK = 256
STEPS = CHUNK // SEGS
RIM = 5
TAPS = 2 * RIM + 1
LOG2E = 1.4426950408889634
LN2 = 0.6931471805599453
DARK = -1e30

FOCAL = 1000.0
LOW_PASS = 0.3
STRUCT_WEIGHT = 0.2
LUMA_TERM = 0.0001
CONTRAST_TERM = 0.0009
ROBUST_TERM = 1e-06
HARMONIC_ZERO = 0.28209479177387814
HARMONIC_ONE = 0.4886025119029199
HARMONIC_TWO = (
    1.0925484305920792,
    -1.0925484305920792,
    0.31539156525252005,
    -1.0925484305920792,
    0.5462742152960396,
)
HARMONIC_THREE = (
    -0.5900435899266435,
    2.890611442640554,
    -0.4570457994644658,
    0.3731763325901154,
    -0.4570457994644658,
    1.445305721320277,
    -0.5900435899266435,
)

HIGH = lax.Precision.HIGHEST
F32 = jnp.float32
BF16 = jnp.bfloat16
ANY = pl.BlockSpec(memory_space=pl.ANY)
SMEM = pl.BlockSpec(memory_space=pltpu.SMEM)
VMEM = pl.BlockSpec(memory_space=pltpu.VMEM)
PARAMS = pltpu.CompilerParams(vmem_limit_bytes=24 * 1024 * 1024)


def harmonics(x, y, z):
    xx, yy, zz = x * x, y * y, z * z
    xy, yz, xz = x * y, y * z, x * z
    return [
        HARMONIC_ZERO * jnp.ones_like(x),
        -HARMONIC_ONE * y,
        HARMONIC_ONE * z,
        -HARMONIC_ONE * x,
        HARMONIC_TWO[0] * xy,
        HARMONIC_TWO[1] * yz,
        HARMONIC_TWO[2] * (2.0 * zz - xx - yy),
        HARMONIC_TWO[3] * xz,
        HARMONIC_TWO[4] * (xx - yy),
        HARMONIC_THREE[0] * y * (3.0 * xx - yy),
        HARMONIC_THREE[1] * xy * z,
        HARMONIC_THREE[2] * y * (4.0 * zz - xx - yy),
        HARMONIC_THREE[3] * z * (2.0 * zz - 3.0 * xx - 3.0 * yy),
        HARMONIC_THREE[4] * x * (4.0 * zz - xx - yy),
        HARMONIC_THREE[5] * z * (xx - yy),
        HARMONIC_THREE[6] * x * (xx - 3.0 * yy),
    ]


def directions(x, y, z):
    length = jnp.sqrt(x * x + y * y + z * z)
    return harmonics(x / length, y / length, z / length)


def conic(mean_x, mean_y, mean_z, log_scale, quat):
    scale = [jnp.exp(s) for s in log_scale]
    norm = jnp.sqrt(quat[0] * quat[0] + quat[1] * quat[1] + quat[2] * quat[2] + quat[3] * quat[3])
    w, i, j, k = (q / norm for q in quat)
    rotation = [
        [1.0 - 2.0 * (j * j + k * k), 2.0 * (i * j - w * k), 2.0 * (i * k + w * j)],
        [2.0 * (i * j + w * k), 1.0 - 2.0 * (i * i + k * k), 2.0 * (j * k - w * i)],
        [2.0 * (i * k - w * j), 2.0 * (j * k + w * i), 1.0 - 2.0 * (i * i + j * j)],
    ]
    scaled = [[rotation[r][c] * scale[c] for c in range(3)] for r in range(3)]

    def sigma(r, c):
        return scaled[r][0] * scaled[c][0] + scaled[r][1] * scaled[c][1] + scaled[r][2] * scaled[c][2]

    s00, s01, s02, s11, s12, s22 = (
        sigma(0, 0), sigma(0, 1), sigma(0, 2), sigma(1, 1), sigma(1, 2), sigma(2, 2),
    )
    inverse_z = 1.0 / mean_z
    diag = FOCAL * inverse_z
    jac_xz = -FOCAL * mean_x * inverse_z * inverse_z
    jac_yz = -FOCAL * mean_y * inverse_z * inverse_z
    u0, u1, u2 = diag * s00 + jac_xz * s02, diag * s01 + jac_xz * s12, diag * s02 + jac_xz * s22
    v1, v2 = diag * s11 + jac_yz * s12, diag * s12 + jac_yz * s22
    cov_uu = u0 * diag + u2 * jac_xz + LOW_PASS
    cov_uv = u1 * diag + u2 * jac_yz
    cov_vv = v1 * diag + v2 * jac_yz + LOW_PASS
    determinant = cov_uu * cov_vv - cov_uv * cov_uv
    half = -0.5 * LOG2E
    xx = half * (cov_vv / determinant)
    xy = (-2.0 * half) * (cov_uv / determinant)
    yy = half * (cov_uu / determinant)
    return xx, xy, yy, FOCAL * mean_x * inverse_z, FOCAL * mean_y * inverse_z


def expanded(xx, xy, yy, pos_u, pos_v, log_opacity):
    x1 = -2.0 * xx * pos_u - xy * pos_v
    y1 = -2.0 * yy * pos_v - xy * pos_u
    one = xx * pos_u * pos_u + xy * pos_u * pos_v + yy * pos_v * pos_v + log_opacity
    return xx, xy, yy, x1, y1, one


def tile_shifts(across, side, height, width):
    column = lax.broadcasted_iota(jnp.int32, (across, LANES), 0).astype(F32)
    column = jnp.concatenate([column] * CAP, axis=0)
    row = lax.axis_index("ty").astype(F32)
    shift_x = (0.5 * width - 0.5 * side - 0.5) - side * column
    shift_y = jnp.full(column.shape, (0.5 * height - 0.5 * side - 0.5) - side * row, F32)
    return shift_x, shift_y


def request_kernel(owned, across, lists, count, order, request, slot, seen):
    base = lax.axis_index("ty") * across
    for o in range(across):
        seen[o] = 0
        for c in range(CAP):
            request[o, 0, c] = -1
    used = count[0, 0]

    def entry(k, _):
        @pl.when(k < used)
        def _():
            block = order[lists[0, 0, k]]
            home = block // owned
            local = block - home * owned
            home = home - base
            at = seen[home]
            seen[home] = at + 1
            request[home, 0, at] = local
            slot[k] = home * CAP + at

        @pl.when(k >= used)
        def _():
            slot[k] = -1

        return 0

    lax.fori_loop(0, slot.shape[0], entry, 0, unroll=True)


def project_kernel(span, gaussians, out):
    def part(n, _):
        rows = pl.ds(pl.multiple_of(n * span, span), span)
        field = [gaussians[f, rows, :] for f in range(11)]
        light = -LOG2E * jnp.log(1.0 + jnp.exp(-field[10])) + float(np.log2(0.99))
        values = list(conic(field[0], field[1], field[2], field[3:6], field[6:10]))
        values.append(jnp.maximum(light, DARK))
        basis = directions(field[0], field[1], field[2])
        for ch in range(3):
            color = 0.5 + basis[0] * gaussians[11 + ch, rows, :]
            for m in range(1, 16):
                color = color + basis[m] * gaussians[11 + 3 * m + ch, rows, :]
            values.append(color)
        for f in range(9):
            out[f, rows, :] = values[f]
        return 0

    lax.fori_loop(0, gaussians.shape[1] // span, part, 0)


def asked_index(asked, across, s):
    c = s // across
    return asked[s - c * across, 0, c]


def serve_kernel(across, side, height, width, asked, projected, send, chosen):
    def pick(s, _):
        index = jnp.maximum(asked_index(asked, across, s), 0)
        for f in range(9):
            chosen[f, pl.ds(s, 1), :] = projected[f, pl.ds(index, 1), :]
        return 0

    lax.fori_loop(0, across * CAP, pick, 0, unroll=True)
    shift_x, shift_y = tile_shifts(across, side, height, width)
    rows = list(
        expanded(
            chosen[0], chosen[1], chosen[2], chosen[3] + shift_x, chosen[4] + shift_y, chosen[5]
        )
    ) + [chosen[6], chosen[7], chosen[8]]
    for c in range(CAP):
        for f in range(9):
            at = c * 8 + f if f < 8 else CAP * 8 + c
            send[:, at, :] = rows[f][c * across : (c + 1) * across]


def monomials(side):
    pixels = side * side
    lane = lax.broadcasted_iota(jnp.int32, (8, pixels), 1)
    row = lax.broadcasted_iota(jnp.int32, (8, pixels), 0)
    x = ((lane & (side - 1)) - side // 2).astype(F32)
    y = ((lane >> (side.bit_length() - 1)) - side // 2).astype(F32)
    mono = jnp.zeros((8, pixels), F32)
    for at, value in enumerate((x * x, x * y, y * y, x, y, jnp.ones_like(x))):
        mono = jnp.where(row == at, value, mono)
    blank = jnp.zeros((8, pixels), F32)
    rest = jnp.zeros((LANES - 48, pixels), F32)
    return jnp.concatenate([mono, blank] * 3 + [rest], axis=0).astype(BF16)


def spreaders():
    row = lax.broadcasted_iota(jnp.int32, (LANES, LANES), 0)
    return jnp.concatenate(
        [jnp.where((row == 6 + c) | (row == 22 + c), 1.0, 0.0).astype(F32) for c in range(3)], axis=1
    ).astype(BF16)


def repeated(x, times):
    return jnp.concatenate([x] * times, axis=1)


def forward_kernel(
    side, slot, recv, target, table, checks, prefix, behind, dense,
    planes, spread, buf_a, buf_b, ends,
):
    lmax = slot.shape[0]
    per = lmax // SEGS
    pixels = prefix.shape[1]
    groups = pixels // LANES
    planes[:, :pixels] = monomials(side)
    planes[:, pixels:] = spreaders()
    zero_rows = jnp.zeros((7, LANES), F32)
    dead = jnp.where(lax.broadcasted_iota(jnp.int32, (16, LANES), 0) == 5, DARK, 0.0)
    is_color = lax.broadcasted_iota(jnp.int32, (16, LANES), 0) >= 6
    filler = jnp.zeros((LANES - 48, LANES), F32)

    def place(m, seg):
        s = slot[seg * per + m]
        live = s >= 0
        s = jnp.maximum(s, 0)
        o = s // CAP
        c = s - o * CAP
        head = recv[o, pl.ds(pl.multiple_of(c * 8, 8), 8), :]
        tail = recv[o, pl.ds(CAP * 8 + c, 1), :]
        rows = jnp.concatenate([head, tail, zero_rows], axis=0)
        rows = jnp.where(live, rows, dead)
        hi = rows.astype(BF16).astype(F32)
        rest = rows - hi
        mid = rest.astype(BF16).astype(F32)
        low = (rest - mid).astype(BF16).astype(F32)
        third = jnp.where(is_color, hi, low)
        stacked = jnp.concatenate([hi, mid, third, filler], axis=0)
        spread[pl.ds(m * (SEGS * LANES) + seg, LANES, stride=SEGS), :] = stacked.T

    for seg in range(SEGS):
        place(0, seg)

    def products(n, buf):
        part = spread[pl.ds(pl.multiple_of(n * CHUNK, CHUNK), CHUNK), :].astype(BF16)
        table[pl.ds(pl.multiple_of(n * CHUNK, CHUNK), CHUNK), :] = part
        buf[...] = jnp.dot(part, planes[...], preferred_element_type=F32)

    def blend(n, buf, carry):
        light, red, green, blue = carry
        checks[n] = light
        for i in range(STEPS):
            rows = pl.ds(i * SEGS, SEGS)
            weight = light * jnp.exp2(buf[rows, :pixels])
            light = light - weight
            red = red + weight * repeated(buf[rows, pixels : pixels + LANES], groups)
            green = green + weight * repeated(buf[rows, pixels + LANES : pixels + 2 * LANES], groups)
            blue = blue + weight * repeated(
                buf[rows, pixels + 2 * LANES : pixels + 3 * LANES], groups
            )
        return light, red, green, blue

    products(0, buf_a)
    chunks = lmax * LANES // CHUNK

    turn = chunks // per
    share = SEGS // turn

    def pair(h, carry):
        n = 2 * h
        m = (n // turn + 1) % per
        products(n + 1, buf_b)
        for q in range(share):
            place(m, (n % turn) * share + q)
        carry = blend(n, buf_a, carry)
        for q in range(share):
            place(m, (n % turn + 1) * share + q)
        products(jnp.minimum(n + 2, chunks - 1), buf_a)
        return blend(n + 1, buf_b, carry)

    start = (jnp.ones((SEGS, pixels), F32),) + (jnp.zeros((SEGS, pixels), F32),) * 3
    carry = lax.fori_loop(0, chunks // 2, pair, start)
    for f in range(4):
        ends[f] = carry[f]
    ahead = jnp.ones((1, pixels), F32)
    for seg in range(SEGS):
        prefix[pl.ds(seg, 1), :] = ahead
        ahead = ahead * ends[0, pl.ds(seg, 1), :]
    for ch in range(3):
        seen = jnp.zeros((1, pixels), F32)
        for seg in reversed(range(SEGS)):
            behind[ch, pl.ds(seg, 1), :] = seen
            seen = ends[1 + ch, pl.ds(seg, 1), :] + ends[0, pl.ds(seg, 1), :] * seen
        for j in range(groups):
            dense[pl.ds(ch * groups + j, 1), :] = seen[:, j * LANES : (j + 1) * LANES]
    dense[3 * groups :, :] = target[...]


def similarity(mean_a, mean_b, square_a, square_b, cross):
    var_a = square_a - mean_a * mean_a
    var_b = square_b - mean_b * mean_b
    covar = cross - mean_a * mean_b
    top = (2.0 * mean_a * mean_b + LUMA_TERM) * (2.0 * covar + CONTRAST_TERM)
    bottom = (mean_a * mean_a + mean_b * mean_b + LUMA_TERM) * (var_a + var_b + CONTRAST_TERM)
    return top / bottom


def tap(distance):
    weights = [float(np.exp(-((k - RIM) ** 2) / 4.5)) for k in range(TAPS)]
    value = jnp.exp(distance * distance * (-1.0 / 4.5)) * (1.0 / sum(weights))
    return jnp.where(jnp.abs(distance) <= RIM, value, 0.0)


def places(shape, dim):
    return lax.broadcasted_iota(jnp.int32, shape, dim)


def bands(side, padded):
    fold = LANES // side
    groups = side // fold
    reach = side + 2 * RIM
    shape = (3 * side, LANES)
    out = places(shape, 1)
    along = tap((places(shape, 0) - side - out + RIM).astype(F32))
    along = jnp.where(out < reach, along, 0.0)
    blank = jnp.zeros((side, LANES), F32)
    fa = jnp.concatenate(
        [
            jnp.concatenate(
                [along[h * side : (h + 1) * side] if u == t else blank for u in range(fold)], axis=1
            )
            for h in range(3)
            for t in range(fold)
        ],
        axis=0,
    )
    block = 3 * groups
    shape = (padded, fold * block)
    out, at = places(shape, 0), places(shape, 1)
    t = jnp.zeros(shape, jnp.int32)
    for k in range(1, fold):
        t = t + jnp.where(at >= k * block, 1, 0)
    source = (at - t * block) * fold + t - side
    fb = jnp.where(out < reach, tap((source - out + RIM).astype(F32)), 0.0)
    shape = (fold * groups, padded)
    row, out = places(shape, 0), places(shape, 1)
    t = jnp.zeros(shape, jnp.int32)
    for k in range(1, fold):
        t = t + jnp.where(row >= k * groups, 1, 0)
    source = (row - t * groups) * fold + t
    fc = jnp.where(out < reach, tap((out - RIM - source).astype(F32)), 0.0)
    shape = (LANES, LANES)
    out, at = places(shape, 0), places(shape, 1)
    back = tap((out - RIM - (at & (side - 1))).astype(F32))
    back = jnp.where(out < reach, back, 0.0)
    fd = jnp.concatenate(
        [jnp.where((at >= t * side) & (at < (t + 1) * side), back, 0.0) for t in range(fold)], axis=0
    )
    return fa, fb, fc, fd


def score_kernel(side, height, width, near, slope, loss):
    fa, fb, fc, fd = bands(side, -(-(side + 2 * RIM) // 8) * 8)
    rows3 = near[4].shape[0] // 2
    groups = rows3 // 3
    fold = LANES // side
    fields = [[], [], [], [], []]
    for v in range(3):
        strip = jnp.concatenate([near[3 * v + h] for h in range(3)], axis=1)
        image, target = strip[:rows3], strip[rows3:]
        for f, plane in enumerate([image, target, image * image, target * target, image * target]):
            fields[f].append(plane)
    stack = jnp.concatenate([fields[f][v] for f in range(5) for v in range(3)], axis=0)
    wide = jnp.dot(stack, fa, precision=HIGH, preferred_element_type=F32)
    columns = []
    for f in range(5):
        for ch in range(3):
            parts = []
            for t in range(fold):
                for v in range(3):
                    at = (f * 3 + v) * rows3 + ch * groups
                    parts.append(wide[at : at + groups, t * LANES : (t + 1) * LANES])
            columns.append(jnp.concatenate(parts, axis=0))
    tall = jnp.concatenate(columns, axis=1)
    maps = jnp.dot(fb, tall, precision=HIGH, preferred_element_type=F32)
    span = 3 * LANES
    score, pull = jax.vjp(similarity, *[maps[:, f * span : (f + 1) * span] for f in range(5)])
    parts = pull(jnp.full(score.shape, -STRUCT_WEIGHT, F32))
    row = lax.broadcasted_iota(jnp.int32, score.shape, 0)
    col = lax.broadcasted_iota(jnp.int32, (score.shape[0], LANES), 1)
    col = jnp.concatenate([col] * 3, axis=1)
    row_at = row - RIM + lax.axis_index("ty") * side
    col_at = col - RIM + lax.axis_index("tx") * side
    reach = side + 2 * RIM
    inside = (
        (row_at >= 0) & (row_at < height) & (col_at >= 0) & (col_at < width)
        & (row < reach) & (col < reach)
    )
    own = (row >= RIM) & (row < RIM + side) & (col >= RIM) & (col < RIM + side)
    coeffs = jnp.concatenate(
        [jnp.where(inside, parts[f], 0.0) for f in (0, 2, 4)], axis=1
    )
    low = jnp.dot(fc, coeffs, precision=HIGH, preferred_element_type=F32)
    rows = []
    for n in range(9):
        rows.append(
            jnp.concatenate(
                [
                    low[t * groups : (t + 1) * groups, n * LANES : (n + 1) * LANES]
                    for t in range(fold)
                ],
                axis=1,
            )
        )
    smooth = jnp.dot(
        jnp.concatenate(rows, axis=0), fd, precision=HIGH, preferred_element_type=F32
    )
    image, target = near[4][:rows3, :], near[4][rows3:, :]
    gap = image - target
    robust = jnp.sqrt(gap * gap + ROBUST_TERM)
    slope[...] = (
        smooth[:rows3]
        + 2.0 * image * smooth[rows3 : 2 * rows3]
        + target * smooth[2 * rows3 :]
        + (1.0 - STRUCT_WEIGHT) * gap / robust
    )
    total = (1.0 - STRUCT_WEIGHT) * jnp.sum(robust) + STRUCT_WEIGHT * jnp.sum(
        jnp.where(own, 1.0 - score, 0.0)
    )
    loss[...] = jnp.full(loss.shape, total, F32)


def score_entry(side, height, width, *refs):
    above, left, own, right, below = refs[:5]
    rows = own.shape[0]
    near = [above[h * rows : (h + 1) * rows, :] for h in range(3)]
    near += [left[...], own[...], right[...]]
    near += [below[h * rows : (h + 1) * rows, :] for h in range(3)]
    score_kernel(side, height, width, near, *refs[5:])


def backward_kernel(
    side, table, checks, prefix, behind, slope, reduce, stage,
    rhs, wide, grows, buf_a, buf_b, weights, sums, moments,
):
    lmax = stage.shape[0]
    per = lmax // SEGS
    pixels = prefix.shape[1]
    groups = pixels // LANES
    chunks = lmax * LANES // CHUNK
    wide[...] = jnp.zeros_like(wide)
    for ch in range(3):
        for j in range(groups):
            lanes = pl.ds(j * LANES, LANES)
            wide[pl.ds(6 + ch, 1), lanes] = slope[pl.ds(ch * groups + j, 1), :]
    for ch in range(3):
        row = wide[pl.ds(6 + ch, 1), :]
        hi = row.astype(BF16).astype(F32)
        grows[ch] = jnp.broadcast_to(row, (SEGS, pixels))
        wide[pl.ds(6 + ch, 1), :] = hi
        wide[pl.ds(22 + ch, 1), :] = hi
        wide[pl.ds(38 + ch, 1), :] = row - hi
    rhs[:, :pixels] = monomials(side)
    rhs[:, pixels:] = wide[...].astype(BF16)

    def products(n, buf):
        part = table[pl.ds(pl.multiple_of(n * CHUNK, CHUNK), CHUNK), :]
        buf[...] = jnp.dot(part, rhs[...], preferred_element_type=F32)

    def sweep(n, buf, back):
        light = checks[n] * prefix[...]
        for i in range(STEPS):
            rows = pl.ds(i * SEGS, SEGS)
            weight = light * jnp.exp2(buf[rows, :pixels])
            light = light - weight
            weights[rows, :] = weight
        for i in reversed(range(STEPS)):
            rows = pl.ds(i * SEGS, SEGS)
            weight = weights[rows, :]
            gap = buf[rows, pixels:] - back
            back = back + jnp.exp2(buf[rows, :pixels]) * gap
            pull = weight * gap
            zero = one = two = None
            for j in reversed(range(groups)):
                piece = pull[:, j * LANES : (j + 1) * LANES]
                zero = piece if zero is None else zero + piece
                if j > 0:
                    one = zero if one is None else one + zero
                    two = one if two is None else two + one
            sums[rows, 0:LANES] = zero
            sums[rows, LANES : 2 * LANES] = one
            sums[rows, 2 * LANES : 3 * LANES] = two
            for ch in range(3):
                tint = weight * grows[ch]
                total = tint[:, :LANES]
                for j in range(1, groups):
                    total = total + tint[:, j * LANES : (j + 1) * LANES]
                sums[rows, (3 + ch) * LANES : (4 + ch) * LANES] = total
        whole = sums[...]
        hi = whole.astype(BF16)
        low = (whole - hi.astype(F32)).astype(BF16)
        both = jnp.dot(
            jnp.concatenate([hi, low], axis=0), reduce[...], preferred_element_type=F32
        )
        moments[pl.ds(pl.multiple_of(n * CHUNK, CHUNK), CHUNK), :] = both[:CHUNK] + both[CHUNK:]
        return back

    back = behind[0] * grows[0] + behind[1] * grows[1] + behind[2] * grows[2]
    products(chunks - 1, buf_a)

    turn = chunks // per
    share = SEGS // turn

    def collect(m, seg):
        block = moments[pl.ds(m * (SEGS * LANES) + seg, LANES, stride=SEGS), :].T
        stage[seg * per + m] = block[:16]

    def pair(h, back):
        n = chunks - 1 - 2 * h
        m = (n // turn + 1) % per
        products(n - 1, buf_b)
        for q in range(share):
            collect(m, (n % turn) * share + q)
        back = sweep(n, buf_a, back)
        for q in range(share):
            collect(m, (n % turn - 1) * share + q)
        products(jnp.maximum(n - 2, 0), buf_a)
        return sweep(n - 1, buf_b, back)

    lax.fori_loop(0, chunks // 2, pair, back)
    for seg in range(SEGS):
        collect(0, seg)


def deliver_kernel(slot, stage, part, *refs):
    reply = refs[-1]
    column = part[...]
    for share in refs[:-1]:
        column = column + share[...]
    for o in range(reply.shape[0]):
        reply[o, pl.ds(reply.shape[1] - 1, 1), :] = column[:1]

    def deliver(k, _):
        s = slot[k]

        @pl.when(s >= 0)
        def _():
            o = s // CAP
            c = s - o * CAP
            reply[o, pl.ds(pl.multiple_of(c * 8, 8), 8), :] = stage[k, :8, :]
            reply[o, pl.ds(CAP * 8 + c, 1), :] = stage[k, 8:9, :]

        return 0

    lax.fori_loop(0, slot.shape[0], deliver, 0)


def gather_kernel(
    across, side, height, width, asked, got, gaussians, grads, loss, sums, zeros, pieces, wanted, sem
):
    owned = gaussians.shape[1]
    parts = owned // 8
    shares = got[:, got.shape[1] - 1, :]
    loss[0] = jnp.sum(shares[:, :1]) * (1.0 / (3.0 * height * width))
    zeros[...] = jnp.zeros_like(zeros)
    sums[...] = jnp.zeros_like(sums)
    for g in range(parts + 1):
        wanted[g] = 0
    for s in range(across * CAP):
        c, t = divmod(s, across)
        index = asked[t, 0, c]
        index = jnp.where(index >= 0, index, owned)
        wanted[index // 8] = 1
        row = pl.ds(index, 1)
        for f in range(9):
            at = c * 8 + f if f < 8 else CAP * 8 + c
            sums[f, row, :] = got[t, at : at + 1, :]
        sums[9, row, :] = jnp.full((1, LANES), t + 1.0, F32)

    def target(g):
        return grads.at[:, pl.ds(pl.multiple_of(g * 8, 8), 8), :]

    def blank(g, _):
        @pl.when(wanted[g] == 0)
        def _():
            pltpu.make_async_copy(zeros, target(g), sem.at[g]).start()

        return 0

    lax.fori_loop(0, parts, blank, 0)
    row_at = lax.axis_index("ty").astype(F32)
    shift_y = (0.5 * height - 0.5 * side - 0.5) - side * row_at

    def solve(g):
        rows = pl.ds(pl.multiple_of(g * 8, 8), 8)
        field = [gaussians[f, rows, :] for f in range(11)]
        tile = sums[9, rows, :]
        live = tile > 0.0
        shift_x = (0.5 * width - 0.5 * side - 0.5) - side * (tile - 1.0)

        def put(f, value):
            pieces[g, f] = jnp.where(live, value, 0.0)

        def shaped(x, y, z, log_scale, quat):
            xx, xy, yy, pos_u, pos_v = conic(x, y, z, log_scale, quat)
            return expanded(xx, xy, yy, pos_u + shift_x, pos_v + shift_y, jnp.zeros_like(x))

        _, pull = jax.vjp(shaped, *field[:3], field[3:6], field[6:10])
        moments = [LN2 * sums[f, rows, :] for f in range(6)]
        gx, gy, gz, gscale, gquat = pull(tuple(moments))
        basis, pull_basis = jax.vjp(directions, *field[:3])
        tints = [sums[6 + ch, rows, :] for ch in range(3)]
        tilts = []
        for m in range(16):
            tilt = None
            for ch in range(3):
                term = tints[ch] * gaussians[11 + 3 * m + ch, rows, :]
                tilt = term if tilt is None else tilt + term
                put(11 + 3 * m + ch, tints[ch] * basis[m])
            tilts.append(tilt)
        dx, dy, dz = pull_basis(tilts)
        put(0, gx + dx)
        put(1, gy + dy)
        put(2, gz + dz)
        for f in range(3):
            put(3 + f, gscale[f])
        for f in range(4):
            put(6 + f, gquat[f])
        put(10, moments[5] * (LOG2E / (1.0 + jnp.exp(field[10]))))
        pltpu.make_async_copy(pieces.at[g], target(g), sem.at[g]).start()

    def part(g, _):
        @pl.when(wanted[g] > 0)
        def _():
            solve(g)

        return 0

    lax.fori_loop(0, parts, part, 0)

    def finish(g, _):
        pltpu.make_async_copy(zeros, target(g), sem.at[g]).wait()
        return 0

    lax.fori_loop(0, parts, finish, 0)


def moment_columns(side):
    lane = np.arange(LANES)
    x = lane % side - side // 2
    t = lane // side - side // 2
    step = LANES // side
    one = np.ones_like(x)
    out = np.zeros((6 * LANES, LANES))
    out[:LANES, :6] = np.stack([x * x, x * t, t * t, x, t, one], axis=1)
    out[LANES : 2 * LANES, 1] = step * x
    out[LANES : 2 * LANES, 2] = 2 * step * t - step * step
    out[LANES : 2 * LANES, 4] = step
    out[2 * LANES : 3 * LANES, 2] = 2 * step * step
    for ch in range(3):
        out[(3 + ch) * LANES : (4 + ch) * LANES, 6 + ch] = 1.0
    return out.astype(ml_dtypes.bfloat16)


def shifted(x, axis):
    size = lax.axis_size(axis)
    up = [(i, i + 1) for i in range(size - 1)]
    return lax.ppermute(x, axis, up), lax.ppermute(x, axis, [(j, i) for i, j in up])


def per_device(gaussians, tile_lists, tile_counts, depth_order, target):
    owned, fields, block = gaussians.shape
    lmax = tile_lists.shape[2]
    side = target.shape[1]
    pixels = side * side
    groups = pixels // LANES
    across = lax.axis_size("tx")
    height = side * lax.axis_size("ty")
    width = side * across
    slots = across * CAP
    depth = -(-(CAP * 9 + 1) // 8) * 8
    f32 = functools.partial(jax.ShapeDtypeStruct, dtype=F32)
    i32 = functools.partial(jax.ShapeDtypeStruct, dtype=jnp.int32)
    reduce = jnp.asarray(moment_columns(side))

    fieldwise = jnp.transpose(gaussians, (1, 0, 2))
    request, slot = pl.pallas_call(
        functools.partial(request_kernel, owned, across),
        out_shape=(i32((across, 1, LANES)), i32((lmax,))),
        in_specs=[SMEM] * 3,
        out_specs=(SMEM, SMEM),
        scratch_shapes=[pltpu.SMEM((across,), jnp.int32)],
        name="request",
    )(tile_lists, tile_counts, depth_order)
    asked = lax.all_to_all(request, "tx", split_axis=0, concat_axis=0, tiled=True)
    projected = pl.pallas_call(
        functools.partial(project_kernel, 16),
        out_shape=f32((9, owned, block)),
        in_specs=[VMEM],
        out_specs=VMEM,
        compiler_params=PARAMS,
        name="project",
    )(fieldwise)
    send = pl.pallas_call(
        functools.partial(serve_kernel, across, side, float(height), float(width)),
        out_shape=f32((across, depth, block)),
        in_specs=[SMEM, VMEM],
        out_specs=VMEM,
        scratch_shapes=[pltpu.VMEM((9, slots, block), F32)],
        compiler_params=PARAMS,
        name="serve",
    )(asked, projected)
    recv = lax.all_to_all(send, "tx", split_axis=0, concat_axis=0, tiled=True)
    chunks = lmax * block // CHUNK
    wide = pixels + 3 * LANES
    table, checks, prefix, behind, dense = pl.pallas_call(
        functools.partial(forward_kernel, side),
        out_shape=(
            jax.ShapeDtypeStruct((lmax * block, LANES), BF16),
            f32((chunks, SEGS, pixels)),
            f32((SEGS, pixels)),
            f32((3, SEGS, pixels)),
            f32((6 * groups, LANES)),
        ),
        in_specs=[SMEM, VMEM, VMEM],
        out_specs=(VMEM,) * 5,
        scratch_shapes=[
            pltpu.VMEM((LANES, wide), BF16),
            pltpu.VMEM((lmax * block, LANES), F32),
            pltpu.VMEM((CHUNK, wide), F32),
            pltpu.VMEM((CHUNK, wide), F32),
            pltpu.VMEM((4, SEGS, pixels), F32),
        ],
        compiler_params=PARAMS,
        name="forward",
    )(slot, recv, target.reshape(3 * groups, LANES))
    left, right = shifted(dense, "tx")
    above, below = shifted(jnp.concatenate([left, dense, right], axis=0), "ty")
    slope, part = pl.pallas_call(
        functools.partial(score_entry, side, height, width),
        out_shape=(f32((3 * groups, LANES)), f32((8, LANES))),
        in_specs=[VMEM] * 5,
        out_specs=(VMEM, VMEM),
        compiler_params=PARAMS,
        name="score",
    )(above, left, dense, right, below)
    down = lax.axis_size("ty")
    shares = [
        lax.ppermute(part, "ty", [(i, (i + k) % down) for i in range(down)]) for k in range(1, down)
    ]
    stage = pl.pallas_call(
        functools.partial(backward_kernel, side),
        out_shape=f32((lmax, 16, LANES)),
        in_specs=[VMEM] * 6,
        out_specs=VMEM,
        scratch_shapes=[
            pltpu.VMEM((LANES, 2 * pixels), BF16),
            pltpu.VMEM((LANES, pixels), F32),
            pltpu.VMEM((3, SEGS, pixels), F32),
            pltpu.VMEM((CHUNK, 2 * pixels), F32),
            pltpu.VMEM((CHUNK, 2 * pixels), F32),
            pltpu.VMEM((CHUNK, pixels), F32),
            pltpu.VMEM((CHUNK, 6 * LANES), F32),
            pltpu.VMEM((lmax * block, LANES), F32),
        ],
        compiler_params=PARAMS,
        name="backward",
    )(table, checks, prefix, behind, slope, reduce)
    reply = pl.pallas_call(
        deliver_kernel,
        out_shape=f32((across, depth, block)),
        in_specs=[SMEM] + [VMEM] * (1 + down),
        out_specs=VMEM,
        compiler_params=PARAMS,
        name="deliver",
    )(slot, stage, part, *shares)
    got = lax.all_to_all(reply, "tx", split_axis=0, concat_axis=0, tiled=True)
    grads, loss = pl.pallas_call(
        functools.partial(gather_kernel, across, side, float(height), float(width)),
        out_shape=(f32((fields, owned, block)), f32((1,))),
        in_specs=[SMEM, VMEM, VMEM],
        out_specs=(ANY, SMEM),
        scratch_shapes=[
            pltpu.VMEM((10, owned + 8, block), F32),
            pltpu.VMEM((fields, 8, block), F32),
            pltpu.VMEM((owned // 8, fields, 8, block), F32),
            pltpu.SMEM((owned // 8 + 1,), jnp.int32),
            pltpu.SemaphoreType.DMA((owned // 8,)),
        ],
        compiler_params=PARAMS,
        name="gather",
    )(asked, got, fieldwise)
    return (jnp.transpose(grads, (1, 0, 2)), loss[0])


def solution(mesh):
    return jax.shard_map(
        per_device,
        mesh=mesh,
        in_specs=(
            P(("ty", "tx"), None, None),
            P("ty", "tx", None),
            P("ty", "tx"),
            P(),
            P(None, "ty", "tx"),
        ),
        out_specs=(P(("ty", "tx"), None, None), P()),
        check_vma=False,
    )
```

```python
import functools

import jax
import jax.numpy as jnp
import ml_dtypes
import numpy as np
from jax import lax
from jax.experimental import pallas as pl
from jax.experimental.pallas import tpu as pltpu
from jax.sharding import PartitionSpec as P

CAP = 3
SEGS = 8
LANES = 128
CHUNK = 256
STEPS = CHUNK // SEGS
SPAN = 4
RIM = 5
TAPS = 2 * RIM + 1
LOG2E = 1.4426950408889634
LN2 = 0.6931471805599453
DARK = -1e30

FOCAL = 1000.0
LOW_PASS = 0.3
STRUCT_WEIGHT = 0.2
LUMA_TERM = 0.0001
CONTRAST_TERM = 0.0009
ROBUST_TERM = 1e-06
HARMONIC_ZERO = 0.28209479177387814
HARMONIC_ONE = 0.4886025119029199
HARMONIC_TWO = (
    1.0925484305920792,
    -1.0925484305920792,
    0.31539156525252005,
    -1.0925484305920792,
    0.5462742152960396,
)
HARMONIC_THREE = (
    -0.5900435899266435,
    2.890611442640554,
    -0.4570457994644658,
    0.3731763325901154,
    -0.4570457994644658,
    1.445305721320277,
    -0.5900435899266435,
)

HIGH = lax.Precision.HIGHEST
F32 = jnp.float32
BF16 = jnp.bfloat16
ANY = pl.BlockSpec(memory_space=pl.ANY)
SMEM = pl.BlockSpec(memory_space=pltpu.SMEM)
VMEM = pl.BlockSpec(memory_space=pltpu.VMEM)
PARAMS = pltpu.CompilerParams(vmem_limit_bytes=24 * 1024 * 1024)


def harmonics(x, y, z):
    xx, yy, zz = x * x, y * y, z * z
    xy, yz, xz = x * y, y * z, x * z
    return [
        HARMONIC_ZERO * jnp.ones_like(x),
        -HARMONIC_ONE * y,
        HARMONIC_ONE * z,
        -HARMONIC_ONE * x,
        HARMONIC_TWO[0] * xy,
        HARMONIC_TWO[1] * yz,
        HARMONIC_TWO[2] * (2.0 * zz - xx - yy),
        HARMONIC_TWO[3] * xz,
        HARMONIC_TWO[4] * (xx - yy),
        HARMONIC_THREE[0] * y * (3.0 * xx - yy),
        HARMONIC_THREE[1] * xy * z,
        HARMONIC_THREE[2] * y * (4.0 * zz - xx - yy),
        HARMONIC_THREE[3] * z * (2.0 * zz - 3.0 * xx - 3.0 * yy),
        HARMONIC_THREE[4] * x * (4.0 * zz - xx - yy),
        HARMONIC_THREE[5] * z * (xx - yy),
        HARMONIC_THREE[6] * x * (xx - 3.0 * yy),
    ]


def directions(x, y, z):
    length = jnp.sqrt(x * x + y * y + z * z)
    return harmonics(x / length, y / length, z / length)


def conic(mean_x, mean_y, mean_z, log_scale, quat):
    scale = [jnp.exp(s) for s in log_scale]
    norm = jnp.sqrt(quat[0] * quat[0] + quat[1] * quat[1] + quat[2] * quat[2] + quat[3] * quat[3])
    w, i, j, k = (q / norm for q in quat)
    rotation = [
        [1.0 - 2.0 * (j * j + k * k), 2.0 * (i * j - w * k), 2.0 * (i * k + w * j)],
        [2.0 * (i * j + w * k), 1.0 - 2.0 * (i * i + k * k), 2.0 * (j * k - w * i)],
        [2.0 * (i * k - w * j), 2.0 * (j * k + w * i), 1.0 - 2.0 * (i * i + j * j)],
    ]
    scaled = [[rotation[r][c] * scale[c] for c in range(3)] for r in range(3)]

    def sigma(r, c):
        return scaled[r][0] * scaled[c][0] + scaled[r][1] * scaled[c][1] + scaled[r][2] * scaled[c][2]

    s00, s01, s02, s11, s12, s22 = (
        sigma(0, 0), sigma(0, 1), sigma(0, 2), sigma(1, 1), sigma(1, 2), sigma(2, 2),
    )
    inverse_z = 1.0 / mean_z
    diag = FOCAL * inverse_z
    jac_xz = -FOCAL * mean_x * inverse_z * inverse_z
    jac_yz = -FOCAL * mean_y * inverse_z * inverse_z
    u0, u1, u2 = diag * s00 + jac_xz * s02, diag * s01 + jac_xz * s12, diag * s02 + jac_xz * s22
    v1, v2 = diag * s11 + jac_yz * s12, diag * s12 + jac_yz * s22
    cov_uu = u0 * diag + u2 * jac_xz + LOW_PASS
    cov_uv = u1 * diag + u2 * jac_yz
    cov_vv = v1 * diag + v2 * jac_yz + LOW_PASS
    determinant = cov_uu * cov_vv - cov_uv * cov_uv
    half = -0.5 * LOG2E
    xx = half * (cov_vv / determinant)
    xy = (-2.0 * half) * (cov_uv / determinant)
    yy = half * (cov_uu / determinant)
    return xx, xy, yy, FOCAL * mean_x * inverse_z, FOCAL * mean_y * inverse_z


def expanded(xx, xy, yy, pos_u, pos_v, log_opacity):
    x1 = -2.0 * xx * pos_u - xy * pos_v
    y1 = -2.0 * yy * pos_v - xy * pos_u
    one = xx * pos_u * pos_u + xy * pos_u * pos_v + yy * pos_v * pos_v + log_opacity
    return xx, xy, yy, x1, y1, one


def tile_shifts(across, side, height, width):
    column = lax.broadcasted_iota(jnp.int32, (across, LANES), 0).astype(F32)
    column = jnp.concatenate([column] * CAP, axis=0)
    row = lax.axis_index("ty").astype(F32)
    shift_x = (0.5 * width - 0.5 * side - 0.5) - side * column
    shift_y = jnp.full(column.shape, (0.5 * height - 0.5 * side - 0.5) - side * row, F32)
    return shift_x, shift_y


def request_kernel(owned, across, lists, count, order, request, slot, seen):
    base = lax.axis_index("ty") * across
    for o in range(across):
        seen[o] = 0
        for c in range(CAP):
            request[o, 0, c] = -1
    used = count[0, 0]

    def entry(k, _):
        @pl.when(k < used)
        def _():
            block = order[lists[0, 0, k]]
            home = block // owned
            local = block - home * owned
            home = home - base
            at = seen[home]
            seen[home] = at + 1
            request[home, 0, at] = local
            slot[k] = home * CAP + at

        return 0

    lax.fori_loop(0, slot.shape[0], entry, 0, unroll=True)
    free = 0
    for o in range(across):
        free = jnp.where(seen[o] < CAP, o * CAP + CAP - 1, free)

    def rest(k, _):
        slot[k] = free
        return 0

    lax.fori_loop(used, slot.shape[0], rest, 0)


def project_kernel(span, gaussians, out):
    def part(n, _):
        rows = pl.ds(pl.multiple_of(n * span, span), span)
        field = [gaussians[f, rows, :] for f in range(11)]
        light = -LOG2E * jnp.log(1.0 + jnp.exp(-field[10])) + float(np.log2(0.99))
        values = list(conic(field[0], field[1], field[2], field[3:6], field[6:10]))
        values.append(jnp.maximum(light, DARK))
        basis = directions(field[0], field[1], field[2])
        for ch in range(3):
            color = 0.5 + basis[0] * gaussians[11 + ch, rows, :]
            for m in range(1, 16):
                color = color + basis[m] * gaussians[11 + 3 * m + ch, rows, :]
            values.append(color)
        for f in range(9):
            out[f, rows, :] = values[f]
        return 0

    lax.fori_loop(0, gaussians.shape[1] // span, part, 0)


def asked_index(asked, across, s):
    c = s // across
    return asked[s - c * across, 0, c]


def serve_kernel(across, side, height, width, asked, projected, send, chosen):
    def pick(s, _):
        index = jnp.maximum(asked_index(asked, across, s), 0)
        for f in range(9):
            chosen[f, pl.ds(s, 1), :] = projected[f, pl.ds(index, 1), :]
        return 0

    lax.fori_loop(0, across * CAP, pick, 0, unroll=True)
    shift_x, shift_y = tile_shifts(across, side, height, width)
    rows = list(
        expanded(
            chosen[0], chosen[1], chosen[2], chosen[3] + shift_x, chosen[4] + shift_y, chosen[5]
        )
    ) + [chosen[6], chosen[7], chosen[8]]
    for c in range(CAP):
        for f in range(9):
            at = c * 8 + f if f < 8 else CAP * 8 + c
            send[:, at, :] = rows[f][c * across : (c + 1) * across]


def monomials(side):
    pixels = side * side
    lane = lax.broadcasted_iota(jnp.int32, (8, pixels), 1)
    row = lax.broadcasted_iota(jnp.int32, (8, pixels), 0)
    x = ((lane & (side - 1)) - side // 2).astype(F32)
    y = ((lane >> (side.bit_length() - 1)) - side // 2).astype(F32)
    mono = jnp.zeros((8, pixels), F32)
    for at, value in enumerate((x * x, x * y, y * y, x, y, jnp.ones_like(x))):
        mono = jnp.where(row == at, value, mono)
    blank = jnp.zeros((8, pixels), F32)
    rest = jnp.zeros((LANES - 48, pixels), F32)
    return jnp.concatenate([mono, blank] * 3 + [rest], axis=0).astype(BF16)


def spreaders():
    row = lax.broadcasted_iota(jnp.int32, (LANES, LANES), 0)
    return jnp.concatenate(
        [jnp.where((row == 6 + c) | (row == 22 + c), 1.0, 0.0).astype(F32) for c in range(3)], axis=1
    ).astype(BF16)


def repeated(x, times):
    return jnp.concatenate([x] * times, axis=1)


def forward_kernel(
    side, slot, count, recv, target, table, checks, prefix, behind, dense,
    planes, spread, buf_a, buf_b, ends,
):
    lmax = slot.shape[0]
    per = lmax // SEGS
    pixels = prefix.shape[1]
    groups = pixels // LANES
    planes[:, :pixels] = monomials(side)
    planes[:, pixels:] = spreaders()
    zero_rows = jnp.zeros((7, LANES), F32)
    dead = jnp.where(lax.broadcasted_iota(jnp.int32, (16, LANES), 0) == 5, DARK, 0.0)
    is_color = lax.broadcasted_iota(jnp.int32, (16, LANES), 0) >= 6
    filler = jnp.zeros((LANES - 48, LANES), F32)

    def place(m, seg):
        s = slot[seg * per + m]
        live = seg * per + m < count[0, 0]
        o = s // CAP
        c = s - o * CAP
        head = recv[o, pl.ds(pl.multiple_of(c * 8, 8), 8), :]
        tail = recv[o, pl.ds(CAP * 8 + c, 1), :]
        rows = jnp.concatenate([head, tail, zero_rows], axis=0)
        rows = jnp.where(live, rows, dead)
        hi = rows.astype(BF16).astype(F32)
        rest = rows - hi
        mid = rest.astype(BF16).astype(F32)
        low = (rest - mid).astype(BF16).astype(F32)
        third = jnp.where(is_color, hi, low)
        stacked = jnp.concatenate([hi, mid, third, filler], axis=0)
        spread[pl.ds(m * (SEGS * LANES) + seg, LANES, stride=SEGS), :] = stacked.T

    for seg in range(SEGS):
        place(0, seg)

    def products(n, buf):
        part = spread[pl.ds(pl.multiple_of(n * CHUNK, CHUNK), CHUNK), :].astype(BF16)
        table[pl.ds(pl.multiple_of(n * CHUNK, CHUNK), CHUNK), :] = part
        buf[...] = jnp.dot(part, planes[...], preferred_element_type=F32)

    def blend(n, buf, carry):
        light, red, green, blue = carry
        for i in range(STEPS):
            rows = pl.ds(i * SEGS, SEGS)
            if i % SPAN == 0:
                checks[n * (STEPS // SPAN) + i // SPAN] = light
            weight = light * jnp.exp2(buf[rows, :pixels])
            light = light - weight
            red = red + weight * repeated(buf[rows, pixels : pixels + LANES], groups)
            green = green + weight * repeated(buf[rows, pixels + LANES : pixels + 2 * LANES], groups)
            blue = blue + weight * repeated(
                buf[rows, pixels + 2 * LANES : pixels + 3 * LANES], groups
            )
        return light, red, green, blue

    products(0, buf_a)
    chunks = lmax * LANES // CHUNK

    turn = chunks // per
    share = SEGS // turn

    def pair(h, carry):
        n = 2 * h
        m = (n // turn + 1) % per
        products(n + 1, buf_b)
        for q in range(share):
            place(m, (n % turn) * share + q)
        carry = blend(n, buf_a, carry)
        for q in range(share):
            place(m, (n % turn + 1) * share + q)
        products(jnp.minimum(n + 2, chunks - 1), buf_a)
        return blend(n + 1, buf_b, carry)

    start = (jnp.ones((SEGS, pixels), F32),) + (jnp.zeros((SEGS, pixels), F32),) * 3
    carry = lax.fori_loop(0, chunks // 2, pair, start)
    for f in range(4):
        ends[f] = carry[f]
    ahead = jnp.ones((1, pixels), F32)
    for seg in range(SEGS):
        prefix[pl.ds(seg, 1), :] = ahead
        ahead = ahead * ends[0, pl.ds(seg, 1), :]
    for ch in range(3):
        seen = jnp.zeros((1, pixels), F32)
        for seg in reversed(range(SEGS)):
            behind[ch, pl.ds(seg, 1), :] = seen
            seen = ends[1 + ch, pl.ds(seg, 1), :] + ends[0, pl.ds(seg, 1), :] * seen
        for j in range(groups):
            dense[pl.ds(ch * groups + j, 1), :] = seen[:, j * LANES : (j + 1) * LANES]
    dense[3 * groups :, :] = target[...]


def similarity(mean_a, mean_b, square_a, square_b, cross):
    var_a = square_a - mean_a * mean_a
    var_b = square_b - mean_b * mean_b
    covar = cross - mean_a * mean_b
    top = (2.0 * mean_a * mean_b + LUMA_TERM) * (2.0 * covar + CONTRAST_TERM)
    bottom = (mean_a * mean_a + mean_b * mean_b + LUMA_TERM) * (var_a + var_b + CONTRAST_TERM)
    return top / bottom


def tap(distance):
    weights = [float(np.exp(-((k - RIM) ** 2) / 4.5)) for k in range(TAPS)]
    value = jnp.exp(distance * distance * (-1.0 / 4.5)) * (1.0 / sum(weights))
    return jnp.where(jnp.abs(distance) <= RIM, value, 0.0)


def places(shape, dim):
    return lax.broadcasted_iota(jnp.int32, shape, dim)


def bands(side, padded):
    fold = LANES // side
    groups = side // fold
    reach = side + 2 * RIM
    shape = (3 * side, LANES)
    out = places(shape, 1)
    along = tap((places(shape, 0) - side - out + RIM).astype(F32))
    along = jnp.where(out < reach, along, 0.0)
    blank = jnp.zeros((side, LANES), F32)
    fa = jnp.concatenate(
        [
            jnp.concatenate(
                [along[h * side : (h + 1) * side] if u == t else blank for u in range(fold)], axis=1
            )
            for h in range(3)
            for t in range(fold)
        ],
        axis=0,
    )
    block = 3 * groups
    shape = (padded, fold * block)
    out, at = places(shape, 0), places(shape, 1)
    t = jnp.zeros(shape, jnp.int32)
    for k in range(1, fold):
        t = t + jnp.where(at >= k * block, 1, 0)
    source = (at - t * block) * fold + t - side
    fb = jnp.where(out < reach, tap((source - out + RIM).astype(F32)), 0.0)
    shape = (fold * groups, padded)
    row, out = places(shape, 0), places(shape, 1)
    t = jnp.zeros(shape, jnp.int32)
    for k in range(1, fold):
        t = t + jnp.where(row >= k * groups, 1, 0)
    source = (row - t * groups) * fold + t
    fc = jnp.where(out < reach, tap((out - RIM - source).astype(F32)), 0.0)
    shape = (LANES, LANES)
    out, at = places(shape, 0), places(shape, 1)
    back = tap((out - RIM - (at & (side - 1))).astype(F32))
    back = jnp.where(out < reach, back, 0.0)
    fd = jnp.concatenate(
        [jnp.where((at >= t * side) & (at < (t + 1) * side), back, 0.0) for t in range(fold)], axis=0
    )
    return fa, fb, fc, fd


def score_kernel(side, height, width, near, slope, loss):
    fa, fb, fc, fd = bands(side, -(-(side + 2 * RIM) // 8) * 8)
    rows3 = near[4].shape[0] // 2
    groups = rows3 // 3
    fold = LANES // side
    fields = [[], [], [], [], []]
    for v in range(3):
        strip = jnp.concatenate([near[3 * v + h] for h in range(3)], axis=1)
        image, target = strip[:rows3], strip[rows3:]
        for f, plane in enumerate([image, target, image * image, target * target, image * target]):
            fields[f].append(plane)
    stack = jnp.concatenate([fields[f][v] for f in range(5) for v in range(3)], axis=0)
    wide = jnp.dot(stack, fa, precision=HIGH, preferred_element_type=F32)
    columns = []
    for f in range(5):
        for ch in range(3):
            parts = []
            for t in range(fold):
                for v in range(3):
                    at = (f * 3 + v) * rows3 + ch * groups
                    parts.append(wide[at : at + groups, t * LANES : (t + 1) * LANES])
            columns.append(jnp.concatenate(parts, axis=0))
    tall = jnp.concatenate(columns, axis=1)
    maps = jnp.dot(fb, tall, precision=HIGH, preferred_element_type=F32)
    span = 3 * LANES
    score, pull = jax.vjp(similarity, *[maps[:, f * span : (f + 1) * span] for f in range(5)])
    parts = pull(jnp.full(score.shape, -STRUCT_WEIGHT, F32))
    row = lax.broadcasted_iota(jnp.int32, score.shape, 0)
    col = lax.broadcasted_iota(jnp.int32, (score.shape[0], LANES), 1)
    col = jnp.concatenate([col] * 3, axis=1)
    row_at = row - RIM + lax.axis_index("ty") * side
    col_at = col - RIM + lax.axis_index("tx") * side
    reach = side + 2 * RIM
    inside = (
        (row_at >= 0) & (row_at < height) & (col_at >= 0) & (col_at < width)
        & (row < reach) & (col < reach)
    )
    own = (row >= RIM) & (row < RIM + side) & (col >= RIM) & (col < RIM + side)
    coeffs = jnp.concatenate(
        [jnp.where(inside, parts[f], 0.0) for f in (0, 2, 4)], axis=1
    )
    low = jnp.dot(fc, coeffs, precision=HIGH, preferred_element_type=F32)
    rows = []
    for n in range(9):
        rows.append(
            jnp.concatenate(
                [
                    low[t * groups : (t + 1) * groups, n * LANES : (n + 1) * LANES]
                    for t in range(fold)
                ],
                axis=1,
            )
        )
    smooth = jnp.dot(
        jnp.concatenate(rows, axis=0), fd, precision=HIGH, preferred_element_type=F32
    )
    image, target = near[4][:rows3, :], near[4][rows3:, :]
    gap = image - target
    robust = jnp.sqrt(gap * gap + ROBUST_TERM)
    slope[...] = (
        smooth[:rows3]
        + 2.0 * image * smooth[rows3 : 2 * rows3]
        + target * smooth[2 * rows3 :]
        + (1.0 - STRUCT_WEIGHT) * gap / robust
    )
    total = (1.0 - STRUCT_WEIGHT) * jnp.sum(robust) + STRUCT_WEIGHT * jnp.sum(
        jnp.where(own, 1.0 - score, 0.0)
    )
    loss[...] = jnp.full(loss.shape, total, F32)


def score_entry(side, height, width, *refs):
    above, left, own, right, below = refs[:5]
    rows = own.shape[0]
    near = [above[h * rows : (h + 1) * rows, :] for h in range(3)]
    near += [left[...], own[...], right[...]]
    near += [below[h * rows : (h + 1) * rows, :] for h in range(3)]
    score_kernel(side, height, width, near, *refs[5:])


def backward_kernel(
    side, table, checks, prefix, behind, slope, reduce, stage,
    rhs, wide, grows, buf_a, buf_b, behinds, sums, moments,
):
    lmax = stage.shape[0]
    per = lmax // SEGS
    pixels = prefix.shape[1]
    groups = pixels // LANES
    chunks = lmax * LANES // CHUNK
    wide[...] = jnp.zeros_like(wide)
    for ch in range(3):
        for j in range(groups):
            lanes = pl.ds(j * LANES, LANES)
            wide[pl.ds(6 + ch, 1), lanes] = slope[pl.ds(ch * groups + j, 1), :]
    for ch in range(3):
        row = wide[pl.ds(6 + ch, 1), :]
        hi = row.astype(BF16).astype(F32)
        grows[ch] = jnp.broadcast_to(row, (SEGS, pixels))
        wide[pl.ds(6 + ch, 1), :] = hi
        wide[pl.ds(22 + ch, 1), :] = hi
        wide[pl.ds(38 + ch, 1), :] = row - hi
    rhs[:, :pixels] = monomials(side)
    rhs[:, pixels:] = wide[...].astype(BF16)

    def products(n, buf):
        part = table[pl.ds(pl.multiple_of(n * CHUNK, CHUNK), CHUNK), :]
        buf[...] = jnp.dot(part, rhs[...], preferred_element_type=F32)

    def block(n, b, buf):
        first = b * SPAN * SEGS
        rows = [pl.ds(first + i * SEGS, SEGS) for i in range(SPAN)]
        totals = [[None] * 6 for _ in range(SPAN)]

        def add(i, f, value):
            totals[i][f] = value if totals[i][f] is None else totals[i][f] + value

        for j in reversed(range(groups)):
            lanes = slice(j * LANES, (j + 1) * LANES)
            light = checks[n * (STEPS // SPAN) + b, :, lanes] * prefix[:, lanes]
            tints = [grows[ch, :, lanes] for ch in range(3)]
            alphas, weights = [], []
            for i in range(SPAN):
                alphas.append(jnp.exp2(buf[rows[i], lanes]))
                weights.append(light * alphas[i])
                light = light - weights[i]
            back = behinds[:, lanes]
            for i in reversed(range(SPAN)):
                gap = buf[rows[i], pixels + j * LANES : pixels + (j + 1) * LANES] - back
                back = back + alphas[i] * gap
                add(i, 0, weights[i] * gap)
                if j > 0:
                    add(i, 1, totals[i][0])
                    add(i, 2, totals[i][1])
                for ch in range(3):
                    add(i, 3 + ch, weights[i] * tints[ch])
            behinds[:, lanes] = back
        for i in range(SPAN):
            for f in range(6):
                sums[rows[i], f * LANES : (f + 1) * LANES] = totals[i][f]

    def sweep(n, buf):
        for b in reversed(range(STEPS // SPAN)):
            block(n, b, buf)
        whole = sums[...]
        hi = whole.astype(BF16)
        low = (whole - hi.astype(F32)).astype(BF16)
        both = jnp.dot(
            jnp.concatenate([hi, low], axis=0), reduce[...], preferred_element_type=F32
        )
        moments[pl.ds(pl.multiple_of(n * CHUNK, CHUNK), CHUNK), :] = both[:CHUNK] + both[CHUNK:]

    behinds[...] = behind[0] * grows[0] + behind[1] * grows[1] + behind[2] * grows[2]
    products(chunks - 1, buf_a)

    turn = chunks // per
    share = SEGS // turn

    def collect(m, seg):
        block = moments[pl.ds(m * (SEGS * LANES) + seg, LANES, stride=SEGS), :].T
        stage[seg * per + m] = block[:16]

    def pair(h, _):
        n = chunks - 1 - 2 * h
        m = (n // turn + 1) % per
        products(n - 1, buf_b)
        for q in range(share):
            collect(m, (n % turn) * share + q)
        sweep(n, buf_a)
        for q in range(share):
            collect(m, (n % turn - 1) * share + q)
        products(jnp.maximum(n - 2, 0), buf_a)
        sweep(n - 1, buf_b)
        return 0

    lax.fori_loop(0, chunks // 2, pair, 0)
    for seg in range(SEGS):
        collect(0, seg)


def deliver_kernel(slot, stage, shares, reply):
    column = shares[0]
    for n in range(1, shares.shape[0]):
        column = column + shares[n]
    for o in range(reply.shape[0]):
        reply[o, pl.ds(reply.shape[1] - 1, 1), :] = column[:1]
    for k in range(slot.shape[0]):
        s = slot[k]
        o = s // CAP
        c = s - o * CAP
        reply[o, pl.ds(pl.multiple_of(c * 8, 8), 8), :] = stage[k, :8, :]
        reply[o, pl.ds(CAP * 8 + c, 1), :] = stage[k, 8:9, :]


def gather_kernel(
    across, side, height, width, asked, got, gaussians, grads, loss, sums, zeros, pieces, wanted, sem
):
    owned = gaussians.shape[1]
    parts = owned // 8
    shares = got[:, got.shape[1] - 1, :]
    loss[0] = jnp.sum(shares[:, :1]) * (1.0 / (3.0 * height * width))
    zeros[...] = jnp.zeros_like(zeros)
    sums[...] = jnp.zeros_like(sums)
    for g in range(parts + 1):
        wanted[g] = 0
    for s in range(across * CAP):
        c, t = divmod(s, across)
        index = asked[t, 0, c]
        index = jnp.where(index >= 0, index, owned)
        wanted[index // 8] = 1
        row = pl.ds(index, 1)
        for f in range(9):
            at = c * 8 + f if f < 8 else CAP * 8 + c
            sums[f, row, :] = got[t, at : at + 1, :]
        sums[9, row, :] = jnp.full((1, LANES), t + 1.0, F32)

    def target(g):
        return grads.at[:, pl.ds(pl.multiple_of(g * 8, 8), 8), :]

    def blank(g, _):
        @pl.when(wanted[g] == 0)
        def _():
            pltpu.make_async_copy(zeros, target(g), sem.at[g]).start()

        return 0

    lax.fori_loop(0, parts, blank, 0)
    row_at = lax.axis_index("ty").astype(F32)
    shift_y = (0.5 * height - 0.5 * side - 0.5) - side * row_at

    def solve(g):
        rows = pl.ds(pl.multiple_of(g * 8, 8), 8)
        field = [gaussians[f, rows, :] for f in range(11)]
        tile = sums[9, rows, :]
        live = tile > 0.0
        shift_x = (0.5 * width - 0.5 * side - 0.5) - side * (tile - 1.0)

        def put(f, value):
            pieces[g, f] = jnp.where(live, value, 0.0)

        def shaped(x, y, z, log_scale, quat):
            xx, xy, yy, pos_u, pos_v = conic(x, y, z, log_scale, quat)
            return expanded(xx, xy, yy, pos_u + shift_x, pos_v + shift_y, jnp.zeros_like(x))

        _, pull = jax.vjp(shaped, *field[:3], field[3:6], field[6:10])
        moments = [LN2 * sums[f, rows, :] for f in range(6)]
        gx, gy, gz, gscale, gquat = pull(tuple(moments))
        basis, pull_basis = jax.vjp(directions, *field[:3])
        tints = [sums[6 + ch, rows, :] for ch in range(3)]
        tilts = []
        for m in range(16):
            tilt = None
            for ch in range(3):
                term = tints[ch] * gaussians[11 + 3 * m + ch, rows, :]
                tilt = term if tilt is None else tilt + term
                put(11 + 3 * m + ch, tints[ch] * basis[m])
            tilts.append(tilt)
        dx, dy, dz = pull_basis(tilts)
        put(0, gx + dx)
        put(1, gy + dy)
        put(2, gz + dz)
        for f in range(3):
            put(3 + f, gscale[f])
        for f in range(4):
            put(6 + f, gquat[f])
        put(10, moments[5] * (LOG2E / (1.0 + jnp.exp(field[10]))))
        pltpu.make_async_copy(pieces.at[g], target(g), sem.at[g]).start()

    def part(g, _):
        @pl.when(wanted[g] > 0)
        def _():
            solve(g)

        return 0

    lax.fori_loop(0, parts, part, 0)

    def finish(g, _):
        pltpu.make_async_copy(zeros, target(g), sem.at[g]).wait()
        return 0

    lax.fori_loop(0, parts, finish, 0)


def moment_columns(side):
    lane = np.arange(LANES)
    x = lane % side - side // 2
    t = lane // side - side // 2
    step = LANES // side
    one = np.ones_like(x)
    out = np.zeros((6 * LANES, LANES))
    out[:LANES, :6] = np.stack([x * x, x * t, t * t, x, t, one], axis=1)
    out[LANES : 2 * LANES, 1] = step * x
    out[LANES : 2 * LANES, 2] = 2 * step * t - step * step
    out[LANES : 2 * LANES, 4] = step
    out[2 * LANES : 3 * LANES, 2] = 2 * step * step
    for ch in range(3):
        out[(3 + ch) * LANES : (4 + ch) * LANES, 6 + ch] = 1.0
    return out.astype(ml_dtypes.bfloat16)


def shifted(x, axis):
    size = lax.axis_size(axis)
    up = [(i, i + 1) for i in range(size - 1)]
    return lax.ppermute(x, axis, up), lax.ppermute(x, axis, [(j, i) for i, j in up])


def per_device(gaussians, tile_lists, tile_counts, depth_order, target):
    owned, fields, block = gaussians.shape
    lmax = tile_lists.shape[2]
    side = target.shape[1]
    pixels = side * side
    groups = pixels // LANES
    across = lax.axis_size("tx")
    down = lax.axis_size("ty")
    height = side * lax.axis_size("ty")
    width = side * across
    slots = across * CAP
    depth = -(-(CAP * 9 + 1) // 8) * 8
    f32 = functools.partial(jax.ShapeDtypeStruct, dtype=F32)
    i32 = functools.partial(jax.ShapeDtypeStruct, dtype=jnp.int32)
    reduce = jnp.asarray(moment_columns(side))

    fieldwise = jnp.transpose(gaussians, (1, 0, 2))
    request, slot = pl.pallas_call(
        functools.partial(request_kernel, owned, across),
        out_shape=(i32((across, 1, LANES)), i32((lmax,))),
        in_specs=[SMEM] * 3,
        out_specs=(SMEM, SMEM),
        scratch_shapes=[pltpu.SMEM((across,), jnp.int32)],
        name="request",
    )(tile_lists, tile_counts, depth_order)
    asked = lax.all_to_all(request, "tx", split_axis=0, concat_axis=0, tiled=True)
    projected = pl.pallas_call(
        functools.partial(project_kernel, 16),
        out_shape=f32((9, owned, block)),
        in_specs=[VMEM],
        out_specs=VMEM,
        compiler_params=PARAMS,
        name="project",
    )(fieldwise)
    send = pl.pallas_call(
        functools.partial(serve_kernel, across, side, float(height), float(width)),
        out_shape=f32((across, depth, block)),
        in_specs=[SMEM, VMEM],
        out_specs=VMEM,
        scratch_shapes=[pltpu.VMEM((9, slots, block), F32)],
        compiler_params=PARAMS,
        name="serve",
    )(asked, projected)
    recv = lax.all_to_all(send, "tx", split_axis=0, concat_axis=0, tiled=True)
    chunks = lmax * block // CHUNK
    wide = pixels + 3 * LANES
    table, checks, prefix, behind, dense = pl.pallas_call(
        functools.partial(forward_kernel, side),
        out_shape=(
            jax.ShapeDtypeStruct((lmax * block, LANES), BF16),
            f32((chunks * (STEPS // SPAN), SEGS, pixels)),
            f32((SEGS, pixels)),
            f32((3, SEGS, pixels)),
            f32((6 * groups, LANES)),
        ),
        in_specs=[SMEM, SMEM, VMEM, VMEM],
        out_specs=(VMEM,) * 5,
        scratch_shapes=[
            pltpu.VMEM((LANES, wide), BF16),
            pltpu.VMEM((lmax * block, LANES), F32),
            pltpu.VMEM((CHUNK, wide), F32),
            pltpu.VMEM((CHUNK, wide), F32),
            pltpu.VMEM((4, SEGS, pixels), F32),
        ],
        compiler_params=PARAMS,
        name="forward",
    )(slot, tile_counts, recv, target.reshape(3 * groups, LANES))
    left, right = shifted(dense, "tx")
    above, below = shifted(jnp.concatenate([left, dense, right], axis=0), "ty")
    slope, part = pl.pallas_call(
        functools.partial(score_entry, side, height, width),
        out_shape=(f32((3 * groups, LANES)), f32((down, 8, LANES))),
        in_specs=[VMEM] * 5,
        out_specs=(VMEM, VMEM),
        compiler_params=PARAMS,
        name="score",
    )(above, left, dense, right, below)
    shares = lax.all_to_all(part, "ty", split_axis=0, concat_axis=0, tiled=True)
    stage = pl.pallas_call(
        functools.partial(backward_kernel, side),
        out_shape=f32((lmax, 16, LANES)),
        in_specs=[VMEM] * 6,
        out_specs=VMEM,
        scratch_shapes=[
            pltpu.VMEM((LANES, 2 * pixels), BF16),
            pltpu.VMEM((LANES, pixels), F32),
            pltpu.VMEM((3, SEGS, pixels), F32),
            pltpu.VMEM((CHUNK, 2 * pixels), F32),
            pltpu.VMEM((CHUNK, 2 * pixels), F32),
            pltpu.VMEM((SEGS, pixels), F32),
            pltpu.VMEM((CHUNK, 6 * LANES), F32),
            pltpu.VMEM((lmax * block, LANES), F32),
        ],
        compiler_params=PARAMS,
        name="backward",
    )(table, checks, prefix, behind, slope, reduce)
    reply = pl.pallas_call(
        deliver_kernel,
        out_shape=f32((across, depth, block)),
        in_specs=[SMEM, VMEM, VMEM],
        out_specs=VMEM,
        compiler_params=PARAMS,
        name="deliver",
    )(slot, stage, shares)
    got = lax.all_to_all(reply, "tx", split_axis=0, concat_axis=0, tiled=True)
    grads, loss = pl.pallas_call(
        functools.partial(gather_kernel, across, side, float(height), float(width)),
        out_shape=(f32((fields, owned, block)), f32((1,))),
        in_specs=[SMEM, VMEM, VMEM],
        out_specs=(ANY, SMEM),
        scratch_shapes=[
            pltpu.VMEM((10, owned + 8, block), F32),
            pltpu.VMEM((fields, 8, block), F32),
            pltpu.VMEM((owned // 8, fields, 8, block), F32),
            pltpu.SMEM((owned // 8 + 1,), jnp.int32),
            pltpu.SemaphoreType.DMA((owned // 8,)),
        ],
        compiler_params=PARAMS,
        name="gather",
    )(asked, got, fieldwise)
    return (jnp.transpose(grads, (1, 0, 2)), loss[0])


def solution(mesh):
    return jax.shard_map(
        per_device,
        mesh=mesh,
        in_specs=(
            P(("ty", "tx"), None, None),
            P("ty", "tx", None),
            P("ty", "tx"),
            P(),
            P(None, "ty", "tx"),
        ),
        out_specs=(P(("ty", "tx"), None, None), P()),
        check_vma=False,
    )
```

```python
import functools

import jax
import jax.numpy as jnp
import ml_dtypes
import numpy as np
from jax import lax
from jax.experimental import pallas as pl
from jax.experimental.pallas import tpu as pltpu
from jax.sharding import PartitionSpec as P

CAP = 3
SEGS = 8
LANES = 128
CHUNK = 256
STEPS = CHUNK // SEGS
SPAN = 4
COLS = 256
RIM = 5
TAPS = 2 * RIM + 1
LOG2E = 1.4426950408889634
LN2 = 0.6931471805599453
DARK = -1e30

FOCAL = 1000.0
LOW_PASS = 0.3
STRUCT_WEIGHT = 0.2
LUMA_TERM = 0.0001
CONTRAST_TERM = 0.0009
ROBUST_TERM = 1e-06
HARMONIC_ZERO = 0.28209479177387814
HARMONIC_ONE = 0.4886025119029199
HARMONIC_TWO = (
    1.0925484305920792,
    -1.0925484305920792,
    0.31539156525252005,
    -1.0925484305920792,
    0.5462742152960396,
)
HARMONIC_THREE = (
    -0.5900435899266435,
    2.890611442640554,
    -0.4570457994644658,
    0.3731763325901154,
    -0.4570457994644658,
    1.445305721320277,
    -0.5900435899266435,
)

HIGH = lax.Precision.HIGHEST
F32 = jnp.float32
BF16 = jnp.bfloat16
ANY = pl.BlockSpec(memory_space=pl.ANY)
SMEM = pl.BlockSpec(memory_space=pltpu.SMEM)
VMEM = pl.BlockSpec(memory_space=pltpu.VMEM)
PARAMS = pltpu.CompilerParams(vmem_limit_bytes=24 * 1024 * 1024)


def harmonics(x, y, z):
    xx, yy, zz = x * x, y * y, z * z
    xy, yz, xz = x * y, y * z, x * z
    return [
        HARMONIC_ZERO * jnp.ones_like(x),
        -HARMONIC_ONE * y,
        HARMONIC_ONE * z,
        -HARMONIC_ONE * x,
        HARMONIC_TWO[0] * xy,
        HARMONIC_TWO[1] * yz,
        HARMONIC_TWO[2] * (2.0 * zz - xx - yy),
        HARMONIC_TWO[3] * xz,
        HARMONIC_TWO[4] * (xx - yy),
        HARMONIC_THREE[0] * y * (3.0 * xx - yy),
        HARMONIC_THREE[1] * xy * z,
        HARMONIC_THREE[2] * y * (4.0 * zz - xx - yy),
        HARMONIC_THREE[3] * z * (2.0 * zz - 3.0 * xx - 3.0 * yy),
        HARMONIC_THREE[4] * x * (4.0 * zz - xx - yy),
        HARMONIC_THREE[5] * z * (xx - yy),
        HARMONIC_THREE[6] * x * (xx - 3.0 * yy),
    ]


def directions(x, y, z):
    length = jnp.sqrt(x * x + y * y + z * z)
    return harmonics(x / length, y / length, z / length)


def conic(mean_x, mean_y, mean_z, log_scale, quat):
    scale = [jnp.exp(s) for s in log_scale]
    norm = jnp.sqrt(quat[0] * quat[0] + quat[1] * quat[1] + quat[2] * quat[2] + quat[3] * quat[3])
    w, i, j, k = (q / norm for q in quat)
    rotation = [
        [1.0 - 2.0 * (j * j + k * k), 2.0 * (i * j - w * k), 2.0 * (i * k + w * j)],
        [2.0 * (i * j + w * k), 1.0 - 2.0 * (i * i + k * k), 2.0 * (j * k - w * i)],
        [2.0 * (i * k - w * j), 2.0 * (j * k + w * i), 1.0 - 2.0 * (i * i + j * j)],
    ]
    scaled = [[rotation[r][c] * scale[c] for c in range(3)] for r in range(3)]

    def sigma(r, c):
        return scaled[r][0] * scaled[c][0] + scaled[r][1] * scaled[c][1] + scaled[r][2] * scaled[c][2]

    s00, s01, s02, s11, s12, s22 = (
        sigma(0, 0), sigma(0, 1), sigma(0, 2), sigma(1, 1), sigma(1, 2), sigma(2, 2),
    )
    inverse_z = 1.0 / mean_z
    diag = FOCAL * inverse_z
    jac_xz = -FOCAL * mean_x * inverse_z * inverse_z
    jac_yz = -FOCAL * mean_y * inverse_z * inverse_z
    u0, u1, u2 = diag * s00 + jac_xz * s02, diag * s01 + jac_xz * s12, diag * s02 + jac_xz * s22
    v1, v2 = diag * s11 + jac_yz * s12, diag * s12 + jac_yz * s22
    cov_uu = u0 * diag + u2 * jac_xz + LOW_PASS
    cov_uv = u1 * diag + u2 * jac_yz
    cov_vv = v1 * diag + v2 * jac_yz + LOW_PASS
    determinant = cov_uu * cov_vv - cov_uv * cov_uv
    half = -0.5 * LOG2E
    xx = half * (cov_vv / determinant)
    xy = (-2.0 * half) * (cov_uv / determinant)
    yy = half * (cov_uu / determinant)
    return xx, xy, yy, FOCAL * mean_x * inverse_z, FOCAL * mean_y * inverse_z


def expanded(xx, xy, yy, pos_u, pos_v, log_opacity):
    x1 = -2.0 * xx * pos_u - xy * pos_v
    y1 = -2.0 * yy * pos_v - xy * pos_u
    one = xx * pos_u * pos_u + xy * pos_u * pos_v + yy * pos_v * pos_v + log_opacity
    return xx, xy, yy, x1, y1, one


def tile_shifts(across, side, height, width):
    column = lax.broadcasted_iota(jnp.int32, (across, LANES), 0).astype(F32)
    column = jnp.concatenate([column] * CAP, axis=0)
    row = lax.axis_index("ty").astype(F32)
    shift_x = (0.5 * width - 0.5 * side - 0.5) - side * column
    shift_y = jnp.full(column.shape, (0.5 * height - 0.5 * side - 0.5) - side * row, F32)
    return shift_x, shift_y


def request_kernel(owned, across, lists, count, order, request, slot, seen):
    base = lax.axis_index("ty") * across
    for o in range(across):
        seen[o] = 0
        for c in range(CAP):
            request[o, 0, c] = -1
    used = count[0, 0]

    def entry(k, _):
        @pl.when(k < used)
        def _():
            block = order[lists[0, 0, k]]
            home = block // owned
            local = block - home * owned
            home = home - base
            at = seen[home]
            seen[home] = at + 1
            request[home, 0, at] = local
            slot[k] = home * CAP + at

        return 0

    lax.fori_loop(0, slot.shape[0], entry, 0, unroll=True)
    free = 0
    for o in range(across):
        free = jnp.where(seen[o] < CAP, o * CAP + CAP - 1, free)

    def rest(k, _):
        slot[k] = free
        return 0

    lax.fori_loop(used, slot.shape[0], rest, 0)


def project_kernel(span, gaussians, out):
    def part(n, _):
        rows = pl.ds(pl.multiple_of(n * span, span), span)
        field = [gaussians[f, rows, :] for f in range(11)]
        light = -LOG2E * jnp.log(1.0 + jnp.exp(-field[10])) + float(np.log2(0.99))
        values = list(conic(field[0], field[1], field[2], field[3:6], field[6:10]))
        values.append(jnp.maximum(light, DARK))
        basis = directions(field[0], field[1], field[2])
        for ch in range(3):
            color = 0.5 + basis[0] * gaussians[11 + ch, rows, :]
            for m in range(1, 16):
                color = color + basis[m] * gaussians[11 + 3 * m + ch, rows, :]
            values.append(color)
        for f in range(9):
            out[f, rows, :] = values[f]
        return 0

    lax.fori_loop(0, gaussians.shape[1] // span, part, 0)


def asked_index(asked, across, s):
    c = s // across
    return asked[s - c * across, 0, c]


def serve_kernel(across, side, height, width, asked, projected, send, chosen):
    def pick(s, _):
        index = jnp.maximum(asked_index(asked, across, s), 0)
        for f in range(9):
            chosen[f, pl.ds(s, 1), :] = projected[f, pl.ds(index, 1), :]
        return 0

    lax.fori_loop(0, across * CAP, pick, 0, unroll=True)
    shift_x, shift_y = tile_shifts(across, side, height, width)
    rows = list(
        expanded(
            chosen[0], chosen[1], chosen[2], chosen[3] + shift_x, chosen[4] + shift_y, chosen[5]
        )
    ) + [chosen[6], chosen[7], chosen[8]]
    for c in range(CAP):
        for f in range(9):
            at = c * 8 + f if f < 8 else CAP * 8 + c
            send[:, at, :] = rows[f][c * across : (c + 1) * across]


def monomials(side):
    pixels = side * side
    lane = lax.broadcasted_iota(jnp.int32, (8, pixels), 1)
    row = lax.broadcasted_iota(jnp.int32, (8, pixels), 0)
    x = ((lane & (side - 1)) - side // 2).astype(F32)
    y = ((lane >> (side.bit_length() - 1)) - side // 2).astype(F32)
    mono = jnp.zeros((8, pixels), F32)
    for at, value in enumerate((x * x, x * y, y * y, x, y, jnp.ones_like(x))):
        mono = jnp.where(row == at, value, mono)
    blank = jnp.zeros((8, pixels), F32)
    rest = jnp.zeros((LANES - 48, pixels), F32)
    return jnp.concatenate([mono, blank] * 3 + [rest], axis=0).astype(BF16)


def spreaders():
    row = lax.broadcasted_iota(jnp.int32, (LANES, LANES), 0)
    return jnp.concatenate(
        [jnp.where((row == 6 + c) | (row == 22 + c), 1.0, 0.0).astype(F32) for c in range(3)], axis=1
    ).astype(BF16)


def repeated(x, times):
    return jnp.concatenate([x] * times, axis=1)


def forward_kernel(
    side, slot, count, recv, target, table, checks, prefix, behind, dense,
    planes, spread, buf_a, buf_b, ends,
):
    lmax = slot.shape[0]
    per = lmax // SEGS
    pixels = prefix.shape[1]
    groups = pixels // LANES
    planes[:, :pixels] = monomials(side)
    planes[:, pixels:] = spreaders()
    zero_rows = jnp.zeros((7, LANES), F32)
    dead = jnp.where(lax.broadcasted_iota(jnp.int32, (16, LANES), 0) == 5, DARK, 0.0)
    is_color = lax.broadcasted_iota(jnp.int32, (16, LANES), 0) >= 6
    filler = jnp.zeros((LANES - 48, LANES), F32)

    def place(m, seg):
        s = slot[seg * per + m]
        live = seg * per + m < count[0, 0]
        o = s // CAP
        c = s - o * CAP
        head = recv[o, pl.ds(pl.multiple_of(c * 8, 8), 8), :]
        tail = recv[o, pl.ds(CAP * 8 + c, 1), :]
        rows = jnp.concatenate([head, tail, zero_rows], axis=0)
        rows = jnp.where(live, rows, dead)
        hi = rows.astype(BF16).astype(F32)
        rest = rows - hi
        mid = rest.astype(BF16).astype(F32)
        low = (rest - mid).astype(BF16).astype(F32)
        third = jnp.where(is_color, hi, low)
        stacked = jnp.concatenate([hi, mid, third, filler], axis=0)
        spread[pl.ds(m * (SEGS * LANES) + seg, LANES, stride=SEGS), :] = stacked.T

    for seg in range(SEGS):
        place(0, seg)

    width = planes.shape[1]
    pieces = -(-width // COLS)

    def product(n, buf, p):
        rows = pl.ds(pl.multiple_of(n * CHUNK, CHUNK), CHUNK)
        if p == 0:
            table[rows, :] = spread[rows, :].astype(BF16)
        cols = slice(p * COLS, min((p + 1) * COLS, width))
        buf[:, cols] = jnp.dot(table[rows, :], planes[:, cols], preferred_element_type=F32)

    def blend(n, b, buf, carry):
        light, red, green, blue = carry
        checks[n * (STEPS // SPAN) + b] = light
        for i in range(b * SPAN, (b + 1) * SPAN):
            rows = pl.ds(i * SEGS, SEGS)
            weight = light * jnp.exp2(buf[rows, :pixels])
            light = light - weight
            red = red + weight * repeated(buf[rows, pixels : pixels + LANES], groups)
            green = green + weight * repeated(buf[rows, pixels + LANES : pixels + 2 * LANES], groups)
            blue = blue + weight * repeated(
                buf[rows, pixels + 2 * LANES : pixels + 3 * LANES], groups
            )
        return light, red, green, blue

    for p in range(pieces):
        product(0, buf_a, p)
    chunks = lmax * LANES // CHUNK
    turn = chunks // per
    share = SEGS // turn

    def pair(h, carry):
        n = 2 * h
        m = (n // turn + 1) % per
        for b in range(STEPS // SPAN):
            if b < pieces:
                product(n + 1, buf_b, b)
            if b % 2 == 0 and b // 2 < 2 * share:
                place(m, (n % turn) * share + b // 2)
            carry = blend(n, b, buf_a, carry)
        for b in range(STEPS // SPAN):
            if b < pieces:
                product(jnp.minimum(n + 2, chunks - 1), buf_a, b)
            carry = blend(n + 1, b, buf_b, carry)
        return carry

    start = (jnp.ones((SEGS, pixels), F32),) + (jnp.zeros((SEGS, pixels), F32),) * 3
    carry = lax.fori_loop(0, chunks // 2, pair, start)
    for f in range(4):
        ends[f] = carry[f]
    ahead = jnp.ones((1, pixels), F32)
    for seg in range(SEGS):
        prefix[pl.ds(seg, 1), :] = ahead
        ahead = ahead * ends[0, pl.ds(seg, 1), :]
    for ch in range(3):
        seen = jnp.zeros((1, pixels), F32)
        for seg in reversed(range(SEGS)):
            behind[ch, pl.ds(seg, 1), :] = seen
            seen = ends[1 + ch, pl.ds(seg, 1), :] + ends[0, pl.ds(seg, 1), :] * seen
        for j in range(groups):
            dense[pl.ds(ch * groups + j, 1), :] = seen[:, j * LANES : (j + 1) * LANES]
    dense[3 * groups :, :] = target[...]


def similarity(mean_a, mean_b, square_a, square_b, cross):
    var_a = square_a - mean_a * mean_a
    var_b = square_b - mean_b * mean_b
    covar = cross - mean_a * mean_b
    top = (2.0 * mean_a * mean_b + LUMA_TERM) * (2.0 * covar + CONTRAST_TERM)
    bottom = (mean_a * mean_a + mean_b * mean_b + LUMA_TERM) * (var_a + var_b + CONTRAST_TERM)
    return top / bottom


def tap(distance):
    weights = [float(np.exp(-((k - RIM) ** 2) / 4.5)) for k in range(TAPS)]
    value = jnp.exp(distance * distance * (-1.0 / 4.5)) * (1.0 / sum(weights))
    return jnp.where(jnp.abs(distance) <= RIM, value, 0.0)


def places(shape, dim):
    return lax.broadcasted_iota(jnp.int32, shape, dim)


def bands(side, padded):
    fold = LANES // side
    groups = side // fold
    reach = side + 2 * RIM
    shape = (3 * side, LANES)
    out = places(shape, 1)
    along = tap((places(shape, 0) - side - out + RIM).astype(F32))
    along = jnp.where(out < reach, along, 0.0)
    blank = jnp.zeros((side, LANES), F32)
    fa = jnp.concatenate(
        [
            jnp.concatenate(
                [along[h * side : (h + 1) * side] if u == t else blank for u in range(fold)], axis=1
            )
            for h in range(3)
            for t in range(fold)
        ],
        axis=0,
    )
    block = 3 * groups
    shape = (padded, fold * block)
    out, at = places(shape, 0), places(shape, 1)
    t = jnp.zeros(shape, jnp.int32)
    for k in range(1, fold):
        t = t + jnp.where(at >= k * block, 1, 0)
    source = (at - t * block) * fold + t - side
    fb = jnp.where(out < reach, tap((source - out + RIM).astype(F32)), 0.0)
    shape = (fold * groups, padded)
    row, out = places(shape, 0), places(shape, 1)
    t = jnp.zeros(shape, jnp.int32)
    for k in range(1, fold):
        t = t + jnp.where(row >= k * groups, 1, 0)
    source = (row - t * groups) * fold + t
    fc = jnp.where(out < reach, tap((out - RIM - source).astype(F32)), 0.0)
    shape = (LANES, LANES)
    out, at = places(shape, 0), places(shape, 1)
    back = tap((out - RIM - (at & (side - 1))).astype(F32))
    back = jnp.where(out < reach, back, 0.0)
    fd = jnp.concatenate(
        [jnp.where((at >= t * side) & (at < (t + 1) * side), back, 0.0) for t in range(fold)], axis=0
    )
    return fa, fb, fc, fd


def score_kernel(side, height, width, near, slope, loss):
    fa, fb, fc, fd = bands(side, -(-(side + 2 * RIM) // 8) * 8)
    rows3 = near[4].shape[0] // 2
    groups = rows3 // 3
    fold = LANES // side
    fields = [[], [], [], [], []]
    for v in range(3):
        strip = jnp.concatenate([near[3 * v + h] for h in range(3)], axis=1)
        image, target = strip[:rows3], strip[rows3:]
        for f, plane in enumerate([image, target, image * image, target * target, image * target]):
            fields[f].append(plane)
    stack = jnp.concatenate([fields[f][v] for f in range(5) for v in range(3)], axis=0)
    wide = jnp.dot(stack, fa, precision=HIGH, preferred_element_type=F32)
    columns = []
    for f in range(5):
        for ch in range(3):
            parts = []
            for t in range(fold):
                for v in range(3):
                    at = (f * 3 + v) * rows3 + ch * groups
                    parts.append(wide[at : at + groups, t * LANES : (t + 1) * LANES])
            columns.append(jnp.concatenate(parts, axis=0))
    tall = jnp.concatenate(columns, axis=1)
    maps = jnp.dot(fb, tall, precision=HIGH, preferred_element_type=F32)
    span = 3 * LANES
    score, pull = jax.vjp(similarity, *[maps[:, f * span : (f + 1) * span] for f in range(5)])
    parts = pull(jnp.full(score.shape, -STRUCT_WEIGHT, F32))
    row = lax.broadcasted_iota(jnp.int32, score.shape, 0)
    col = lax.broadcasted_iota(jnp.int32, (score.shape[0], LANES), 1)
    col = jnp.concatenate([col] * 3, axis=1)
    row_at = row - RIM + lax.axis_index("ty") * side
    col_at = col - RIM + lax.axis_index("tx") * side
    reach = side + 2 * RIM
    inside = (
        (row_at >= 0) & (row_at < height) & (col_at >= 0) & (col_at < width)
        & (row < reach) & (col < reach)
    )
    own = (row >= RIM) & (row < RIM + side) & (col >= RIM) & (col < RIM + side)
    coeffs = jnp.concatenate(
        [jnp.where(inside, parts[f], 0.0) for f in (0, 2, 4)], axis=1
    )
    low = jnp.dot(fc, coeffs, precision=HIGH, preferred_element_type=F32)
    rows = []
    for n in range(9):
        rows.append(
            jnp.concatenate(
                [
                    low[t * groups : (t + 1) * groups, n * LANES : (n + 1) * LANES]
                    for t in range(fold)
                ],
                axis=1,
            )
        )
    smooth = jnp.dot(
        jnp.concatenate(rows, axis=0), fd, precision=HIGH, preferred_element_type=F32
    )
    image, target = near[4][:rows3, :], near[4][rows3:, :]
    gap = image - target
    robust = jnp.sqrt(gap * gap + ROBUST_TERM)
    slope[...] = (
        smooth[:rows3]
        + 2.0 * image * smooth[rows3 : 2 * rows3]
        + target * smooth[2 * rows3 :]
        + (1.0 - STRUCT_WEIGHT) * gap / robust
    )
    total = (1.0 - STRUCT_WEIGHT) * jnp.sum(robust) + STRUCT_WEIGHT * jnp.sum(
        jnp.where(own, 1.0 - score, 0.0)
    )
    loss[...] = jnp.full(loss.shape, total, F32)


def score_entry(side, height, width, *refs):
    above, left, own, right, below = refs[:5]
    rows = own.shape[0]
    near = [above[h * rows : (h + 1) * rows, :] for h in range(3)]
    near += [left[...], own[...], right[...]]
    near += [below[h * rows : (h + 1) * rows, :] for h in range(3)]
    score_kernel(side, height, width, near, *refs[5:])


def backward_kernel(
    side, table, checks, prefix, behind, slope, reduce, stage,
    rhs, wide, grows, buf_a, buf_b, behinds, sums_a, sums_b, moments,
):
    lmax = stage.shape[0]
    per = lmax // SEGS
    pixels = prefix.shape[1]
    groups = pixels // LANES
    chunks = lmax * LANES // CHUNK
    wide[...] = jnp.zeros_like(wide)
    for ch in range(3):
        for j in range(groups):
            lanes = pl.ds(j * LANES, LANES)
            wide[pl.ds(6 + ch, 1), lanes] = slope[pl.ds(ch * groups + j, 1), :]
    for ch in range(3):
        row = wide[pl.ds(6 + ch, 1), :]
        hi = row.astype(BF16).astype(F32)
        grows[ch] = jnp.broadcast_to(row, (SEGS, pixels))
        wide[pl.ds(6 + ch, 1), :] = hi
        wide[pl.ds(22 + ch, 1), :] = hi
        wide[pl.ds(38 + ch, 1), :] = row - hi
    rhs[:, :pixels] = monomials(side)
    rhs[:, pixels:] = wide[...].astype(BF16)

    def product(n, buf, p):
        rows = pl.ds(pl.multiple_of(n * CHUNK, CHUNK), CHUNK)
        cols = slice(p * COLS, (p + 1) * COLS)
        buf[:, cols] = jnp.dot(table[rows, :], rhs[:, cols], preferred_element_type=F32)

    def reduced(n, sums, low):
        rows = pl.ds(pl.multiple_of(n * CHUNK, CHUNK), CHUNK)
        part = sums[...].astype(BF16)
        if low:
            part = (sums[...] - part.astype(F32)).astype(BF16)
        value = jnp.dot(part, reduce[...], preferred_element_type=F32)
        moments[rows, :] = moments[rows, :] + value if low else value

    lane = lax.broadcasted_iota(jnp.int32, (SEGS, LANES), 1)
    front = lane < LANES // 2
    even = (lane & (LANES // 4)) == 0

    def folded(a, b):
        return jnp.where(front, a, b) + pltpu.roll(jnp.where(front, b, a), LANES // 2, 1)

    def packed(a, b, c, d):
        ab, cd = folded(a, b), folded(c, d)
        ab = ab + pltpu.roll(ab, LANES - LANES // 4, 1)
        cd = cd + pltpu.roll(cd, LANES // 4, 1)
        return jnp.where(even, ab, cd)

    def block(n, b, buf, sums):
        first = b * SPAN * SEGS
        rows = [pl.ds(first + i * SEGS, SEGS) for i in range(SPAN)]
        totals = [[None] * 6 for _ in range(SPAN)]

        def add(i, f, value):
            totals[i][f] = value if totals[i][f] is None else totals[i][f] + value

        for q in reversed(range(groups // 2)):
            lanes = slice(q * 2 * LANES, (q + 1) * 2 * LANES)
            light = checks[n * (STEPS // SPAN) + b, :, lanes] * prefix[:, lanes]
            tints = [grows[ch, :, lanes] for ch in range(3)]
            alphas, weights = [], []
            for i in range(SPAN):
                alphas.append(jnp.exp2(buf[rows[i], lanes]))
                weights.append(light * alphas[i])
                light = light - weights[i]
            back = behinds[:, lanes]
            for i in reversed(range(SPAN)):
                gap = buf[rows[i], pixels + q * 2 * LANES : pixels + (q + 1) * 2 * LANES] - back
                back = back + alphas[i] * gap
                pull = weights[i] * gap
                add(i, 0, pull[:, LANES:])
                add(i, 1, totals[i][0])
                add(i, 2, totals[i][1])
                add(i, 0, pull[:, :LANES])
                if q > 0:
                    add(i, 1, totals[i][0])
                    add(i, 2, totals[i][1])
                for ch in range(3):
                    tint = weights[i] * tints[ch]
                    add(i, 3 + ch, tint[:, LANES:] + tint[:, :LANES])
            behinds[:, lanes] = back
        for i in range(SPAN):
            zero, one, two, red, green, blue = totals[i]
            sums[rows[i], 0:LANES] = zero
            sums[rows[i], LANES : 2 * LANES] = one
            sums[rows[i], 2 * LANES : 3 * LANES] = packed(red, green, blue, two)

    behinds[...] = behind[0] * grows[0] + behind[1] * grows[1] + behind[2] * grows[2]
    pieces = 2 * pixels // COLS
    for p in range(pieces):
        product(chunks - 1, buf_a, p)
    turn = chunks // per
    share = SEGS // turn

    def collect(m, seg):
        moved = moments[pl.ds(m * (SEGS * LANES) + seg, LANES, stride=SEGS), :].T
        stage[seg * per + m] = moved[:16]

    def half(n, ahead, buf, other, sums, last, seg):
        m = (n // turn + 1) % per
        spans = STEPS // SPAN
        for at in range(spans):
            for p in range(at * pieces // spans, (at + 1) * pieces // spans):
                product(ahead, other, p)
            if at == 1 or at == 3:
                reduced(n + 1, last, at == 3)
            block(n, spans - 1 - at, buf, sums)
        for q in range(share):
            collect(m, seg * share + q)

    def pair(h, _):
        n = chunks - 1 - 2 * h
        half(n, n - 1, buf_a, buf_b, sums_a, sums_b, n % turn)
        half(n - 1, jnp.maximum(n - 2, 0), buf_b, buf_a, sums_b, sums_a, n % turn - 1)
        return 0

    lax.fori_loop(0, chunks // 2, pair, 0)
    reduced(0, sums_b, False)
    reduced(0, sums_b, True)
    for seg in range(SEGS):
        collect(0, seg)


def deliver_kernel(slot, stage, *refs):
    reply = refs[-1]
    column = refs[0][...]
    for share in refs[1:-1]:
        column = column + share[...]
    for o in range(reply.shape[0]):
        reply[o, pl.ds(reply.shape[1] - 1, 1), :] = column[:1]
    for k in range(slot.shape[0]):
        s = slot[k]
        o = s // CAP
        c = s - o * CAP
        reply[o, pl.ds(pl.multiple_of(c * 8, 8), 8), :] = stage[k, :8, :]
        reply[o, pl.ds(CAP * 8 + c, 1), :] = stage[k, 8:9, :]


def gather_kernel(
    across, side, height, width, asked, got, gaussians, grads, loss, sums, zeros, pieces, wanted, sem
):
    owned = gaussians.shape[1]
    parts = owned // 8
    shares = got[:, got.shape[1] - 1, :]
    loss[0] = jnp.sum(shares[:, :1]) * (1.0 / (3.0 * height * width))
    zeros[...] = jnp.zeros_like(zeros)
    sums[...] = jnp.zeros_like(sums)
    for g in range(parts + 1):
        wanted[g] = 0
    for s in range(across * CAP):
        c, t = divmod(s, across)
        index = asked[t, 0, c]
        index = jnp.where(index >= 0, index, owned)
        wanted[index // 8] = 1
        row = pl.ds(index, 1)
        for f in range(9):
            at = c * 8 + f if f < 8 else CAP * 8 + c
            sums[f, row, :] = got[t, at : at + 1, :]
        sums[9, row, :] = jnp.full((1, LANES), t + 1.0, F32)

    def target(g):
        return grads.at[:, pl.ds(pl.multiple_of(g * 8, 8), 8), :]

    def blank(g, _):
        @pl.when(wanted[g] == 0)
        def _():
            pltpu.make_async_copy(zeros, target(g), sem.at[g]).start()

        return 0

    lax.fori_loop(0, parts, blank, 0)
    row_at = lax.axis_index("ty").astype(F32)
    shift_y = (0.5 * height - 0.5 * side - 0.5) - side * row_at

    def solve(g):
        rows = pl.ds(pl.multiple_of(g * 8, 8), 8)
        field = [gaussians[f, rows, :] for f in range(11)]
        tile = sums[9, rows, :]
        live = tile > 0.0
        shift_x = (0.5 * width - 0.5 * side - 0.5) - side * (tile - 1.0)

        def put(f, value):
            pieces[g, f] = jnp.where(live, value, 0.0)

        def shaped(x, y, z, log_scale, quat):
            xx, xy, yy, pos_u, pos_v = conic(x, y, z, log_scale, quat)
            return expanded(xx, xy, yy, pos_u + shift_x, pos_v + shift_y, jnp.zeros_like(x))

        _, pull = jax.vjp(shaped, *field[:3], field[3:6], field[6:10])
        moments = [LN2 * sums[f, rows, :] for f in range(6)]
        gx, gy, gz, gscale, gquat = pull(tuple(moments))
        basis, pull_basis = jax.vjp(directions, *field[:3])
        tints = [sums[6 + ch, rows, :] for ch in range(3)]
        tilts = []
        for m in range(16):
            tilt = None
            for ch in range(3):
                term = tints[ch] * gaussians[11 + 3 * m + ch, rows, :]
                tilt = term if tilt is None else tilt + term
                put(11 + 3 * m + ch, tints[ch] * basis[m])
            tilts.append(tilt)
        dx, dy, dz = pull_basis(tilts)
        put(0, gx + dx)
        put(1, gy + dy)
        put(2, gz + dz)
        for f in range(3):
            put(3 + f, gscale[f])
        for f in range(4):
            put(6 + f, gquat[f])
        put(10, moments[5] * (LOG2E / (1.0 + jnp.exp(field[10]))))
        pltpu.make_async_copy(pieces.at[g], target(g), sem.at[g]).start()

    def part(g, _):
        @pl.when(wanted[g] > 0)
        def _():
            solve(g)

        return 0

    lax.fori_loop(0, parts, part, 0)

    def finish(g, _):
        pltpu.make_async_copy(zeros, target(g), sem.at[g]).wait()
        return 0

    lax.fori_loop(0, parts, finish, 0)


def moment_columns(side):
    lane = np.arange(LANES)
    x = lane % side - side // 2
    t = lane // side - side // 2
    step = LANES // side
    one = np.ones_like(x)
    out = np.zeros((3 * LANES, LANES))
    out[:LANES, :6] = np.stack([x * x, x * t, t * t, x, t, one], axis=1)
    out[LANES : 2 * LANES, 1] = step * x
    out[LANES : 2 * LANES, 2] = 2 * step * t - step * step
    out[LANES : 2 * LANES, 4] = step
    quarter = LANES // 4
    for n, (column, weight) in enumerate(((6, 1), (8, 1), (7, 1), (2, 2 * step * step))):
        at = 2 * LANES + n * quarter
        out[at : at + quarter, column] = weight
    return out.astype(ml_dtypes.bfloat16)


def shifted(x, axis):
    size = lax.axis_size(axis)
    up = [(i, i + 1) for i in range(size - 1)]
    return lax.ppermute(x, axis, up), lax.ppermute(x, axis, [(j, i) for i, j in up])


def per_device(gaussians, tile_lists, tile_counts, depth_order, target):
    owned, fields, block = gaussians.shape
    lmax = tile_lists.shape[2]
    side = target.shape[1]
    pixels = side * side
    groups = pixels // LANES
    across = lax.axis_size("tx")
    down = lax.axis_size("ty")
    height = side * lax.axis_size("ty")
    width = side * across
    slots = across * CAP
    depth = -(-(CAP * 9 + 1) // 8) * 8
    f32 = functools.partial(jax.ShapeDtypeStruct, dtype=F32)
    i32 = functools.partial(jax.ShapeDtypeStruct, dtype=jnp.int32)
    reduce = jnp.asarray(moment_columns(side))

    fieldwise = jnp.transpose(gaussians, (1, 0, 2))
    request, slot = pl.pallas_call(
        functools.partial(request_kernel, owned, across),
        out_shape=(i32((across, 1, LANES)), i32((lmax,))),
        in_specs=[SMEM] * 3,
        out_specs=(SMEM, SMEM),
        scratch_shapes=[pltpu.SMEM((across,), jnp.int32)],
        name="request",
    )(tile_lists, tile_counts, depth_order)
    asked = lax.all_to_all(request, "tx", split_axis=0, concat_axis=0, tiled=True)
    projected = pl.pallas_call(
        functools.partial(project_kernel, 16),
        out_shape=f32((9, owned, block)),
        in_specs=[VMEM],
        out_specs=VMEM,
        compiler_params=PARAMS,
        name="project",
    )(fieldwise)
    send = pl.pallas_call(
        functools.partial(serve_kernel, across, side, float(height), float(width)),
        out_shape=f32((across, depth, block)),
        in_specs=[SMEM, VMEM],
        out_specs=VMEM,
        scratch_shapes=[pltpu.VMEM((9, slots, block), F32)],
        compiler_params=PARAMS,
        name="serve",
    )(asked, projected)
    recv = lax.all_to_all(send, "tx", split_axis=0, concat_axis=0, tiled=True)
    chunks = lmax * block // CHUNK
    wide = pixels + 3 * LANES
    table, checks, prefix, behind, dense = pl.pallas_call(
        functools.partial(forward_kernel, side),
        out_shape=(
            jax.ShapeDtypeStruct((lmax * block, LANES), BF16),
            f32((chunks * (STEPS // SPAN), SEGS, pixels)),
            f32((SEGS, pixels)),
            f32((3, SEGS, pixels)),
            f32((6 * groups, LANES)),
        ),
        in_specs=[SMEM, SMEM, VMEM, VMEM],
        out_specs=(VMEM,) * 5,
        scratch_shapes=[
            pltpu.VMEM((LANES, wide), BF16),
            pltpu.VMEM((lmax * block, LANES), F32),
            pltpu.VMEM((CHUNK, wide), F32),
            pltpu.VMEM((CHUNK, wide), F32),
            pltpu.VMEM((4, SEGS, pixels), F32),
        ],
        compiler_params=PARAMS,
        name="forward",
    )(slot, tile_counts, recv, target.reshape(3 * groups, LANES))
    left, right = shifted(dense, "tx")
    above, below = shifted(jnp.concatenate([left, dense, right], axis=0), "ty")
    slope, part = pl.pallas_call(
        functools.partial(score_entry, side, height, width),
        out_shape=(f32((3 * groups, LANES)), f32((8, LANES))),
        in_specs=[VMEM] * 5,
        out_specs=(VMEM, VMEM),
        compiler_params=PARAMS,
        name="score",
    )(above, left, dense, right, below)
    shares = [
        lax.ppermute(part, "ty", [(i, (i + k) % down) for i in range(down)]) for k in range(1, down)
    ]
    stage = pl.pallas_call(
        functools.partial(backward_kernel, side),
        out_shape=f32((lmax, 16, LANES)),
        in_specs=[VMEM] * 6,
        out_specs=VMEM,
        scratch_shapes=[
            pltpu.VMEM((LANES, 2 * pixels), BF16),
            pltpu.VMEM((LANES, pixels), F32),
            pltpu.VMEM((3, SEGS, pixels), F32),
            pltpu.VMEM((CHUNK, 2 * pixels), F32),
            pltpu.VMEM((CHUNK, 2 * pixels), F32),
            pltpu.VMEM((SEGS, pixels), F32),
            pltpu.VMEM((CHUNK, 3 * LANES), F32),
            pltpu.VMEM((CHUNK, 3 * LANES), F32),
            pltpu.VMEM((lmax * block + CHUNK, LANES), F32),
        ],
        compiler_params=PARAMS,
        name="backward",
    )(table, checks, prefix, behind, slope, reduce)
    reply = pl.pallas_call(
        deliver_kernel,
        out_shape=f32((across, depth, block)),
        in_specs=[SMEM] + [VMEM] * (1 + down),
        out_specs=VMEM,
        compiler_params=PARAMS,
        name="deliver",
    )(slot, stage, part, *shares)
    got = lax.all_to_all(reply, "tx", split_axis=0, concat_axis=0, tiled=True)
    grads, loss = pl.pallas_call(
        functools.partial(gather_kernel, across, side, float(height), float(width)),
        out_shape=(f32((fields, owned, block)), f32((1,))),
        in_specs=[SMEM, VMEM, VMEM],
        out_specs=(ANY, SMEM),
        scratch_shapes=[
            pltpu.VMEM((10, owned + 8, block), F32),
            pltpu.VMEM((fields, 8, block), F32),
            pltpu.VMEM((owned // 8, fields, 8, block), F32),
            pltpu.SMEM((owned // 8 + 1,), jnp.int32),
            pltpu.SemaphoreType.DMA((owned // 8,)),
        ],
        compiler_params=PARAMS,
        name="gather",
    )(asked, got, fieldwise)
    return (jnp.transpose(grads, (1, 0, 2)), loss[0])


def solution(mesh):
    return jax.shard_map(
        per_device,
        mesh=mesh,
        in_specs=(
            P(("ty", "tx"), None, None),
            P("ty", "tx", None),
            P("ty", "tx"),
            P(),
            P(None, "ty", "tx"),
        ),
        out_specs=(P(("ty", "tx"), None, None), P()),
        check_vma=False,
    )
```

```python
import functools

import jax
import jax.numpy as jnp
import ml_dtypes
import numpy as np
from jax import lax
from jax.experimental import pallas as pl
from jax.experimental.pallas import tpu as pltpu
from jax.sharding import PartitionSpec as P

CAP = 3
SEGS = 8
LANES = 128
CHUNK = 256
STEPS = CHUNK // SEGS
SPAN = 4
COLS = 256
RIM = 5
TAPS = 2 * RIM + 1
LOG2E = 1.4426950408889634
LN2 = 0.6931471805599453
DARK = -1e30

FOCAL = 1000.0
LOW_PASS = 0.3
STRUCT_WEIGHT = 0.2
LUMA_TERM = 0.0001
CONTRAST_TERM = 0.0009
ROBUST_TERM = 1e-06
HARMONIC_ZERO = 0.28209479177387814
HARMONIC_ONE = 0.4886025119029199
HARMONIC_TWO = (
    1.0925484305920792,
    -1.0925484305920792,
    0.31539156525252005,
    -1.0925484305920792,
    0.5462742152960396,
)
HARMONIC_THREE = (
    -0.5900435899266435,
    2.890611442640554,
    -0.4570457994644658,
    0.3731763325901154,
    -0.4570457994644658,
    1.445305721320277,
    -0.5900435899266435,
)

HIGH = lax.Precision.HIGHEST
F32 = jnp.float32
BF16 = jnp.bfloat16
ANY = pl.BlockSpec(memory_space=pl.ANY)
SMEM = pl.BlockSpec(memory_space=pltpu.SMEM)
VMEM = pl.BlockSpec(memory_space=pltpu.VMEM)
PARAMS = pltpu.CompilerParams(vmem_limit_bytes=24 * 1024 * 1024)


def harmonics(x, y, z):
    xx, yy, zz = x * x, y * y, z * z
    xy, yz, xz = x * y, y * z, x * z
    return [
        HARMONIC_ZERO * jnp.ones_like(x),
        -HARMONIC_ONE * y,
        HARMONIC_ONE * z,
        -HARMONIC_ONE * x,
        HARMONIC_TWO[0] * xy,
        HARMONIC_TWO[1] * yz,
        HARMONIC_TWO[2] * (2.0 * zz - xx - yy),
        HARMONIC_TWO[3] * xz,
        HARMONIC_TWO[4] * (xx - yy),
        HARMONIC_THREE[0] * y * (3.0 * xx - yy),
        HARMONIC_THREE[1] * xy * z,
        HARMONIC_THREE[2] * y * (4.0 * zz - xx - yy),
        HARMONIC_THREE[3] * z * (2.0 * zz - 3.0 * xx - 3.0 * yy),
        HARMONIC_THREE[4] * x * (4.0 * zz - xx - yy),
        HARMONIC_THREE[5] * z * (xx - yy),
        HARMONIC_THREE[6] * x * (xx - 3.0 * yy),
    ]


def directions(x, y, z):
    length = jnp.sqrt(x * x + y * y + z * z)
    return harmonics(x / length, y / length, z / length)


def conic(mean_x, mean_y, mean_z, log_scale, quat):
    scale = [jnp.exp(s) for s in log_scale]
    norm = jnp.sqrt(quat[0] * quat[0] + quat[1] * quat[1] + quat[2] * quat[2] + quat[3] * quat[3])
    w, i, j, k = (q / norm for q in quat)
    rotation = [
        [1.0 - 2.0 * (j * j + k * k), 2.0 * (i * j - w * k), 2.0 * (i * k + w * j)],
        [2.0 * (i * j + w * k), 1.0 - 2.0 * (i * i + k * k), 2.0 * (j * k - w * i)],
        [2.0 * (i * k - w * j), 2.0 * (j * k + w * i), 1.0 - 2.0 * (i * i + j * j)],
    ]
    scaled = [[rotation[r][c] * scale[c] for c in range(3)] for r in range(3)]

    def sigma(r, c):
        return scaled[r][0] * scaled[c][0] + scaled[r][1] * scaled[c][1] + scaled[r][2] * scaled[c][2]

    s00, s01, s02, s11, s12, s22 = (
        sigma(0, 0), sigma(0, 1), sigma(0, 2), sigma(1, 1), sigma(1, 2), sigma(2, 2),
    )
    inverse_z = 1.0 / mean_z
    diag = FOCAL * inverse_z
    jac_xz = -FOCAL * mean_x * inverse_z * inverse_z
    jac_yz = -FOCAL * mean_y * inverse_z * inverse_z
    u0, u1, u2 = diag * s00 + jac_xz * s02, diag * s01 + jac_xz * s12, diag * s02 + jac_xz * s22
    v1, v2 = diag * s11 + jac_yz * s12, diag * s12 + jac_yz * s22
    cov_uu = u0 * diag + u2 * jac_xz + LOW_PASS
    cov_uv = u1 * diag + u2 * jac_yz
    cov_vv = v1 * diag + v2 * jac_yz + LOW_PASS
    determinant = cov_uu * cov_vv - cov_uv * cov_uv
    half = -0.5 * LOG2E
    xx = half * (cov_vv / determinant)
    xy = (-2.0 * half) * (cov_uv / determinant)
    yy = half * (cov_uu / determinant)
    return xx, xy, yy, FOCAL * mean_x * inverse_z, FOCAL * mean_y * inverse_z


def expanded(xx, xy, yy, pos_u, pos_v, log_opacity):
    x1 = -2.0 * xx * pos_u - xy * pos_v
    y1 = -2.0 * yy * pos_v - xy * pos_u
    one = xx * pos_u * pos_u + xy * pos_u * pos_v + yy * pos_v * pos_v + log_opacity
    return xx, xy, yy, x1, y1, one


def tile_shifts(across, side, height, width):
    column = lax.broadcasted_iota(jnp.int32, (across, LANES), 0).astype(F32)
    column = jnp.concatenate([column] * CAP, axis=0)
    row = lax.axis_index("ty").astype(F32)
    shift_x = (0.5 * width - 0.5 * side - 0.5) - side * column
    shift_y = jnp.full(column.shape, (0.5 * height - 0.5 * side - 0.5) - side * row, F32)
    return shift_x, shift_y


def request_kernel(owned, across, lists, count, order, request, slot, seen):
    base = lax.axis_index("ty") * across
    for o in range(across):
        seen[o] = 0
        for c in range(CAP):
            request[o, 0, c] = -1
    used = count[0, 0]

    def entry(k, _):
        @pl.when(k < used)
        def _():
            block = order[lists[0, 0, k]]
            home = block // owned
            local = block - home * owned
            home = home - base
            at = seen[home]
            seen[home] = at + 1
            request[home, 0, at] = local
            slot[k] = home * CAP + at

        return 0

    lax.fori_loop(0, slot.shape[0], entry, 0, unroll=True)
    free = 0
    for o in range(across):
        free = jnp.where(seen[o] < CAP, o * CAP + CAP - 1, free)

    def rest(k, _):
        slot[k] = free
        return 0

    lax.fori_loop(used, slot.shape[0], rest, 0)


def project_kernel(span, gaussians, out):
    def part(n, _):
        rows = pl.ds(pl.multiple_of(n * span, span), span)
        field = [gaussians[f, rows, :] for f in range(11)]
        light = -LOG2E * jnp.log(1.0 + jnp.exp(-field[10])) + float(np.log2(0.99))
        values = list(conic(field[0], field[1], field[2], field[3:6], field[6:10]))
        values.append(jnp.maximum(light, DARK))
        basis = directions(field[0], field[1], field[2])
        for ch in range(3):
            color = 0.5 + basis[0] * gaussians[11 + ch, rows, :]
            for m in range(1, 16):
                color = color + basis[m] * gaussians[11 + 3 * m + ch, rows, :]
            values.append(color)
        for f in range(9):
            out[f, rows, :] = values[f]
        return 0

    lax.fori_loop(0, gaussians.shape[1] // span, part, 0)


def asked_index(asked, across, s):
    c = s // across
    return asked[s - c * across, 0, c]


def serve_kernel(across, side, height, width, asked, projected, send, chosen):
    def pick(s, _):
        index = jnp.maximum(asked_index(asked, across, s), 0)
        for f in range(9):
            chosen[f, pl.ds(s, 1), :] = projected[f, pl.ds(index, 1), :]
        return 0

    lax.fori_loop(0, across * CAP, pick, 0, unroll=True)
    shift_x, shift_y = tile_shifts(across, side, height, width)
    rows = list(
        expanded(
            chosen[0], chosen[1], chosen[2], chosen[3] + shift_x, chosen[4] + shift_y, chosen[5]
        )
    ) + [chosen[6], chosen[7], chosen[8]]
    for c in range(CAP):
        for f in range(9):
            at = c * 8 + f if f < 8 else CAP * 8 + c
            send[:, at, :] = rows[f][c * across : (c + 1) * across]


def monomials(side):
    pixels = side * side
    lane = lax.broadcasted_iota(jnp.int32, (8, pixels), 1)
    row = lax.broadcasted_iota(jnp.int32, (8, pixels), 0)
    x = ((lane & (side - 1)) - side // 2).astype(F32)
    y = ((lane >> (side.bit_length() - 1)) - side // 2).astype(F32)
    mono = jnp.zeros((8, pixels), F32)
    for at, value in enumerate((x * x, x * y, y * y, x, y, jnp.ones_like(x))):
        mono = jnp.where(row == at, value, mono)
    blank = jnp.zeros((8, pixels), F32)
    rest = jnp.zeros((LANES - 48, pixels), F32)
    return jnp.concatenate([mono, blank] * 3 + [rest], axis=0).astype(BF16)


def spreaders():
    row = lax.broadcasted_iota(jnp.int32, (LANES, LANES), 0)
    return jnp.concatenate(
        [jnp.where((row == 6 + c) | (row == 22 + c), 1.0, 0.0).astype(F32) for c in range(3)], axis=1
    ).astype(BF16)


def repeated(x, times):
    return jnp.concatenate([x] * times, axis=1)


def forward_kernel(
    side, slot, count, recv, target, table, alphas, checks, prefix, behind, dense,
    planes, spread, buf_a, buf_b, ends,
):
    lmax = slot.shape[0]
    per = lmax // SEGS
    pixels = prefix.shape[1]
    groups = pixels // LANES
    planes[:, :pixels] = monomials(side)
    planes[:, pixels:] = spreaders()
    zero_rows = jnp.zeros((7, LANES), F32)
    dead = jnp.where(lax.broadcasted_iota(jnp.int32, (16, LANES), 0) == 5, DARK, 0.0)
    is_color = lax.broadcasted_iota(jnp.int32, (16, LANES), 0) >= 6
    filler = jnp.zeros((LANES - 48, LANES), F32)

    def place(m, seg):
        s = slot[seg * per + m]
        live = seg * per + m < count[0, 0]
        o = s // CAP
        c = s - o * CAP
        head = recv[o, pl.ds(pl.multiple_of(c * 8, 8), 8), :]
        tail = recv[o, pl.ds(CAP * 8 + c, 1), :]
        rows = jnp.concatenate([head, tail, zero_rows], axis=0)
        rows = jnp.where(live, rows, dead)
        hi = rows.astype(BF16).astype(F32)
        rest = rows - hi
        mid = rest.astype(BF16).astype(F32)
        low = (rest - mid).astype(BF16).astype(F32)
        third = jnp.where(is_color, hi, low)
        stacked = jnp.concatenate([hi, mid, third, filler], axis=0)
        spread[pl.ds(m * (SEGS * LANES) + seg, LANES, stride=SEGS), :] = stacked.T

    for seg in range(SEGS):
        place(0, seg)

    width = planes.shape[1]
    pieces = -(-width // COLS)

    def product(n, buf, p):
        rows = pl.ds(pl.multiple_of(n * CHUNK, CHUNK), CHUNK)
        if p == 0:
            table[rows, :] = spread[rows, :].astype(BF16)
        cols = slice(p * COLS, min((p + 1) * COLS, width))
        buf[:, cols] = jnp.dot(table[rows, :], planes[:, cols], preferred_element_type=F32)

    def blend(n, b, buf, carry):
        light, red, green, blue = carry
        checks[n * (STEPS // SPAN) + b] = light
        for i in range(b * SPAN, (b + 1) * SPAN):
            rows = pl.ds(i * SEGS, SEGS)
            alpha = jnp.exp2(buf[rows, :pixels])
            alphas[pl.ds(pl.multiple_of(n * CHUNK + i * SEGS, SEGS), SEGS), :] = alpha
            weight = light * alpha
            light = light - weight
            red = red + weight * repeated(buf[rows, pixels : pixels + LANES], groups)
            green = green + weight * repeated(buf[rows, pixels + LANES : pixels + 2 * LANES], groups)
            blue = blue + weight * repeated(
                buf[rows, pixels + 2 * LANES : pixels + 3 * LANES], groups
            )
        return light, red, green, blue

    for p in range(pieces):
        product(0, buf_a, p)
    chunks = lmax * LANES // CHUNK
    turn = chunks // per
    share = SEGS // turn

    def pair(h, carry):
        n = 2 * h
        m = (n // turn + 1) % per
        for b in range(STEPS // SPAN):
            if b < pieces:
                product(n + 1, buf_b, b)
            if b % 2 == 0 and b // 2 < 2 * share:
                place(m, (n % turn) * share + b // 2)
            carry = blend(n, b, buf_a, carry)
        for b in range(STEPS // SPAN):
            if b < pieces:
                product(jnp.minimum(n + 2, chunks - 1), buf_a, b)
            carry = blend(n + 1, b, buf_b, carry)
        return carry

    start = (jnp.ones((SEGS, pixels), F32),) + (jnp.zeros((SEGS, pixels), F32),) * 3
    carry = lax.fori_loop(0, chunks // 2, pair, start)
    for f in range(4):
        ends[f] = carry[f]
    ahead = jnp.ones((1, pixels), F32)
    for seg in range(SEGS):
        prefix[pl.ds(seg, 1), :] = ahead
        ahead = ahead * ends[0, pl.ds(seg, 1), :]
    for ch in range(3):
        seen = jnp.zeros((1, pixels), F32)
        for seg in reversed(range(SEGS)):
            behind[ch, pl.ds(seg, 1), :] = seen
            seen = ends[1 + ch, pl.ds(seg, 1), :] + ends[0, pl.ds(seg, 1), :] * seen
        for j in range(groups):
            dense[pl.ds(ch * groups + j, 1), :] = seen[:, j * LANES : (j + 1) * LANES]
    dense[3 * groups :, :] = target[...]


def similarity(mean_a, mean_b, square_a, square_b, cross):
    var_a = square_a - mean_a * mean_a
    var_b = square_b - mean_b * mean_b
    covar = cross - mean_a * mean_b
    top = (2.0 * mean_a * mean_b + LUMA_TERM) * (2.0 * covar + CONTRAST_TERM)
    bottom = (mean_a * mean_a + mean_b * mean_b + LUMA_TERM) * (var_a + var_b + CONTRAST_TERM)
    return top / bottom


def tap(distance):
    weights = [float(np.exp(-((k - RIM) ** 2) / 4.5)) for k in range(TAPS)]
    value = jnp.exp(distance * distance * (-1.0 / 4.5)) * (1.0 / sum(weights))
    return jnp.where(jnp.abs(distance) <= RIM, value, 0.0)


def places(shape, dim):
    return lax.broadcasted_iota(jnp.int32, shape, dim)


def bands(side, padded):
    fold = LANES // side
    groups = side // fold
    reach = side + 2 * RIM
    shape = (3 * side, LANES)
    out = places(shape, 1)
    along = tap((places(shape, 0) - side - out + RIM).astype(F32))
    along = jnp.where(out < reach, along, 0.0)
    blank = jnp.zeros((side, LANES), F32)
    fa = jnp.concatenate(
        [
            jnp.concatenate(
                [along[h * side : (h + 1) * side] if u == t else blank for u in range(fold)], axis=1
            )
            for h in range(3)
            for t in range(fold)
        ],
        axis=0,
    )
    block = 3 * groups
    shape = (padded, fold * block)
    out, at = places(shape, 0), places(shape, 1)
    t = jnp.zeros(shape, jnp.int32)
    for k in range(1, fold):
        t = t + jnp.where(at >= k * block, 1, 0)
    source = (at - t * block) * fold + t - side
    fb = jnp.where(out < reach, tap((source - out + RIM).astype(F32)), 0.0)
    shape = (fold * groups, padded)
    row, out = places(shape, 0), places(shape, 1)
    t = jnp.zeros(shape, jnp.int32)
    for k in range(1, fold):
        t = t + jnp.where(row >= k * groups, 1, 0)
    source = (row - t * groups) * fold + t
    fc = jnp.where(out < reach, tap((out - RIM - source).astype(F32)), 0.0)
    shape = (LANES, LANES)
    out, at = places(shape, 0), places(shape, 1)
    back = tap((out - RIM - (at & (side - 1))).astype(F32))
    back = jnp.where(out < reach, back, 0.0)
    fd = jnp.concatenate(
        [jnp.where((at >= t * side) & (at < (t + 1) * side), back, 0.0) for t in range(fold)], axis=0
    )
    return fa, fb, fc, fd


def score_kernel(side, height, width, near, slope, loss):
    fa, fb, fc, fd = bands(side, -(-(side + 2 * RIM) // 8) * 8)
    rows3 = near[4].shape[0] // 2
    groups = rows3 // 3
    fold = LANES // side
    fields = [[], [], [], [], []]
    for v in range(3):
        strip = jnp.concatenate([near[3 * v + h] for h in range(3)], axis=1)
        image, target = strip[:rows3], strip[rows3:]
        for f, plane in enumerate([image, target, image * image, target * target, image * target]):
            fields[f].append(plane)
    stack = jnp.concatenate([fields[f][v] for f in range(5) for v in range(3)], axis=0)
    wide = jnp.dot(stack, fa, precision=HIGH, preferred_element_type=F32)
    columns = []
    for f in range(5):
        for ch in range(3):
            parts = []
            for t in range(fold):
                for v in range(3):
                    at = (f * 3 + v) * rows3 + ch * groups
                    parts.append(wide[at : at + groups, t * LANES : (t + 1) * LANES])
            columns.append(jnp.concatenate(parts, axis=0))
    tall = jnp.concatenate(columns, axis=1)
    maps = jnp.dot(fb, tall, precision=HIGH, preferred_element_type=F32)
    span = 3 * LANES
    score, pull = jax.vjp(similarity, *[maps[:, f * span : (f + 1) * span] for f in range(5)])
    parts = pull(jnp.full(score.shape, -STRUCT_WEIGHT, F32))
    row = lax.broadcasted_iota(jnp.int32, score.shape, 0)
    col = lax.broadcasted_iota(jnp.int32, (score.shape[0], LANES), 1)
    col = jnp.concatenate([col] * 3, axis=1)
    row_at = row - RIM + lax.axis_index("ty") * side
    col_at = col - RIM + lax.axis_index("tx") * side
    reach = side + 2 * RIM
    inside = (
        (row_at >= 0) & (row_at < height) & (col_at >= 0) & (col_at < width)
        & (row < reach) & (col < reach)
    )
    own = (row >= RIM) & (row < RIM + side) & (col >= RIM) & (col < RIM + side)
    coeffs = jnp.concatenate(
        [jnp.where(inside, parts[f], 0.0) for f in (0, 2, 4)], axis=1
    )
    low = jnp.dot(fc, coeffs, precision=HIGH, preferred_element_type=F32)
    rows = []
    for n in range(9):
        rows.append(
            jnp.concatenate(
                [
                    low[t * groups : (t + 1) * groups, n * LANES : (n + 1) * LANES]
                    for t in range(fold)
                ],
                axis=1,
            )
        )
    smooth = jnp.dot(
        jnp.concatenate(rows, axis=0), fd, precision=HIGH, preferred_element_type=F32
    )
    image, target = near[4][:rows3, :], near[4][rows3:, :]
    gap = image - target
    robust = jnp.sqrt(gap * gap + ROBUST_TERM)
    slope[...] = (
        smooth[:rows3]
        + 2.0 * image * smooth[rows3 : 2 * rows3]
        + target * smooth[2 * rows3 :]
        + (1.0 - STRUCT_WEIGHT) * gap / robust
    )
    total = (1.0 - STRUCT_WEIGHT) * jnp.sum(robust) + STRUCT_WEIGHT * jnp.sum(
        jnp.where(own, 1.0 - score, 0.0)
    )
    loss[...] = jnp.full(loss.shape, total, F32)


def score_entry(side, height, width, *refs):
    above, left, own, right, below = refs[:5]
    rows = own.shape[0]
    near = [above[h * rows : (h + 1) * rows, :] for h in range(3)]
    near += [left[...], own[...], right[...]]
    near += [below[h * rows : (h + 1) * rows, :] for h in range(3)]
    score_kernel(side, height, width, near, *refs[5:])


def backward_kernel(
    table, alphas, checks, prefix, behind, slope, reduce, stage,
    rhs, wide, grows, buf_a, buf_b, behinds, sums_a, sums_b, moments,
):
    lmax = stage.shape[0]
    per = lmax // SEGS
    pixels = prefix.shape[1]
    groups = pixels // LANES
    chunks = lmax * LANES // CHUNK
    wide[...] = jnp.zeros_like(wide)
    for ch in range(3):
        for j in range(groups):
            lanes = pl.ds(j * LANES, LANES)
            wide[pl.ds(6 + ch, 1), lanes] = slope[pl.ds(ch * groups + j, 1), :]
    for ch in range(3):
        row = wide[pl.ds(6 + ch, 1), :]
        hi = row.astype(BF16).astype(F32)
        grows[ch] = jnp.broadcast_to(row, (SEGS, pixels))
        wide[pl.ds(6 + ch, 1), :] = hi
        wide[pl.ds(22 + ch, 1), :] = hi
        wide[pl.ds(38 + ch, 1), :] = row - hi
    rhs[...] = wide[...].astype(BF16)

    def product(n, buf, p):
        rows = pl.ds(pl.multiple_of(n * CHUNK, CHUNK), CHUNK)
        cols = slice(p * COLS, (p + 1) * COLS)
        buf[:, cols] = jnp.dot(table[rows, :], rhs[:, cols], preferred_element_type=F32)

    def reduced(n, sums, low):
        rows = pl.ds(pl.multiple_of(n * CHUNK, CHUNK), CHUNK)
        part = sums[...].astype(BF16)
        if low:
            part = (sums[...] - part.astype(F32)).astype(BF16)
        value = jnp.dot(part, reduce[...], preferred_element_type=F32)
        moments[rows, :] = moments[rows, :] + value if low else value

    lane = lax.broadcasted_iota(jnp.int32, (SEGS, LANES), 1)
    front = lane < LANES // 2
    even = (lane & (LANES // 4)) == 0

    def folded(a, b):
        return jnp.where(front, a, b) + pltpu.roll(jnp.where(front, b, a), LANES // 2, 1)

    def packed(a, b, c, d):
        ab, cd = folded(a, b), folded(c, d)
        ab = ab + pltpu.roll(ab, LANES - LANES // 4, 1)
        cd = cd + pltpu.roll(cd, LANES // 4, 1)
        return jnp.where(even, ab, cd)

    def block(n, b, buf, sums):
        first = b * SPAN * SEGS
        rows = [pl.ds(first + i * SEGS, SEGS) for i in range(SPAN)]
        totals = [[None] * 6 for _ in range(SPAN)]

        def add(i, f, value):
            totals[i][f] = value if totals[i][f] is None else totals[i][f] + value

        for q in reversed(range(groups // 2)):
            lanes = slice(q * 2 * LANES, (q + 1) * 2 * LANES)
            light = checks[n * (STEPS // SPAN) + b, :, lanes] * prefix[:, lanes]
            tints = [grows[ch, :, lanes] for ch in range(3)]
            kept, weights = [], []
            for i in range(SPAN):
                at = pl.multiple_of(n * CHUNK + first + i * SEGS, SEGS)
                kept.append(alphas[pl.ds(at, SEGS), lanes])
                weights.append(light * kept[i])
                light = light - weights[i]
            back = behinds[:, lanes]
            for i in reversed(range(SPAN)):
                gap = buf[rows[i], lanes] - back
                back = back + kept[i] * gap
                pull = weights[i] * gap
                add(i, 0, pull[:, LANES:])
                add(i, 1, totals[i][0])
                add(i, 2, totals[i][1])
                add(i, 0, pull[:, :LANES])
                if q > 0:
                    add(i, 1, totals[i][0])
                    add(i, 2, totals[i][1])
                for ch in range(3):
                    tint = weights[i] * tints[ch]
                    add(i, 3 + ch, tint[:, LANES:] + tint[:, :LANES])
            behinds[:, lanes] = back
        for i in range(SPAN):
            zero, one, two, red, green, blue = totals[i]
            sums[rows[i], 0:LANES] = zero
            sums[rows[i], LANES : 2 * LANES] = one
            sums[rows[i], 2 * LANES : 3 * LANES] = packed(red, green, blue, two)

    behinds[...] = behind[0] * grows[0] + behind[1] * grows[1] + behind[2] * grows[2]
    pieces = pixels // COLS
    for p in range(pieces):
        product(chunks - 1, buf_a, p)
    turn = chunks // per
    share = SEGS // turn

    def collect(m, seg):
        moved = moments[pl.ds(m * (SEGS * LANES) + seg, LANES, stride=SEGS), :].T
        stage[seg * per + m] = moved[:16]

    def half(n, ahead, buf, other, sums, last, seg):
        m = (n // turn + 1) % per
        spans = STEPS // SPAN
        for at in range(spans):
            for p in range(at * pieces // spans, (at + 1) * pieces // spans):
                product(ahead, other, p)
            if at == 1 or at == 3:
                reduced(n + 1, last, at == 3)
            block(n, spans - 1 - at, buf, sums)
        for q in range(share):
            collect(m, seg * share + q)

    def pair(h, _):
        n = chunks - 1 - 2 * h
        half(n, n - 1, buf_a, buf_b, sums_a, sums_b, n % turn)
        half(n - 1, jnp.maximum(n - 2, 0), buf_b, buf_a, sums_b, sums_a, n % turn - 1)
        return 0

    lax.fori_loop(0, chunks // 2, pair, 0)
    reduced(0, sums_b, False)
    reduced(0, sums_b, True)
    for seg in range(SEGS):
        collect(0, seg)


def deliver_kernel(slot, stage, *refs):
    reply = refs[-1]
    column = refs[0][...]
    for share in refs[1:-1]:
        column = column + share[...]
    for o in range(reply.shape[0]):
        reply[o, pl.ds(reply.shape[1] - 1, 1), :] = column[:1]
    for k in range(slot.shape[0]):
        s = slot[k]
        o = s // CAP
        c = s - o * CAP
        reply[o, pl.ds(pl.multiple_of(c * 8, 8), 8), :] = stage[k, :8, :]
        reply[o, pl.ds(CAP * 8 + c, 1), :] = stage[k, 8:9, :]


def gather_kernel(
    across, side, height, width, asked, got, gaussians, grads, loss, sums, zeros, pieces, wanted, sem
):
    owned = gaussians.shape[1]
    parts = owned // 8
    shares = got[:, got.shape[1] - 1, :]
    loss[0] = jnp.sum(shares[:, :1]) * (1.0 / (3.0 * height * width))
    zeros[...] = jnp.zeros_like(zeros)
    sums[...] = jnp.zeros_like(sums)
    for g in range(parts + 1):
        wanted[g] = 0
    for s in range(across * CAP):
        c, t = divmod(s, across)
        index = asked[t, 0, c]
        index = jnp.where(index >= 0, index, owned)
        wanted[index // 8] = 1
        row = pl.ds(index, 1)
        for f in range(9):
            at = c * 8 + f if f < 8 else CAP * 8 + c
            sums[f, row, :] = got[t, at : at + 1, :]
        sums[9, row, :] = jnp.full((1, LANES), t + 1.0, F32)

    def target(g):
        return grads.at[:, pl.ds(pl.multiple_of(g * 8, 8), 8), :]

    def blank(g, _):
        @pl.when(wanted[g] == 0)
        def _():
            pltpu.make_async_copy(zeros, target(g), sem.at[g]).start()

        return 0

    lax.fori_loop(0, parts, blank, 0)
    row_at = lax.axis_index("ty").astype(F32)
    shift_y = (0.5 * height - 0.5 * side - 0.5) - side * row_at

    def solve(g):
        rows = pl.ds(pl.multiple_of(g * 8, 8), 8)
        field = [gaussians[f, rows, :] for f in range(11)]
        tile = sums[9, rows, :]
        live = tile > 0.0
        shift_x = (0.5 * width - 0.5 * side - 0.5) - side * (tile - 1.0)

        def put(f, value):
            pieces[g, f] = jnp.where(live, value, 0.0)

        def shaped(x, y, z, log_scale, quat):
            xx, xy, yy, pos_u, pos_v = conic(x, y, z, log_scale, quat)
            return expanded(xx, xy, yy, pos_u + shift_x, pos_v + shift_y, jnp.zeros_like(x))

        _, pull = jax.vjp(shaped, *field[:3], field[3:6], field[6:10])
        moments = [LN2 * sums[f, rows, :] for f in range(6)]
        gx, gy, gz, gscale, gquat = pull(tuple(moments))
        basis, pull_basis = jax.vjp(directions, *field[:3])
        tints = [sums[6 + ch, rows, :] for ch in range(3)]
        tilts = []
        for m in range(16):
            tilt = None
            for ch in range(3):
                term = tints[ch] * gaussians[11 + 3 * m + ch, rows, :]
                tilt = term if tilt is None else tilt + term
                put(11 + 3 * m + ch, tints[ch] * basis[m])
            tilts.append(tilt)
        dx, dy, dz = pull_basis(tilts)
        put(0, gx + dx)
        put(1, gy + dy)
        put(2, gz + dz)
        for f in range(3):
            put(3 + f, gscale[f])
        for f in range(4):
            put(6 + f, gquat[f])
        put(10, moments[5] * (LOG2E / (1.0 + jnp.exp(field[10]))))
        pltpu.make_async_copy(pieces.at[g], target(g), sem.at[g]).start()

    def part(g, _):
        @pl.when(wanted[g] > 0)
        def _():
            solve(g)

        return 0

    lax.fori_loop(0, parts, part, 0)

    def finish(g, _):
        pltpu.make_async_copy(zeros, target(g), sem.at[g]).wait()
        return 0

    lax.fori_loop(0, parts, finish, 0)


def moment_columns(side):
    lane = np.arange(LANES)
    x = lane % side - side // 2
    t = lane // side - side // 2
    step = LANES // side
    one = np.ones_like(x)
    out = np.zeros((3 * LANES, LANES))
    out[:LANES, :6] = np.stack([x * x, x * t, t * t, x, t, one], axis=1)
    out[LANES : 2 * LANES, 1] = step * x
    out[LANES : 2 * LANES, 2] = 2 * step * t - step * step
    out[LANES : 2 * LANES, 4] = step
    quarter = LANES // 4
    for n, (column, weight) in enumerate(((6, 1), (8, 1), (7, 1), (2, 2 * step * step))):
        at = 2 * LANES + n * quarter
        out[at : at + quarter, column] = weight
    return out.astype(ml_dtypes.bfloat16)


def shifted(x, axis):
    size = lax.axis_size(axis)
    up = [(i, i + 1) for i in range(size - 1)]
    return lax.ppermute(x, axis, up), lax.ppermute(x, axis, [(j, i) for i, j in up])


def per_device(gaussians, tile_lists, tile_counts, depth_order, target):
    owned, fields, block = gaussians.shape
    lmax = tile_lists.shape[2]
    side = target.shape[1]
    pixels = side * side
    groups = pixels // LANES
    across = lax.axis_size("tx")
    down = lax.axis_size("ty")
    height = side * lax.axis_size("ty")
    width = side * across
    slots = across * CAP
    depth = -(-(CAP * 9 + 1) // 8) * 8
    f32 = functools.partial(jax.ShapeDtypeStruct, dtype=F32)
    i32 = functools.partial(jax.ShapeDtypeStruct, dtype=jnp.int32)
    reduce = jnp.asarray(moment_columns(side))

    fieldwise = jnp.transpose(gaussians, (1, 0, 2))
    request, slot = pl.pallas_call(
        functools.partial(request_kernel, owned, across),
        out_shape=(i32((across, 1, LANES)), i32((lmax,))),
        in_specs=[SMEM] * 3,
        out_specs=(SMEM, SMEM),
        scratch_shapes=[pltpu.SMEM((across,), jnp.int32)],
        name="request",
    )(tile_lists, tile_counts, depth_order)
    asked = lax.all_to_all(request, "tx", split_axis=0, concat_axis=0, tiled=True)
    projected = pl.pallas_call(
        functools.partial(project_kernel, 16),
        out_shape=f32((9, owned, block)),
        in_specs=[VMEM],
        out_specs=VMEM,
        compiler_params=PARAMS,
        name="project",
    )(fieldwise)
    send = pl.pallas_call(
        functools.partial(serve_kernel, across, side, float(height), float(width)),
        out_shape=f32((across, depth, block)),
        in_specs=[SMEM, VMEM],
        out_specs=VMEM,
        scratch_shapes=[pltpu.VMEM((9, slots, block), F32)],
        compiler_params=PARAMS,
        name="serve",
    )(asked, projected)
    recv = lax.all_to_all(send, "tx", split_axis=0, concat_axis=0, tiled=True)
    chunks = lmax * block // CHUNK
    wide = pixels + 3 * LANES
    table, alphas, checks, prefix, behind, dense = pl.pallas_call(
        functools.partial(forward_kernel, side),
        out_shape=(
            jax.ShapeDtypeStruct((lmax * block, LANES), BF16),
            f32((lmax * block, pixels)),
            f32((chunks * (STEPS // SPAN), SEGS, pixels)),
            f32((SEGS, pixels)),
            f32((3, SEGS, pixels)),
            f32((6 * groups, LANES)),
        ),
        in_specs=[SMEM, SMEM, VMEM, VMEM],
        out_specs=(VMEM,) * 6,
        scratch_shapes=[
            pltpu.VMEM((LANES, wide), BF16),
            pltpu.VMEM((lmax * block, LANES), F32),
            pltpu.VMEM((CHUNK, wide), F32),
            pltpu.VMEM((CHUNK, wide), F32),
            pltpu.VMEM((4, SEGS, pixels), F32),
        ],
        compiler_params=PARAMS,
        name="forward",
    )(slot, tile_counts, recv, target.reshape(3 * groups, LANES))
    left, right = shifted(dense, "tx")
    above, below = shifted(jnp.concatenate([left, dense, right], axis=0), "ty")
    slope, part = pl.pallas_call(
        functools.partial(score_entry, side, height, width),
        out_shape=(f32((3 * groups, LANES)), f32((8, LANES))),
        in_specs=[VMEM] * 5,
        out_specs=(VMEM, VMEM),
        compiler_params=PARAMS,
        name="score",
    )(above, left, dense, right, below)
    shares = [
        lax.ppermute(part, "ty", [(i, (i + k) % down) for i in range(down)]) for k in range(1, down)
    ]
    stage = pl.pallas_call(
        backward_kernel,
        out_shape=f32((lmax, 16, LANES)),
        in_specs=[VMEM] * 7,
        out_specs=VMEM,
        scratch_shapes=[
            pltpu.VMEM((LANES, pixels), BF16),
            pltpu.VMEM((LANES, pixels), F32),
            pltpu.VMEM((3, SEGS, pixels), F32),
            pltpu.VMEM((CHUNK, pixels), F32),
            pltpu.VMEM((CHUNK, pixels), F32),
            pltpu.VMEM((SEGS, pixels), F32),
            pltpu.VMEM((CHUNK, 3 * LANES), F32),
            pltpu.VMEM((CHUNK, 3 * LANES), F32),
            pltpu.VMEM((lmax * block + CHUNK, LANES), F32),
        ],
        compiler_params=PARAMS,
        name="backward",
    )(table, alphas, checks, prefix, behind, slope, reduce)
    reply = pl.pallas_call(
        deliver_kernel,
        out_shape=f32((across, depth, block)),
        in_specs=[SMEM] + [VMEM] * (1 + down),
        out_specs=VMEM,
        compiler_params=PARAMS,
        name="deliver",
    )(slot, stage, part, *shares)
    got = lax.all_to_all(reply, "tx", split_axis=0, concat_axis=0, tiled=True)
    grads, loss = pl.pallas_call(
        functools.partial(gather_kernel, across, side, float(height), float(width)),
        out_shape=(f32((fields, owned, block)), f32((1,))),
        in_specs=[SMEM, VMEM, VMEM],
        out_specs=(ANY, SMEM),
        scratch_shapes=[
            pltpu.VMEM((10, owned + 8, block), F32),
            pltpu.VMEM((fields, 8, block), F32),
            pltpu.VMEM((owned // 8, fields, 8, block), F32),
            pltpu.SMEM((owned // 8 + 1,), jnp.int32),
            pltpu.SemaphoreType.DMA((owned // 8,)),
        ],
        compiler_params=PARAMS,
        name="gather",
    )(asked, got, fieldwise)
    return (jnp.transpose(grads, (1, 0, 2)), loss[0])


def solution(mesh):
    return jax.shard_map(
        per_device,
        mesh=mesh,
        in_specs=(
            P(("ty", "tx"), None, None),
            P("ty", "tx", None),
            P("ty", "tx"),
            P(),
            P(None, "ty", "tx"),
        ),
        out_specs=(P(("ty", "tx"), None, None), P()),
        check_vma=False,
    )
```

```python
import functools

import jax
import jax.numpy as jnp
import ml_dtypes
import numpy as np
from jax import lax
from jax.experimental import pallas as pl
from jax.experimental.pallas import tpu as pltpu
from jax.sharding import PartitionSpec as P

CAP = 3
SEGS = 8
LANES = 128
CHUNK = 256
STEPS = CHUNK // SEGS
SPAN = 4
COLS = 256
RIM = 5
TAPS = 2 * RIM + 1
LOG2E = 1.4426950408889634
LN2 = 0.6931471805599453
DARK = -1e30

FOCAL = 1000.0
LOW_PASS = 0.3
STRUCT_WEIGHT = 0.2
LUMA_TERM = 0.0001
CONTRAST_TERM = 0.0009
ROBUST_TERM = 1e-06
HARMONIC_ZERO = 0.28209479177387814
HARMONIC_ONE = 0.4886025119029199
HARMONIC_TWO = (
    1.0925484305920792,
    -1.0925484305920792,
    0.31539156525252005,
    -1.0925484305920792,
    0.5462742152960396,
)
HARMONIC_THREE = (
    -0.5900435899266435,
    2.890611442640554,
    -0.4570457994644658,
    0.3731763325901154,
    -0.4570457994644658,
    1.445305721320277,
    -0.5900435899266435,
)

HIGH = lax.Precision.HIGHEST
F32 = jnp.float32
BF16 = jnp.bfloat16
ANY = pl.BlockSpec(memory_space=pl.ANY)
SMEM = pl.BlockSpec(memory_space=pltpu.SMEM)
VMEM = pl.BlockSpec(memory_space=pltpu.VMEM)
PARAMS = pltpu.CompilerParams(vmem_limit_bytes=24 * 1024 * 1024)


def harmonics(x, y, z):
    xx, yy, zz = x * x, y * y, z * z
    xy, yz, xz = x * y, y * z, x * z
    return [
        HARMONIC_ZERO * jnp.ones_like(x),
        -HARMONIC_ONE * y,
        HARMONIC_ONE * z,
        -HARMONIC_ONE * x,
        HARMONIC_TWO[0] * xy,
        HARMONIC_TWO[1] * yz,
        HARMONIC_TWO[2] * (2.0 * zz - xx - yy),
        HARMONIC_TWO[3] * xz,
        HARMONIC_TWO[4] * (xx - yy),
        HARMONIC_THREE[0] * y * (3.0 * xx - yy),
        HARMONIC_THREE[1] * xy * z,
        HARMONIC_THREE[2] * y * (4.0 * zz - xx - yy),
        HARMONIC_THREE[3] * z * (2.0 * zz - 3.0 * xx - 3.0 * yy),
        HARMONIC_THREE[4] * x * (4.0 * zz - xx - yy),
        HARMONIC_THREE[5] * z * (xx - yy),
        HARMONIC_THREE[6] * x * (xx - 3.0 * yy),
    ]


def directions(x, y, z):
    length = jnp.sqrt(x * x + y * y + z * z)
    return harmonics(x / length, y / length, z / length)


def conic(mean_x, mean_y, mean_z, log_scale, quat):
    scale = [jnp.exp(s) for s in log_scale]
    norm = jnp.sqrt(quat[0] * quat[0] + quat[1] * quat[1] + quat[2] * quat[2] + quat[3] * quat[3])
    w, i, j, k = (q / norm for q in quat)
    rotation = [
        [1.0 - 2.0 * (j * j + k * k), 2.0 * (i * j - w * k), 2.0 * (i * k + w * j)],
        [2.0 * (i * j + w * k), 1.0 - 2.0 * (i * i + k * k), 2.0 * (j * k - w * i)],
        [2.0 * (i * k - w * j), 2.0 * (j * k + w * i), 1.0 - 2.0 * (i * i + j * j)],
    ]
    scaled = [[rotation[r][c] * scale[c] for c in range(3)] for r in range(3)]

    def sigma(r, c):
        return scaled[r][0] * scaled[c][0] + scaled[r][1] * scaled[c][1] + scaled[r][2] * scaled[c][2]

    s00, s01, s02, s11, s12, s22 = (
        sigma(0, 0), sigma(0, 1), sigma(0, 2), sigma(1, 1), sigma(1, 2), sigma(2, 2),
    )
    inverse_z = 1.0 / mean_z
    diag = FOCAL * inverse_z
    jac_xz = -FOCAL * mean_x * inverse_z * inverse_z
    jac_yz = -FOCAL * mean_y * inverse_z * inverse_z
    u0, u1, u2 = diag * s00 + jac_xz * s02, diag * s01 + jac_xz * s12, diag * s02 + jac_xz * s22
    v1, v2 = diag * s11 + jac_yz * s12, diag * s12 + jac_yz * s22
    cov_uu = u0 * diag + u2 * jac_xz + LOW_PASS
    cov_uv = u1 * diag + u2 * jac_yz
    cov_vv = v1 * diag + v2 * jac_yz + LOW_PASS
    determinant = cov_uu * cov_vv - cov_uv * cov_uv
    half = -0.5 * LOG2E
    xx = half * (cov_vv / determinant)
    xy = (-2.0 * half) * (cov_uv / determinant)
    yy = half * (cov_uu / determinant)
    return xx, xy, yy, FOCAL * mean_x * inverse_z, FOCAL * mean_y * inverse_z


def expanded(xx, xy, yy, pos_u, pos_v, log_opacity):
    x1 = -2.0 * xx * pos_u - xy * pos_v
    y1 = -2.0 * yy * pos_v - xy * pos_u
    one = xx * pos_u * pos_u + xy * pos_u * pos_v + yy * pos_v * pos_v + log_opacity
    return xx, xy, yy, x1, y1, one


def tile_shifts(across, side, height, width):
    column = lax.broadcasted_iota(jnp.int32, (across, LANES), 0).astype(F32)
    column = jnp.concatenate([column] * CAP, axis=0)
    row = lax.axis_index("ty").astype(F32)
    shift_x = (0.5 * width - 0.5 * side - 0.5) - side * column
    shift_y = jnp.full(column.shape, (0.5 * height - 0.5 * side - 0.5) - side * row, F32)
    return shift_x, shift_y


def request_kernel(owned, across, lists, count, order, request, slot, seen):
    base = lax.axis_index("ty") * across
    for o in range(across):
        seen[o] = 0
        for c in range(CAP):
            request[o, 0, c] = -1
    used = count[0, 0]

    def entry(k, _):
        @pl.when(k < used)
        def _():
            block = order[lists[0, 0, k]]
            home = block // owned
            local = block - home * owned
            home = home - base
            at = seen[home]
            seen[home] = at + 1
            request[home, 0, at] = local
            slot[k] = home * CAP + at

        return 0

    lax.fori_loop(0, slot.shape[0], entry, 0, unroll=True)
    free = 0
    for o in range(across):
        free = jnp.where(seen[o] < CAP, o * CAP + CAP - 1, free)

    def rest(k, _):
        slot[k] = free
        return 0

    lax.fori_loop(used, slot.shape[0], rest, 0)


def project_kernel(span, gaussians, out):
    def part(n, _):
        rows = pl.ds(pl.multiple_of(n * span, span), span)
        field = [gaussians[f, rows, :] for f in range(11)]
        light = -LOG2E * jnp.log(1.0 + jnp.exp(-field[10])) + float(np.log2(0.99))
        values = list(conic(field[0], field[1], field[2], field[3:6], field[6:10]))
        values.append(jnp.maximum(light, DARK))
        basis = directions(field[0], field[1], field[2])
        for ch in range(3):
            color = 0.5 + basis[0] * gaussians[11 + ch, rows, :]
            for m in range(1, 16):
                color = color + basis[m] * gaussians[11 + 3 * m + ch, rows, :]
            values.append(color)
        for f in range(9):
            out[f, rows, :] = values[f]
        return 0

    lax.fori_loop(0, gaussians.shape[1] // span, part, 0)


def asked_index(asked, across, s):
    c = s // across
    return asked[s - c * across, 0, c]


def serve_kernel(across, side, height, width, asked, projected, send, chosen):
    def pick(s, _):
        index = jnp.maximum(asked_index(asked, across, s), 0)
        for f in range(9):
            chosen[f, pl.ds(s, 1), :] = projected[f, pl.ds(index, 1), :]
        return 0

    lax.fori_loop(0, across * CAP, pick, 0, unroll=True)
    shift_x, shift_y = tile_shifts(across, side, height, width)
    rows = list(
        expanded(
            chosen[0], chosen[1], chosen[2], chosen[3] + shift_x, chosen[4] + shift_y, chosen[5]
        )
    ) + [chosen[6], chosen[7], chosen[8]]
    for c in range(CAP):
        for f in range(9):
            at = c * 8 + f if f < 8 else CAP * 8 + c
            send[:, at, :] = rows[f][c * across : (c + 1) * across]


def monomials(side):
    pixels = side * side
    lane = lax.broadcasted_iota(jnp.int32, (8, pixels), 1)
    row = lax.broadcasted_iota(jnp.int32, (8, pixels), 0)
    x = ((lane & (side - 1)) - side // 2).astype(F32)
    y = ((lane >> (side.bit_length() - 1)) - side // 2).astype(F32)
    mono = jnp.zeros((8, pixels), F32)
    for at, value in enumerate((x * x, x * y, y * y, x, y, jnp.ones_like(x))):
        mono = jnp.where(row == at, value, mono)
    blank = jnp.zeros((8, pixels), F32)
    rest = jnp.zeros((LANES - 48, pixels), F32)
    return jnp.concatenate([mono, blank] * 3 + [rest], axis=0).astype(BF16)


def spreaders():
    row = lax.broadcasted_iota(jnp.int32, (LANES, LANES), 0)
    return jnp.concatenate(
        [jnp.where((row == 6 + c) | (row == 22 + c), 1.0, 0.0).astype(F32) for c in range(3)], axis=1
    ).astype(BF16)


def repeated(x, times):
    return jnp.concatenate([x] * times, axis=1)


def forward_kernel(
    side, slot, count, recv, target, table, alphas, checks, prefix, behind, dense,
    planes, spread, buf_a, buf_b, ends,
):
    lmax = slot.shape[0]
    per = lmax // SEGS
    pixels = prefix.shape[1]
    groups = pixels // LANES
    planes[:, :pixels] = monomials(side)
    planes[:, pixels:] = spreaders()
    zero_rows = jnp.zeros((7, LANES), F32)
    dead = jnp.where(lax.broadcasted_iota(jnp.int32, (16, LANES), 0) == 5, DARK, 0.0)
    is_color = lax.broadcasted_iota(jnp.int32, (16, LANES), 0) >= 6
    filler = jnp.zeros((LANES - 48, LANES), F32)

    def place(m, seg):
        s = slot[seg * per + m]
        live = seg * per + m < count[0, 0]
        o = s // CAP
        c = s - o * CAP
        head = recv[o, pl.ds(pl.multiple_of(c * 8, 8), 8), :]
        tail = recv[o, pl.ds(CAP * 8 + c, 1), :]
        rows = jnp.concatenate([head, tail, zero_rows], axis=0)
        rows = jnp.where(live, rows, dead)
        hi = rows.astype(BF16).astype(F32)
        rest = rows - hi
        mid = rest.astype(BF16).astype(F32)
        low = (rest - mid).astype(BF16).astype(F32)
        third = jnp.where(is_color, hi, low)
        stacked = jnp.concatenate([hi, mid, third, filler], axis=0)
        spread[pl.ds(m * (SEGS * LANES) + seg, LANES, stride=SEGS), :] = stacked.T

    for seg in range(SEGS):
        place(0, seg)

    width = planes.shape[1]
    pieces = -(-width // COLS)

    def product(n, buf, p):
        rows = pl.ds(pl.multiple_of(n * CHUNK, CHUNK), CHUNK)
        if p == 0:
            table[rows, :] = spread[rows, :].astype(BF16)
        cols = slice(p * COLS, min((p + 1) * COLS, width))
        buf[:, cols] = jnp.dot(table[rows, :], planes[:, cols], preferred_element_type=F32)

    def blend(n, b, buf, carry):
        light, red, green, blue = carry
        spans = STEPS // SPAN
        own = alphas.at[pl.ds(pl.multiple_of(n * CHUNK, CHUNK), CHUNK)]
        lights = checks.at[pl.ds(n * spans, spans)]
        lights[b] = light
        for i in range(b * SPAN, (b + 1) * SPAN):
            rows = pl.ds(i * SEGS, SEGS)
            alpha = jnp.exp2(buf[rows, :pixels])
            own[rows, :] = alpha
            weight = light * alpha
            light = light - weight
            red = red + weight * repeated(buf[rows, pixels : pixels + LANES], groups)
            green = green + weight * repeated(buf[rows, pixels + LANES : pixels + 2 * LANES], groups)
            blue = blue + weight * repeated(
                buf[rows, pixels + 2 * LANES : pixels + 3 * LANES], groups
            )
        return light, red, green, blue

    for p in range(pieces):
        product(0, buf_a, p)
    chunks = lmax * LANES // CHUNK
    turn = chunks // per
    share = SEGS // turn

    def pair(h, carry):
        n = 2 * h
        m = (n // turn + 1) % per
        for b in range(STEPS // SPAN):
            if b < pieces:
                product(n + 1, buf_b, b)
            if b % 2 == 0 and b // 2 < 2 * share:
                place(m, (n % turn) * share + b // 2)
            carry = blend(n, b, buf_a, carry)
        for b in range(STEPS // SPAN):
            if b < pieces:
                product(jnp.minimum(n + 2, chunks - 1), buf_a, b)
            carry = blend(n + 1, b, buf_b, carry)
        return carry

    start = (jnp.ones((SEGS, pixels), F32),) + (jnp.zeros((SEGS, pixels), F32),) * 3
    carry = lax.fori_loop(0, chunks // 2, pair, start)
    for f in range(4):
        ends[f] = carry[f]
    ahead = jnp.ones((1, pixels), F32)
    for seg in range(SEGS):
        prefix[pl.ds(seg, 1), :] = ahead
        ahead = ahead * ends[0, pl.ds(seg, 1), :]
    for ch in range(3):
        seen = jnp.zeros((1, pixels), F32)
        for seg in reversed(range(SEGS)):
            behind[ch, pl.ds(seg, 1), :] = seen
            seen = ends[1 + ch, pl.ds(seg, 1), :] + ends[0, pl.ds(seg, 1), :] * seen
        for j in range(groups):
            dense[pl.ds(ch * groups + j, 1), :] = seen[:, j * LANES : (j + 1) * LANES]
    dense[3 * groups :, :] = target[...]


def similarity(mean_a, mean_b, square_a, square_b, cross):
    var_a = square_a - mean_a * mean_a
    var_b = square_b - mean_b * mean_b
    covar = cross - mean_a * mean_b
    top = (2.0 * mean_a * mean_b + LUMA_TERM) * (2.0 * covar + CONTRAST_TERM)
    bottom = (mean_a * mean_a + mean_b * mean_b + LUMA_TERM) * (var_a + var_b + CONTRAST_TERM)
    return top / bottom


def tap(distance):
    weights = [float(np.exp(-((k - RIM) ** 2) / 4.5)) for k in range(TAPS)]
    value = jnp.exp(distance * distance * (-1.0 / 4.5)) * (1.0 / sum(weights))
    return jnp.where(jnp.abs(distance) <= RIM, value, 0.0)


def places(shape, dim):
    return lax.broadcasted_iota(jnp.int32, shape, dim)


def bands(side, padded):
    fold = LANES // side
    groups = side // fold
    reach = side + 2 * RIM
    shape = (3 * side, LANES)
    out = places(shape, 1)
    along = tap((places(shape, 0) - side - out + RIM).astype(F32))
    along = jnp.where(out < reach, along, 0.0)
    blank = jnp.zeros((side, LANES), F32)
    fa = jnp.concatenate(
        [
            jnp.concatenate(
                [along[h * side : (h + 1) * side] if u == t else blank for u in range(fold)], axis=1
            )
            for h in range(3)
            for t in range(fold)
        ],
        axis=0,
    )
    block = 3 * groups
    shape = (padded, fold * block)
    out, at = places(shape, 0), places(shape, 1)
    t = jnp.zeros(shape, jnp.int32)
    for k in range(1, fold):
        t = t + jnp.where(at >= k * block, 1, 0)
    source = (at - t * block) * fold + t - side
    fb = jnp.where(out < reach, tap((source - out + RIM).astype(F32)), 0.0)
    shape = (fold * groups, padded)
    row, out = places(shape, 0), places(shape, 1)
    t = jnp.zeros(shape, jnp.int32)
    for k in range(1, fold):
        t = t + jnp.where(row >= k * groups, 1, 0)
    source = (row - t * groups) * fold + t
    fc = jnp.where(out < reach, tap((out - RIM - source).astype(F32)), 0.0)
    shape = (LANES, LANES)
    out, at = places(shape, 0), places(shape, 1)
    back = tap((out - RIM - (at & (side - 1))).astype(F32))
    back = jnp.where(out < reach, back, 0.0)
    fd = jnp.concatenate(
        [jnp.where((at >= t * side) & (at < (t + 1) * side), back, 0.0) for t in range(fold)], axis=0
    )
    return fa, fb, fc, fd


def score_kernel(side, height, width, near, slope, loss):
    fa, fb, fc, fd = bands(side, -(-(side + 2 * RIM) // 8) * 8)
    rows3 = near[4].shape[0] // 2
    groups = rows3 // 3
    fold = LANES // side
    fields = [[], [], [], [], []]
    for v in range(3):
        strip = jnp.concatenate([near[3 * v + h] for h in range(3)], axis=1)
        image, target = strip[:rows3], strip[rows3:]
        for f, plane in enumerate([image, target, image * image, target * target, image * target]):
            fields[f].append(plane)
    stack = jnp.concatenate([fields[f][v] for f in range(5) for v in range(3)], axis=0)
    wide = jnp.dot(stack, fa, precision=HIGH, preferred_element_type=F32)
    columns = []
    for f in range(5):
        for ch in range(3):
            parts = []
            for t in range(fold):
                for v in range(3):
                    at = (f * 3 + v) * rows3 + ch * groups
                    parts.append(wide[at : at + groups, t * LANES : (t + 1) * LANES])
            columns.append(jnp.concatenate(parts, axis=0))
    tall = jnp.concatenate(columns, axis=1)
    maps = jnp.dot(fb, tall, precision=HIGH, preferred_element_type=F32)
    span = 3 * LANES
    score, pull = jax.vjp(similarity, *[maps[:, f * span : (f + 1) * span] for f in range(5)])
    parts = pull(jnp.full(score.shape, -STRUCT_WEIGHT, F32))
    row = lax.broadcasted_iota(jnp.int32, score.shape, 0)
    col = lax.broadcasted_iota(jnp.int32, (score.shape[0], LANES), 1)
    col = jnp.concatenate([col] * 3, axis=1)
    row_at = row - RIM + lax.axis_index("ty") * side
    col_at = col - RIM + lax.axis_index("tx") * side
    reach = side + 2 * RIM
    inside = (
        (row_at >= 0) & (row_at < height) & (col_at >= 0) & (col_at < width)
        & (row < reach) & (col < reach)
    )
    own = (row >= RIM) & (row < RIM + side) & (col >= RIM) & (col < RIM + side)
    coeffs = jnp.concatenate(
        [jnp.where(inside, parts[f], 0.0) for f in (0, 2, 4)], axis=1
    )
    low = jnp.dot(fc, coeffs, precision=HIGH, preferred_element_type=F32)
    rows = []
    for n in range(9):
        rows.append(
            jnp.concatenate(
                [
                    low[t * groups : (t + 1) * groups, n * LANES : (n + 1) * LANES]
                    for t in range(fold)
                ],
                axis=1,
            )
        )
    smooth = jnp.dot(
        jnp.concatenate(rows, axis=0), fd, precision=HIGH, preferred_element_type=F32
    )
    image, target = near[4][:rows3, :], near[4][rows3:, :]
    gap = image - target
    robust = jnp.sqrt(gap * gap + ROBUST_TERM)
    slope[...] = (
        smooth[:rows3]
        + 2.0 * image * smooth[rows3 : 2 * rows3]
        + target * smooth[2 * rows3 :]
        + (1.0 - STRUCT_WEIGHT) * gap / robust
    )
    total = (1.0 - STRUCT_WEIGHT) * jnp.sum(robust) + STRUCT_WEIGHT * jnp.sum(
        jnp.where(own, 1.0 - score, 0.0)
    )
    loss[...] = jnp.full(loss.shape, total, F32)


def score_entry(side, height, width, *refs):
    above, left, own, right, below = refs[:5]
    rows = own.shape[0]
    near = [above[h * rows : (h + 1) * rows, :] for h in range(3)]
    near += [left[...], own[...], right[...]]
    near += [below[h * rows : (h + 1) * rows, :] for h in range(3)]
    score_kernel(side, height, width, near, *refs[5:])


def backward_kernel(
    table, alphas, checks, prefix, behind, slope, reduce, stage,
    rhs, wide, grows, buf_a, buf_b, behinds, sums_a, sums_b, moments,
):
    lmax = stage.shape[0]
    per = lmax // SEGS
    pixels = prefix.shape[1]
    groups = pixels // LANES
    chunks = lmax * LANES // CHUNK
    wide[...] = jnp.zeros_like(wide)
    for ch in range(3):
        for j in range(groups):
            lanes = pl.ds(j * LANES, LANES)
            wide[pl.ds(6 + ch, 1), lanes] = slope[pl.ds(ch * groups + j, 1), :]
    for ch in range(3):
        row = wide[pl.ds(6 + ch, 1), :]
        hi = row.astype(BF16).astype(F32)
        grows[ch] = jnp.broadcast_to(row, (SEGS, pixels))
        wide[pl.ds(6 + ch, 1), :] = hi
        wide[pl.ds(22 + ch, 1), :] = hi
        wide[pl.ds(38 + ch, 1), :] = row - hi
    rhs[...] = wide[...].astype(BF16)

    def product(n, buf, p):
        rows = pl.ds(pl.multiple_of(n * CHUNK, CHUNK), CHUNK)
        cols = slice(p * COLS, (p + 1) * COLS)
        buf[:, cols] = jnp.dot(table[rows, :], rhs[:, cols], preferred_element_type=F32)

    def reduced(n, sums, low):
        rows = pl.ds(pl.multiple_of(n * CHUNK, CHUNK), CHUNK)
        part = sums[...].astype(BF16)
        if low:
            part = (sums[...] - part.astype(F32)).astype(BF16)
        value = jnp.dot(part, reduce[...], preferred_element_type=F32)
        moments[rows, :] = moments[rows, :] + value if low else value

    lane = lax.broadcasted_iota(jnp.int32, (SEGS, LANES), 1)
    front = lane < LANES // 2
    even = (lane & (LANES // 4)) == 0

    def folded(a, b):
        return jnp.where(front, a, b) + pltpu.roll(jnp.where(front, b, a), LANES // 2, 1)

    def packed(a, b, c, d):
        ab, cd = folded(a, b), folded(c, d)
        ab = ab + pltpu.roll(ab, LANES - LANES // 4, 1)
        cd = cd + pltpu.roll(cd, LANES // 4, 1)
        return jnp.where(even, ab, cd)

    def block(n, b, buf, sums):
        first = b * SPAN * SEGS
        spans = STEPS // SPAN
        own = alphas.at[pl.ds(pl.multiple_of(n * CHUNK, CHUNK), CHUNK)]
        lights = checks.at[pl.ds(n * spans, spans)]
        rows = [pl.ds(first + i * SEGS, SEGS) for i in range(SPAN)]
        totals = [[None] * 6 for _ in range(SPAN)]

        def add(i, f, value):
            totals[i][f] = value if totals[i][f] is None else totals[i][f] + value

        for q in reversed(range(groups // 2)):
            lanes = slice(q * 2 * LANES, (q + 1) * 2 * LANES)
            light = lights[b, :, lanes] * prefix[:, lanes]
            tints = [grows[ch, :, lanes] for ch in range(3)]
            kept, weights = [], []
            for i in range(SPAN):
                kept.append(own[rows[i], lanes])
                weights.append(light * kept[i])
                light = light - weights[i]
            back = behinds[:, lanes]
            for i in reversed(range(SPAN)):
                gap = buf[rows[i], lanes] - back
                back = back + kept[i] * gap
                pull = weights[i] * gap
                add(i, 0, pull[:, LANES:])
                add(i, 1, totals[i][0])
                add(i, 2, totals[i][1])
                add(i, 0, pull[:, :LANES])
                if q > 0:
                    add(i, 1, totals[i][0])
                    add(i, 2, totals[i][1])
                for ch in range(3):
                    tint = weights[i] * tints[ch]
                    add(i, 3 + ch, tint[:, LANES:] + tint[:, :LANES])
            behinds[:, lanes] = back
        for i in range(SPAN):
            zero, one, two, red, green, blue = totals[i]
            sums[rows[i], 0:LANES] = zero
            sums[rows[i], LANES : 2 * LANES] = one
            sums[rows[i], 2 * LANES : 3 * LANES] = packed(red, green, blue, two)

    behinds[...] = behind[0] * grows[0] + behind[1] * grows[1] + behind[2] * grows[2]
    pieces = pixels // COLS
    for p in range(pieces):
        product(chunks - 1, buf_a, p)
    turn = chunks // per
    share = SEGS // turn

    def collect(m, seg):
        moved = moments[pl.ds(m * (SEGS * LANES) + seg, LANES, stride=SEGS), :].T
        stage[seg * per + m] = moved[:16]

    def half(n, ahead, buf, other, sums, last, seg):
        m = (n // turn + 1) % per
        spans = STEPS // SPAN
        for at in range(spans):
            for p in range(at * pieces // spans, (at + 1) * pieces // spans):
                product(ahead, other, p)
            if at == 1 or at == 3:
                reduced(n + 1, last, at == 3)
            block(n, spans - 1 - at, buf, sums)
        for q in range(share):
            collect(m, seg * share + q)

    def pair(h, _):
        n = chunks - 1 - 2 * h
        half(n, n - 1, buf_a, buf_b, sums_a, sums_b, n % turn)
        half(n - 1, jnp.maximum(n - 2, 0), buf_b, buf_a, sums_b, sums_a, n % turn - 1)
        return 0

    lax.fori_loop(0, chunks // 2, pair, 0)
    reduced(0, sums_b, False)
    reduced(0, sums_b, True)
    for seg in range(SEGS):
        collect(0, seg)


def deliver_kernel(slot, stage, *refs):
    reply = refs[-1]
    column = refs[0][...]
    for share in refs[1:-1]:
        column = column + share[...]
    for o in range(reply.shape[0]):
        reply[o, pl.ds(reply.shape[1] - 1, 1), :] = column[:1]
    for k in range(slot.shape[0]):
        s = slot[k]
        o = s // CAP
        c = s - o * CAP
        reply[o, pl.ds(pl.multiple_of(c * 8, 8), 8), :] = stage[k, :8, :]
        reply[o, pl.ds(CAP * 8 + c, 1), :] = stage[k, 8:9, :]


def gather_kernel(
    across, side, height, width, asked, got, gaussians, grads, loss, sums, zeros, pieces, wanted, sem
):
    owned = gaussians.shape[1]
    parts = owned // 8
    shares = got[:, got.shape[1] - 1, :]
    loss[0] = jnp.sum(shares[:, :1]) * (1.0 / (3.0 * height * width))
    zeros[...] = jnp.zeros_like(zeros)
    sums[...] = jnp.zeros_like(sums)
    for g in range(parts + 1):
        wanted[g] = 0
    for s in range(across * CAP):
        c, t = divmod(s, across)
        index = asked[t, 0, c]
        index = jnp.where(index >= 0, index, owned)
        wanted[index // 8] = 1
        row = pl.ds(index, 1)
        for f in range(9):
            at = c * 8 + f if f < 8 else CAP * 8 + c
            sums[f, row, :] = got[t, at : at + 1, :]
        sums[9, row, :] = jnp.full((1, LANES), t + 1.0, F32)

    def target(g):
        return grads.at[:, pl.ds(pl.multiple_of(g * 8, 8), 8), :]

    def blank(g, _):
        @pl.when(wanted[g] == 0)
        def _():
            pltpu.make_async_copy(zeros, target(g), sem.at[g]).start()

        return 0

    lax.fori_loop(0, parts, blank, 0)
    row_at = lax.axis_index("ty").astype(F32)
    shift_y = (0.5 * height - 0.5 * side - 0.5) - side * row_at

    def solve(g):
        rows = pl.ds(pl.multiple_of(g * 8, 8), 8)
        field = [gaussians[f, rows, :] for f in range(11)]
        tile = sums[9, rows, :]
        live = tile > 0.0
        shift_x = (0.5 * width - 0.5 * side - 0.5) - side * (tile - 1.0)

        def put(f, value):
            pieces[g, f] = jnp.where(live, value, 0.0)

        def shaped(x, y, z, log_scale, quat):
            xx, xy, yy, pos_u, pos_v = conic(x, y, z, log_scale, quat)
            return expanded(xx, xy, yy, pos_u + shift_x, pos_v + shift_y, jnp.zeros_like(x))

        _, pull = jax.vjp(shaped, *field[:3], field[3:6], field[6:10])
        moments = [LN2 * sums[f, rows, :] for f in range(6)]
        gx, gy, gz, gscale, gquat = pull(tuple(moments))
        basis, pull_basis = jax.vjp(directions, *field[:3])
        tints = [sums[6 + ch, rows, :] for ch in range(3)]
        tilts = []
        for m in range(16):
            tilt = None
            for ch in range(3):
                term = tints[ch] * gaussians[11 + 3 * m + ch, rows, :]
                tilt = term if tilt is None else tilt + term
                put(11 + 3 * m + ch, tints[ch] * basis[m])
            tilts.append(tilt)
        dx, dy, dz = pull_basis(tilts)
        put(0, gx + dx)
        put(1, gy + dy)
        put(2, gz + dz)
        for f in range(3):
            put(3 + f, gscale[f])
        for f in range(4):
            put(6 + f, gquat[f])
        put(10, moments[5] * (LOG2E / (1.0 + jnp.exp(field[10]))))
        pltpu.make_async_copy(pieces.at[g], target(g), sem.at[g]).start()

    def part(g, _):
        @pl.when(wanted[g] > 0)
        def _():
            solve(g)

        return 0

    lax.fori_loop(0, parts, part, 0)

    def finish(g, _):
        pltpu.make_async_copy(zeros, target(g), sem.at[g]).wait()
        return 0

    lax.fori_loop(0, parts, finish, 0)


def moment_columns(side):
    lane = np.arange(LANES)
    x = lane % side - side // 2
    t = lane // side - side // 2
    step = LANES // side
    one = np.ones_like(x)
    out = np.zeros((3 * LANES, LANES))
    out[:LANES, :6] = np.stack([x * x, x * t, t * t, x, t, one], axis=1)
    out[LANES : 2 * LANES, 1] = step * x
    out[LANES : 2 * LANES, 2] = 2 * step * t - step * step
    out[LANES : 2 * LANES, 4] = step
    quarter = LANES // 4
    for n, (column, weight) in enumerate(((6, 1), (8, 1), (7, 1), (2, 2 * step * step))):
        at = 2 * LANES + n * quarter
        out[at : at + quarter, column] = weight
    return out.astype(ml_dtypes.bfloat16)


def shifted(x, axis):
    size = lax.axis_size(axis)
    up = [(i, i + 1) for i in range(size - 1)]
    return lax.ppermute(x, axis, up), lax.ppermute(x, axis, [(j, i) for i, j in up])


def per_device(gaussians, tile_lists, tile_counts, depth_order, target):
    owned, fields, block = gaussians.shape
    lmax = tile_lists.shape[2]
    side = target.shape[1]
    pixels = side * side
    groups = pixels // LANES
    across = lax.axis_size("tx")
    down = lax.axis_size("ty")
    height = side * lax.axis_size("ty")
    width = side * across
    slots = across * CAP
    depth = -(-(CAP * 9 + 1) // 8) * 8
    f32 = functools.partial(jax.ShapeDtypeStruct, dtype=F32)
    i32 = functools.partial(jax.ShapeDtypeStruct, dtype=jnp.int32)
    reduce = jnp.asarray(moment_columns(side))

    fieldwise = jnp.transpose(gaussians, (1, 0, 2))
    request, slot = pl.pallas_call(
        functools.partial(request_kernel, owned, across),
        out_shape=(i32((across, 1, LANES)), i32((lmax,))),
        in_specs=[SMEM] * 3,
        out_specs=(SMEM, SMEM),
        scratch_shapes=[pltpu.SMEM((across,), jnp.int32)],
        name="request",
    )(tile_lists, tile_counts, depth_order)
    asked = lax.all_to_all(request, "tx", split_axis=0, concat_axis=0, tiled=True)
    projected = pl.pallas_call(
        functools.partial(project_kernel, 16),
        out_shape=f32((9, owned, block)),
        in_specs=[VMEM],
        out_specs=VMEM,
        compiler_params=PARAMS,
        name="project",
    )(fieldwise)
    send = pl.pallas_call(
        functools.partial(serve_kernel, across, side, float(height), float(width)),
        out_shape=f32((across, depth, block)),
        in_specs=[SMEM, VMEM],
        out_specs=VMEM,
        scratch_shapes=[pltpu.VMEM((9, slots, block), F32)],
        compiler_params=PARAMS,
        name="serve",
    )(asked, projected)
    recv = lax.all_to_all(send, "tx", split_axis=0, concat_axis=0, tiled=True)
    chunks = lmax * block // CHUNK
    wide = pixels + 3 * LANES
    table, alphas, checks, prefix, behind, dense = pl.pallas_call(
        functools.partial(forward_kernel, side),
        out_shape=(
            jax.ShapeDtypeStruct((lmax * block, LANES), BF16),
            f32((lmax * block, pixels)),
            f32((chunks * (STEPS // SPAN), SEGS, pixels)),
            f32((SEGS, pixels)),
            f32((3, SEGS, pixels)),
            f32((6 * groups, LANES)),
        ),
        in_specs=[SMEM, SMEM, VMEM, VMEM],
        out_specs=(VMEM,) * 6,
        scratch_shapes=[
            pltpu.VMEM((LANES, wide), BF16),
            pltpu.VMEM((lmax * block, LANES), F32),
            pltpu.VMEM((CHUNK, wide), F32),
            pltpu.VMEM((CHUNK, wide), F32),
            pltpu.VMEM((4, SEGS, pixels), F32),
        ],
        compiler_params=PARAMS,
        name="forward",
    )(slot, tile_counts, recv, target.reshape(3 * groups, LANES))
    left, right = shifted(dense, "tx")
    above, below = shifted(jnp.concatenate([left, dense, right], axis=0), "ty")
    slope, part = pl.pallas_call(
        functools.partial(score_entry, side, height, width),
        out_shape=(f32((3 * groups, LANES)), f32((8, LANES))),
        in_specs=[VMEM] * 5,
        out_specs=(VMEM, VMEM),
        compiler_params=PARAMS,
        name="score",
    )(above, left, dense, right, below)
    shares = [
        lax.ppermute(part, "ty", [(i, (i + k) % down) for i in range(down)]) for k in range(1, down)
    ]
    stage = pl.pallas_call(
        backward_kernel,
        out_shape=f32((lmax, 16, LANES)),
        in_specs=[VMEM] * 7,
        out_specs=VMEM,
        scratch_shapes=[
            pltpu.VMEM((LANES, pixels), BF16),
            pltpu.VMEM((LANES, pixels), F32),
            pltpu.VMEM((3, SEGS, pixels), F32),
            pltpu.VMEM((CHUNK, pixels), F32),
            pltpu.VMEM((CHUNK, pixels), F32),
            pltpu.VMEM((SEGS, pixels), F32),
            pltpu.VMEM((CHUNK, 3 * LANES), F32),
            pltpu.VMEM((CHUNK, 3 * LANES), F32),
            pltpu.VMEM((lmax * block + CHUNK, LANES), F32),
        ],
        compiler_params=PARAMS,
        name="backward",
    )(table, alphas, checks, prefix, behind, slope, reduce)
    reply = pl.pallas_call(
        deliver_kernel,
        out_shape=f32((across, depth, block)),
        in_specs=[SMEM] + [VMEM] * (1 + down),
        out_specs=VMEM,
        compiler_params=PARAMS,
        name="deliver",
    )(slot, stage, part, *shares)
    got = lax.all_to_all(reply, "tx", split_axis=0, concat_axis=0, tiled=True)
    grads, loss = pl.pallas_call(
        functools.partial(gather_kernel, across, side, float(height), float(width)),
        out_shape=(f32((fields, owned, block)), f32((1,))),
        in_specs=[SMEM, VMEM, VMEM],
        out_specs=(ANY, SMEM),
        scratch_shapes=[
            pltpu.VMEM((10, owned + 8, block), F32),
            pltpu.VMEM((fields, 8, block), F32),
            pltpu.VMEM((owned // 8, fields, 8, block), F32),
            pltpu.SMEM((owned // 8 + 1,), jnp.int32),
            pltpu.SemaphoreType.DMA((owned // 8,)),
        ],
        compiler_params=PARAMS,
        name="gather",
    )(asked, got, fieldwise)
    return (jnp.transpose(grads, (1, 0, 2)), loss[0])


def solution(mesh):
    return jax.shard_map(
        per_device,
        mesh=mesh,
        in_specs=(
            P(("ty", "tx"), None, None),
            P("ty", "tx", None),
            P("ty", "tx"),
            P(),
            P(None, "ty", "tx"),
        ),
        out_specs=(P(("ty", "tx"), None, None), P()),
        check_vma=False,
    )
```

```python
import functools

import jax
import jax.numpy as jnp
import ml_dtypes
import numpy as np
from jax import lax
from jax.experimental import pallas as pl
from jax.experimental.pallas import tpu as pltpu
from jax.sharding import PartitionSpec as P

CAP = 3
SEGS = 8
LANES = 128
CHUNK = 256
STEPS = CHUNK // SEGS
SPAN = 4
COLS = 256
RIM = 5
TAPS = 2 * RIM + 1
LOG2E = 1.4426950408889634
LN2 = 0.6931471805599453
DARK = -1e30

FOCAL = 1000.0
LOW_PASS = 0.3
STRUCT_WEIGHT = 0.2
LUMA_TERM = 0.0001
CONTRAST_TERM = 0.0009
ROBUST_TERM = 1e-06
HARMONIC_ZERO = 0.28209479177387814
HARMONIC_ONE = 0.4886025119029199
HARMONIC_TWO = (
    1.0925484305920792,
    -1.0925484305920792,
    0.31539156525252005,
    -1.0925484305920792,
    0.5462742152960396,
)
HARMONIC_THREE = (
    -0.5900435899266435,
    2.890611442640554,
    -0.4570457994644658,
    0.3731763325901154,
    -0.4570457994644658,
    1.445305721320277,
    -0.5900435899266435,
)

HIGH = lax.Precision.HIGHEST
F32 = jnp.float32
BF16 = jnp.bfloat16
ANY = pl.BlockSpec(memory_space=pl.ANY)
SMEM = pl.BlockSpec(memory_space=pltpu.SMEM)
VMEM = pl.BlockSpec(memory_space=pltpu.VMEM)
PARAMS = pltpu.CompilerParams(vmem_limit_bytes=24 * 1024 * 1024)


def harmonics(x, y, z):
    xx, yy, zz = x * x, y * y, z * z
    xy, yz, xz = x * y, y * z, x * z
    return [
        HARMONIC_ZERO * jnp.ones_like(x),
        -HARMONIC_ONE * y,
        HARMONIC_ONE * z,
        -HARMONIC_ONE * x,
        HARMONIC_TWO[0] * xy,
        HARMONIC_TWO[1] * yz,
        HARMONIC_TWO[2] * (2.0 * zz - xx - yy),
        HARMONIC_TWO[3] * xz,
        HARMONIC_TWO[4] * (xx - yy),
        HARMONIC_THREE[0] * y * (3.0 * xx - yy),
        HARMONIC_THREE[1] * xy * z,
        HARMONIC_THREE[2] * y * (4.0 * zz - xx - yy),
        HARMONIC_THREE[3] * z * (2.0 * zz - 3.0 * xx - 3.0 * yy),
        HARMONIC_THREE[4] * x * (4.0 * zz - xx - yy),
        HARMONIC_THREE[5] * z * (xx - yy),
        HARMONIC_THREE[6] * x * (xx - 3.0 * yy),
    ]


def directions(x, y, z):
    length = jnp.sqrt(x * x + y * y + z * z)
    return harmonics(x / length, y / length, z / length)


def conic(mean_x, mean_y, mean_z, log_scale, quat):
    scale = [jnp.exp(s) for s in log_scale]
    norm = jnp.sqrt(quat[0] * quat[0] + quat[1] * quat[1] + quat[2] * quat[2] + quat[3] * quat[3])
    w, i, j, k = (q / norm for q in quat)
    rotation = [
        [1.0 - 2.0 * (j * j + k * k), 2.0 * (i * j - w * k), 2.0 * (i * k + w * j)],
        [2.0 * (i * j + w * k), 1.0 - 2.0 * (i * i + k * k), 2.0 * (j * k - w * i)],
        [2.0 * (i * k - w * j), 2.0 * (j * k + w * i), 1.0 - 2.0 * (i * i + j * j)],
    ]
    scaled = [[rotation[r][c] * scale[c] for c in range(3)] for r in range(3)]

    def sigma(r, c):
        return scaled[r][0] * scaled[c][0] + scaled[r][1] * scaled[c][1] + scaled[r][2] * scaled[c][2]

    s00, s01, s02, s11, s12, s22 = (
        sigma(0, 0), sigma(0, 1), sigma(0, 2), sigma(1, 1), sigma(1, 2), sigma(2, 2),
    )
    inverse_z = 1.0 / mean_z
    diag = FOCAL * inverse_z
    jac_xz = -FOCAL * mean_x * inverse_z * inverse_z
    jac_yz = -FOCAL * mean_y * inverse_z * inverse_z
    u0, u1, u2 = diag * s00 + jac_xz * s02, diag * s01 + jac_xz * s12, diag * s02 + jac_xz * s22
    v1, v2 = diag * s11 + jac_yz * s12, diag * s12 + jac_yz * s22
    cov_uu = u0 * diag + u2 * jac_xz + LOW_PASS
    cov_uv = u1 * diag + u2 * jac_yz
    cov_vv = v1 * diag + v2 * jac_yz + LOW_PASS
    determinant = cov_uu * cov_vv - cov_uv * cov_uv
    half = -0.5 * LOG2E
    xx = half * (cov_vv / determinant)
    xy = (-2.0 * half) * (cov_uv / determinant)
    yy = half * (cov_uu / determinant)
    return xx, xy, yy, FOCAL * mean_x * inverse_z, FOCAL * mean_y * inverse_z


def expanded(xx, xy, yy, pos_u, pos_v, log_opacity):
    x1 = -2.0 * xx * pos_u - xy * pos_v
    y1 = -2.0 * yy * pos_v - xy * pos_u
    one = xx * pos_u * pos_u + xy * pos_u * pos_v + yy * pos_v * pos_v + log_opacity
    return xx, xy, yy, x1, y1, one


def tile_shifts(across, side, height, width):
    column = lax.broadcasted_iota(jnp.int32, (across, LANES), 0).astype(F32)
    column = jnp.concatenate([column] * CAP, axis=0)
    row = lax.axis_index("ty").astype(F32)
    shift_x = (0.5 * width - 0.5 * side - 0.5) - side * column
    shift_y = jnp.full(column.shape, (0.5 * height - 0.5 * side - 0.5) - side * row, F32)
    return shift_x, shift_y


def request_kernel(owned, across, lists, count, order, request, slot, seen):
    base = lax.axis_index("ty") * across
    for o in range(across):
        seen[o] = 0
        for c in range(CAP):
            request[o, 0, c] = -1
    used = count[0, 0]

    def entry(k, _):
        @pl.when(k < used)
        def _():
            block = order[lists[0, 0, k]]
            home = block // owned
            local = block - home * owned
            home = home - base
            at = seen[home]
            seen[home] = at + 1
            request[home, 0, at] = local
            slot[k] = home * CAP + at

        return 0

    lax.fori_loop(0, slot.shape[0], entry, 0, unroll=True)
    free = 0
    for o in range(across):
        free = jnp.where(seen[o] < CAP, o * CAP + CAP - 1, free)

    def rest(k, _):
        slot[k] = free
        return 0

    lax.fori_loop(used, slot.shape[0], rest, 0)


def project_kernel(span, gaussians, out):
    def part(n, _):
        rows = pl.ds(pl.multiple_of(n * span, span), span)
        field = [gaussians[f, rows, :] for f in range(11)]
        light = -LOG2E * jnp.log(1.0 + jnp.exp(-field[10])) + float(np.log2(0.99))
        values = list(conic(field[0], field[1], field[2], field[3:6], field[6:10]))
        values.append(jnp.maximum(light, DARK))
        basis = directions(field[0], field[1], field[2])
        for ch in range(3):
            color = 0.5 + basis[0] * gaussians[11 + ch, rows, :]
            for m in range(1, 16):
                color = color + basis[m] * gaussians[11 + 3 * m + ch, rows, :]
            values.append(color)
        for f in range(9):
            out[f, rows, :] = values[f]
        return 0

    lax.fori_loop(0, gaussians.shape[1] // span, part, 0)


def asked_index(asked, across, s):
    c = s // across
    return asked[s - c * across, 0, c]


def serve_kernel(across, side, height, width, asked, projected, send, chosen):
    def pick(s, _):
        index = jnp.maximum(asked_index(asked, across, s), 0)
        for f in range(9):
            chosen[f, pl.ds(s, 1), :] = projected[f, pl.ds(index, 1), :]
        return 0

    lax.fori_loop(0, across * CAP, pick, 0, unroll=True)
    shift_x, shift_y = tile_shifts(across, side, height, width)
    rows = list(
        expanded(
            chosen[0], chosen[1], chosen[2], chosen[3] + shift_x, chosen[4] + shift_y, chosen[5]
        )
    ) + [chosen[6], chosen[7], chosen[8]]
    for c in range(CAP):
        for f in range(9):
            at = c * 8 + f if f < 8 else CAP * 8 + c
            send[:, at, :] = rows[f][c * across : (c + 1) * across]


def monomials(side):
    pixels = side * side
    lane = lax.broadcasted_iota(jnp.int32, (8, pixels), 1)
    row = lax.broadcasted_iota(jnp.int32, (8, pixels), 0)
    x = ((lane & (side - 1)) - side // 2).astype(F32)
    y = ((lane >> (side.bit_length() - 1)) - side // 2).astype(F32)
    mono = jnp.zeros((8, pixels), F32)
    for at, value in enumerate((x * x, x * y, y * y, x, y, jnp.ones_like(x))):
        mono = jnp.where(row == at, value, mono)
    blank = jnp.zeros((8, pixels), F32)
    rest = jnp.zeros((LANES - 48, pixels), F32)
    return jnp.concatenate([mono, blank] * 3 + [rest], axis=0).astype(BF16)


def spreaders():
    row = lax.broadcasted_iota(jnp.int32, (LANES, LANES), 0)
    return jnp.concatenate(
        [jnp.where((row == 6 + c) | (row == 22 + c), 1.0, 0.0).astype(F32) for c in range(3)], axis=1
    ).astype(BF16)


def repeated(x, times):
    return jnp.concatenate([x] * times, axis=1)


def forward_kernel(
    side, slot, count, recv, target, table, checks, prefix, behind, dense,
    planes, spread, buf_a, buf_b, ends, part, lights,
):
    lmax = slot.shape[0]
    per = lmax // SEGS
    pixels = prefix.shape[1]
    groups = pixels // LANES
    planes[:, :pixels] = monomials(side)
    planes[:, pixels:] = spreaders()
    zero_rows = jnp.zeros((7, LANES), F32)
    dead = jnp.where(lax.broadcasted_iota(jnp.int32, (16, LANES), 0) == 5, DARK, 0.0)
    is_color = lax.broadcasted_iota(jnp.int32, (16, LANES), 0) >= 6
    filler = jnp.zeros((LANES - 48, LANES), F32)

    def place(m, seg):
        s = slot[seg * per + m]
        live = seg * per + m < count[0, 0]
        o = s // CAP
        c = s - o * CAP
        head = recv[o, pl.ds(pl.multiple_of(c * 8, 8), 8), :]
        tail = recv[o, pl.ds(CAP * 8 + c, 1), :]
        rows = jnp.concatenate([head, tail, zero_rows], axis=0)
        rows = jnp.where(live, rows, dead)
        hi = rows.astype(BF16).astype(F32)
        rest = rows - hi
        mid = rest.astype(BF16).astype(F32)
        low = (rest - mid).astype(BF16).astype(F32)
        third = jnp.where(is_color, hi, low)
        stacked = jnp.concatenate([hi, mid, third, filler], axis=0)
        spread[pl.ds(m * (SEGS * LANES) + seg, LANES, stride=SEGS), :] = stacked.T

    for seg in range(SEGS):
        place(0, seg)

    width = planes.shape[1]
    pieces = -(-width // COLS)

    def product(n, buf, p):
        rows = pl.ds(pl.multiple_of(n * CHUNK, CHUNK), CHUNK)
        if p == 0:
            part[...] = spread[rows, :].astype(BF16)
            table[rows, :] = part[...]
        cols = slice(p * COLS, min((p + 1) * COLS, width))
        buf[:, cols] = jnp.dot(part[...], planes[:, cols], preferred_element_type=F32)

    def blend(n, b, buf, carry):
        light, red, green, blue = carry
        lights[b] = light
        for i in range(b * SPAN, (b + 1) * SPAN):
            rows = pl.ds(i * SEGS, SEGS)
            weight = light * jnp.exp2(buf[rows, :pixels])
            light = light - weight
            red = red + weight * repeated(buf[rows, pixels : pixels + LANES], groups)
            green = green + weight * repeated(buf[rows, pixels + LANES : pixels + 2 * LANES], groups)
            blue = blue + weight * repeated(
                buf[rows, pixels + 2 * LANES : pixels + 3 * LANES], groups
            )
        return light, red, green, blue

    for p in range(pieces):
        product(0, buf_a, p)
    chunks = lmax * LANES // CHUNK
    turn = chunks // per
    share = SEGS // turn

    def keep(n):
        spans = STEPS // SPAN
        checks[pl.ds(n * spans, spans)] = lights[...]

    def pair(h, carry):
        n = 2 * h
        m = (n // turn + 1) % per
        for q in range(2 * share):
            place(m, (n % turn) * share + q)
        for b in range(STEPS // SPAN):
            if b < pieces:
                product(n + 1, buf_b, b)
            carry = blend(n, b, buf_a, carry)
        keep(n)
        for b in range(STEPS // SPAN):
            if b < pieces:
                product(jnp.minimum(n + 2, chunks - 1), buf_a, b)
            carry = blend(n + 1, b, buf_b, carry)
        keep(n + 1)
        return carry

    start = (jnp.ones((SEGS, pixels), F32),) + (jnp.zeros((SEGS, pixels), F32),) * 3
    carry = lax.fori_loop(0, chunks // 2, pair, start)
    for f in range(4):
        ends[f] = carry[f]
    ahead = jnp.ones((1, pixels), F32)
    for seg in range(SEGS):
        prefix[pl.ds(seg, 1), :] = ahead
        ahead = ahead * ends[0, pl.ds(seg, 1), :]
    for ch in range(3):
        seen = jnp.zeros((1, pixels), F32)
        for seg in reversed(range(SEGS)):
            behind[ch, pl.ds(seg, 1), :] = seen
            seen = ends[1 + ch, pl.ds(seg, 1), :] + ends[0, pl.ds(seg, 1), :] * seen
        for j in range(groups):
            dense[pl.ds(ch * groups + j, 1), :] = seen[:, j * LANES : (j + 1) * LANES]
    dense[3 * groups :, :] = target[...]


def similarity(mean_a, mean_b, square_a, square_b, cross):
    var_a = square_a - mean_a * mean_a
    var_b = square_b - mean_b * mean_b
    covar = cross - mean_a * mean_b
    top = (2.0 * mean_a * mean_b + LUMA_TERM) * (2.0 * covar + CONTRAST_TERM)
    bottom = (mean_a * mean_a + mean_b * mean_b + LUMA_TERM) * (var_a + var_b + CONTRAST_TERM)
    return top / bottom


def tap(distance):
    weights = [float(np.exp(-((k - RIM) ** 2) / 4.5)) for k in range(TAPS)]
    value = jnp.exp(distance * distance * (-1.0 / 4.5)) * (1.0 / sum(weights))
    return jnp.where(jnp.abs(distance) <= RIM, value, 0.0)


def places(shape, dim):
    return lax.broadcasted_iota(jnp.int32, shape, dim)


def bands(side, padded):
    fold = LANES // side
    groups = side // fold
    reach = side + 2 * RIM
    shape = (3 * side, LANES)
    out = places(shape, 1)
    along = tap((places(shape, 0) - side - out + RIM).astype(F32))
    along = jnp.where(out < reach, along, 0.0)
    blank = jnp.zeros((side, LANES), F32)
    fa = jnp.concatenate(
        [
            jnp.concatenate(
                [along[h * side : (h + 1) * side] if u == t else blank for u in range(fold)], axis=1
            )
            for h in range(3)
            for t in range(fold)
        ],
        axis=0,
    )
    block = 3 * groups
    shape = (padded, fold * block)
    out, at = places(shape, 0), places(shape, 1)
    t = jnp.zeros(shape, jnp.int32)
    for k in range(1, fold):
        t = t + jnp.where(at >= k * block, 1, 0)
    source = (at - t * block) * fold + t - side
    fb = jnp.where(out < reach, tap((source - out + RIM).astype(F32)), 0.0)
    shape = (fold * groups, padded)
    row, out = places(shape, 0), places(shape, 1)
    t = jnp.zeros(shape, jnp.int32)
    for k in range(1, fold):
        t = t + jnp.where(row >= k * groups, 1, 0)
    source = (row - t * groups) * fold + t
    fc = jnp.where(out < reach, tap((out - RIM - source).astype(F32)), 0.0)
    shape = (LANES, LANES)
    out, at = places(shape, 0), places(shape, 1)
    back = tap((out - RIM - (at & (side - 1))).astype(F32))
    back = jnp.where(out < reach, back, 0.0)
    fd = jnp.concatenate(
        [jnp.where((at >= t * side) & (at < (t + 1) * side), back, 0.0) for t in range(fold)], axis=0
    )
    return fa, fb, fc, fd


def score_kernel(side, height, width, near, slope, loss):
    fa, fb, fc, fd = bands(side, -(-(side + 2 * RIM) // 8) * 8)
    rows3 = near[4].shape[0] // 2
    groups = rows3 // 3
    fold = LANES // side
    fields = [[], [], [], [], []]
    for v in range(3):
        strip = jnp.concatenate([near[3 * v + h] for h in range(3)], axis=1)
        image, target = strip[:rows3], strip[rows3:]
        for f, plane in enumerate([image, target, image * image, target * target, image * target]):
            fields[f].append(plane)
    stack = jnp.concatenate([fields[f][v] for f in range(5) for v in range(3)], axis=0)
    wide = jnp.dot(stack, fa, precision=HIGH, preferred_element_type=F32)
    columns = []
    for f in range(5):
        for ch in range(3):
            parts = []
            for t in range(fold):
                for v in range(3):
                    at = (f * 3 + v) * rows3 + ch * groups
                    parts.append(wide[at : at + groups, t * LANES : (t + 1) * LANES])
            columns.append(jnp.concatenate(parts, axis=0))
    tall = jnp.concatenate(columns, axis=1)
    maps = jnp.dot(fb, tall, precision=HIGH, preferred_element_type=F32)
    span = 3 * LANES
    score, pull = jax.vjp(similarity, *[maps[:, f * span : (f + 1) * span] for f in range(5)])
    parts = pull(jnp.full(score.shape, -STRUCT_WEIGHT, F32))
    row = lax.broadcasted_iota(jnp.int32, score.shape, 0)
    col = lax.broadcasted_iota(jnp.int32, (score.shape[0], LANES), 1)
    col = jnp.concatenate([col] * 3, axis=1)
    row_at = row - RIM + lax.axis_index("ty") * side
    col_at = col - RIM + lax.axis_index("tx") * side
    reach = side + 2 * RIM
    inside = (
        (row_at >= 0) & (row_at < height) & (col_at >= 0) & (col_at < width)
        & (row < reach) & (col < reach)
    )
    own = (row >= RIM) & (row < RIM + side) & (col >= RIM) & (col < RIM + side)
    coeffs = jnp.concatenate(
        [jnp.where(inside, parts[f], 0.0) for f in (0, 2, 4)], axis=1
    )
    low = jnp.dot(fc, coeffs, precision=HIGH, preferred_element_type=F32)
    rows = []
    for n in range(9):
        rows.append(
            jnp.concatenate(
                [
                    low[t * groups : (t + 1) * groups, n * LANES : (n + 1) * LANES]
                    for t in range(fold)
                ],
                axis=1,
            )
        )
    smooth = jnp.dot(
        jnp.concatenate(rows, axis=0), fd, precision=HIGH, preferred_element_type=F32
    )
    image, target = near[4][:rows3, :], near[4][rows3:, :]
    gap = image - target
    robust = jnp.sqrt(gap * gap + ROBUST_TERM)
    slope[...] = (
        smooth[:rows3]
        + 2.0 * image * smooth[rows3 : 2 * rows3]
        + target * smooth[2 * rows3 :]
        + (1.0 - STRUCT_WEIGHT) * gap / robust
    )
    total = (1.0 - STRUCT_WEIGHT) * jnp.sum(robust) + STRUCT_WEIGHT * jnp.sum(
        jnp.where(own, 1.0 - score, 0.0)
    )
    loss[...] = jnp.full(loss.shape, total, F32)


def score_entry(side, height, width, *refs):
    above, left, own, right, below = refs[:5]
    rows = own.shape[0]
    near = [above[h * rows : (h + 1) * rows, :] for h in range(3)]
    near += [left[...], own[...], right[...]]
    near += [below[h * rows : (h + 1) * rows, :] for h in range(3)]
    score_kernel(side, height, width, near, *refs[5:])


def backward_kernel(
    side, table, checks, prefix, behind, slope, reduce, stage,
    rhs, wide, grows, buf_a, buf_b, behinds, sums_a, sums_b, moments, part, lights,
):
    lmax = stage.shape[0]
    per = lmax // SEGS
    pixels = prefix.shape[1]
    groups = pixels // LANES
    chunks = lmax * LANES // CHUNK
    wide[...] = jnp.zeros_like(wide)
    for ch in range(3):
        for j in range(groups):
            lanes = pl.ds(j * LANES, LANES)
            wide[pl.ds(6 + ch, 1), lanes] = slope[pl.ds(ch * groups + j, 1), :]
    for ch in range(3):
        row = wide[pl.ds(6 + ch, 1), :]
        hi = row.astype(BF16).astype(F32)
        grows[ch] = jnp.broadcast_to(row, (SEGS, pixels))
        wide[pl.ds(6 + ch, 1), :] = hi
        wide[pl.ds(22 + ch, 1), :] = hi
        wide[pl.ds(38 + ch, 1), :] = row - hi
    rhs[:, :pixels] = monomials(side)
    rhs[:, pixels:] = wide[...].astype(BF16)

    def product(n, buf, p):
        if p == 0:
            part[...] = table[pl.ds(pl.multiple_of(n * CHUNK, CHUNK), CHUNK), :]
        cols = slice(p * COLS, (p + 1) * COLS)
        buf[:, cols] = jnp.dot(part[...], rhs[:, cols], preferred_element_type=F32)

    def reduced(sums):
        hi = sums[...].astype(BF16)
        low = (sums[...] - hi.astype(F32)).astype(BF16)
        both = jnp.dot(
            jnp.concatenate([hi, low], axis=0), reduce[...], preferred_element_type=F32
        )
        return both[:CHUNK] + both[CHUNK:]

    def record(n, value):
        moments[pl.ds(pl.multiple_of(n * CHUNK, CHUNK), CHUNK), :] = value

    lane = lax.broadcasted_iota(jnp.int32, (SEGS, LANES), 1)
    front = lane < LANES // 2
    even = (lane & (LANES // 4)) == 0

    def folded(a, b):
        return jnp.where(front, a, b) + pltpu.roll(jnp.where(front, b, a), LANES // 2, 1)

    def packed(a, b, c, d):
        ab, cd = folded(a, b), folded(c, d)
        ab = ab + pltpu.roll(ab, LANES - LANES // 4, 1)
        cd = cd + pltpu.roll(cd, LANES // 4, 1)
        return jnp.where(even, ab, cd)

    def block(b, buf, sums):
        first = b * SPAN * SEGS
        rows = [pl.ds(first + i * SEGS, SEGS) for i in range(SPAN)]
        totals = [[None] * 6 for _ in range(SPAN)]

        def add(i, f, value):
            totals[i][f] = value if totals[i][f] is None else totals[i][f] + value

        for q in reversed(range(groups // 2)):
            lanes = slice(q * 2 * LANES, (q + 1) * 2 * LANES)
            light = lights[b, :, lanes] * prefix[:, lanes]
            tints = [grows[ch, :, lanes] for ch in range(3)]
            alphas, weights = [], []
            for i in range(SPAN):
                alphas.append(jnp.exp2(buf[rows[i], lanes]))
                weights.append(light * alphas[i])
                light = light - weights[i]
            back = behinds[:, lanes]
            for i in reversed(range(SPAN)):
                gap = buf[rows[i], pixels + q * 2 * LANES : pixels + (q + 1) * 2 * LANES] - back
                back = back + alphas[i] * gap
                pull = weights[i] * gap
                add(i, 0, pull[:, LANES:])
                add(i, 1, totals[i][0])
                add(i, 2, totals[i][1])
                add(i, 0, pull[:, :LANES])
                if q > 0:
                    add(i, 1, totals[i][0])
                    add(i, 2, totals[i][1])
                for ch in range(3):
                    tint = weights[i] * tints[ch]
                    add(i, 3 + ch, tint[:, LANES:] + tint[:, :LANES])
            behinds[:, lanes] = back
        for i in range(SPAN):
            zero, one, two, red, green, blue = totals[i]
            sums[rows[i], 0:LANES] = zero
            sums[rows[i], LANES : 2 * LANES] = one
            sums[rows[i], 2 * LANES : 3 * LANES] = packed(red, green, blue, two)

    behinds[...] = behind[0] * grows[0] + behind[1] * grows[1] + behind[2] * grows[2]
    pieces = 2 * pixels // COLS
    for p in range(pieces):
        product(chunks - 1, buf_a, p)
    turn = chunks // per
    share = SEGS // turn

    def collect(m, seg):
        moved = moments[pl.ds(m * (SEGS * LANES) + seg, LANES, stride=SEGS), :].T
        stage[seg * per + m] = moved[:16]

    def half(n, ahead, buf, other, sums, last, seg):
        m = (n // turn + 1) % per
        spans = STEPS // SPAN
        lights[...] = checks[pl.ds(n * spans, spans)]
        for at in range(spans):
            for p in range(at * pieces // spans, (at + 1) * pieces // spans):
                product(ahead, other, p)
            if at == spans // 2:
                value = reduced(last)
            block(spans - 1 - at, buf, sums)
        record(n + 1, value)
        for q in range(share):
            collect(m, seg * share + q)

    def pair(h, _):
        n = chunks - 1 - 2 * h
        half(n, n - 1, buf_a, buf_b, sums_a, sums_b, n % turn)
        half(n - 1, jnp.maximum(n - 2, 0), buf_b, buf_a, sums_b, sums_a, n % turn - 1)
        return 0

    lax.fori_loop(0, chunks // 2, pair, 0)
    record(0, reduced(sums_b))
    for seg in range(SEGS):
        collect(0, seg)


def deliver_kernel(slot, stage, *refs):
    reply = refs[-1]
    column = refs[0][...]
    for share in refs[1:-1]:
        column = column + share[...]
    for o in range(reply.shape[0]):
        reply[o, pl.ds(reply.shape[1] - 1, 1), :] = column[:1]
    for k in range(slot.shape[0]):
        s = slot[k]
        o = s // CAP
        c = s - o * CAP
        reply[o, pl.ds(pl.multiple_of(c * 8, 8), 8), :] = stage[k, :8, :]
        reply[o, pl.ds(CAP * 8 + c, 1), :] = stage[k, 8:9, :]


def gather_kernel(
    across, side, height, width, asked, got, gaussians, grads, loss, sums, zeros, pieces, wanted, sem
):
    owned = gaussians.shape[1]
    parts = owned // 8
    shares = got[:, got.shape[1] - 1, :]
    loss[0] = jnp.sum(shares[:, :1]) * (1.0 / (3.0 * height * width))
    zeros[...] = jnp.zeros_like(zeros)
    sums[...] = jnp.zeros_like(sums)
    for g in range(parts + 1):
        wanted[g] = 0
    for s in range(across * CAP):
        c, t = divmod(s, across)
        index = asked[t, 0, c]
        index = jnp.where(index >= 0, index, owned)
        wanted[index // 8] = 1
        row = pl.ds(index, 1)
        for f in range(9):
            at = c * 8 + f if f < 8 else CAP * 8 + c
            sums[f, row, :] = got[t, at : at + 1, :]
        sums[9, row, :] = jnp.full((1, LANES), t + 1.0, F32)

    def target(g):
        return grads.at[:, pl.ds(pl.multiple_of(g * 8, 8), 8), :]

    def blank(g, _):
        @pl.when(wanted[g] == 0)
        def _():
            pltpu.make_async_copy(zeros, target(g), sem.at[g]).start()

        return 0

    lax.fori_loop(0, parts, blank, 0)
    row_at = lax.axis_index("ty").astype(F32)
    shift_y = (0.5 * height - 0.5 * side - 0.5) - side * row_at

    def solve(g):
        rows = pl.ds(pl.multiple_of(g * 8, 8), 8)
        field = [gaussians[f, rows, :] for f in range(11)]
        tile = sums[9, rows, :]
        live = tile > 0.0
        shift_x = (0.5 * width - 0.5 * side - 0.5) - side * (tile - 1.0)

        def put(f, value):
            pieces[g, f] = jnp.where(live, value, 0.0)

        def shaped(x, y, z, log_scale, quat):
            xx, xy, yy, pos_u, pos_v = conic(x, y, z, log_scale, quat)
            return expanded(xx, xy, yy, pos_u + shift_x, pos_v + shift_y, jnp.zeros_like(x))

        _, pull = jax.vjp(shaped, *field[:3], field[3:6], field[6:10])
        moments = [LN2 * sums[f, rows, :] for f in range(6)]
        gx, gy, gz, gscale, gquat = pull(tuple(moments))
        basis, pull_basis = jax.vjp(directions, *field[:3])
        tints = [sums[6 + ch, rows, :] for ch in range(3)]
        tilts = []
        for m in range(16):
            tilt = None
            for ch in range(3):
                term = tints[ch] * gaussians[11 + 3 * m + ch, rows, :]
                tilt = term if tilt is None else tilt + term
                put(11 + 3 * m + ch, tints[ch] * basis[m])
            tilts.append(tilt)
        dx, dy, dz = pull_basis(tilts)
        put(0, gx + dx)
        put(1, gy + dy)
        put(2, gz + dz)
        for f in range(3):
            put(3 + f, gscale[f])
        for f in range(4):
            put(6 + f, gquat[f])
        put(10, moments[5] * (LOG2E / (1.0 + jnp.exp(field[10]))))
        pltpu.make_async_copy(pieces.at[g], target(g), sem.at[g]).start()

    def part(g, _):
        @pl.when(wanted[g] > 0)
        def _():
            solve(g)

        return 0

    lax.fori_loop(0, parts, part, 0)

    def finish(g, _):
        pltpu.make_async_copy(zeros, target(g), sem.at[g]).wait()
        return 0

    lax.fori_loop(0, parts, finish, 0)


def moment_columns(side):
    lane = np.arange(LANES)
    x = lane % side - side // 2
    t = lane // side - side // 2
    step = LANES // side
    one = np.ones_like(x)
    out = np.zeros((3 * LANES, LANES))
    out[:LANES, :6] = np.stack([x * x, x * t, t * t, x, t, one], axis=1)
    out[LANES : 2 * LANES, 1] = step * x
    out[LANES : 2 * LANES, 2] = 2 * step * t - step * step
    out[LANES : 2 * LANES, 4] = step
    quarter = LANES // 4
    for n, (column, weight) in enumerate(((6, 1), (8, 1), (7, 1), (2, 2 * step * step))):
        at = 2 * LANES + n * quarter
        out[at : at + quarter, column] = weight
    return out.astype(ml_dtypes.bfloat16)


def shifted(x, axis):
    size = lax.axis_size(axis)
    up = [(i, i + 1) for i in range(size - 1)]
    return lax.ppermute(x, axis, up), lax.ppermute(x, axis, [(j, i) for i, j in up])


def per_device(gaussians, tile_lists, tile_counts, depth_order, target):
    owned, fields, block = gaussians.shape
    lmax = tile_lists.shape[2]
    side = target.shape[1]
    pixels = side * side
    groups = pixels // LANES
    across = lax.axis_size("tx")
    down = lax.axis_size("ty")
    height = side * lax.axis_size("ty")
    width = side * across
    slots = across * CAP
    depth = -(-(CAP * 9 + 1) // 8) * 8
    f32 = functools.partial(jax.ShapeDtypeStruct, dtype=F32)
    i32 = functools.partial(jax.ShapeDtypeStruct, dtype=jnp.int32)
    reduce = jnp.asarray(moment_columns(side))

    fieldwise = jnp.transpose(gaussians, (1, 0, 2))
    request, slot = pl.pallas_call(
        functools.partial(request_kernel, owned, across),
        out_shape=(i32((across, 1, LANES)), i32((lmax,))),
        in_specs=[SMEM] * 3,
        out_specs=(SMEM, SMEM),
        scratch_shapes=[pltpu.SMEM((across,), jnp.int32)],
        name="request",
    )(tile_lists, tile_counts, depth_order)
    asked = lax.all_to_all(request, "tx", split_axis=0, concat_axis=0, tiled=True)
    projected = pl.pallas_call(
        functools.partial(project_kernel, 16),
        out_shape=f32((9, owned, block)),
        in_specs=[VMEM],
        out_specs=VMEM,
        compiler_params=PARAMS,
        name="project",
    )(fieldwise)
    send = pl.pallas_call(
        functools.partial(serve_kernel, across, side, float(height), float(width)),
        out_shape=f32((across, depth, block)),
        in_specs=[SMEM, VMEM],
        out_specs=VMEM,
        scratch_shapes=[pltpu.VMEM((9, slots, block), F32)],
        compiler_params=PARAMS,
        name="serve",
    )(asked, projected)
    recv = lax.all_to_all(send, "tx", split_axis=0, concat_axis=0, tiled=True)
    chunks = lmax * block // CHUNK
    wide = pixels + 3 * LANES
    table, checks, prefix, behind, dense = pl.pallas_call(
        functools.partial(forward_kernel, side),
        out_shape=(
            jax.ShapeDtypeStruct((lmax * block, LANES), BF16),
            f32((chunks * (STEPS // SPAN), SEGS, pixels)),
            f32((SEGS, pixels)),
            f32((3, SEGS, pixels)),
            f32((6 * groups, LANES)),
        ),
        in_specs=[SMEM, SMEM, VMEM, VMEM],
        out_specs=(VMEM,) * 5,
        scratch_shapes=[
            pltpu.VMEM((LANES, wide), BF16),
            pltpu.VMEM((lmax * block, LANES), F32),
            pltpu.VMEM((CHUNK, wide), F32),
            pltpu.VMEM((CHUNK, wide), F32),
            pltpu.VMEM((4, SEGS, pixels), F32),
            pltpu.VMEM((CHUNK, LANES), BF16),
            pltpu.VMEM((STEPS // SPAN, SEGS, pixels), F32),
        ],
        compiler_params=PARAMS,
        name="forward",
    )(slot, tile_counts, recv, target.reshape(3 * groups, LANES))
    left, right = shifted(dense, "tx")
    above, below = shifted(jnp.concatenate([left, dense, right], axis=0), "ty")
    slope, part = pl.pallas_call(
        functools.partial(score_entry, side, height, width),
        out_shape=(f32((3 * groups, LANES)), f32((8, LANES))),
        in_specs=[VMEM] * 5,
        out_specs=(VMEM, VMEM),
        compiler_params=PARAMS,
        name="score",
    )(above, left, dense, right, below)
    shares = [
        lax.ppermute(part, "ty", [(i, (i + k) % down) for i in range(down)]) for k in range(1, down)
    ]
    stage = pl.pallas_call(
        functools.partial(backward_kernel, side),
        out_shape=f32((lmax, 16, LANES)),
        in_specs=[VMEM] * 6,
        out_specs=VMEM,
        scratch_shapes=[
            pltpu.VMEM((LANES, 2 * pixels), BF16),
            pltpu.VMEM((LANES, pixels), F32),
            pltpu.VMEM((3, SEGS, pixels), F32),
            pltpu.VMEM((CHUNK, 2 * pixels), F32),
            pltpu.VMEM((CHUNK, 2 * pixels), F32),
            pltpu.VMEM((SEGS, pixels), F32),
            pltpu.VMEM((CHUNK, 3 * LANES), F32),
            pltpu.VMEM((CHUNK, 3 * LANES), F32),
            pltpu.VMEM((lmax * block + CHUNK, LANES), F32),
            pltpu.VMEM((CHUNK, LANES), BF16),
            pltpu.VMEM((STEPS // SPAN, SEGS, pixels), F32),
        ],
        compiler_params=PARAMS,
        name="backward",
    )(table, checks, prefix, behind, slope, reduce)
    reply = pl.pallas_call(
        deliver_kernel,
        out_shape=f32((across, depth, block)),
        in_specs=[SMEM] + [VMEM] * (1 + down),
        out_specs=VMEM,
        compiler_params=PARAMS,
        name="deliver",
    )(slot, stage, part, *shares)
    got = lax.all_to_all(reply, "tx", split_axis=0, concat_axis=0, tiled=True)
    grads, loss = pl.pallas_call(
        functools.partial(gather_kernel, across, side, float(height), float(width)),
        out_shape=(f32((fields, owned, block)), f32((1,))),
        in_specs=[SMEM, VMEM, VMEM],
        out_specs=(ANY, SMEM),
        scratch_shapes=[
            pltpu.VMEM((10, owned + 8, block), F32),
            pltpu.VMEM((fields, 8, block), F32),
            pltpu.VMEM((owned // 8, fields, 8, block), F32),
            pltpu.SMEM((owned // 8 + 1,), jnp.int32),
            pltpu.SemaphoreType.DMA((owned // 8,)),
        ],
        compiler_params=PARAMS,
        name="gather",
    )(asked, got, fieldwise)
    return (jnp.transpose(grads, (1, 0, 2)), loss[0])


def solution(mesh):
    return jax.shard_map(
        per_device,
        mesh=mesh,
        in_specs=(
            P(("ty", "tx"), None, None),
            P("ty", "tx", None),
            P("ty", "tx"),
            P(),
            P(None, "ty", "tx"),
        ),
        out_specs=(P(("ty", "tx"), None, None), P()),
        check_vma=False,
    )
```

```python
import functools

import jax
import jax.numpy as jnp
import ml_dtypes
import numpy as np
from jax import lax
from jax.experimental import pallas as pl
from jax.experimental.pallas import tpu as pltpu
from jax.sharding import PartitionSpec as P

CAP = 3
SEGS = 8
LANES = 128
CHUNK = 256
STEPS = CHUNK // SEGS
SPAN = 4
COLS = 256
RIM = 5
TAPS = 2 * RIM + 1
LOG2E = 1.4426950408889634
LN2 = 0.6931471805599453
DARK = -1e30

FOCAL = 1000.0
LOW_PASS = 0.3
STRUCT_WEIGHT = 0.2
LUMA_TERM = 0.0001
CONTRAST_TERM = 0.0009
ROBUST_TERM = 1e-06
HARMONIC_ZERO = 0.28209479177387814
HARMONIC_ONE = 0.4886025119029199
HARMONIC_TWO = (
    1.0925484305920792,
    -1.0925484305920792,
    0.31539156525252005,
    -1.0925484305920792,
    0.5462742152960396,
)
HARMONIC_THREE = (
    -0.5900435899266435,
    2.890611442640554,
    -0.4570457994644658,
    0.3731763325901154,
    -0.4570457994644658,
    1.445305721320277,
    -0.5900435899266435,
)

HIGH = lax.Precision.HIGHEST
F32 = jnp.float32
BF16 = jnp.bfloat16
ANY = pl.BlockSpec(memory_space=pl.ANY)
SMEM = pl.BlockSpec(memory_space=pltpu.SMEM)
VMEM = pl.BlockSpec(memory_space=pltpu.VMEM)
PARAMS = pltpu.CompilerParams(vmem_limit_bytes=24 * 1024 * 1024)


def harmonics(x, y, z):
    xx, yy, zz = x * x, y * y, z * z
    xy, yz, xz = x * y, y * z, x * z
    return [
        HARMONIC_ZERO * jnp.ones_like(x),
        -HARMONIC_ONE * y,
        HARMONIC_ONE * z,
        -HARMONIC_ONE * x,
        HARMONIC_TWO[0] * xy,
        HARMONIC_TWO[1] * yz,
        HARMONIC_TWO[2] * (2.0 * zz - xx - yy),
        HARMONIC_TWO[3] * xz,
        HARMONIC_TWO[4] * (xx - yy),
        HARMONIC_THREE[0] * y * (3.0 * xx - yy),
        HARMONIC_THREE[1] * xy * z,
        HARMONIC_THREE[2] * y * (4.0 * zz - xx - yy),
        HARMONIC_THREE[3] * z * (2.0 * zz - 3.0 * xx - 3.0 * yy),
        HARMONIC_THREE[4] * x * (4.0 * zz - xx - yy),
        HARMONIC_THREE[5] * z * (xx - yy),
        HARMONIC_THREE[6] * x * (xx - 3.0 * yy),
    ]


def directions(x, y, z):
    length = jnp.sqrt(x * x + y * y + z * z)
    return harmonics(x / length, y / length, z / length)


def conic(mean_x, mean_y, mean_z, log_scale, quat):
    scale = [jnp.exp(s) for s in log_scale]
    norm = jnp.sqrt(quat[0] * quat[0] + quat[1] * quat[1] + quat[2] * quat[2] + quat[3] * quat[3])
    w, i, j, k = (q / norm for q in quat)
    rotation = [
        [1.0 - 2.0 * (j * j + k * k), 2.0 * (i * j - w * k), 2.0 * (i * k + w * j)],
        [2.0 * (i * j + w * k), 1.0 - 2.0 * (i * i + k * k), 2.0 * (j * k - w * i)],
        [2.0 * (i * k - w * j), 2.0 * (j * k + w * i), 1.0 - 2.0 * (i * i + j * j)],
    ]
    scaled = [[rotation[r][c] * scale[c] for c in range(3)] for r in range(3)]

    def sigma(r, c):
        return scaled[r][0] * scaled[c][0] + scaled[r][1] * scaled[c][1] + scaled[r][2] * scaled[c][2]

    s00, s01, s02, s11, s12, s22 = (
        sigma(0, 0), sigma(0, 1), sigma(0, 2), sigma(1, 1), sigma(1, 2), sigma(2, 2),
    )
    inverse_z = 1.0 / mean_z
    diag = FOCAL * inverse_z
    jac_xz = -FOCAL * mean_x * inverse_z * inverse_z
    jac_yz = -FOCAL * mean_y * inverse_z * inverse_z
    u0, u1, u2 = diag * s00 + jac_xz * s02, diag * s01 + jac_xz * s12, diag * s02 + jac_xz * s22
    v1, v2 = diag * s11 + jac_yz * s12, diag * s12 + jac_yz * s22
    cov_uu = u0 * diag + u2 * jac_xz + LOW_PASS
    cov_uv = u1 * diag + u2 * jac_yz
    cov_vv = v1 * diag + v2 * jac_yz + LOW_PASS
    determinant = cov_uu * cov_vv - cov_uv * cov_uv
    half = -0.5 * LOG2E
    xx = half * (cov_vv / determinant)
    xy = (-2.0 * half) * (cov_uv / determinant)
    yy = half * (cov_uu / determinant)
    return xx, xy, yy, FOCAL * mean_x * inverse_z, FOCAL * mean_y * inverse_z


def expanded(xx, xy, yy, pos_u, pos_v, log_opacity):
    x1 = -2.0 * xx * pos_u - xy * pos_v
    y1 = -2.0 * yy * pos_v - xy * pos_u
    one = xx * pos_u * pos_u + xy * pos_u * pos_v + yy * pos_v * pos_v + log_opacity
    return xx, xy, yy, x1, y1, one


def tile_shifts(across, side, height, width):
    column = lax.broadcasted_iota(jnp.int32, (across, LANES), 0).astype(F32)
    column = jnp.concatenate([column] * CAP, axis=0)
    row = lax.axis_index("ty").astype(F32)
    shift_x = (0.5 * width - 0.5 * side - 0.5) - side * column
    shift_y = jnp.full(column.shape, (0.5 * height - 0.5 * side - 0.5) - side * row, F32)
    return shift_x, shift_y


def request_kernel(owned, across, lists, count, order, request, slot, seen):
    base = lax.axis_index("ty") * across
    for o in range(across):
        seen[o] = 0
        for c in range(CAP):
            request[o, 0, c] = -1
    used = count[0, 0]

    def entry(k, _):
        @pl.when(k < used)
        def _():
            block = order[lists[0, 0, k]]
            home = block // owned
            local = block - home * owned
            home = home - base
            at = seen[home]
            seen[home] = at + 1
            request[home, 0, at] = local
            slot[k] = home * CAP + at

        return 0

    lax.fori_loop(0, slot.shape[0], entry, 0, unroll=True)
    free = 0
    for o in range(across):
        free = jnp.where(seen[o] < CAP, o * CAP + CAP - 1, free)

    def rest(k, _):
        slot[k] = free
        return 0

    lax.fori_loop(used, slot.shape[0], rest, 0)


def project_kernel(span, gaussians, out):
    def part(n, _):
        rows = pl.ds(pl.multiple_of(n * span, span), span)
        field = [gaussians[f, rows, :] for f in range(11)]
        light = -LOG2E * jnp.log(1.0 + jnp.exp(-field[10])) + float(np.log2(0.99))
        values = list(conic(field[0], field[1], field[2], field[3:6], field[6:10]))
        values.append(jnp.maximum(light, DARK))
        basis = directions(field[0], field[1], field[2])
        for ch in range(3):
            color = 0.5 + basis[0] * gaussians[11 + ch, rows, :]
            for m in range(1, 16):
                color = color + basis[m] * gaussians[11 + 3 * m + ch, rows, :]
            values.append(color)
        for f in range(9):
            out[f, rows, :] = values[f]
        return 0

    lax.fori_loop(0, gaussians.shape[1] // span, part, 0)


def asked_index(asked, across, s):
    c = s // across
    return asked[s - c * across, 0, c]


def serve_kernel(across, side, height, width, asked, projected, send, chosen):
    def pick(s, _):
        index = jnp.maximum(asked_index(asked, across, s), 0)
        for f in range(9):
            chosen[f, pl.ds(s, 1), :] = projected[f, pl.ds(index, 1), :]
        return 0

    lax.fori_loop(0, across * CAP, pick, 0, unroll=True)
    shift_x, shift_y = tile_shifts(across, side, height, width)
    rows = list(
        expanded(
            chosen[0], chosen[1], chosen[2], chosen[3] + shift_x, chosen[4] + shift_y, chosen[5]
        )
    ) + [chosen[6], chosen[7], chosen[8]]
    for c in range(CAP):
        for f in range(9):
            at = c * 8 + f if f < 8 else CAP * 8 + c
            send[:, at, :] = rows[f][c * across : (c + 1) * across]


def monomials(side):
    pixels = side * side
    lane = lax.broadcasted_iota(jnp.int32, (8, pixels), 1)
    row = lax.broadcasted_iota(jnp.int32, (8, pixels), 0)
    x = ((lane & (side - 1)) - side // 2).astype(F32)
    y = ((lane >> (side.bit_length() - 1)) - side // 2).astype(F32)
    mono = jnp.zeros((8, pixels), F32)
    for at, value in enumerate((x * x, x * y, y * y, x, y, jnp.ones_like(x))):
        mono = jnp.where(row == at, value, mono)
    blank = jnp.zeros((8, pixels), F32)
    rest = jnp.zeros((LANES - 48, pixels), F32)
    return jnp.concatenate([mono, blank] * 3 + [rest], axis=0).astype(BF16)


def repeated(x, times):
    return jnp.concatenate([x] * times, axis=1)


def forward_kernel(
    side, slot, count, recv, target, table, checks, prefix, behind, dense,
    planes, spread, buf_a, buf_b, ends, part, hues_a, hues_b,
):
    lmax = slot.shape[0]
    per = lmax // SEGS
    pixels = prefix.shape[1]
    groups = pixels // LANES
    planes[...] = monomials(side)
    zero_rows = jnp.zeros((7, LANES), F32)
    dead = jnp.where(lax.broadcasted_iota(jnp.int32, (16, LANES), 0) == 5, DARK, 0.0)
    is_color = lax.broadcasted_iota(jnp.int32, (16, LANES), 0) >= 6
    filler = jnp.zeros((LANES - 64, LANES), F32)

    def place(m, seg):
        s = slot[seg * per + m]
        live = seg * per + m < count[0, 0]
        o = s // CAP
        c = s - o * CAP
        head = recv[o, pl.ds(pl.multiple_of(c * 8, 8), 8), :]
        tail = recv[o, pl.ds(CAP * 8 + c, 1), :]
        rows = jnp.concatenate([head, tail, zero_rows], axis=0)
        rows = jnp.where(live, rows, dead)
        hi = rows.astype(BF16).astype(F32)
        rest = rows - hi
        mid = rest.astype(BF16).astype(F32)
        low = (rest - mid).astype(BF16).astype(F32)
        third = jnp.where(is_color, hi, low)
        stacked = jnp.concatenate([hi, mid, third, rows, filler], axis=0)
        spread[pl.ds(m * (SEGS * LANES) + seg, LANES, stride=SEGS), :] = stacked.T

    for seg in range(SEGS):
        place(0, seg)

    width = planes.shape[1]
    pieces = -(-width // COLS)

    def product(n, buf, hues, p):
        rows = pl.ds(pl.multiple_of(n * CHUNK, CHUNK), CHUNK)
        if p == 0:
            whole = spread[rows, :]
            hues[...] = whole
            part[...] = whole.astype(BF16)
            table[rows, :] = part[...]
        cols = slice(p * COLS, min((p + 1) * COLS, width))
        buf[:, cols] = jnp.dot(part[...], planes[:, cols], preferred_element_type=F32)

    def blend(n, b, buf, hues, carry):
        light, red, green, blue = carry
        checks[n * (STEPS // SPAN) + b] = light
        for i in range(b * SPAN, (b + 1) * SPAN):
            rows = pl.ds(i * SEGS, SEGS)
            weight = light * jnp.exp2(buf[rows, :pixels])
            light = light - weight
            shades = [
                repeated(jnp.broadcast_to(hues[rows, 54 + c : 55 + c], (SEGS, LANES)), groups)
                for c in range(3)
            ]
            red = red + weight * shades[0]
            green = green + weight * shades[1]
            blue = blue + weight * shades[2]
        return light, red, green, blue

    for p in range(pieces):
        product(0, buf_a, hues_a, p)
    chunks = lmax * LANES // CHUNK
    turn = chunks // per
    share = SEGS // turn

    def pair(h, carry):
        n = 2 * h
        m = (n // turn + 1) % per
        for b in range(STEPS // SPAN):
            if b < pieces:
                product(n + 1, buf_b, hues_b, b)
            if b % 2 == 0 and b // 2 < 2 * share:
                place(m, (n % turn) * share + b // 2)
            carry = blend(n, b, buf_a, hues_a, carry)
        for b in range(STEPS // SPAN):
            if b < pieces:
                product(jnp.minimum(n + 2, chunks - 1), buf_a, hues_a, b)
            carry = blend(n + 1, b, buf_b, hues_b, carry)
        return carry

    start = (jnp.ones((SEGS, pixels), F32),) + (jnp.zeros((SEGS, pixels), F32),) * 3
    carry = lax.fori_loop(0, chunks // 2, pair, start)
    for f in range(4):
        ends[f] = carry[f]
    ahead = jnp.ones((1, pixels), F32)
    for seg in range(SEGS):
        prefix[pl.ds(seg, 1), :] = ahead
        ahead = ahead * ends[0, pl.ds(seg, 1), :]
    for ch in range(3):
        seen = jnp.zeros((1, pixels), F32)
        for seg in reversed(range(SEGS)):
            behind[ch, pl.ds(seg, 1), :] = seen
            seen = ends[1 + ch, pl.ds(seg, 1), :] + ends[0, pl.ds(seg, 1), :] * seen
        for j in range(groups):
            dense[pl.ds(ch * groups + j, 1), :] = seen[:, j * LANES : (j + 1) * LANES]
    dense[3 * groups :, :] = target[...]


def similarity(mean_a, mean_b, square_a, square_b, cross):
    var_a = square_a - mean_a * mean_a
    var_b = square_b - mean_b * mean_b
    covar = cross - mean_a * mean_b
    top = (2.0 * mean_a * mean_b + LUMA_TERM) * (2.0 * covar + CONTRAST_TERM)
    bottom = (mean_a * mean_a + mean_b * mean_b + LUMA_TERM) * (var_a + var_b + CONTRAST_TERM)
    return top / bottom


def tap(distance):
    weights = [float(np.exp(-((k - RIM) ** 2) / 4.5)) for k in range(TAPS)]
    value = jnp.exp(distance * distance * (-1.0 / 4.5)) * (1.0 / sum(weights))
    return jnp.where(jnp.abs(distance) <= RIM, value, 0.0)


def places(shape, dim):
    return lax.broadcasted_iota(jnp.int32, shape, dim)


def bands(side, padded):
    fold = LANES // side
    groups = side // fold
    reach = side + 2 * RIM
    shape = (3 * side, LANES)
    out = places(shape, 1)
    along = tap((places(shape, 0) - side - out + RIM).astype(F32))
    along = jnp.where(out < reach, along, 0.0)
    blank = jnp.zeros((side, LANES), F32)
    fa = jnp.concatenate(
        [
            jnp.concatenate(
                [along[h * side : (h + 1) * side] if u == t else blank for u in range(fold)], axis=1
            )
            for h in range(3)
            for t in range(fold)
        ],
        axis=0,
    )
    block = 3 * groups
    shape = (padded, fold * block)
    out, at = places(shape, 0), places(shape, 1)
    t = jnp.zeros(shape, jnp.int32)
    for k in range(1, fold):
        t = t + jnp.where(at >= k * block, 1, 0)
    source = (at - t * block) * fold + t - side
    fb = jnp.where(out < reach, tap((source - out + RIM).astype(F32)), 0.0)
    shape = (fold * groups, padded)
    row, out = places(shape, 0), places(shape, 1)
    t = jnp.zeros(shape, jnp.int32)
    for k in range(1, fold):
        t = t + jnp.where(row >= k * groups, 1, 0)
    source = (row - t * groups) * fold + t
    fc = jnp.where(out < reach, tap((out - RIM - source).astype(F32)), 0.0)
    shape = (LANES, LANES)
    out, at = places(shape, 0), places(shape, 1)
    back = tap((out - RIM - (at & (side - 1))).astype(F32))
    back = jnp.where(out < reach, back, 0.0)
    fd = jnp.concatenate(
        [jnp.where((at >= t * side) & (at < (t + 1) * side), back, 0.0) for t in range(fold)], axis=0
    )
    return fa, fb, fc, fd


def score_kernel(side, height, width, near, slope, loss):
    fa, fb, fc, fd = bands(side, -(-(side + 2 * RIM) // 8) * 8)
    rows3 = near[4].shape[0] // 2
    groups = rows3 // 3
    fold = LANES // side
    fields = [[], [], [], [], []]
    for v in range(3):
        strip = jnp.concatenate([near[3 * v + h] for h in range(3)], axis=1)
        image, target = strip[:rows3], strip[rows3:]
        for f, plane in enumerate([image, target, image * image, target * target, image * target]):
            fields[f].append(plane)
    stack = jnp.concatenate([fields[f][v] for f in range(5) for v in range(3)], axis=0)
    wide = jnp.dot(stack, fa, precision=HIGH, preferred_element_type=F32)
    columns = []
    for f in range(5):
        for ch in range(3):
            parts = []
            for t in range(fold):
                for v in range(3):
                    at = (f * 3 + v) * rows3 + ch * groups
                    parts.append(wide[at : at + groups, t * LANES : (t + 1) * LANES])
            columns.append(jnp.concatenate(parts, axis=0))
    tall = jnp.concatenate(columns, axis=1)
    maps = jnp.dot(fb, tall, precision=HIGH, preferred_element_type=F32)
    span = 3 * LANES
    score, pull = jax.vjp(similarity, *[maps[:, f * span : (f + 1) * span] for f in range(5)])
    parts = pull(jnp.full(score.shape, -STRUCT_WEIGHT, F32))
    row = lax.broadcasted_iota(jnp.int32, score.shape, 0)
    col = lax.broadcasted_iota(jnp.int32, (score.shape[0], LANES), 1)
    col = jnp.concatenate([col] * 3, axis=1)
    row_at = row - RIM + lax.axis_index("ty") * side
    col_at = col - RIM + lax.axis_index("tx") * side
    reach = side + 2 * RIM
    inside = (
        (row_at >= 0) & (row_at < height) & (col_at >= 0) & (col_at < width)
        & (row < reach) & (col < reach)
    )
    own = (row >= RIM) & (row < RIM + side) & (col >= RIM) & (col < RIM + side)
    coeffs = jnp.concatenate(
        [jnp.where(inside, parts[f], 0.0) for f in (0, 2, 4)], axis=1
    )
    low = jnp.dot(fc, coeffs, precision=HIGH, preferred_element_type=F32)
    rows = []
    for n in range(9):
        rows.append(
            jnp.concatenate(
                [
                    low[t * groups : (t + 1) * groups, n * LANES : (n + 1) * LANES]
                    for t in range(fold)
                ],
                axis=1,
            )
        )
    smooth = jnp.dot(
        jnp.concatenate(rows, axis=0), fd, precision=HIGH, preferred_element_type=F32
    )
    image, target = near[4][:rows3, :], near[4][rows3:, :]
    gap = image - target
    robust = jnp.sqrt(gap * gap + ROBUST_TERM)
    slope[...] = (
        smooth[:rows3]
        + 2.0 * image * smooth[rows3 : 2 * rows3]
        + target * smooth[2 * rows3 :]
        + (1.0 - STRUCT_WEIGHT) * gap / robust
    )
    total = (1.0 - STRUCT_WEIGHT) * jnp.sum(robust) + STRUCT_WEIGHT * jnp.sum(
        jnp.where(own, 1.0 - score, 0.0)
    )
    loss[...] = jnp.full(loss.shape, total, F32)


def score_entry(side, height, width, *refs):
    above, left, own, right, below = refs[:5]
    rows = own.shape[0]
    near = [above[h * rows : (h + 1) * rows, :] for h in range(3)]
    near += [left[...], own[...], right[...]]
    near += [below[h * rows : (h + 1) * rows, :] for h in range(3)]
    score_kernel(side, height, width, near, *refs[5:])


def backward_kernel(
    side, table, checks, prefix, behind, slope, reduce, stage,
    rhs, wide, grows, buf_a, buf_b, behinds, sums_a, sums_b, moments, part, lights,
):
    lmax = stage.shape[0]
    per = lmax // SEGS
    pixels = prefix.shape[1]
    groups = pixels // LANES
    chunks = lmax * LANES // CHUNK
    wide[...] = jnp.zeros_like(wide)
    for ch in range(3):
        for j in range(groups):
            lanes = pl.ds(j * LANES, LANES)
            wide[pl.ds(6 + ch, 1), lanes] = slope[pl.ds(ch * groups + j, 1), :]
    for ch in range(3):
        row = wide[pl.ds(6 + ch, 1), :]
        hi = row.astype(BF16).astype(F32)
        grows[ch] = jnp.broadcast_to(row, (SEGS, pixels))
        wide[pl.ds(6 + ch, 1), :] = hi
        wide[pl.ds(22 + ch, 1), :] = hi
        wide[pl.ds(38 + ch, 1), :] = row - hi
    rhs[:, :pixels] = monomials(side)
    rhs[:, pixels:] = wide[...].astype(BF16)

    def product(n, buf, p):
        if p == 0:
            part[...] = table[pl.ds(pl.multiple_of(n * CHUNK, CHUNK), CHUNK), :]
        cols = slice(p * COLS, (p + 1) * COLS)
        buf[:, cols] = jnp.dot(part[...], rhs[:, cols], preferred_element_type=F32)

    def reduced(sums):
        hi = sums[...].astype(BF16)
        low = (sums[...] - hi.astype(F32)).astype(BF16)
        both = jnp.dot(
            jnp.concatenate([hi, low], axis=0), reduce[...], preferred_element_type=F32
        )
        return both[:CHUNK] + both[CHUNK:]

    def record(n, value):
        moments[pl.ds(pl.multiple_of(n * CHUNK, CHUNK), CHUNK), :] = value

    lane = lax.broadcasted_iota(jnp.int32, (SEGS, LANES), 1)
    front = lane < LANES // 2
    even = (lane & (LANES // 4)) == 0

    def folded(a, b):
        return jnp.where(front, a, b) + pltpu.roll(jnp.where(front, b, a), LANES // 2, 1)

    def packed(a, b, c, d):
        ab, cd = folded(a, b), folded(c, d)
        ab = ab + pltpu.roll(ab, LANES - LANES // 4, 1)
        cd = cd + pltpu.roll(cd, LANES // 4, 1)
        return jnp.where(even, ab, cd)

    def block(b, buf, sums):
        first = b * SPAN * SEGS
        rows = [pl.ds(first + i * SEGS, SEGS) for i in range(SPAN)]
        totals = [[None] * 6 for _ in range(SPAN)]

        def add(i, f, value):
            totals[i][f] = value if totals[i][f] is None else totals[i][f] + value

        for q in reversed(range(groups // 2)):
            lanes = slice(q * 2 * LANES, (q + 1) * 2 * LANES)
            light = lights[b, :, lanes] * prefix[:, lanes]
            tints = [grows[ch, :, lanes] for ch in range(3)]
            alphas, weights = [], []
            for i in range(SPAN):
                alphas.append(jnp.exp2(buf[rows[i], lanes]))
                weights.append(light * alphas[i])
                light = light - weights[i]
            back = behinds[:, lanes]
            for i in reversed(range(SPAN)):
                gap = buf[rows[i], pixels + q * 2 * LANES : pixels + (q + 1) * 2 * LANES] - back
                back = back + alphas[i] * gap
                pull = weights[i] * gap
                add(i, 0, pull[:, LANES:])
                add(i, 1, totals[i][0])
                add(i, 2, totals[i][1])
                add(i, 0, pull[:, :LANES])
                if q > 0:
                    add(i, 1, totals[i][0])
                    add(i, 2, totals[i][1])
                for ch in range(3):
                    tint = weights[i] * tints[ch]
                    add(i, 3 + ch, tint[:, LANES:] + tint[:, :LANES])
            behinds[:, lanes] = back
        for i in range(SPAN):
            zero, one, two, red, green, blue = totals[i]
            sums[rows[i], 0:LANES] = zero
            sums[rows[i], LANES : 2 * LANES] = one
            sums[rows[i], 2 * LANES : 3 * LANES] = packed(red, green, blue, two)

    behinds[...] = behind[0] * grows[0] + behind[1] * grows[1] + behind[2] * grows[2]
    pieces = 2 * pixels // COLS
    for p in range(pieces):
        product(chunks - 1, buf_a, p)
    turn = chunks // per
    share = SEGS // turn

    def collect(m, seg):
        moved = moments[pl.ds(m * (SEGS * LANES) + seg, LANES, stride=SEGS), :].T
        stage[seg * per + m] = moved[:16]

    def half(n, ahead, buf, other, sums, last, seg):
        m = (n // turn + 1) % per
        spans = STEPS // SPAN
        lights[...] = checks[pl.ds(n * spans, spans)]
        for at in range(spans):
            for p in range(at * pieces // spans, (at + 1) * pieces // spans):
                product(ahead, other, p)
            if at == spans // 2:
                value = reduced(last)
            block(spans - 1 - at, buf, sums)
        record(n + 1, value)
        for q in range(share):
            collect(m, seg * share + q)

    def pair(h, _):
        n = chunks - 1 - 2 * h
        half(n, n - 1, buf_a, buf_b, sums_a, sums_b, n % turn)
        half(n - 1, jnp.maximum(n - 2, 0), buf_b, buf_a, sums_b, sums_a, n % turn - 1)
        return 0

    lax.fori_loop(0, chunks // 2, pair, 0)
    record(0, reduced(sums_b))
    for seg in range(SEGS):
        collect(0, seg)


def deliver_kernel(slot, stage, *refs):
    reply = refs[-1]
    column = refs[0][...]
    for share in refs[1:-1]:
        column = column + share[...]
    for o in range(reply.shape[0]):
        reply[o, pl.ds(reply.shape[1] - 1, 1), :] = column[:1]
    for k in range(slot.shape[0]):
        s = slot[k]
        o = s // CAP
        c = s - o * CAP
        reply[o, pl.ds(pl.multiple_of(c * 8, 8), 8), :] = stage[k, :8, :]
        reply[o, pl.ds(CAP * 8 + c, 1), :] = stage[k, 8:9, :]


def gather_kernel(
    across, side, height, width, asked, got, gaussians, grads, loss, sums, zeros, pieces, wanted, sem
):
    owned = gaussians.shape[1]
    parts = owned // 8
    shares = got[:, got.shape[1] - 1, :]
    loss[0] = jnp.sum(shares[:, :1]) * (1.0 / (3.0 * height * width))
    zeros[...] = jnp.zeros_like(zeros)
    sums[...] = jnp.zeros_like(sums)
    for g in range(parts + 1):
        wanted[g] = 0
    for s in range(across * CAP):
        c, t = divmod(s, across)
        index = asked[t, 0, c]
        index = jnp.where(index >= 0, index, owned)
        wanted[index // 8] = 1
        row = pl.ds(index, 1)
        for f in range(9):
            at = c * 8 + f if f < 8 else CAP * 8 + c
            sums[f, row, :] = got[t, at : at + 1, :]
        sums[9, row, :] = jnp.full((1, LANES), t + 1.0, F32)

    def target(g):
        return grads.at[:, pl.ds(pl.multiple_of(g * 8, 8), 8), :]

    def blank(g, _):
        @pl.when(wanted[g] == 0)
        def _():
            pltpu.make_async_copy(zeros, target(g), sem.at[g]).start()

        return 0

    lax.fori_loop(0, parts, blank, 0)
    row_at = lax.axis_index("ty").astype(F32)
    shift_y = (0.5 * height - 0.5 * side - 0.5) - side * row_at

    def solve(g):
        rows = pl.ds(pl.multiple_of(g * 8, 8), 8)
        field = [gaussians[f, rows, :] for f in range(11)]
        tile = sums[9, rows, :]
        live = tile > 0.0
        shift_x = (0.5 * width - 0.5 * side - 0.5) - side * (tile - 1.0)

        def put(f, value):
            pieces[g, f] = jnp.where(live, value, 0.0)

        def shaped(x, y, z, log_scale, quat):
            xx, xy, yy, pos_u, pos_v = conic(x, y, z, log_scale, quat)
            return expanded(xx, xy, yy, pos_u + shift_x, pos_v + shift_y, jnp.zeros_like(x))

        _, pull = jax.vjp(shaped, *field[:3], field[3:6], field[6:10])
        moments = [LN2 * sums[f, rows, :] for f in range(6)]
        gx, gy, gz, gscale, gquat = pull(tuple(moments))
        basis, pull_basis = jax.vjp(directions, *field[:3])
        tints = [sums[6 + ch, rows, :] for ch in range(3)]
        tilts = []
        for m in range(16):
            tilt = None
            for ch in range(3):
                term = tints[ch] * gaussians[11 + 3 * m + ch, rows, :]
                tilt = term if tilt is None else tilt + term
                put(11 + 3 * m + ch, tints[ch] * basis[m])
            tilts.append(tilt)
        dx, dy, dz = pull_basis(tilts)
        put(0, gx + dx)
        put(1, gy + dy)
        put(2, gz + dz)
        for f in range(3):
            put(3 + f, gscale[f])
        for f in range(4):
            put(6 + f, gquat[f])
        put(10, moments[5] * (LOG2E / (1.0 + jnp.exp(field[10]))))
        pltpu.make_async_copy(pieces.at[g], target(g), sem.at[g]).start()

    def part(g, _):
        @pl.when(wanted[g] > 0)
        def _():
            solve(g)

        return 0

    lax.fori_loop(0, parts, part, 0)

    def finish(g, _):
        pltpu.make_async_copy(zeros, target(g), sem.at[g]).wait()
        return 0

    lax.fori_loop(0, parts, finish, 0)


def moment_columns(side):
    lane = np.arange(LANES)
    x = lane % side - side // 2
    t = lane // side - side // 2
    step = LANES // side
    one = np.ones_like(x)
    out = np.zeros((3 * LANES, LANES))
    out[:LANES, :6] = np.stack([x * x, x * t, t * t, x, t, one], axis=1)
    out[LANES : 2 * LANES, 1] = step * x
    out[LANES : 2 * LANES, 2] = 2 * step * t - step * step
    out[LANES : 2 * LANES, 4] = step
    quarter = LANES // 4
    for n, (column, weight) in enumerate(((6, 1), (8, 1), (7, 1), (2, 2 * step * step))):
        at = 2 * LANES + n * quarter
        out[at : at + quarter, column] = weight
    return out.astype(ml_dtypes.bfloat16)


def shifted(x, axis):
    size = lax.axis_size(axis)
    up = [(i, i + 1) for i in range(size - 1)]
    return lax.ppermute(x, axis, up), lax.ppermute(x, axis, [(j, i) for i, j in up])


def per_device(gaussians, tile_lists, tile_counts, depth_order, target):
    owned, fields, block = gaussians.shape
    lmax = tile_lists.shape[2]
    side = target.shape[1]
    pixels = side * side
    groups = pixels // LANES
    across = lax.axis_size("tx")
    down = lax.axis_size("ty")
    height = side * lax.axis_size("ty")
    width = side * across
    slots = across * CAP
    depth = -(-(CAP * 9 + 1) // 8) * 8
    f32 = functools.partial(jax.ShapeDtypeStruct, dtype=F32)
    i32 = functools.partial(jax.ShapeDtypeStruct, dtype=jnp.int32)
    reduce = jnp.asarray(moment_columns(side))

    fieldwise = jnp.transpose(gaussians, (1, 0, 2))
    request, slot = pl.pallas_call(
        functools.partial(request_kernel, owned, across),
        out_shape=(i32((across, 1, LANES)), i32((lmax,))),
        in_specs=[SMEM] * 3,
        out_specs=(SMEM, SMEM),
        scratch_shapes=[pltpu.SMEM((across,), jnp.int32)],
        name="request",
    )(tile_lists, tile_counts, depth_order)
    asked = lax.all_to_all(request, "tx", split_axis=0, concat_axis=0, tiled=True)
    projected = pl.pallas_call(
        functools.partial(project_kernel, 16),
        out_shape=f32((9, owned, block)),
        in_specs=[VMEM],
        out_specs=VMEM,
        compiler_params=PARAMS,
        name="project",
    )(fieldwise)
    send = pl.pallas_call(
        functools.partial(serve_kernel, across, side, float(height), float(width)),
        out_shape=f32((across, depth, block)),
        in_specs=[SMEM, VMEM],
        out_specs=VMEM,
        scratch_shapes=[pltpu.VMEM((9, slots, block), F32)],
        compiler_params=PARAMS,
        name="serve",
    )(asked, projected)
    recv = lax.all_to_all(send, "tx", split_axis=0, concat_axis=0, tiled=True)
    chunks = lmax * block // CHUNK
    table, checks, prefix, behind, dense = pl.pallas_call(
        functools.partial(forward_kernel, side),
        out_shape=(
            jax.ShapeDtypeStruct((lmax * block, LANES), BF16),
            f32((chunks * (STEPS // SPAN), SEGS, pixels)),
            f32((SEGS, pixels)),
            f32((3, SEGS, pixels)),
            f32((6 * groups, LANES)),
        ),
        in_specs=[SMEM, SMEM, VMEM, VMEM],
        out_specs=(VMEM,) * 5,
        scratch_shapes=[
            pltpu.VMEM((LANES, pixels), BF16),
            pltpu.VMEM((lmax * block, LANES), F32),
            pltpu.VMEM((CHUNK, pixels), F32),
            pltpu.VMEM((CHUNK, pixels), F32),
            pltpu.VMEM((4, SEGS, pixels), F32),
            pltpu.VMEM((CHUNK, LANES), BF16),
            pltpu.VMEM((CHUNK, LANES), F32),
            pltpu.VMEM((CHUNK, LANES), F32),
        ],
        compiler_params=PARAMS,
        name="forward",
    )(slot, tile_counts, recv, target.reshape(3 * groups, LANES))
    left, right = shifted(dense, "tx")
    above, below = shifted(jnp.concatenate([left, dense, right], axis=0), "ty")
    slope, part = pl.pallas_call(
        functools.partial(score_entry, side, height, width),
        out_shape=(f32((3 * groups, LANES)), f32((8, LANES))),
        in_specs=[VMEM] * 5,
        out_specs=(VMEM, VMEM),
        compiler_params=PARAMS,
        name="score",
    )(above, left, dense, right, below)
    shares = [
        lax.ppermute(part, "ty", [(i, (i + k) % down) for i in range(down)]) for k in range(1, down)
    ]
    stage = pl.pallas_call(
        functools.partial(backward_kernel, side),
        out_shape=f32((lmax, 16, LANES)),
        in_specs=[VMEM] * 6,
        out_specs=VMEM,
        scratch_shapes=[
            pltpu.VMEM((LANES, 2 * pixels), BF16),
            pltpu.VMEM((LANES, pixels), F32),
            pltpu.VMEM((3, SEGS, pixels), F32),
            pltpu.VMEM((CHUNK, 2 * pixels), F32),
            pltpu.VMEM((CHUNK, 2 * pixels), F32),
            pltpu.VMEM((SEGS, pixels), F32),
            pltpu.VMEM((CHUNK, 3 * LANES), F32),
            pltpu.VMEM((CHUNK, 3 * LANES), F32),
            pltpu.VMEM((lmax * block + CHUNK, LANES), F32),
            pltpu.VMEM((CHUNK, LANES), BF16),
            pltpu.VMEM((STEPS // SPAN, SEGS, pixels), F32),
        ],
        compiler_params=PARAMS,
        name="backward",
    )(table, checks, prefix, behind, slope, reduce)
    reply = pl.pallas_call(
        deliver_kernel,
        out_shape=f32((across, depth, block)),
        in_specs=[SMEM] + [VMEM] * (1 + down),
        out_specs=VMEM,
        compiler_params=PARAMS,
        name="deliver",
    )(slot, stage, part, *shares)
    got = lax.all_to_all(reply, "tx", split_axis=0, concat_axis=0, tiled=True)
    grads, loss = pl.pallas_call(
        functools.partial(gather_kernel, across, side, float(height), float(width)),
        out_shape=(f32((fields, owned, block)), f32((1,))),
        in_specs=[SMEM, VMEM, VMEM],
        out_specs=(ANY, SMEM),
        scratch_shapes=[
            pltpu.VMEM((10, owned + 8, block), F32),
            pltpu.VMEM((fields, 8, block), F32),
            pltpu.VMEM((owned // 8, fields, 8, block), F32),
            pltpu.SMEM((owned // 8 + 1,), jnp.int32),
            pltpu.SemaphoreType.DMA((owned // 8,)),
        ],
        compiler_params=PARAMS,
        name="gather",
    )(asked, got, fieldwise)
    return (jnp.transpose(grads, (1, 0, 2)), loss[0])


def solution(mesh):
    return jax.shard_map(
        per_device,
        mesh=mesh,
        in_specs=(
            P(("ty", "tx"), None, None),
            P("ty", "tx", None),
            P("ty", "tx"),
            P(),
            P(None, "ty", "tx"),
        ),
        out_specs=(P(("ty", "tx"), None, None), P()),
        check_vma=False,
    )
```

```python
import functools

import jax
import jax.numpy as jnp
import ml_dtypes
import numpy as np
from jax import lax
from jax.experimental import pallas as pl
from jax.experimental.pallas import tpu as pltpu
from jax.sharding import PartitionSpec as P

CAP = 3
SEGS = 8
LANES = 128
CHUNK = 256
STEPS = CHUNK // SEGS
SPAN = 4
COLS = 256
DEEP = 64
RIM = 5
TAPS = 2 * RIM + 1
LOG2E = 1.4426950408889634
LN2 = 0.6931471805599453
DARK = -1e30

FOCAL = 1000.0
LOW_PASS = 0.3
STRUCT_WEIGHT = 0.2
LUMA_TERM = 0.0001
CONTRAST_TERM = 0.0009
ROBUST_TERM = 1e-06
HARMONIC_ZERO = 0.28209479177387814
HARMONIC_ONE = 0.4886025119029199
HARMONIC_TWO = (
    1.0925484305920792,
    -1.0925484305920792,
    0.31539156525252005,
    -1.0925484305920792,
    0.5462742152960396,
)
HARMONIC_THREE = (
    -0.5900435899266435,
    2.890611442640554,
    -0.4570457994644658,
    0.3731763325901154,
    -0.4570457994644658,
    1.445305721320277,
    -0.5900435899266435,
)

HIGH = lax.Precision.HIGHEST
F32 = jnp.float32
BF16 = jnp.bfloat16
ANY = pl.BlockSpec(memory_space=pl.ANY)
SMEM = pl.BlockSpec(memory_space=pltpu.SMEM)
VMEM = pl.BlockSpec(memory_space=pltpu.VMEM)
PARAMS = pltpu.CompilerParams(vmem_limit_bytes=24 * 1024 * 1024)


def harmonics(x, y, z):
    xx, yy, zz = x * x, y * y, z * z
    xy, yz, xz = x * y, y * z, x * z
    return [
        HARMONIC_ZERO * jnp.ones_like(x),
        -HARMONIC_ONE * y,
        HARMONIC_ONE * z,
        -HARMONIC_ONE * x,
        HARMONIC_TWO[0] * xy,
        HARMONIC_TWO[1] * yz,
        HARMONIC_TWO[2] * (2.0 * zz - xx - yy),
        HARMONIC_TWO[3] * xz,
        HARMONIC_TWO[4] * (xx - yy),
        HARMONIC_THREE[0] * y * (3.0 * xx - yy),
        HARMONIC_THREE[1] * xy * z,
        HARMONIC_THREE[2] * y * (4.0 * zz - xx - yy),
        HARMONIC_THREE[3] * z * (2.0 * zz - 3.0 * xx - 3.0 * yy),
        HARMONIC_THREE[4] * x * (4.0 * zz - xx - yy),
        HARMONIC_THREE[5] * z * (xx - yy),
        HARMONIC_THREE[6] * x * (xx - 3.0 * yy),
    ]


def directions(x, y, z):
    length = jnp.sqrt(x * x + y * y + z * z)
    return harmonics(x / length, y / length, z / length)


def conic(mean_x, mean_y, mean_z, log_scale, quat):
    scale = [jnp.exp(s) for s in log_scale]
    norm = jnp.sqrt(quat[0] * quat[0] + quat[1] * quat[1] + quat[2] * quat[2] + quat[3] * quat[3])
    w, i, j, k = (q / norm for q in quat)
    rotation = [
        [1.0 - 2.0 * (j * j + k * k), 2.0 * (i * j - w * k), 2.0 * (i * k + w * j)],
        [2.0 * (i * j + w * k), 1.0 - 2.0 * (i * i + k * k), 2.0 * (j * k - w * i)],
        [2.0 * (i * k - w * j), 2.0 * (j * k + w * i), 1.0 - 2.0 * (i * i + j * j)],
    ]
    scaled = [[rotation[r][c] * scale[c] for c in range(3)] for r in range(3)]

    def sigma(r, c):
        return scaled[r][0] * scaled[c][0] + scaled[r][1] * scaled[c][1] + scaled[r][2] * scaled[c][2]

    s00, s01, s02, s11, s12, s22 = (
        sigma(0, 0), sigma(0, 1), sigma(0, 2), sigma(1, 1), sigma(1, 2), sigma(2, 2),
    )
    inverse_z = 1.0 / mean_z
    diag = FOCAL * inverse_z
    jac_xz = -FOCAL * mean_x * inverse_z * inverse_z
    jac_yz = -FOCAL * mean_y * inverse_z * inverse_z
    u0, u1, u2 = diag * s00 + jac_xz * s02, diag * s01 + jac_xz * s12, diag * s02 + jac_xz * s22
    v1, v2 = diag * s11 + jac_yz * s12, diag * s12 + jac_yz * s22
    cov_uu = u0 * diag + u2 * jac_xz + LOW_PASS
    cov_uv = u1 * diag + u2 * jac_yz
    cov_vv = v1 * diag + v2 * jac_yz + LOW_PASS
    determinant = cov_uu * cov_vv - cov_uv * cov_uv
    half = -0.5 * LOG2E
    xx = half * (cov_vv / determinant)
    xy = (-2.0 * half) * (cov_uv / determinant)
    yy = half * (cov_uu / determinant)
    return xx, xy, yy, FOCAL * mean_x * inverse_z, FOCAL * mean_y * inverse_z


def expanded(xx, xy, yy, pos_u, pos_v, log_opacity):
    x1 = -2.0 * xx * pos_u - xy * pos_v
    y1 = -2.0 * yy * pos_v - xy * pos_u
    one = xx * pos_u * pos_u + xy * pos_u * pos_v + yy * pos_v * pos_v + log_opacity
    return xx, xy, yy, x1, y1, one


def tile_shifts(across, side, height, width):
    column = lax.broadcasted_iota(jnp.int32, (across, LANES), 0).astype(F32)
    column = jnp.concatenate([column] * CAP, axis=0)
    row = lax.axis_index("ty").astype(F32)
    shift_x = (0.5 * width - 0.5 * side - 0.5) - side * column
    shift_y = jnp.full(column.shape, (0.5 * height - 0.5 * side - 0.5) - side * row, F32)
    return shift_x, shift_y


def request_kernel(owned, across, lists, count, order, request, slot, seen):
    base = lax.axis_index("ty") * across
    for o in range(across):
        seen[o] = 0
        for c in range(CAP):
            request[o, 0, c] = -1
    used = count[0, 0]

    def entry(k, _):
        @pl.when(k < used)
        def _():
            block = order[lists[0, 0, k]]
            home = block // owned
            local = block - home * owned
            home = home - base
            at = seen[home]
            seen[home] = at + 1
            request[home, 0, at] = local
            slot[k] = home * CAP + at

        return 0

    lax.fori_loop(0, slot.shape[0], entry, 0, unroll=True)
    free = 0
    for o in range(across):
        free = jnp.where(seen[o] < CAP, o * CAP + CAP - 1, free)

    def rest(k, _):
        slot[k] = free
        return 0

    lax.fori_loop(used, slot.shape[0], rest, 0)


def project_kernel(span, gaussians, out):
    def part(n, _):
        rows = pl.ds(pl.multiple_of(n * span, span), span)
        field = [gaussians[f, rows, :] for f in range(11)]
        light = -LOG2E * jnp.log(1.0 + jnp.exp(-field[10])) + float(np.log2(0.99))
        values = list(conic(field[0], field[1], field[2], field[3:6], field[6:10]))
        values.append(jnp.maximum(light, DARK))
        basis = directions(field[0], field[1], field[2])
        for ch in range(3):
            color = 0.5 + basis[0] * gaussians[11 + ch, rows, :]
            for m in range(1, 16):
                color = color + basis[m] * gaussians[11 + 3 * m + ch, rows, :]
            values.append(color)
        for f in range(9):
            out[f, rows, :] = values[f]
        return 0

    lax.fori_loop(0, gaussians.shape[1] // span, part, 0)


def asked_index(asked, across, s):
    c = s // across
    return asked[s - c * across, 0, c]


def serve_kernel(across, side, height, width, asked, projected, send, chosen):
    def pick(s, _):
        index = jnp.maximum(asked_index(asked, across, s), 0)
        for f in range(9):
            chosen[f, pl.ds(s, 1), :] = projected[f, pl.ds(index, 1), :]
        return 0

    lax.fori_loop(0, across * CAP, pick, 0, unroll=True)
    shift_x, shift_y = tile_shifts(across, side, height, width)
    rows = list(
        expanded(
            chosen[0], chosen[1], chosen[2], chosen[3] + shift_x, chosen[4] + shift_y, chosen[5]
        )
    ) + [chosen[6], chosen[7], chosen[8]]
    for c in range(CAP):
        for f in range(9):
            at = c * 8 + f if f < 8 else CAP * 8 + c
            send[:, at, :] = rows[f][c * across : (c + 1) * across]


def monomials(side):
    pixels = side * side
    lane = lax.broadcasted_iota(jnp.int32, (8, pixels), 1)
    row = lax.broadcasted_iota(jnp.int32, (8, pixels), 0)
    x = ((lane & (side - 1)) - side // 2).astype(F32)
    y = ((lane >> (side.bit_length() - 1)) - side // 2).astype(F32)
    mono = jnp.zeros((8, pixels), F32)
    for at, value in enumerate((x * x, x * y, y * y, x, y, jnp.ones_like(x))):
        mono = jnp.where(row == at, value, mono)
    blank = jnp.zeros((8, pixels), F32)
    rest = jnp.zeros((DEEP - 48, pixels), F32)
    return jnp.concatenate([mono, blank] * 3 + [rest], axis=0).astype(BF16)


def repeated(x, times):
    return jnp.concatenate([x] * times, axis=1)


def forward_kernel(
    side, slot, count, recv, target, table, checks, prefix, behind, dense,
    planes, spread, buf_a, buf_b, ends, part, hues_a, hues_b,
):
    lmax = slot.shape[0]
    per = lmax // SEGS
    pixels = prefix.shape[1]
    groups = pixels // LANES
    planes[...] = monomials(side)
    zero_rows = jnp.zeros((7, LANES), F32)
    dead = jnp.where(lax.broadcasted_iota(jnp.int32, (16, LANES), 0) == 5, DARK, 0.0)
    is_color = lax.broadcasted_iota(jnp.int32, (16, LANES), 0) >= 6

    def place(m, seg):
        s = slot[seg * per + m]
        live = seg * per + m < count[0, 0]
        o = s // CAP
        c = s - o * CAP
        head = recv[o, pl.ds(pl.multiple_of(c * 8, 8), 8), :]
        tail = recv[o, pl.ds(CAP * 8 + c, 1), :]
        rows = jnp.concatenate([head, tail, zero_rows], axis=0)
        rows = jnp.where(live, rows, dead)
        hi = rows.astype(BF16).astype(F32)
        rest = rows - hi
        mid = rest.astype(BF16).astype(F32)
        low = (rest - mid).astype(BF16).astype(F32)
        third = jnp.where(is_color, hi, low)
        stacked = jnp.concatenate([hi, mid, third, rows], axis=0)
        spread[pl.ds(m * (SEGS * LANES) + seg, LANES, stride=SEGS), :] = stacked.T

    for seg in range(SEGS):
        place(0, seg)

    width = planes.shape[1]
    pieces = -(-width // COLS)

    def product(n, buf, hues, p):
        rows = pl.ds(pl.multiple_of(n * CHUNK, CHUNK), CHUNK)
        if p == 0:
            whole = spread[rows, :]
            hues[...] = whole
            part[...] = whole.astype(BF16)
            table[rows, :] = part[...]
        cols = slice(p * COLS, min((p + 1) * COLS, width))
        buf[:, cols] = jnp.dot(part[...], planes[:, cols], preferred_element_type=F32)

    def blend(n, b, buf, hues, carry):
        light, red, green, blue = carry
        checks[n * (STEPS // SPAN) + b] = light
        for i in range(b * SPAN, (b + 1) * SPAN):
            rows = pl.ds(i * SEGS, SEGS)
            weight = light * jnp.exp2(buf[rows, :pixels])
            light = light - weight
            shades = [
                repeated(jnp.broadcast_to(hues[rows, 54 + c : 55 + c], (SEGS, LANES)), groups)
                for c in range(3)
            ]
            red = red + weight * shades[0]
            green = green + weight * shades[1]
            blue = blue + weight * shades[2]
        return light, red, green, blue

    for p in range(pieces):
        product(0, buf_a, hues_a, p)
    chunks = lmax * LANES // CHUNK
    turn = chunks // per
    share = SEGS // turn

    def pair(h, carry):
        n = 2 * h
        m = (n // turn + 1) % per
        for b in range(STEPS // SPAN):
            if b < pieces:
                product(n + 1, buf_b, hues_b, b)
            if b % 2 == 0 and b // 2 < 2 * share:
                place(m, (n % turn) * share + b // 2)
            carry = blend(n, b, buf_a, hues_a, carry)
        for b in range(STEPS // SPAN):
            if b < pieces:
                product(jnp.minimum(n + 2, chunks - 1), buf_a, hues_a, b)
            carry = blend(n + 1, b, buf_b, hues_b, carry)
        return carry

    start = (jnp.ones((SEGS, pixels), F32),) + (jnp.zeros((SEGS, pixels), F32),) * 3
    carry = lax.fori_loop(0, chunks // 2, pair, start)
    for f in range(4):
        ends[f] = carry[f]
    ahead = jnp.ones((1, pixels), F32)
    for seg in range(SEGS):
        prefix[pl.ds(seg, 1), :] = ahead
        ahead = ahead * ends[0, pl.ds(seg, 1), :]
    for ch in range(3):
        seen = jnp.zeros((1, pixels), F32)
        for seg in reversed(range(SEGS)):
            behind[ch, pl.ds(seg, 1), :] = seen
            seen = ends[1 + ch, pl.ds(seg, 1), :] + ends[0, pl.ds(seg, 1), :] * seen
        for j in range(groups):
            dense[pl.ds(ch * groups + j, 1), :] = seen[:, j * LANES : (j + 1) * LANES]
    dense[3 * groups :, :] = target[...]


def similarity(mean_a, mean_b, square_a, square_b, cross):
    var_a = square_a - mean_a * mean_a
    var_b = square_b - mean_b * mean_b
    covar = cross - mean_a * mean_b
    top = (2.0 * mean_a * mean_b + LUMA_TERM) * (2.0 * covar + CONTRAST_TERM)
    bottom = (mean_a * mean_a + mean_b * mean_b + LUMA_TERM) * (var_a + var_b + CONTRAST_TERM)
    return top / bottom


def tap(distance):
    weights = [float(np.exp(-((k - RIM) ** 2) / 4.5)) for k in range(TAPS)]
    value = jnp.exp(distance * distance * (-1.0 / 4.5)) * (1.0 / sum(weights))
    return jnp.where(jnp.abs(distance) <= RIM, value, 0.0)


def places(shape, dim):
    return lax.broadcasted_iota(jnp.int32, shape, dim)


def bands(side, padded):
    fold = LANES // side
    groups = side // fold
    reach = side + 2 * RIM
    shape = (3 * side, LANES)
    out = places(shape, 1)
    along = tap((places(shape, 0) - side - out + RIM).astype(F32))
    along = jnp.where(out < reach, along, 0.0)
    blank = jnp.zeros((side, LANES), F32)
    fa = jnp.concatenate(
        [
            jnp.concatenate(
                [along[h * side : (h + 1) * side] if u == t else blank for u in range(fold)], axis=1
            )
            for h in range(3)
            for t in range(fold)
        ],
        axis=0,
    )
    block = 3 * groups
    shape = (padded, fold * block)
    out, at = places(shape, 0), places(shape, 1)
    t = jnp.zeros(shape, jnp.int32)
    for k in range(1, fold):
        t = t + jnp.where(at >= k * block, 1, 0)
    source = (at - t * block) * fold + t - side
    fb = jnp.where(out < reach, tap((source - out + RIM).astype(F32)), 0.0)
    shape = (fold * groups, padded)
    row, out = places(shape, 0), places(shape, 1)
    t = jnp.zeros(shape, jnp.int32)
    for k in range(1, fold):
        t = t + jnp.where(row >= k * groups, 1, 0)
    source = (row - t * groups) * fold + t
    fc = jnp.where(out < reach, tap((out - RIM - source).astype(F32)), 0.0)
    shape = (LANES, LANES)
    out, at = places(shape, 0), places(shape, 1)
    back = tap((out - RIM - (at & (side - 1))).astype(F32))
    back = jnp.where(out < reach, back, 0.0)
    fd = jnp.concatenate(
        [jnp.where((at >= t * side) & (at < (t + 1) * side), back, 0.0) for t in range(fold)], axis=0
    )
    return fa, fb, fc, fd


def score_kernel(side, height, width, near, slope, loss):
    fa, fb, fc, fd = bands(side, -(-(side + 2 * RIM) // 8) * 8)
    rows3 = near[4].shape[0] // 2
    groups = rows3 // 3
    fold = LANES // side
    fields = [[], [], [], [], []]
    for v in range(3):
        strip = jnp.concatenate([near[3 * v + h] for h in range(3)], axis=1)
        image, target = strip[:rows3], strip[rows3:]
        for f, plane in enumerate([image, target, image * image, target * target, image * target]):
            fields[f].append(plane)
    stack = jnp.concatenate([fields[f][v] for f in range(5) for v in range(3)], axis=0)
    wide = jnp.dot(stack, fa, precision=HIGH, preferred_element_type=F32)
    columns = []
    for f in range(5):
        for ch in range(3):
            parts = []
            for t in range(fold):
                for v in range(3):
                    at = (f * 3 + v) * rows3 + ch * groups
                    parts.append(wide[at : at + groups, t * LANES : (t + 1) * LANES])
            columns.append(jnp.concatenate(parts, axis=0))
    tall = jnp.concatenate(columns, axis=1)
    maps = jnp.dot(fb, tall, precision=HIGH, preferred_element_type=F32)
    span = 3 * LANES
    score, pull = jax.vjp(similarity, *[maps[:, f * span : (f + 1) * span] for f in range(5)])
    parts = pull(jnp.full(score.shape, -STRUCT_WEIGHT, F32))
    row = lax.broadcasted_iota(jnp.int32, score.shape, 0)
    col = lax.broadcasted_iota(jnp.int32, (score.shape[0], LANES), 1)
    col = jnp.concatenate([col] * 3, axis=1)
    row_at = row - RIM + lax.axis_index("ty") * side
    col_at = col - RIM + lax.axis_index("tx") * side
    reach = side + 2 * RIM
    inside = (
        (row_at >= 0) & (row_at < height) & (col_at >= 0) & (col_at < width)
        & (row < reach) & (col < reach)
    )
    own = (row >= RIM) & (row < RIM + side) & (col >= RIM) & (col < RIM + side)
    coeffs = jnp.concatenate(
        [jnp.where(inside, parts[f], 0.0) for f in (0, 2, 4)], axis=1
    )
    low = jnp.dot(fc, coeffs, precision=HIGH, preferred_element_type=F32)
    rows = []
    for n in range(9):
        rows.append(
            jnp.concatenate(
                [
                    low[t * groups : (t + 1) * groups, n * LANES : (n + 1) * LANES]
                    for t in range(fold)
                ],
                axis=1,
            )
        )
    smooth = jnp.dot(
        jnp.concatenate(rows, axis=0), fd, precision=HIGH, preferred_element_type=F32
    )
    image, target = near[4][:rows3, :], near[4][rows3:, :]
    gap = image - target
    robust = jnp.sqrt(gap * gap + ROBUST_TERM)
    slope[...] = (
        smooth[:rows3]
        + 2.0 * image * smooth[rows3 : 2 * rows3]
        + target * smooth[2 * rows3 :]
        + (1.0 - STRUCT_WEIGHT) * gap / robust
    )
    total = (1.0 - STRUCT_WEIGHT) * jnp.sum(robust) + STRUCT_WEIGHT * jnp.sum(
        jnp.where(own, 1.0 - score, 0.0)
    )
    loss[...] = jnp.full(loss.shape, total, F32)


def score_entry(side, height, width, *refs):
    above, left, own, right, below = refs[:5]
    rows = own.shape[0]
    near = [above[h * rows : (h + 1) * rows, :] for h in range(3)]
    near += [left[...], own[...], right[...]]
    near += [below[h * rows : (h + 1) * rows, :] for h in range(3)]
    score_kernel(side, height, width, near, *refs[5:])


def backward_kernel(
    side, table, checks, prefix, behind, slope, reduce, stage,
    rhs, wide, grows, buf_a, buf_b, behinds, sums_a, sums_b, moments, part, lights,
):
    lmax = stage.shape[0]
    per = lmax // SEGS
    pixels = prefix.shape[1]
    groups = pixels // LANES
    chunks = lmax * LANES // CHUNK
    wide[...] = jnp.zeros_like(wide)
    for ch in range(3):
        for j in range(groups):
            lanes = pl.ds(j * LANES, LANES)
            wide[pl.ds(6 + ch, 1), lanes] = slope[pl.ds(ch * groups + j, 1), :]
    for ch in range(3):
        row = wide[pl.ds(6 + ch, 1), :]
        hi = row.astype(BF16).astype(F32)
        grows[ch] = jnp.broadcast_to(row, (SEGS, pixels))
        wide[pl.ds(6 + ch, 1), :] = hi
        wide[pl.ds(22 + ch, 1), :] = hi
        wide[pl.ds(38 + ch, 1), :] = row - hi
    rhs[:, :pixels] = monomials(side)
    rhs[:, pixels:] = wide[...].astype(BF16)

    def product(n, buf, p):
        if p == 0:
            part[...] = table[pl.ds(pl.multiple_of(n * CHUNK, CHUNK), CHUNK), :]
        cols = slice(p * COLS, (p + 1) * COLS)
        buf[:, cols] = jnp.dot(part[...], rhs[:, cols], preferred_element_type=F32)

    def reduced(sums):
        hi = sums[...].astype(BF16)
        low = (sums[...] - hi.astype(F32)).astype(BF16)
        both = jnp.dot(
            jnp.concatenate([hi, low], axis=0), reduce[...], preferred_element_type=F32
        )
        return both[:CHUNK] + both[CHUNK:]

    def record(n, value):
        moments[pl.ds(pl.multiple_of(n * CHUNK, CHUNK), CHUNK), :] = value

    lane = lax.broadcasted_iota(jnp.int32, (SEGS, LANES), 1)
    front = lane < LANES // 2
    even = (lane & (LANES // 4)) == 0

    def folded(a, b):
        return jnp.where(front, a, b) + pltpu.roll(jnp.where(front, b, a), LANES // 2, 1)

    def packed(a, b, c, d):
        ab, cd = folded(a, b), folded(c, d)
        ab = ab + pltpu.roll(ab, LANES - LANES // 4, 1)
        cd = cd + pltpu.roll(cd, LANES // 4, 1)
        return jnp.where(even, ab, cd)

    def block(b, buf, sums):
        first = b * SPAN * SEGS
        rows = [pl.ds(first + i * SEGS, SEGS) for i in range(SPAN)]
        totals = [[None] * 6 for _ in range(SPAN)]

        def add(i, f, value):
            totals[i][f] = value if totals[i][f] is None else totals[i][f] + value

        for q in reversed(range(groups // 2)):
            lanes = slice(q * 2 * LANES, (q + 1) * 2 * LANES)
            light = lights[b, :, lanes] * prefix[:, lanes]
            tints = [grows[ch, :, lanes] for ch in range(3)]
            alphas, weights = [], []
            for i in range(SPAN):
                alphas.append(jnp.exp2(buf[rows[i], lanes]))
                weights.append(light * alphas[i])
                light = light - weights[i]
            back = behinds[:, lanes]
            for i in reversed(range(SPAN)):
                gap = buf[rows[i], pixels + q * 2 * LANES : pixels + (q + 1) * 2 * LANES] - back
                back = back + alphas[i] * gap
                pull = weights[i] * gap
                add(i, 0, pull[:, LANES:])
                add(i, 1, totals[i][0])
                add(i, 2, totals[i][1])
                add(i, 0, pull[:, :LANES])
                if q > 0:
                    add(i, 1, totals[i][0])
                    add(i, 2, totals[i][1])
                for ch in range(3):
                    tint = weights[i] * tints[ch]
                    add(i, 3 + ch, tint[:, LANES:] + tint[:, :LANES])
            behinds[:, lanes] = back
        for i in range(SPAN):
            zero, one, two, red, green, blue = totals[i]
            sums[rows[i], 0:LANES] = zero
            sums[rows[i], LANES : 2 * LANES] = one
            sums[rows[i], 2 * LANES : 3 * LANES] = packed(red, green, blue, two)

    behinds[...] = behind[0] * grows[0] + behind[1] * grows[1] + behind[2] * grows[2]
    pieces = 2 * pixels // COLS
    for p in range(pieces):
        product(chunks - 1, buf_a, p)
    turn = chunks // per
    share = SEGS // turn

    def collect(m, seg):
        moved = moments[pl.ds(m * (SEGS * LANES) + seg, LANES, stride=SEGS), :]
        stage[seg * per + m] = moved[:, :16].T

    def half(n, ahead, buf, other, sums, last, seg):
        m = (n // turn + 1) % per
        spans = STEPS // SPAN
        lights[...] = checks[pl.ds(n * spans, spans)]
        for at in range(spans):
            for p in range(at * pieces // spans, (at + 1) * pieces // spans):
                product(ahead, other, p)
            if at == spans // 2:
                value = reduced(last)
            block(spans - 1 - at, buf, sums)
        record(n + 1, value)
        for q in range(share):
            collect(m, seg * share + q)

    def pair(h, _):
        n = chunks - 1 - 2 * h
        half(n, n - 1, buf_a, buf_b, sums_a, sums_b, n % turn)
        half(n - 1, jnp.maximum(n - 2, 0), buf_b, buf_a, sums_b, sums_a, n % turn - 1)
        return 0

    lax.fori_loop(0, chunks // 2, pair, 0)
    record(0, reduced(sums_b))
    for seg in range(SEGS):
        collect(0, seg)


def deliver_kernel(slot, stage, *refs):
    reply = refs[-1]
    column = refs[0][...]
    for share in refs[1:-1]:
        column = column + share[...]
    for o in range(reply.shape[0]):
        reply[o, pl.ds(reply.shape[1] - 1, 1), :] = column[:1]
    for k in range(slot.shape[0]):
        s = slot[k]
        o = s // CAP
        c = s - o * CAP
        reply[o, pl.ds(pl.multiple_of(c * 8, 8), 8), :] = stage[k, :8, :]
        reply[o, pl.ds(CAP * 8 + c, 1), :] = stage[k, 8:9, :]


def gather_kernel(
    across, side, height, width, asked, got, gaussians, grads, loss, sums, zeros, pieces, wanted, sem
):
    owned = gaussians.shape[1]
    parts = owned // 8
    shares = got[:, got.shape[1] - 1, :]
    loss[0] = jnp.sum(shares[:, :1]) * (1.0 / (3.0 * height * width))
    zeros[...] = jnp.zeros_like(zeros)
    sums[...] = jnp.zeros_like(sums)
    for g in range(parts + 1):
        wanted[g] = 0
    for s in range(across * CAP):
        c, t = divmod(s, across)
        index = asked[t, 0, c]
        index = jnp.where(index >= 0, index, owned)
        wanted[index // 8] = 1
        row = pl.ds(index, 1)
        for f in range(9):
            at = c * 8 + f if f < 8 else CAP * 8 + c
            sums[f, row, :] = got[t, at : at + 1, :]
        sums[9, row, :] = jnp.full((1, LANES), t + 1.0, F32)

    def target(g):
        return grads.at[:, pl.ds(pl.multiple_of(g * 8, 8), 8), :]

    def blank(g, _):
        @pl.when(wanted[g] == 0)
        def _():
            pltpu.make_async_copy(zeros, target(g), sem.at[g]).start()

        return 0

    lax.fori_loop(0, parts, blank, 0)
    row_at = lax.axis_index("ty").astype(F32)
    shift_y = (0.5 * height - 0.5 * side - 0.5) - side * row_at

    def solve(g):
        rows = pl.ds(pl.multiple_of(g * 8, 8), 8)
        field = [gaussians[f, rows, :] for f in range(11)]
        tile = sums[9, rows, :]
        live = tile > 0.0
        shift_x = (0.5 * width - 0.5 * side - 0.5) - side * (tile - 1.0)

        def put(f, value):
            pieces[g, f] = jnp.where(live, value, 0.0)

        def shaped(x, y, z, log_scale, quat):
            xx, xy, yy, pos_u, pos_v = conic(x, y, z, log_scale, quat)
            return expanded(xx, xy, yy, pos_u + shift_x, pos_v + shift_y, jnp.zeros_like(x))

        _, pull = jax.vjp(shaped, *field[:3], field[3:6], field[6:10])
        moments = [LN2 * sums[f, rows, :] for f in range(6)]
        gx, gy, gz, gscale, gquat = pull(tuple(moments))
        basis, pull_basis = jax.vjp(directions, *field[:3])
        tints = [sums[6 + ch, rows, :] for ch in range(3)]
        tilts = []
        for m in range(16):
            tilt = None
            for ch in range(3):
                term = tints[ch] * gaussians[11 + 3 * m + ch, rows, :]
                tilt = term if tilt is None else tilt + term
                put(11 + 3 * m + ch, tints[ch] * basis[m])
            tilts.append(tilt)
        dx, dy, dz = pull_basis(tilts)
        put(0, gx + dx)
        put(1, gy + dy)
        put(2, gz + dz)
        for f in range(3):
            put(3 + f, gscale[f])
        for f in range(4):
            put(6 + f, gquat[f])
        put(10, moments[5] * (LOG2E / (1.0 + jnp.exp(field[10]))))
        pltpu.make_async_copy(pieces.at[g], target(g), sem.at[g]).start()

    def part(g, _):
        @pl.when(wanted[g] > 0)
        def _():
            solve(g)

        return 0

    lax.fori_loop(0, parts, part, 0)

    def finish(g, _):
        pltpu.make_async_copy(zeros, target(g), sem.at[g]).wait()
        return 0

    lax.fori_loop(0, parts, finish, 0)


def moment_columns(side):
    lane = np.arange(LANES)
    x = lane % side - side // 2
    t = lane // side - side // 2
    step = LANES // side
    one = np.ones_like(x)
    out = np.zeros((3 * LANES, LANES))
    out[:LANES, :6] = np.stack([x * x, x * t, t * t, x, t, one], axis=1)
    out[LANES : 2 * LANES, 1] = step * x
    out[LANES : 2 * LANES, 2] = 2 * step * t - step * step
    out[LANES : 2 * LANES, 4] = step
    quarter = LANES // 4
    for n, (column, weight) in enumerate(((6, 1), (8, 1), (7, 1), (2, 2 * step * step))):
        at = 2 * LANES + n * quarter
        out[at : at + quarter, column] = weight
    return out.astype(ml_dtypes.bfloat16)


def shifted(x, axis):
    size = lax.axis_size(axis)
    up = [(i, i + 1) for i in range(size - 1)]
    return lax.ppermute(x, axis, up), lax.ppermute(x, axis, [(j, i) for i, j in up])


def per_device(gaussians, tile_lists, tile_counts, depth_order, target):
    owned, fields, block = gaussians.shape
    lmax = tile_lists.shape[2]
    side = target.shape[1]
    pixels = side * side
    groups = pixels // LANES
    across = lax.axis_size("tx")
    down = lax.axis_size("ty")
    height = side * lax.axis_size("ty")
    width = side * across
    slots = across * CAP
    depth = -(-(CAP * 9 + 1) // 8) * 8
    f32 = functools.partial(jax.ShapeDtypeStruct, dtype=F32)
    i32 = functools.partial(jax.ShapeDtypeStruct, dtype=jnp.int32)
    reduce = jnp.asarray(moment_columns(side))

    fieldwise = jnp.transpose(gaussians, (1, 0, 2))
    request, slot = pl.pallas_call(
        functools.partial(request_kernel, owned, across),
        out_shape=(i32((across, 1, LANES)), i32((lmax,))),
        in_specs=[SMEM] * 3,
        out_specs=(SMEM, SMEM),
        scratch_shapes=[pltpu.SMEM((across,), jnp.int32)],
        name="request",
    )(tile_lists, tile_counts, depth_order)
    asked = lax.all_to_all(request, "tx", split_axis=0, concat_axis=0, tiled=True)
    projected = pl.pallas_call(
        functools.partial(project_kernel, 16),
        out_shape=f32((9, owned, block)),
        in_specs=[VMEM],
        out_specs=VMEM,
        compiler_params=PARAMS,
        name="project",
    )(fieldwise)
    send = pl.pallas_call(
        functools.partial(serve_kernel, across, side, float(height), float(width)),
        out_shape=f32((across, depth, block)),
        in_specs=[SMEM, VMEM],
        out_specs=VMEM,
        scratch_shapes=[pltpu.VMEM((9, slots, block), F32)],
        compiler_params=PARAMS,
        name="serve",
    )(asked, projected)
    recv = lax.all_to_all(send, "tx", split_axis=0, concat_axis=0, tiled=True)
    chunks = lmax * block // CHUNK
    table, checks, prefix, behind, dense = pl.pallas_call(
        functools.partial(forward_kernel, side),
        out_shape=(
            jax.ShapeDtypeStruct((lmax * block, DEEP), BF16),
            f32((chunks * (STEPS // SPAN), SEGS, pixels)),
            f32((SEGS, pixels)),
            f32((3, SEGS, pixels)),
            f32((6 * groups, LANES)),
        ),
        in_specs=[SMEM, SMEM, VMEM, VMEM],
        out_specs=(VMEM,) * 5,
        scratch_shapes=[
            pltpu.VMEM((DEEP, pixels), BF16),
            pltpu.VMEM((lmax * block, DEEP), F32),
            pltpu.VMEM((CHUNK, pixels), F32),
            pltpu.VMEM((CHUNK, pixels), F32),
            pltpu.VMEM((4, SEGS, pixels), F32),
            pltpu.VMEM((CHUNK, DEEP), BF16),
            pltpu.VMEM((CHUNK, DEEP), F32),
            pltpu.VMEM((CHUNK, DEEP), F32),
        ],
        compiler_params=PARAMS,
        name="forward",
    )(slot, tile_counts, recv, target.reshape(3 * groups, LANES))
    left, right = shifted(dense, "tx")
    above, below = shifted(jnp.concatenate([left, dense, right], axis=0), "ty")
    slope, part = pl.pallas_call(
        functools.partial(score_entry, side, height, width),
        out_shape=(f32((3 * groups, LANES)), f32((8, LANES))),
        in_specs=[VMEM] * 5,
        out_specs=(VMEM, VMEM),
        compiler_params=PARAMS,
        name="score",
    )(above, left, dense, right, below)
    shares = [
        lax.ppermute(part, "ty", [(i, (i + k) % down) for i in range(down)]) for k in range(1, down)
    ]
    stage = pl.pallas_call(
        functools.partial(backward_kernel, side),
        out_shape=f32((lmax, 16, LANES)),
        in_specs=[VMEM] * 6,
        out_specs=VMEM,
        scratch_shapes=[
            pltpu.VMEM((DEEP, 2 * pixels), BF16),
            pltpu.VMEM((DEEP, pixels), F32),
            pltpu.VMEM((3, SEGS, pixels), F32),
            pltpu.VMEM((CHUNK, 2 * pixels), F32),
            pltpu.VMEM((CHUNK, 2 * pixels), F32),
            pltpu.VMEM((SEGS, pixels), F32),
            pltpu.VMEM((CHUNK, 3 * LANES), F32),
            pltpu.VMEM((CHUNK, 3 * LANES), F32),
            pltpu.VMEM((lmax * block + CHUNK, LANES), F32),
            pltpu.VMEM((CHUNK, DEEP), BF16),
            pltpu.VMEM((STEPS // SPAN, SEGS, pixels), F32),
        ],
        compiler_params=PARAMS,
        name="backward",
    )(table, checks, prefix, behind, slope, reduce)
    reply = pl.pallas_call(
        deliver_kernel,
        out_shape=f32((across, depth, block)),
        in_specs=[SMEM] + [VMEM] * (1 + down),
        out_specs=VMEM,
        compiler_params=PARAMS,
        name="deliver",
    )(slot, stage, part, *shares)
    got = lax.all_to_all(reply, "tx", split_axis=0, concat_axis=0, tiled=True)
    grads, loss = pl.pallas_call(
        functools.partial(gather_kernel, across, side, float(height), float(width)),
        out_shape=(f32((fields, owned, block)), f32((1,))),
        in_specs=[SMEM, VMEM, VMEM],
        out_specs=(ANY, SMEM),
        scratch_shapes=[
            pltpu.VMEM((10, owned + 8, block), F32),
            pltpu.VMEM((fields, 8, block), F32),
            pltpu.VMEM((owned // 8, fields, 8, block), F32),
            pltpu.SMEM((owned // 8 + 1,), jnp.int32),
            pltpu.SemaphoreType.DMA((owned // 8,)),
        ],
        compiler_params=PARAMS,
        name="gather",
    )(asked, got, fieldwise)
    return (jnp.transpose(grads, (1, 0, 2)), loss[0])


def solution(mesh):
    return jax.shard_map(
        per_device,
        mesh=mesh,
        in_specs=(
            P(("ty", "tx"), None, None),
            P("ty", "tx", None),
            P("ty", "tx"),
            P(),
            P(None, "ty", "tx"),
        ),
        out_specs=(P(("ty", "tx"), None, None), P()),
        check_vma=False,
    )
```

```python
import functools

import jax
import jax.numpy as jnp
import ml_dtypes
import numpy as np
from jax import lax
from jax.experimental import pallas as pl
from jax.experimental.pallas import tpu as pltpu
from jax.sharding import PartitionSpec as P

CAP = 3
SEGS = 8
LANES = 128
CHUNK = 512
STEPS = CHUNK // SEGS
SPAN = 4
COLS = 256
DEEP = 64
RIM = 5
TAPS = 2 * RIM + 1
LOG2E = 1.4426950408889634
LN2 = 0.6931471805599453
DARK = -1e30

FOCAL = 1000.0
LOW_PASS = 0.3
STRUCT_WEIGHT = 0.2
LUMA_TERM = 0.0001
CONTRAST_TERM = 0.0009
ROBUST_TERM = 1e-06
HARMONIC_ZERO = 0.28209479177387814
HARMONIC_ONE = 0.4886025119029199
HARMONIC_TWO = (
    1.0925484305920792,
    -1.0925484305920792,
    0.31539156525252005,
    -1.0925484305920792,
    0.5462742152960396,
)
HARMONIC_THREE = (
    -0.5900435899266435,
    2.890611442640554,
    -0.4570457994644658,
    0.3731763325901154,
    -0.4570457994644658,
    1.445305721320277,
    -0.5900435899266435,
)

HIGH = lax.Precision.HIGHEST
F32 = jnp.float32
BF16 = jnp.bfloat16
ANY = pl.BlockSpec(memory_space=pl.ANY)
SMEM = pl.BlockSpec(memory_space=pltpu.SMEM)
VMEM = pl.BlockSpec(memory_space=pltpu.VMEM)
PARAMS = pltpu.CompilerParams(vmem_limit_bytes=24 * 1024 * 1024)


def harmonics(x, y, z):
    xx, yy, zz = x * x, y * y, z * z
    xy, yz, xz = x * y, y * z, x * z
    return [
        HARMONIC_ZERO * jnp.ones_like(x),
        -HARMONIC_ONE * y,
        HARMONIC_ONE * z,
        -HARMONIC_ONE * x,
        HARMONIC_TWO[0] * xy,
        HARMONIC_TWO[1] * yz,
        HARMONIC_TWO[2] * (2.0 * zz - xx - yy),
        HARMONIC_TWO[3] * xz,
        HARMONIC_TWO[4] * (xx - yy),
        HARMONIC_THREE[0] * y * (3.0 * xx - yy),
        HARMONIC_THREE[1] * xy * z,
        HARMONIC_THREE[2] * y * (4.0 * zz - xx - yy),
        HARMONIC_THREE[3] * z * (2.0 * zz - 3.0 * xx - 3.0 * yy),
        HARMONIC_THREE[4] * x * (4.0 * zz - xx - yy),
        HARMONIC_THREE[5] * z * (xx - yy),
        HARMONIC_THREE[6] * x * (xx - 3.0 * yy),
    ]


def directions(x, y, z):
    length = jnp.sqrt(x * x + y * y + z * z)
    return harmonics(x / length, y / length, z / length)


def conic(mean_x, mean_y, mean_z, log_scale, quat):
    scale = [jnp.exp(s) for s in log_scale]
    norm = jnp.sqrt(quat[0] * quat[0] + quat[1] * quat[1] + quat[2] * quat[2] + quat[3] * quat[3])
    w, i, j, k = (q / norm for q in quat)
    rotation = [
        [1.0 - 2.0 * (j * j + k * k), 2.0 * (i * j - w * k), 2.0 * (i * k + w * j)],
        [2.0 * (i * j + w * k), 1.0 - 2.0 * (i * i + k * k), 2.0 * (j * k - w * i)],
        [2.0 * (i * k - w * j), 2.0 * (j * k + w * i), 1.0 - 2.0 * (i * i + j * j)],
    ]
    scaled = [[rotation[r][c] * scale[c] for c in range(3)] for r in range(3)]

    def sigma(r, c):
        return scaled[r][0] * scaled[c][0] + scaled[r][1] * scaled[c][1] + scaled[r][2] * scaled[c][2]

    s00, s01, s02, s11, s12, s22 = (
        sigma(0, 0), sigma(0, 1), sigma(0, 2), sigma(1, 1), sigma(1, 2), sigma(2, 2),
    )
    inverse_z = 1.0 / mean_z
    diag = FOCAL * inverse_z
    jac_xz = -FOCAL * mean_x * inverse_z * inverse_z
    jac_yz = -FOCAL * mean_y * inverse_z * inverse_z
    u0, u1, u2 = diag * s00 + jac_xz * s02, diag * s01 + jac_xz * s12, diag * s02 + jac_xz * s22
    v1, v2 = diag * s11 + jac_yz * s12, diag * s12 + jac_yz * s22
    cov_uu = u0 * diag + u2 * jac_xz + LOW_PASS
    cov_uv = u1 * diag + u2 * jac_yz
    cov_vv = v1 * diag + v2 * jac_yz + LOW_PASS
    determinant = cov_uu * cov_vv - cov_uv * cov_uv
    half = -0.5 * LOG2E
    xx = half * (cov_vv / determinant)
    xy = (-2.0 * half) * (cov_uv / determinant)
    yy = half * (cov_uu / determinant)
    return xx, xy, yy, FOCAL * mean_x * inverse_z, FOCAL * mean_y * inverse_z


def expanded(xx, xy, yy, pos_u, pos_v, log_opacity):
    x1 = -2.0 * xx * pos_u - xy * pos_v
    y1 = -2.0 * yy * pos_v - xy * pos_u
    one = xx * pos_u * pos_u + xy * pos_u * pos_v + yy * pos_v * pos_v + log_opacity
    return xx, xy, yy, x1, y1, one


def tile_shifts(across, side, height, width):
    column = lax.broadcasted_iota(jnp.int32, (across, LANES), 0).astype(F32)
    column = jnp.concatenate([column] * CAP, axis=0)
    row = lax.axis_index("ty").astype(F32)
    shift_x = (0.5 * width - 0.5 * side - 0.5) - side * column
    shift_y = jnp.full(column.shape, (0.5 * height - 0.5 * side - 0.5) - side * row, F32)
    return shift_x, shift_y


def request_kernel(owned, across, lists, count, order, request, slot, seen):
    base = lax.axis_index("ty") * across
    for o in range(across):
        seen[o] = 0
        for c in range(CAP):
            request[o, 0, c] = -1
    used = count[0, 0]

    def entry(k, _):
        @pl.when(k < used)
        def _():
            block = order[lists[0, 0, k]]
            home = block // owned
            local = block - home * owned
            home = home - base
            at = seen[home]
            seen[home] = at + 1
            request[home, 0, at] = local
            slot[k] = home * CAP + at

        return 0

    lax.fori_loop(0, slot.shape[0], entry, 0, unroll=True)
    free = 0
    for o in range(across):
        free = jnp.where(seen[o] < CAP, o * CAP + CAP - 1, free)

    def rest(k, _):
        slot[k] = free
        return 0

    lax.fori_loop(used, slot.shape[0], rest, 0)


def project_kernel(span, gaussians, out):
    def part(n, _):
        rows = pl.ds(pl.multiple_of(n * span, span), span)
        field = [gaussians[f, rows, :] for f in range(11)]
        light = -LOG2E * jnp.log(1.0 + jnp.exp(-field[10])) + float(np.log2(0.99))
        values = list(conic(field[0], field[1], field[2], field[3:6], field[6:10]))
        values.append(jnp.maximum(light, DARK))
        basis = directions(field[0], field[1], field[2])
        for ch in range(3):
            color = 0.5 + basis[0] * gaussians[11 + ch, rows, :]
            for m in range(1, 16):
                color = color + basis[m] * gaussians[11 + 3 * m + ch, rows, :]
            values.append(color)
        for f in range(9):
            out[f, rows, :] = values[f]
        return 0

    lax.fori_loop(0, gaussians.shape[1] // span, part, 0)


def asked_index(asked, across, s):
    c = s // across
    return asked[s - c * across, 0, c]


def serve_kernel(across, side, height, width, asked, projected, send, chosen):
    def pick(s, _):
        index = jnp.maximum(asked_index(asked, across, s), 0)
        for f in range(9):
            chosen[f, pl.ds(s, 1), :] = projected[f, pl.ds(index, 1), :]
        return 0

    lax.fori_loop(0, across * CAP, pick, 0, unroll=True)
    shift_x, shift_y = tile_shifts(across, side, height, width)
    rows = list(
        expanded(
            chosen[0], chosen[1], chosen[2], chosen[3] + shift_x, chosen[4] + shift_y, chosen[5]
        )
    ) + [chosen[6], chosen[7], chosen[8]]
    for c in range(CAP):
        for f in range(9):
            at = c * 8 + f if f < 8 else CAP * 8 + c
            send[:, at, :] = rows[f][c * across : (c + 1) * across]


def monomials(side):
    pixels = side * side
    lane = lax.broadcasted_iota(jnp.int32, (8, pixels), 1)
    row = lax.broadcasted_iota(jnp.int32, (8, pixels), 0)
    x = ((lane & (side - 1)) - side // 2).astype(F32)
    y = ((lane >> (side.bit_length() - 1)) - side // 2).astype(F32)
    mono = jnp.zeros((8, pixels), F32)
    for at, value in enumerate((x * x, x * y, y * y, x, y, jnp.ones_like(x))):
        mono = jnp.where(row == at, value, mono)
    blank = jnp.zeros((8, pixels), F32)
    rest = jnp.zeros((DEEP - 48, pixels), F32)
    return jnp.concatenate([mono, blank] * 3 + [rest], axis=0).astype(BF16)


def repeated(x, times):
    return jnp.concatenate([x] * times, axis=1)


def forward_kernel(
    side, slot, count, recv, target, table, checks, prefix, behind, dense,
    planes, spread, buf_a, buf_b, ends, part, hues_a, hues_b,
):
    lmax = slot.shape[0]
    per = lmax // SEGS
    pixels = prefix.shape[1]
    groups = pixels // LANES
    planes[...] = monomials(side)
    zero_rows = jnp.zeros((7, LANES), F32)
    dead = jnp.where(lax.broadcasted_iota(jnp.int32, (16, LANES), 0) == 5, DARK, 0.0)
    is_color = lax.broadcasted_iota(jnp.int32, (16, LANES), 0) >= 6

    def place(m, seg):
        s = slot[seg * per + m]
        live = seg * per + m < count[0, 0]
        o = s // CAP
        c = s - o * CAP
        head = recv[o, pl.ds(pl.multiple_of(c * 8, 8), 8), :]
        tail = recv[o, pl.ds(CAP * 8 + c, 1), :]
        rows = jnp.concatenate([head, tail, zero_rows], axis=0)
        rows = jnp.where(live, rows, dead)
        hi = rows.astype(BF16).astype(F32)
        rest = rows - hi
        mid = rest.astype(BF16).astype(F32)
        low = (rest - mid).astype(BF16).astype(F32)
        third = jnp.where(is_color, hi, low)
        stacked = jnp.concatenate([hi, mid, third, rows], axis=0)
        spread[pl.ds(m * (SEGS * LANES) + seg, LANES, stride=SEGS), :] = stacked.T

    for seg in range(SEGS):
        place(0, seg)

    width = planes.shape[1]
    pieces = -(-width // COLS)

    def product(n, buf, hues, p):
        rows = pl.ds(pl.multiple_of(n * CHUNK, CHUNK), CHUNK)
        if p == 0:
            whole = spread[rows, :]
            hues[...] = whole
            part[...] = whole.astype(BF16)
            table[rows, :] = part[...]
        cols = slice(p * COLS, min((p + 1) * COLS, width))
        buf[:, cols] = jnp.dot(part[...], planes[:, cols], preferred_element_type=F32)

    def blend(n, b, buf, hues, carry):
        light, red, green, blue = carry
        checks[n * (STEPS // SPAN) + b] = light
        for i in range(b * SPAN, (b + 1) * SPAN):
            rows = pl.ds(i * SEGS, SEGS)
            weight = light * jnp.exp2(buf[rows, :pixels])
            light = light - weight
            shades = [
                repeated(jnp.broadcast_to(hues[rows, 54 + c : 55 + c], (SEGS, LANES)), groups)
                for c in range(3)
            ]
            red = red + weight * shades[0]
            green = green + weight * shades[1]
            blue = blue + weight * shades[2]
        return light, red, green, blue

    for p in range(pieces):
        product(0, buf_a, hues_a, p)
    chunks = lmax * LANES // CHUNK
    turn = chunks // per
    share = SEGS // turn

    def pair(h, carry):
        n = 2 * h
        m = (n // turn + 1) % per
        for b in range(STEPS // SPAN):
            if b < pieces:
                product(n + 1, buf_b, hues_b, b)
            if b % 2 == 0 and b // 2 < 2 * share:
                place(m, (n % turn) * share + b // 2)
            carry = blend(n, b, buf_a, hues_a, carry)
        for b in range(STEPS // SPAN):
            if b < pieces:
                product(jnp.minimum(n + 2, chunks - 1), buf_a, hues_a, b)
            carry = blend(n + 1, b, buf_b, hues_b, carry)
        return carry

    start = (jnp.ones((SEGS, pixels), F32),) + (jnp.zeros((SEGS, pixels), F32),) * 3
    carry = lax.fori_loop(0, chunks // 2, pair, start)
    for f in range(4):
        ends[f] = carry[f]
    ahead = jnp.ones((1, pixels), F32)
    for seg in range(SEGS):
        prefix[pl.ds(seg, 1), :] = ahead
        ahead = ahead * ends[0, pl.ds(seg, 1), :]
    for ch in range(3):
        seen = jnp.zeros((1, pixels), F32)
        for seg in reversed(range(SEGS)):
            behind[ch, pl.ds(seg, 1), :] = seen
            seen = ends[1 + ch, pl.ds(seg, 1), :] + ends[0, pl.ds(seg, 1), :] * seen
        for j in range(groups):
            dense[pl.ds(ch * groups + j, 1), :] = seen[:, j * LANES : (j + 1) * LANES]
    dense[3 * groups :, :] = target[...]


def similarity(mean_a, mean_b, square_a, square_b, cross):
    var_a = square_a - mean_a * mean_a
    var_b = square_b - mean_b * mean_b
    covar = cross - mean_a * mean_b
    top = (2.0 * mean_a * mean_b + LUMA_TERM) * (2.0 * covar + CONTRAST_TERM)
    bottom = (mean_a * mean_a + mean_b * mean_b + LUMA_TERM) * (var_a + var_b + CONTRAST_TERM)
    return top / bottom


def tap(distance):
    weights = [float(np.exp(-((k - RIM) ** 2) / 4.5)) for k in range(TAPS)]
    value = jnp.exp(distance * distance * (-1.0 / 4.5)) * (1.0 / sum(weights))
    return jnp.where(jnp.abs(distance) <= RIM, value, 0.0)


def places(shape, dim):
    return lax.broadcasted_iota(jnp.int32, shape, dim)


def bands(side, padded):
    fold = LANES // side
    groups = side // fold
    reach = side + 2 * RIM
    shape = (3 * side, LANES)
    out = places(shape, 1)
    along = tap((places(shape, 0) - side - out + RIM).astype(F32))
    along = jnp.where(out < reach, along, 0.0)
    blank = jnp.zeros((side, LANES), F32)
    fa = jnp.concatenate(
        [
            jnp.concatenate(
                [along[h * side : (h + 1) * side] if u == t else blank for u in range(fold)], axis=1
            )
            for h in range(3)
            for t in range(fold)
        ],
        axis=0,
    )
    block = 3 * groups
    shape = (padded, fold * block)
    out, at = places(shape, 0), places(shape, 1)
    t = jnp.zeros(shape, jnp.int32)
    for k in range(1, fold):
        t = t + jnp.where(at >= k * block, 1, 0)
    source = (at - t * block) * fold + t - side
    fb = jnp.where(out < reach, tap((source - out + RIM).astype(F32)), 0.0)
    shape = (fold * groups, padded)
    row, out = places(shape, 0), places(shape, 1)
    t = jnp.zeros(shape, jnp.int32)
    for k in range(1, fold):
        t = t + jnp.where(row >= k * groups, 1, 0)
    source = (row - t * groups) * fold + t
    fc = jnp.where(out < reach, tap((out - RIM - source).astype(F32)), 0.0)
    shape = (LANES, LANES)
    out, at = places(shape, 0), places(shape, 1)
    back = tap((out - RIM - (at & (side - 1))).astype(F32))
    back = jnp.where(out < reach, back, 0.0)
    fd = jnp.concatenate(
        [jnp.where((at >= t * side) & (at < (t + 1) * side), back, 0.0) for t in range(fold)], axis=0
    )
    return fa, fb, fc, fd


def score_kernel(side, height, width, near, slope, loss):
    fa, fb, fc, fd = bands(side, -(-(side + 2 * RIM) // 8) * 8)
    rows3 = near[4].shape[0] // 2
    groups = rows3 // 3
    fold = LANES // side
    fields = [[], [], [], [], []]
    for v in range(3):
        strip = jnp.concatenate([near[3 * v + h] for h in range(3)], axis=1)
        image, target = strip[:rows3], strip[rows3:]
        for f, plane in enumerate([image, target, image * image, target * target, image * target]):
            fields[f].append(plane)
    stack = jnp.concatenate([fields[f][v] for f in range(5) for v in range(3)], axis=0)
    wide = jnp.dot(stack, fa, precision=HIGH, preferred_element_type=F32)
    columns = []
    for f in range(5):
        for ch in range(3):
            parts = []
            for t in range(fold):
                for v in range(3):
                    at = (f * 3 + v) * rows3 + ch * groups
                    parts.append(wide[at : at + groups, t * LANES : (t + 1) * LANES])
            columns.append(jnp.concatenate(parts, axis=0))
    tall = jnp.concatenate(columns, axis=1)
    maps = jnp.dot(fb, tall, precision=HIGH, preferred_element_type=F32)
    span = 3 * LANES
    score, pull = jax.vjp(similarity, *[maps[:, f * span : (f + 1) * span] for f in range(5)])
    parts = pull(jnp.full(score.shape, -STRUCT_WEIGHT, F32))
    row = lax.broadcasted_iota(jnp.int32, score.shape, 0)
    col = lax.broadcasted_iota(jnp.int32, (score.shape[0], LANES), 1)
    col = jnp.concatenate([col] * 3, axis=1)
    row_at = row - RIM + lax.axis_index("ty") * side
    col_at = col - RIM + lax.axis_index("tx") * side
    reach = side + 2 * RIM
    inside = (
        (row_at >= 0) & (row_at < height) & (col_at >= 0) & (col_at < width)
        & (row < reach) & (col < reach)
    )
    own = (row >= RIM) & (row < RIM + side) & (col >= RIM) & (col < RIM + side)
    coeffs = jnp.concatenate(
        [jnp.where(inside, parts[f], 0.0) for f in (0, 2, 4)], axis=1
    )
    low = jnp.dot(fc, coeffs, precision=HIGH, preferred_element_type=F32)
    rows = []
    for n in range(9):
        rows.append(
            jnp.concatenate(
                [
                    low[t * groups : (t + 1) * groups, n * LANES : (n + 1) * LANES]
                    for t in range(fold)
                ],
                axis=1,
            )
        )
    smooth = jnp.dot(
        jnp.concatenate(rows, axis=0), fd, precision=HIGH, preferred_element_type=F32
    )
    image, target = near[4][:rows3, :], near[4][rows3:, :]
    gap = image - target
    robust = jnp.sqrt(gap * gap + ROBUST_TERM)
    slope[...] = (
        smooth[:rows3]
        + 2.0 * image * smooth[rows3 : 2 * rows3]
        + target * smooth[2 * rows3 :]
        + (1.0 - STRUCT_WEIGHT) * gap / robust
    )
    total = (1.0 - STRUCT_WEIGHT) * jnp.sum(robust) + STRUCT_WEIGHT * jnp.sum(
        jnp.where(own, 1.0 - score, 0.0)
    )
    loss[...] = jnp.full(loss.shape, total, F32)


def score_entry(side, height, width, *refs):
    above, left, own, right, below = refs[:5]
    rows = own.shape[0]
    near = [above[h * rows : (h + 1) * rows, :] for h in range(3)]
    near += [left[...], own[...], right[...]]
    near += [below[h * rows : (h + 1) * rows, :] for h in range(3)]
    score_kernel(side, height, width, near, *refs[5:])


def backward_kernel(
    side, table, checks, prefix, behind, slope, reduce, stage,
    rhs, wide, grows, buf_a, buf_b, behinds, sums_a, sums_b, moments, part, lights,
):
    lmax = stage.shape[0]
    per = lmax // SEGS
    pixels = prefix.shape[1]
    groups = pixels // LANES
    chunks = lmax * LANES // CHUNK
    wide[...] = jnp.zeros_like(wide)
    for ch in range(3):
        for j in range(groups):
            lanes = pl.ds(j * LANES, LANES)
            wide[pl.ds(6 + ch, 1), lanes] = slope[pl.ds(ch * groups + j, 1), :]
    for ch in range(3):
        row = wide[pl.ds(6 + ch, 1), :]
        hi = row.astype(BF16).astype(F32)
        grows[ch] = jnp.broadcast_to(row, (SEGS, pixels))
        wide[pl.ds(6 + ch, 1), :] = hi
        wide[pl.ds(22 + ch, 1), :] = hi
        wide[pl.ds(38 + ch, 1), :] = row - hi
    rhs[:, :pixels] = monomials(side)
    rhs[:, pixels:] = wide[...].astype(BF16)

    def product(n, buf, p):
        if p == 0:
            part[...] = table[pl.ds(pl.multiple_of(n * CHUNK, CHUNK), CHUNK), :]
        cols = slice(p * COLS, (p + 1) * COLS)
        buf[:, cols] = jnp.dot(part[...], rhs[:, cols], preferred_element_type=F32)

    def reduced(sums):
        hi = sums[...].astype(BF16)
        low = (sums[...] - hi.astype(F32)).astype(BF16)
        both = jnp.dot(
            jnp.concatenate([hi, low], axis=0), reduce[...], preferred_element_type=F32
        )
        return both[:CHUNK] + both[CHUNK:]

    def record(n, value):
        moments[pl.ds(pl.multiple_of(n * CHUNK, CHUNK), CHUNK), :] = value

    lane = lax.broadcasted_iota(jnp.int32, (SEGS, LANES), 1)
    front = lane < LANES // 2
    even = (lane & (LANES // 4)) == 0

    def folded(a, b):
        return jnp.where(front, a, b) + pltpu.roll(jnp.where(front, b, a), LANES // 2, 1)

    def packed(a, b, c, d):
        ab, cd = folded(a, b), folded(c, d)
        ab = ab + pltpu.roll(ab, LANES - LANES // 4, 1)
        cd = cd + pltpu.roll(cd, LANES // 4, 1)
        return jnp.where(even, ab, cd)

    def block(b, buf, sums):
        first = b * SPAN * SEGS
        rows = [pl.ds(first + i * SEGS, SEGS) for i in range(SPAN)]
        totals = [[None] * 6 for _ in range(SPAN)]

        def add(i, f, value):
            totals[i][f] = value if totals[i][f] is None else totals[i][f] + value

        for q in reversed(range(groups // 2)):
            lanes = slice(q * 2 * LANES, (q + 1) * 2 * LANES)
            light = lights[b, :, lanes] * prefix[:, lanes]
            tints = [grows[ch, :, lanes] for ch in range(3)]
            alphas, weights = [], []
            for i in range(SPAN):
                alphas.append(jnp.exp2(buf[rows[i], lanes]))
                weights.append(light * alphas[i])
                light = light - weights[i]
            back = behinds[:, lanes]
            for i in reversed(range(SPAN)):
                gap = buf[rows[i], pixels + q * 2 * LANES : pixels + (q + 1) * 2 * LANES] - back
                back = back + alphas[i] * gap
                pull = weights[i] * gap
                add(i, 0, pull[:, LANES:])
                add(i, 1, totals[i][0])
                add(i, 2, totals[i][1])
                add(i, 0, pull[:, :LANES])
                if q > 0:
                    add(i, 1, totals[i][0])
                    add(i, 2, totals[i][1])
                for ch in range(3):
                    tint = weights[i] * tints[ch]
                    add(i, 3 + ch, tint[:, LANES:] + tint[:, :LANES])
            behinds[:, lanes] = back
        for i in range(SPAN):
            zero, one, two, red, green, blue = totals[i]
            sums[rows[i], 0:LANES] = zero
            sums[rows[i], LANES : 2 * LANES] = one
            sums[rows[i], 2 * LANES : 3 * LANES] = packed(red, green, blue, two)

    behinds[...] = behind[0] * grows[0] + behind[1] * grows[1] + behind[2] * grows[2]
    pieces = 2 * pixels // COLS
    for p in range(pieces):
        product(chunks - 1, buf_a, p)
    turn = chunks // per
    share = SEGS // turn

    def collect(m, seg):
        moved = moments[pl.ds(m * (SEGS * LANES) + seg, LANES, stride=SEGS), :]
        stage[seg * per + m] = moved[:, :16].T

    def half(n, ahead, buf, other, sums, last, seg):
        m = (n // turn + 1) % per
        spans = STEPS // SPAN
        lights[...] = checks[pl.ds(n * spans, spans)]
        for at in range(spans):
            for p in range(at * pieces // spans, (at + 1) * pieces // spans):
                product(ahead, other, p)
            if at == spans // 2:
                value = reduced(last)
            block(spans - 1 - at, buf, sums)
        record(n + 1, value)
        for q in range(share):
            collect(m, seg * share + q)

    def pair(h, _):
        n = chunks - 1 - 2 * h
        half(n, n - 1, buf_a, buf_b, sums_a, sums_b, n % turn)
        half(n - 1, jnp.maximum(n - 2, 0), buf_b, buf_a, sums_b, sums_a, n % turn - 1)
        return 0

    lax.fori_loop(0, chunks // 2, pair, 0)
    record(0, reduced(sums_b))
    for seg in range(SEGS):
        collect(0, seg)


def deliver_kernel(slot, stage, *refs):
    reply = refs[-1]
    column = refs[0][...]
    for share in refs[1:-1]:
        column = column + share[...]
    for o in range(reply.shape[0]):
        reply[o, pl.ds(reply.shape[1] - 1, 1), :] = column[:1]
    for k in range(slot.shape[0]):
        s = slot[k]
        o = s // CAP
        c = s - o * CAP
        reply[o, pl.ds(pl.multiple_of(c * 8, 8), 8), :] = stage[k, :8, :]
        reply[o, pl.ds(CAP * 8 + c, 1), :] = stage[k, 8:9, :]


def gather_kernel(
    across, side, height, width, asked, got, gaussians, grads, loss, sums, zeros, pieces, wanted, sem
):
    owned = gaussians.shape[1]
    parts = owned // 8
    shares = got[:, got.shape[1] - 1, :]
    loss[0] = jnp.sum(shares[:, :1]) * (1.0 / (3.0 * height * width))
    zeros[...] = jnp.zeros_like(zeros)
    sums[...] = jnp.zeros_like(sums)
    for g in range(parts + 1):
        wanted[g] = 0
    for s in range(across * CAP):
        c, t = divmod(s, across)
        index = asked[t, 0, c]
        index = jnp.where(index >= 0, index, owned)
        wanted[index // 8] = 1
        row = pl.ds(index, 1)
        for f in range(9):
            at = c * 8 + f if f < 8 else CAP * 8 + c
            sums[f, row, :] = got[t, at : at + 1, :]
        sums[9, row, :] = jnp.full((1, LANES), t + 1.0, F32)

    def target(g):
        return grads.at[:, pl.ds(pl.multiple_of(g * 8, 8), 8), :]

    def blank(g, _):
        @pl.when(wanted[g] == 0)
        def _():
            pltpu.make_async_copy(zeros, target(g), sem.at[g]).start()

        return 0

    lax.fori_loop(0, parts, blank, 0)
    row_at = lax.axis_index("ty").astype(F32)
    shift_y = (0.5 * height - 0.5 * side - 0.5) - side * row_at

    def solve(g):
        rows = pl.ds(pl.multiple_of(g * 8, 8), 8)
        field = [gaussians[f, rows, :] for f in range(11)]
        tile = sums[9, rows, :]
        live = tile > 0.0
        shift_x = (0.5 * width - 0.5 * side - 0.5) - side * (tile - 1.0)

        def put(f, value):
            pieces[g, f] = jnp.where(live, value, 0.0)

        def shaped(x, y, z, log_scale, quat):
            xx, xy, yy, pos_u, pos_v = conic(x, y, z, log_scale, quat)
            return expanded(xx, xy, yy, pos_u + shift_x, pos_v + shift_y, jnp.zeros_like(x))

        _, pull = jax.vjp(shaped, *field[:3], field[3:6], field[6:10])
        moments = [LN2 * sums[f, rows, :] for f in range(6)]
        gx, gy, gz, gscale, gquat = pull(tuple(moments))
        basis, pull_basis = jax.vjp(directions, *field[:3])
        tints = [sums[6 + ch, rows, :] for ch in range(3)]
        tilts = []
        for m in range(16):
            tilt = None
            for ch in range(3):
                term = tints[ch] * gaussians[11 + 3 * m + ch, rows, :]
                tilt = term if tilt is None else tilt + term
                put(11 + 3 * m + ch, tints[ch] * basis[m])
            tilts.append(tilt)
        dx, dy, dz = pull_basis(tilts)
        put(0, gx + dx)
        put(1, gy + dy)
        put(2, gz + dz)
        for f in range(3):
            put(3 + f, gscale[f])
        for f in range(4):
            put(6 + f, gquat[f])
        put(10, moments[5] * (LOG2E / (1.0 + jnp.exp(field[10]))))
        pltpu.make_async_copy(pieces.at[g], target(g), sem.at[g]).start()

    def part(g, _):
        @pl.when(wanted[g] > 0)
        def _():
            solve(g)

        return 0

    lax.fori_loop(0, parts, part, 0)

    def finish(g, _):
        pltpu.make_async_copy(zeros, target(g), sem.at[g]).wait()
        return 0

    lax.fori_loop(0, parts, finish, 0)


def moment_columns(side):
    lane = np.arange(LANES)
    x = lane % side - side // 2
    t = lane // side - side // 2
    step = LANES // side
    one = np.ones_like(x)
    out = np.zeros((3 * LANES, LANES))
    out[:LANES, :6] = np.stack([x * x, x * t, t * t, x, t, one], axis=1)
    out[LANES : 2 * LANES, 1] = step * x
    out[LANES : 2 * LANES, 2] = 2 * step * t - step * step
    out[LANES : 2 * LANES, 4] = step
    quarter = LANES // 4
    for n, (column, weight) in enumerate(((6, 1), (8, 1), (7, 1), (2, 2 * step * step))):
        at = 2 * LANES + n * quarter
        out[at : at + quarter, column] = weight
    return out.astype(ml_dtypes.bfloat16)


def shifted(x, axis):
    size = lax.axis_size(axis)
    up = [(i, i + 1) for i in range(size - 1)]
    return lax.ppermute(x, axis, up), lax.ppermute(x, axis, [(j, i) for i, j in up])


def per_device(gaussians, tile_lists, tile_counts, depth_order, target):
    owned, fields, block = gaussians.shape
    lmax = tile_lists.shape[2]
    side = target.shape[1]
    pixels = side * side
    groups = pixels // LANES
    across = lax.axis_size("tx")
    down = lax.axis_size("ty")
    height = side * lax.axis_size("ty")
    width = side * across
    slots = across * CAP
    depth = -(-(CAP * 9 + 1) // 8) * 8
    f32 = functools.partial(jax.ShapeDtypeStruct, dtype=F32)
    i32 = functools.partial(jax.ShapeDtypeStruct, dtype=jnp.int32)
    reduce = jnp.asarray(moment_columns(side))

    fieldwise = jnp.transpose(gaussians, (1, 0, 2))
    request, slot = pl.pallas_call(
        functools.partial(request_kernel, owned, across),
        out_shape=(i32((across, 1, LANES)), i32((lmax,))),
        in_specs=[SMEM] * 3,
        out_specs=(SMEM, SMEM),
        scratch_shapes=[pltpu.SMEM((across,), jnp.int32)],
        name="request",
    )(tile_lists, tile_counts, depth_order)
    asked = lax.all_to_all(request, "tx", split_axis=0, concat_axis=0, tiled=True)
    projected = pl.pallas_call(
        functools.partial(project_kernel, 16),
        out_shape=f32((9, owned, block)),
        in_specs=[VMEM],
        out_specs=VMEM,
        compiler_params=PARAMS,
        name="project",
    )(fieldwise)
    send = pl.pallas_call(
        functools.partial(serve_kernel, across, side, float(height), float(width)),
        out_shape=f32((across, depth, block)),
        in_specs=[SMEM, VMEM],
        out_specs=VMEM,
        scratch_shapes=[pltpu.VMEM((9, slots, block), F32)],
        compiler_params=PARAMS,
        name="serve",
    )(asked, projected)
    recv = lax.all_to_all(send, "tx", split_axis=0, concat_axis=0, tiled=True)
    chunks = lmax * block // CHUNK
    table, checks, prefix, behind, dense = pl.pallas_call(
        functools.partial(forward_kernel, side),
        out_shape=(
            jax.ShapeDtypeStruct((lmax * block, DEEP), BF16),
            f32((chunks * (STEPS // SPAN), SEGS, pixels)),
            f32((SEGS, pixels)),
            f32((3, SEGS, pixels)),
            f32((6 * groups, LANES)),
        ),
        in_specs=[SMEM, SMEM, VMEM, VMEM],
        out_specs=(VMEM,) * 5,
        scratch_shapes=[
            pltpu.VMEM((DEEP, pixels), BF16),
            pltpu.VMEM((lmax * block, DEEP), F32),
            pltpu.VMEM((CHUNK, pixels), F32),
            pltpu.VMEM((CHUNK, pixels), F32),
            pltpu.VMEM((4, SEGS, pixels), F32),
            pltpu.VMEM((CHUNK, DEEP), BF16),
            pltpu.VMEM((CHUNK, DEEP), F32),
            pltpu.VMEM((CHUNK, DEEP), F32),
        ],
        compiler_params=PARAMS,
        name="forward",
    )(slot, tile_counts, recv, target.reshape(3 * groups, LANES))
    left, right = shifted(dense, "tx")
    above, below = shifted(jnp.concatenate([left, dense, right], axis=0), "ty")
    slope, part = pl.pallas_call(
        functools.partial(score_entry, side, height, width),
        out_shape=(f32((3 * groups, LANES)), f32((8, LANES))),
        in_specs=[VMEM] * 5,
        out_specs=(VMEM, VMEM),
        compiler_params=PARAMS,
        name="score",
    )(above, left, dense, right, below)
    shares = [
        lax.ppermute(part, "ty", [(i, (i + k) % down) for i in range(down)]) for k in range(1, down)
    ]
    stage = pl.pallas_call(
        functools.partial(backward_kernel, side),
        out_shape=f32((lmax, 16, LANES)),
        in_specs=[VMEM] * 6,
        out_specs=VMEM,
        scratch_shapes=[
            pltpu.VMEM((DEEP, 2 * pixels), BF16),
            pltpu.VMEM((DEEP, pixels), F32),
            pltpu.VMEM((3, SEGS, pixels), F32),
            pltpu.VMEM((CHUNK, 2 * pixels), F32),
            pltpu.VMEM((CHUNK, 2 * pixels), F32),
            pltpu.VMEM((SEGS, pixels), F32),
            pltpu.VMEM((CHUNK, 3 * LANES), F32),
            pltpu.VMEM((CHUNK, 3 * LANES), F32),
            pltpu.VMEM((lmax * block + CHUNK, LANES), F32),
            pltpu.VMEM((CHUNK, DEEP), BF16),
            pltpu.VMEM((STEPS // SPAN, SEGS, pixels), F32),
        ],
        compiler_params=PARAMS,
        name="backward",
    )(table, checks, prefix, behind, slope, reduce)
    reply = pl.pallas_call(
        deliver_kernel,
        out_shape=f32((across, depth, block)),
        in_specs=[SMEM] + [VMEM] * (1 + down),
        out_specs=VMEM,
        compiler_params=PARAMS,
        name="deliver",
    )(slot, stage, part, *shares)
    got = lax.all_to_all(reply, "tx", split_axis=0, concat_axis=0, tiled=True)
    grads, loss = pl.pallas_call(
        functools.partial(gather_kernel, across, side, float(height), float(width)),
        out_shape=(f32((fields, owned, block)), f32((1,))),
        in_specs=[SMEM, VMEM, VMEM],
        out_specs=(ANY, SMEM),
        scratch_shapes=[
            pltpu.VMEM((10, owned + 8, block), F32),
            pltpu.VMEM((fields, 8, block), F32),
            pltpu.VMEM((owned // 8, fields, 8, block), F32),
            pltpu.SMEM((owned // 8 + 1,), jnp.int32),
            pltpu.SemaphoreType.DMA((owned // 8,)),
        ],
        compiler_params=PARAMS,
        name="gather",
    )(asked, got, fieldwise)
    return (jnp.transpose(grads, (1, 0, 2)), loss[0])


def solution(mesh):
    return jax.shard_map(
        per_device,
        mesh=mesh,
        in_specs=(
            P(("ty", "tx"), None, None),
            P("ty", "tx", None),
            P("ty", "tx"),
            P(),
            P(None, "ty", "tx"),
        ),
        out_specs=(P(("ty", "tx"), None, None), P()),
        check_vma=False,
    )
```

```python
import functools

import jax
import jax.numpy as jnp
import ml_dtypes
import numpy as np
from jax import lax
from jax.experimental import pallas as pl
from jax.experimental.pallas import tpu as pltpu
from jax.sharding import PartitionSpec as P

CAP = 3
SEGS = 8
LANES = 128
CHUNK = 128
STEPS = CHUNK // SEGS
SPAN = 4
COLS = 256
DEEP = 64
RIM = 5
TAPS = 2 * RIM + 1
LOG2E = 1.4426950408889634
LN2 = 0.6931471805599453
DARK = -1e30

FOCAL = 1000.0
LOW_PASS = 0.3
STRUCT_WEIGHT = 0.2
LUMA_TERM = 0.0001
CONTRAST_TERM = 0.0009
ROBUST_TERM = 1e-06
HARMONIC_ZERO = 0.28209479177387814
HARMONIC_ONE = 0.4886025119029199
HARMONIC_TWO = (
    1.0925484305920792,
    -1.0925484305920792,
    0.31539156525252005,
    -1.0925484305920792,
    0.5462742152960396,
)
HARMONIC_THREE = (
    -0.5900435899266435,
    2.890611442640554,
    -0.4570457994644658,
    0.3731763325901154,
    -0.4570457994644658,
    1.445305721320277,
    -0.5900435899266435,
)

HIGH = lax.Precision.HIGHEST
F32 = jnp.float32
BF16 = jnp.bfloat16
ANY = pl.BlockSpec(memory_space=pl.ANY)
SMEM = pl.BlockSpec(memory_space=pltpu.SMEM)
VMEM = pl.BlockSpec(memory_space=pltpu.VMEM)
PARAMS = pltpu.CompilerParams(vmem_limit_bytes=24 * 1024 * 1024)


def harmonics(x, y, z):
    xx, yy, zz = x * x, y * y, z * z
    xy, yz, xz = x * y, y * z, x * z
    return [
        HARMONIC_ZERO * jnp.ones_like(x),
        -HARMONIC_ONE * y,
        HARMONIC_ONE * z,
        -HARMONIC_ONE * x,
        HARMONIC_TWO[0] * xy,
        HARMONIC_TWO[1] * yz,
        HARMONIC_TWO[2] * (2.0 * zz - xx - yy),
        HARMONIC_TWO[3] * xz,
        HARMONIC_TWO[4] * (xx - yy),
        HARMONIC_THREE[0] * y * (3.0 * xx - yy),
        HARMONIC_THREE[1] * xy * z,
        HARMONIC_THREE[2] * y * (4.0 * zz - xx - yy),
        HARMONIC_THREE[3] * z * (2.0 * zz - 3.0 * xx - 3.0 * yy),
        HARMONIC_THREE[4] * x * (4.0 * zz - xx - yy),
        HARMONIC_THREE[5] * z * (xx - yy),
        HARMONIC_THREE[6] * x * (xx - 3.0 * yy),
    ]


def directions(x, y, z):
    length = jnp.sqrt(x * x + y * y + z * z)
    return harmonics(x / length, y / length, z / length)


def conic(mean_x, mean_y, mean_z, log_scale, quat):
    scale = [jnp.exp(s) for s in log_scale]
    norm = jnp.sqrt(quat[0] * quat[0] + quat[1] * quat[1] + quat[2] * quat[2] + quat[3] * quat[3])
    w, i, j, k = (q / norm for q in quat)
    rotation = [
        [1.0 - 2.0 * (j * j + k * k), 2.0 * (i * j - w * k), 2.0 * (i * k + w * j)],
        [2.0 * (i * j + w * k), 1.0 - 2.0 * (i * i + k * k), 2.0 * (j * k - w * i)],
        [2.0 * (i * k - w * j), 2.0 * (j * k + w * i), 1.0 - 2.0 * (i * i + j * j)],
    ]
    scaled = [[rotation[r][c] * scale[c] for c in range(3)] for r in range(3)]

    def sigma(r, c):
        return scaled[r][0] * scaled[c][0] + scaled[r][1] * scaled[c][1] + scaled[r][2] * scaled[c][2]

    s00, s01, s02, s11, s12, s22 = (
        sigma(0, 0), sigma(0, 1), sigma(0, 2), sigma(1, 1), sigma(1, 2), sigma(2, 2),
    )
    inverse_z = 1.0 / mean_z
    diag = FOCAL * inverse_z
    jac_xz = -FOCAL * mean_x * inverse_z * inverse_z
    jac_yz = -FOCAL * mean_y * inverse_z * inverse_z
    u0, u1, u2 = diag * s00 + jac_xz * s02, diag * s01 + jac_xz * s12, diag * s02 + jac_xz * s22
    v1, v2 = diag * s11 + jac_yz * s12, diag * s12 + jac_yz * s22
    cov_uu = u0 * diag + u2 * jac_xz + LOW_PASS
    cov_uv = u1 * diag + u2 * jac_yz
    cov_vv = v1 * diag + v2 * jac_yz + LOW_PASS
    determinant = cov_uu * cov_vv - cov_uv * cov_uv
    half = -0.5 * LOG2E
    xx = half * (cov_vv / determinant)
    xy = (-2.0 * half) * (cov_uv / determinant)
    yy = half * (cov_uu / determinant)
    return xx, xy, yy, FOCAL * mean_x * inverse_z, FOCAL * mean_y * inverse_z


def expanded(xx, xy, yy, pos_u, pos_v, log_opacity):
    x1 = -2.0 * xx * pos_u - xy * pos_v
    y1 = -2.0 * yy * pos_v - xy * pos_u
    one = xx * pos_u * pos_u + xy * pos_u * pos_v + yy * pos_v * pos_v + log_opacity
    return xx, xy, yy, x1, y1, one


def tile_shifts(across, side, height, width):
    column = lax.broadcasted_iota(jnp.int32, (across, LANES), 0).astype(F32)
    column = jnp.concatenate([column] * CAP, axis=0)
    row = lax.axis_index("ty").astype(F32)
    shift_x = (0.5 * width - 0.5 * side - 0.5) - side * column
    shift_y = jnp.full(column.shape, (0.5 * height - 0.5 * side - 0.5) - side * row, F32)
    return shift_x, shift_y


def request_kernel(owned, across, lists, count, order, request, slot, seen):
    base = lax.axis_index("ty") * across
    for o in range(across):
        seen[o] = 0
        for c in range(CAP):
            request[o, 0, c] = -1
    used = count[0, 0]

    def entry(k, _):
        @pl.when(k < used)
        def _():
            block = order[lists[0, 0, k]]
            home = block // owned
            local = block - home * owned
            home = home - base
            at = seen[home]
            seen[home] = at + 1
            request[home, 0, at] = local
            slot[k] = home * CAP + at

        return 0

    lax.fori_loop(0, slot.shape[0], entry, 0, unroll=True)
    free = 0
    for o in range(across):
        free = jnp.where(seen[o] < CAP, o * CAP + CAP - 1, free)

    def rest(k, _):
        slot[k] = free
        return 0

    lax.fori_loop(used, slot.shape[0], rest, 0)


def project_kernel(span, gaussians, out):
    def part(n, _):
        rows = pl.ds(pl.multiple_of(n * span, span), span)
        field = [gaussians[f, rows, :] for f in range(11)]
        light = -LOG2E * jnp.log(1.0 + jnp.exp(-field[10])) + float(np.log2(0.99))
        values = list(conic(field[0], field[1], field[2], field[3:6], field[6:10]))
        values.append(jnp.maximum(light, DARK))
        basis = directions(field[0], field[1], field[2])
        for ch in range(3):
            color = 0.5 + basis[0] * gaussians[11 + ch, rows, :]
            for m in range(1, 16):
                color = color + basis[m] * gaussians[11 + 3 * m + ch, rows, :]
            values.append(color)
        for f in range(9):
            out[f, rows, :] = values[f]
        return 0

    lax.fori_loop(0, gaussians.shape[1] // span, part, 0)


def asked_index(asked, across, s):
    c = s // across
    return asked[s - c * across, 0, c]


def serve_kernel(across, side, height, width, asked, projected, send, chosen):
    def pick(s, _):
        index = jnp.maximum(asked_index(asked, across, s), 0)
        for f in range(9):
            chosen[f, pl.ds(s, 1), :] = projected[f, pl.ds(index, 1), :]
        return 0

    lax.fori_loop(0, across * CAP, pick, 0, unroll=True)
    shift_x, shift_y = tile_shifts(across, side, height, width)
    rows = list(
        expanded(
            chosen[0], chosen[1], chosen[2], chosen[3] + shift_x, chosen[4] + shift_y, chosen[5]
        )
    ) + [chosen[6], chosen[7], chosen[8]]
    for c in range(CAP):
        for f in range(9):
            at = c * 8 + f if f < 8 else CAP * 8 + c
            send[:, at, :] = rows[f][c * across : (c + 1) * across]


def monomials(side):
    pixels = side * side
    lane = lax.broadcasted_iota(jnp.int32, (8, pixels), 1)
    row = lax.broadcasted_iota(jnp.int32, (8, pixels), 0)
    x = ((lane & (side - 1)) - side // 2).astype(F32)
    y = ((lane >> (side.bit_length() - 1)) - side // 2).astype(F32)
    mono = jnp.zeros((8, pixels), F32)
    for at, value in enumerate((x * x, x * y, y * y, x, y, jnp.ones_like(x))):
        mono = jnp.where(row == at, value, mono)
    blank = jnp.zeros((8, pixels), F32)
    rest = jnp.zeros((DEEP - 48, pixels), F32)
    return jnp.concatenate([mono, blank] * 3 + [rest], axis=0).astype(BF16)


def repeated(x, times):
    return jnp.concatenate([x] * times, axis=1)


def forward_kernel(
    side, slot, count, recv, target, table, checks, prefix, behind, dense,
    planes, spread, buf_a, buf_b, ends, part, hues_a, hues_b,
):
    lmax = slot.shape[0]
    per = lmax // SEGS
    pixels = prefix.shape[1]
    groups = pixels // LANES
    planes[...] = monomials(side)
    zero_rows = jnp.zeros((7, LANES), F32)
    dead = jnp.where(lax.broadcasted_iota(jnp.int32, (16, LANES), 0) == 5, DARK, 0.0)
    is_color = lax.broadcasted_iota(jnp.int32, (16, LANES), 0) >= 6

    def place(m, seg):
        s = slot[seg * per + m]
        live = seg * per + m < count[0, 0]
        o = s // CAP
        c = s - o * CAP
        head = recv[o, pl.ds(pl.multiple_of(c * 8, 8), 8), :]
        tail = recv[o, pl.ds(CAP * 8 + c, 1), :]
        rows = jnp.concatenate([head, tail, zero_rows], axis=0)
        rows = jnp.where(live, rows, dead)
        hi = rows.astype(BF16).astype(F32)
        rest = rows - hi
        mid = rest.astype(BF16).astype(F32)
        low = (rest - mid).astype(BF16).astype(F32)
        third = jnp.where(is_color, hi, low)
        stacked = jnp.concatenate([hi, mid, third, rows], axis=0)
        spread[pl.ds(m * (SEGS * LANES) + seg, LANES, stride=SEGS), :] = stacked.T

    for seg in range(SEGS):
        place(0, seg)

    width = planes.shape[1]
    pieces = -(-width // COLS)

    def product(n, buf, hues, p):
        rows = pl.ds(pl.multiple_of(n * CHUNK, CHUNK), CHUNK)
        if p == 0:
            whole = spread[rows, :]
            hues[...] = whole
            part[...] = whole.astype(BF16)
            table[rows, :] = part[...]
        cols = slice(p * COLS, min((p + 1) * COLS, width))
        buf[:, cols] = jnp.dot(part[...], planes[:, cols], preferred_element_type=F32)

    def blend(n, b, buf, hues, carry):
        light, red, green, blue = carry
        checks[n * (STEPS // SPAN) + b] = light
        for i in range(b * SPAN, (b + 1) * SPAN):
            rows = pl.ds(i * SEGS, SEGS)
            weight = light * jnp.exp2(buf[rows, :pixels])
            light = light - weight
            shades = [
                repeated(jnp.broadcast_to(hues[rows, 54 + c : 55 + c], (SEGS, LANES)), groups)
                for c in range(3)
            ]
            red = red + weight * shades[0]
            green = green + weight * shades[1]
            blue = blue + weight * shades[2]
        return light, red, green, blue

    for p in range(pieces):
        product(0, buf_a, hues_a, p)
    chunks = lmax * LANES // CHUNK
    turn = chunks // per
    share = SEGS // turn

    def pair(h, carry):
        n = 2 * h
        m = (n // turn + 1) % per
        for b in range(STEPS // SPAN):
            if b < pieces:
                product(n + 1, buf_b, hues_b, b)
            if b % 2 == 0 and b // 2 < 2 * share:
                place(m, (n % turn) * share + b // 2)
            carry = blend(n, b, buf_a, hues_a, carry)
        for b in range(STEPS // SPAN):
            if b < pieces:
                product(jnp.minimum(n + 2, chunks - 1), buf_a, hues_a, b)
            carry = blend(n + 1, b, buf_b, hues_b, carry)
        return carry

    start = (jnp.ones((SEGS, pixels), F32),) + (jnp.zeros((SEGS, pixels), F32),) * 3
    carry = lax.fori_loop(0, chunks // 2, pair, start)
    for f in range(4):
        ends[f] = carry[f]
    ahead = jnp.ones((1, pixels), F32)
    for seg in range(SEGS):
        prefix[pl.ds(seg, 1), :] = ahead
        ahead = ahead * ends[0, pl.ds(seg, 1), :]
    for ch in range(3):
        seen = jnp.zeros((1, pixels), F32)
        for seg in reversed(range(SEGS)):
            behind[ch, pl.ds(seg, 1), :] = seen
            seen = ends[1 + ch, pl.ds(seg, 1), :] + ends[0, pl.ds(seg, 1), :] * seen
        for j in range(groups):
            dense[pl.ds(ch * groups + j, 1), :] = seen[:, j * LANES : (j + 1) * LANES]
    dense[3 * groups :, :] = target[...]


def similarity(mean_a, mean_b, square_a, square_b, cross):
    var_a = square_a - mean_a * mean_a
    var_b = square_b - mean_b * mean_b
    covar = cross - mean_a * mean_b
    top = (2.0 * mean_a * mean_b + LUMA_TERM) * (2.0 * covar + CONTRAST_TERM)
    bottom = (mean_a * mean_a + mean_b * mean_b + LUMA_TERM) * (var_a + var_b + CONTRAST_TERM)
    return top / bottom


def tap(distance):
    weights = [float(np.exp(-((k - RIM) ** 2) / 4.5)) for k in range(TAPS)]
    value = jnp.exp(distance * distance * (-1.0 / 4.5)) * (1.0 / sum(weights))
    return jnp.where(jnp.abs(distance) <= RIM, value, 0.0)


def places(shape, dim):
    return lax.broadcasted_iota(jnp.int32, shape, dim)


def bands(side, padded):
    fold = LANES // side
    groups = side // fold
    reach = side + 2 * RIM
    shape = (3 * side, LANES)
    out = places(shape, 1)
    along = tap((places(shape, 0) - side - out + RIM).astype(F32))
    along = jnp.where(out < reach, along, 0.0)
    blank = jnp.zeros((side, LANES), F32)
    fa = jnp.concatenate(
        [
            jnp.concatenate(
                [along[h * side : (h + 1) * side] if u == t else blank for u in range(fold)], axis=1
            )
            for h in range(3)
            for t in range(fold)
        ],
        axis=0,
    )
    block = 3 * groups
    shape = (padded, fold * block)
    out, at = places(shape, 0), places(shape, 1)
    t = jnp.zeros(shape, jnp.int32)
    for k in range(1, fold):
        t = t + jnp.where(at >= k * block, 1, 0)
    source = (at - t * block) * fold + t - side
    fb = jnp.where(out < reach, tap((source - out + RIM).astype(F32)), 0.0)
    shape = (fold * groups, padded)
    row, out = places(shape, 0), places(shape, 1)
    t = jnp.zeros(shape, jnp.int32)
    for k in range(1, fold):
        t = t + jnp.where(row >= k * groups, 1, 0)
    source = (row - t * groups) * fold + t
    fc = jnp.where(out < reach, tap((out - RIM - source).astype(F32)), 0.0)
    shape = (LANES, LANES)
    out, at = places(shape, 0), places(shape, 1)
    back = tap((out - RIM - (at & (side - 1))).astype(F32))
    back = jnp.where(out < reach, back, 0.0)
    fd = jnp.concatenate(
        [jnp.where((at >= t * side) & (at < (t + 1) * side), back, 0.0) for t in range(fold)], axis=0
    )
    return fa, fb, fc, fd


def score_kernel(side, height, width, near, slope, loss):
    fa, fb, fc, fd = bands(side, -(-(side + 2 * RIM) // 8) * 8)
    rows3 = near[4].shape[0] // 2
    groups = rows3 // 3
    fold = LANES // side
    fields = [[], [], [], [], []]
    for v in range(3):
        strip = jnp.concatenate([near[3 * v + h] for h in range(3)], axis=1)
        image, target = strip[:rows3], strip[rows3:]
        for f, plane in enumerate([image, target, image * image, target * target, image * target]):
            fields[f].append(plane)
    stack = jnp.concatenate([fields[f][v] for f in range(5) for v in range(3)], axis=0)
    wide = jnp.dot(stack, fa, precision=HIGH, preferred_element_type=F32)
    columns = []
    for f in range(5):
        for ch in range(3):
            parts = []
            for t in range(fold):
                for v in range(3):
                    at = (f * 3 + v) * rows3 + ch * groups
                    parts.append(wide[at : at + groups, t * LANES : (t + 1) * LANES])
            columns.append(jnp.concatenate(parts, axis=0))
    tall = jnp.concatenate(columns, axis=1)
    maps = jnp.dot(fb, tall, precision=HIGH, preferred_element_type=F32)
    span = 3 * LANES
    score, pull = jax.vjp(similarity, *[maps[:, f * span : (f + 1) * span] for f in range(5)])
    parts = pull(jnp.full(score.shape, -STRUCT_WEIGHT, F32))
    row = lax.broadcasted_iota(jnp.int32, score.shape, 0)
    col = lax.broadcasted_iota(jnp.int32, (score.shape[0], LANES), 1)
    col = jnp.concatenate([col] * 3, axis=1)
    row_at = row - RIM + lax.axis_index("ty") * side
    col_at = col - RIM + lax.axis_index("tx") * side
    reach = side + 2 * RIM
    inside = (
        (row_at >= 0) & (row_at < height) & (col_at >= 0) & (col_at < width)
        & (row < reach) & (col < reach)
    )
    own = (row >= RIM) & (row < RIM + side) & (col >= RIM) & (col < RIM + side)
    coeffs = jnp.concatenate(
        [jnp.where(inside, parts[f], 0.0) for f in (0, 2, 4)], axis=1
    )
    low = jnp.dot(fc, coeffs, precision=HIGH, preferred_element_type=F32)
    rows = []
    for n in range(9):
        rows.append(
            jnp.concatenate(
                [
                    low[t * groups : (t + 1) * groups, n * LANES : (n + 1) * LANES]
                    for t in range(fold)
                ],
                axis=1,
            )
        )
    smooth = jnp.dot(
        jnp.concatenate(rows, axis=0), fd, precision=HIGH, preferred_element_type=F32
    )
    image, target = near[4][:rows3, :], near[4][rows3:, :]
    gap = image - target
    robust = jnp.sqrt(gap * gap + ROBUST_TERM)
    slope[...] = (
        smooth[:rows3]
        + 2.0 * image * smooth[rows3 : 2 * rows3]
        + target * smooth[2 * rows3 :]
        + (1.0 - STRUCT_WEIGHT) * gap / robust
    )
    total = (1.0 - STRUCT_WEIGHT) * jnp.sum(robust) + STRUCT_WEIGHT * jnp.sum(
        jnp.where(own, 1.0 - score, 0.0)
    )
    loss[...] = jnp.full(loss.shape, total, F32)


def score_entry(side, height, width, *refs):
    above, left, own, right, below = refs[:5]
    rows = own.shape[0]
    near = [above[h * rows : (h + 1) * rows, :] for h in range(3)]
    near += [left[...], own[...], right[...]]
    near += [below[h * rows : (h + 1) * rows, :] for h in range(3)]
    score_kernel(side, height, width, near, *refs[5:])


def backward_kernel(
    side, table, checks, prefix, behind, slope, reduce, stage,
    rhs, wide, grows, buf_a, buf_b, behinds, sums_a, sums_b, moments, part, lights,
):
    lmax = stage.shape[0]
    per = lmax // SEGS
    pixels = prefix.shape[1]
    groups = pixels // LANES
    chunks = lmax * LANES // CHUNK
    wide[...] = jnp.zeros_like(wide)
    for ch in range(3):
        for j in range(groups):
            lanes = pl.ds(j * LANES, LANES)
            wide[pl.ds(6 + ch, 1), lanes] = slope[pl.ds(ch * groups + j, 1), :]
    for ch in range(3):
        row = wide[pl.ds(6 + ch, 1), :]
        hi = row.astype(BF16).astype(F32)
        grows[ch] = jnp.broadcast_to(row, (SEGS, pixels))
        wide[pl.ds(6 + ch, 1), :] = hi
        wide[pl.ds(22 + ch, 1), :] = hi
        wide[pl.ds(38 + ch, 1), :] = row - hi
    rhs[:, :pixels] = monomials(side)
    rhs[:, pixels:] = wide[...].astype(BF16)

    def product(n, buf, p):
        if p == 0:
            part[...] = table[pl.ds(pl.multiple_of(n * CHUNK, CHUNK), CHUNK), :]
        cols = slice(p * COLS, (p + 1) * COLS)
        buf[:, cols] = jnp.dot(part[...], rhs[:, cols], preferred_element_type=F32)

    def reduced(sums):
        hi = sums[...].astype(BF16)
        low = (sums[...] - hi.astype(F32)).astype(BF16)
        both = jnp.dot(
            jnp.concatenate([hi, low], axis=0), reduce[...], preferred_element_type=F32
        )
        return both[:CHUNK] + both[CHUNK:]

    def record(n, value):
        moments[pl.ds(pl.multiple_of(n * CHUNK, CHUNK), CHUNK), :] = value

    lane = lax.broadcasted_iota(jnp.int32, (SEGS, LANES), 1)
    front = lane < LANES // 2
    even = (lane & (LANES // 4)) == 0

    def folded(a, b):
        return jnp.where(front, a, b) + pltpu.roll(jnp.where(front, b, a), LANES // 2, 1)

    def packed(a, b, c, d):
        ab, cd = folded(a, b), folded(c, d)
        ab = ab + pltpu.roll(ab, LANES - LANES // 4, 1)
        cd = cd + pltpu.roll(cd, LANES // 4, 1)
        return jnp.where(even, ab, cd)

    def block(b, buf, sums):
        first = b * SPAN * SEGS
        rows = [pl.ds(first + i * SEGS, SEGS) for i in range(SPAN)]
        totals = [[None] * 6 for _ in range(SPAN)]

        def add(i, f, value):
            totals[i][f] = value if totals[i][f] is None else totals[i][f] + value

        for q in reversed(range(groups // 2)):
            lanes = slice(q * 2 * LANES, (q + 1) * 2 * LANES)
            light = lights[b, :, lanes] * prefix[:, lanes]
            tints = [grows[ch, :, lanes] for ch in range(3)]
            alphas, weights = [], []
            for i in range(SPAN):
                alphas.append(jnp.exp2(buf[rows[i], lanes]))
                weights.append(light * alphas[i])
                light = light - weights[i]
            back = behinds[:, lanes]
            for i in reversed(range(SPAN)):
                gap = buf[rows[i], pixels + q * 2 * LANES : pixels + (q + 1) * 2 * LANES] - back
                back = back + alphas[i] * gap
                pull = weights[i] * gap
                add(i, 0, pull[:, LANES:])
                add(i, 1, totals[i][0])
                add(i, 2, totals[i][1])
                add(i, 0, pull[:, :LANES])
                if q > 0:
                    add(i, 1, totals[i][0])
                    add(i, 2, totals[i][1])
                for ch in range(3):
                    tint = weights[i] * tints[ch]
                    add(i, 3 + ch, tint[:, LANES:] + tint[:, :LANES])
            behinds[:, lanes] = back
        for i in range(SPAN):
            zero, one, two, red, green, blue = totals[i]
            sums[rows[i], 0:LANES] = zero
            sums[rows[i], LANES : 2 * LANES] = one
            sums[rows[i], 2 * LANES : 3 * LANES] = packed(red, green, blue, two)

    behinds[...] = behind[0] * grows[0] + behind[1] * grows[1] + behind[2] * grows[2]
    pieces = 2 * pixels // COLS
    for p in range(pieces):
        product(chunks - 1, buf_a, p)
    turn = chunks // per
    share = SEGS // turn

    def collect(m, seg):
        moved = moments[pl.ds(m * (SEGS * LANES) + seg, LANES, stride=SEGS), :]
        stage[seg * per + m] = moved[:, :16].T

    def half(n, ahead, buf, other, sums, last, seg):
        m = (n // turn + 1) % per
        spans = STEPS // SPAN
        lights[...] = checks[pl.ds(n * spans, spans)]
        for at in range(spans):
            for p in range(at * pieces // spans, (at + 1) * pieces // spans):
                product(ahead, other, p)
            if at == spans // 2:
                value = reduced(last)
            block(spans - 1 - at, buf, sums)
        record(n + 1, value)
        for q in range(share):
            collect(m, seg * share + q)

    def pair(h, _):
        n = chunks - 1 - 2 * h
        half(n, n - 1, buf_a, buf_b, sums_a, sums_b, n % turn)
        half(n - 1, jnp.maximum(n - 2, 0), buf_b, buf_a, sums_b, sums_a, n % turn - 1)
        return 0

    lax.fori_loop(0, chunks // 2, pair, 0)
    record(0, reduced(sums_b))
    for seg in range(SEGS):
        collect(0, seg)


def deliver_kernel(slot, stage, *refs):
    reply = refs[-1]
    column = refs[0][...]
    for share in refs[1:-1]:
        column = column + share[...]
    for o in range(reply.shape[0]):
        reply[o, pl.ds(reply.shape[1] - 1, 1), :] = column[:1]
    for k in range(slot.shape[0]):
        s = slot[k]
        o = s // CAP
        c = s - o * CAP
        reply[o, pl.ds(pl.multiple_of(c * 8, 8), 8), :] = stage[k, :8, :]
        reply[o, pl.ds(CAP * 8 + c, 1), :] = stage[k, 8:9, :]


def gather_kernel(
    across, side, height, width, asked, got, gaussians, grads, loss, sums, zeros, pieces, wanted, sem
):
    owned = gaussians.shape[1]
    parts = owned // 8
    shares = got[:, got.shape[1] - 1, :]
    loss[0] = jnp.sum(shares[:, :1]) * (1.0 / (3.0 * height * width))
    zeros[...] = jnp.zeros_like(zeros)
    sums[...] = jnp.zeros_like(sums)
    for g in range(parts + 1):
        wanted[g] = 0
    for s in range(across * CAP):
        c, t = divmod(s, across)
        index = asked[t, 0, c]
        index = jnp.where(index >= 0, index, owned)
        wanted[index // 8] = 1
        row = pl.ds(index, 1)
        for f in range(9):
            at = c * 8 + f if f < 8 else CAP * 8 + c
            sums[f, row, :] = got[t, at : at + 1, :]
        sums[9, row, :] = jnp.full((1, LANES), t + 1.0, F32)

    def target(g):
        return grads.at[:, pl.ds(pl.multiple_of(g * 8, 8), 8), :]

    def blank(g, _):
        @pl.when(wanted[g] == 0)
        def _():
            pltpu.make_async_copy(zeros, target(g), sem.at[g]).start()

        return 0

    lax.fori_loop(0, parts, blank, 0)
    row_at = lax.axis_index("ty").astype(F32)
    shift_y = (0.5 * height - 0.5 * side - 0.5) - side * row_at

    def solve(g):
        rows = pl.ds(pl.multiple_of(g * 8, 8), 8)
        field = [gaussians[f, rows, :] for f in range(11)]
        tile = sums[9, rows, :]
        live = tile > 0.0
        shift_x = (0.5 * width - 0.5 * side - 0.5) - side * (tile - 1.0)

        def put(f, value):
            pieces[g, f] = jnp.where(live, value, 0.0)

        def shaped(x, y, z, log_scale, quat):
            xx, xy, yy, pos_u, pos_v = conic(x, y, z, log_scale, quat)
            return expanded(xx, xy, yy, pos_u + shift_x, pos_v + shift_y, jnp.zeros_like(x))

        _, pull = jax.vjp(shaped, *field[:3], field[3:6], field[6:10])
        moments = [LN2 * sums[f, rows, :] for f in range(6)]
        gx, gy, gz, gscale, gquat = pull(tuple(moments))
        basis, pull_basis = jax.vjp(directions, *field[:3])
        tints = [sums[6 + ch, rows, :] for ch in range(3)]
        tilts = []
        for m in range(16):
            tilt = None
            for ch in range(3):
                term = tints[ch] * gaussians[11 + 3 * m + ch, rows, :]
                tilt = term if tilt is None else tilt + term
                put(11 + 3 * m + ch, tints[ch] * basis[m])
            tilts.append(tilt)
        dx, dy, dz = pull_basis(tilts)
        put(0, gx + dx)
        put(1, gy + dy)
        put(2, gz + dz)
        for f in range(3):
            put(3 + f, gscale[f])
        for f in range(4):
            put(6 + f, gquat[f])
        put(10, moments[5] * (LOG2E / (1.0 + jnp.exp(field[10]))))
        pltpu.make_async_copy(pieces.at[g], target(g), sem.at[g]).start()

    def part(g, _):
        @pl.when(wanted[g] > 0)
        def _():
            solve(g)

        return 0

    lax.fori_loop(0, parts, part, 0)

    def finish(g, _):
        pltpu.make_async_copy(zeros, target(g), sem.at[g]).wait()
        return 0

    lax.fori_loop(0, parts, finish, 0)


def moment_columns(side):
    lane = np.arange(LANES)
    x = lane % side - side // 2
    t = lane // side - side // 2
    step = LANES // side
    one = np.ones_like(x)
    out = np.zeros((3 * LANES, LANES))
    out[:LANES, :6] = np.stack([x * x, x * t, t * t, x, t, one], axis=1)
    out[LANES : 2 * LANES, 1] = step * x
    out[LANES : 2 * LANES, 2] = 2 * step * t - step * step
    out[LANES : 2 * LANES, 4] = step
    quarter = LANES // 4
    for n, (column, weight) in enumerate(((6, 1), (8, 1), (7, 1), (2, 2 * step * step))):
        at = 2 * LANES + n * quarter
        out[at : at + quarter, column] = weight
    return out.astype(ml_dtypes.bfloat16)


def shifted(x, axis):
    size = lax.axis_size(axis)
    up = [(i, i + 1) for i in range(size - 1)]
    return lax.ppermute(x, axis, up), lax.ppermute(x, axis, [(j, i) for i, j in up])


def per_device(gaussians, tile_lists, tile_counts, depth_order, target):
    owned, fields, block = gaussians.shape
    lmax = tile_lists.shape[2]
    side = target.shape[1]
    pixels = side * side
    groups = pixels // LANES
    across = lax.axis_size("tx")
    down = lax.axis_size("ty")
    height = side * lax.axis_size("ty")
    width = side * across
    slots = across * CAP
    depth = -(-(CAP * 9 + 1) // 8) * 8
    f32 = functools.partial(jax.ShapeDtypeStruct, dtype=F32)
    i32 = functools.partial(jax.ShapeDtypeStruct, dtype=jnp.int32)
    reduce = jnp.asarray(moment_columns(side))

    fieldwise = jnp.transpose(gaussians, (1, 0, 2))
    request, slot = pl.pallas_call(
        functools.partial(request_kernel, owned, across),
        out_shape=(i32((across, 1, LANES)), i32((lmax,))),
        in_specs=[SMEM] * 3,
        out_specs=(SMEM, SMEM),
        scratch_shapes=[pltpu.SMEM((across,), jnp.int32)],
        name="request",
    )(tile_lists, tile_counts, depth_order)
    asked = lax.all_to_all(request, "tx", split_axis=0, concat_axis=0, tiled=True)
    projected = pl.pallas_call(
        functools.partial(project_kernel, 16),
        out_shape=f32((9, owned, block)),
        in_specs=[VMEM],
        out_specs=VMEM,
        compiler_params=PARAMS,
        name="project",
    )(fieldwise)
    send = pl.pallas_call(
        functools.partial(serve_kernel, across, side, float(height), float(width)),
        out_shape=f32((across, depth, block)),
        in_specs=[SMEM, VMEM],
        out_specs=VMEM,
        scratch_shapes=[pltpu.VMEM((9, slots, block), F32)],
        compiler_params=PARAMS,
        name="serve",
    )(asked, projected)
    recv = lax.all_to_all(send, "tx", split_axis=0, concat_axis=0, tiled=True)
    chunks = lmax * block // CHUNK
    table, checks, prefix, behind, dense = pl.pallas_call(
        functools.partial(forward_kernel, side),
        out_shape=(
            jax.ShapeDtypeStruct((lmax * block, DEEP), BF16),
            f32((chunks * (STEPS // SPAN), SEGS, pixels)),
            f32((SEGS, pixels)),
            f32((3, SEGS, pixels)),
            f32((6 * groups, LANES)),
        ),
        in_specs=[SMEM, SMEM, VMEM, VMEM],
        out_specs=(VMEM,) * 5,
        scratch_shapes=[
            pltpu.VMEM((DEEP, pixels), BF16),
            pltpu.VMEM((lmax * block, DEEP), F32),
            pltpu.VMEM((CHUNK, pixels), F32),
            pltpu.VMEM((CHUNK, pixels), F32),
            pltpu.VMEM((4, SEGS, pixels), F32),
            pltpu.VMEM((CHUNK, DEEP), BF16),
            pltpu.VMEM((CHUNK, DEEP), F32),
            pltpu.VMEM((CHUNK, DEEP), F32),
        ],
        compiler_params=PARAMS,
        name="forward",
    )(slot, tile_counts, recv, target.reshape(3 * groups, LANES))
    left, right = shifted(dense, "tx")
    above, below = shifted(jnp.concatenate([left, dense, right], axis=0), "ty")
    slope, part = pl.pallas_call(
        functools.partial(score_entry, side, height, width),
        out_shape=(f32((3 * groups, LANES)), f32((8, LANES))),
        in_specs=[VMEM] * 5,
        out_specs=(VMEM, VMEM),
        compiler_params=PARAMS,
        name="score",
    )(above, left, dense, right, below)
    shares = [
        lax.ppermute(part, "ty", [(i, (i + k) % down) for i in range(down)]) for k in range(1, down)
    ]
    stage = pl.pallas_call(
        functools.partial(backward_kernel, side),
        out_shape=f32((lmax, 16, LANES)),
        in_specs=[VMEM] * 6,
        out_specs=VMEM,
        scratch_shapes=[
            pltpu.VMEM((DEEP, 2 * pixels), BF16),
            pltpu.VMEM((DEEP, pixels), F32),
            pltpu.VMEM((3, SEGS, pixels), F32),
            pltpu.VMEM((CHUNK, 2 * pixels), F32),
            pltpu.VMEM((CHUNK, 2 * pixels), F32),
            pltpu.VMEM((SEGS, pixels), F32),
            pltpu.VMEM((CHUNK, 3 * LANES), F32),
            pltpu.VMEM((CHUNK, 3 * LANES), F32),
            pltpu.VMEM((lmax * block + CHUNK, LANES), F32),
            pltpu.VMEM((CHUNK, DEEP), BF16),
            pltpu.VMEM((STEPS // SPAN, SEGS, pixels), F32),
        ],
        compiler_params=PARAMS,
        name="backward",
    )(table, checks, prefix, behind, slope, reduce)
    reply = pl.pallas_call(
        deliver_kernel,
        out_shape=f32((across, depth, block)),
        in_specs=[SMEM] + [VMEM] * (1 + down),
        out_specs=VMEM,
        compiler_params=PARAMS,
        name="deliver",
    )(slot, stage, part, *shares)
    got = lax.all_to_all(reply, "tx", split_axis=0, concat_axis=0, tiled=True)
    grads, loss = pl.pallas_call(
        functools.partial(gather_kernel, across, side, float(height), float(width)),
        out_shape=(f32((fields, owned, block)), f32((1,))),
        in_specs=[SMEM, VMEM, VMEM],
        out_specs=(ANY, SMEM),
        scratch_shapes=[
            pltpu.VMEM((10, owned + 8, block), F32),
            pltpu.VMEM((fields, 8, block), F32),
            pltpu.VMEM((owned // 8, fields, 8, block), F32),
            pltpu.SMEM((owned // 8 + 1,), jnp.int32),
            pltpu.SemaphoreType.DMA((owned // 8,)),
        ],
        compiler_params=PARAMS,
        name="gather",
    )(asked, got, fieldwise)
    return (jnp.transpose(grads, (1, 0, 2)), loss[0])


def solution(mesh):
    return jax.shard_map(
        per_device,
        mesh=mesh,
        in_specs=(
            P(("ty", "tx"), None, None),
            P("ty", "tx", None),
            P("ty", "tx"),
            P(),
            P(None, "ty", "tx"),
        ),
        out_specs=(P(("ty", "tx"), None, None), P()),
        check_vma=False,
    )
```
